32 devices in a mesh: ctx: 16 (over z, y, core), fsdp: 2 (over x).
Axes of the slice: x: 2, y: 2, z: 4, core: 2. Of those that a mesh axis runs over, the one named last changes fastest.
Arguments:
- tokens: bfloat16 [2, 4096, 1280], P('fsdp', 'ctx'), may hold values from -6 to 6
- cotangent: bfloat16 [2, 4096, 1280], P('fsdp', 'ctx'), may hold values from -6 to 6
- lengths: int32 [2, 8], P('fsdp'), may hold values from 1 to 2048, as said below
- deal: int32 [32], replicated, may hold values from 0 to 31, as said below
- gain_attn: float32 [1280], P('fsdp'), may hold values from 0.5 to 1.5
- query_weight: float32 [1280, 1280], P('fsdp'), may hold values from -0.25 to 0.25
- query_bias: float32 [1280], P('fsdp'), may hold values from -3 to 3
- key_weight: float32 [1280, 1280], P('fsdp'), may hold values from -0.15625 to 0.15625
- value_weight: float32 [1280, 1280], P('fsdp'), may hold values from -0.15625 to 0.15625
- value_bias: float32 [1280], P('fsdp'), may hold values from -3 to 3
- query_scale: float32 [80], P('fsdp'), may hold values from -0.5 to 1.5
- proj_weight: float32 [1280, 1280], P('fsdp'), may hold values from -0.625 to 0.625
- gain_ffn: float32 [1280], P('fsdp'), may hold values from 0.5 to 1.5
- up_weight: float32 [1280, 1280], P('fsdp'), may hold values from -0.15625 to 0.15625
- down_weight: float32 [1280, 1280], P('fsdp'), may hold values from -0.15625 to 0.15625
Outputs:
- layer_out: bfloat16 [2, 4096, 1280], P('fsdp', 'ctx')
- grad_tokens: float32 [2, 4096, 1280], P('fsdp', 'ctx')
- grad_gain_attn: float32 [1280], P('fsdp')
- grad_query_weight: float32 [1280, 1280], P('fsdp')
- grad_query_bias: float32 [1280], P('fsdp')
- grad_key_weight: float32 [1280, 1280], P('fsdp')
- grad_value_weight: float32 [1280, 1280], P('fsdp')
- grad_value_bias: float32 [1280], P('fsdp')
- grad_query_scale: float32 [80], P('fsdp')
- grad_proj_weight: float32 [1280, 1280], P('fsdp')
- grad_gain_ffn: float32 [1280], P('fsdp')
- grad_up_weight: float32 [1280, 1280], P('fsdp')
- grad_down_weight: float32 [1280, 1280], P('fsdp')
The draws below stay inside these ranges and needn't reach their ends.
Inputs may be any that keep to these rules, and one draw needn't show every extreme that they name: `lengths`: each row sums to 4096; its first or its last entry is 2048. `deal`: a permutation; the entries at positions 2 i and 2 i + 1 are j and 31 - j for some j below 16.
All inputs are finite; a program needn't handle non-finite values.
Results may differ from the reference program's by a relative error of at most 0.022.
Values may be sent and summed in bfloat16 or wider, within the bound.
A program may use at most 192 MiB of HBM per device.

```python
import math
import jax
import jax.numpy as jnp
from jax import lax

D = 1280
H = 16
HD = 80
FF = 1280
TOK_DEV = 256
BLK = 128
SEQS = 8
GROUP = 4096
NB = 32
N_FSDP = 2


def draw_lengths(key, part):
    key = jax.random.fold_in(key, 11)

    def per_group(group_key):
        cut_key, side_key = jax.random.split(group_key)
        half = GROUP // 2
        cuts = jax.random.permutation(cut_key, half - 1)[:SEQS - 2] + 1
        cuts = jnp.sort(cuts).astype(jnp.int32)
        edges = jnp.concatenate([jnp.zeros((1,), jnp.int32), cuts, jnp.full((1,), half, jnp.int32)])
        others = (edges[1:] - edges[:-1]).astype(jnp.int32)
        longest = jnp.full((1,), half, jnp.int32)
        side = jax.random.randint(side_key, (), 0, 2)
        front = jnp.concatenate([longest, others])
        back = jnp.concatenate([others, longest])
        return jnp.where(side == 1, front, back).astype(jnp.int32)
    group_keys = jax.random.split(key, N_FSDP)
    return jax.vmap(per_group)(group_keys)


def draw_deal(key, part):
    key = jax.random.fold_in(key, 23)
    pairs = jax.random.permutation(key, NB // 2).astype(jnp.int32)
    pairs = pairs.reshape(NB // (TOK_DEV // BLK), TOK_DEV // BLK // 2)
    stacked = jnp.stack([pairs, NB - 1 - pairs], axis=-1)
    return stacked.reshape(NB).astype(jnp.int32)


def block_scale(stream_key, shape, pieces, low, top_value):
    def one(dim, parts):
        steps = jax.random.uniform(jax.random.fold_in(jax.random.fold_in(stream_key, 6), dim), (parts,), jnp.float32, low / len(pieces), top_value / len(pieces))
        return jnp.repeat(jnp.exp(steps), shape[dim] // parts).reshape((-1,) + (1,) * (len(shape) - dim - 1))

    loudness = one(*pieces[0])
    for cut in pieces[1:]:
        loudness = loudness * one(*cut)
    return loudness


def bell_draw(own_key, shape, deviation, reach, shards=(), dtype=jnp.bfloat16):
    values = deviation * jax.random.normal(own_key, shape, jnp.float32)
    if shards:
        values = values * block_scale(own_key, shape, shards, -0.22, 0.18)
    return jnp.clip(values, -reach, reach).astype(dtype)


def setup_inputs(seed: int = 0) -> dict:
    key_list = jax.random.split(jax.random.key(seed), 16)
    tokens = bell_draw(key_list[0], (N_FSDP, GROUP, D), 1.0, 6.0, ((0, 2), (1, 16)))
    cotangent = bell_draw(key_list[1], (N_FSDP, GROUP, D), 1.0, 6.0, ((0, 2), (1, 16)))
    lengths = draw_lengths(jax.random.fold_in(key_list[15], 71), 0)
    deal = draw_deal(jax.random.fold_in(key_list[15], 71), 0)
    gain_attn = jnp.clip(1.0 + 0.1 * jax.random.normal(key_list[4], (D,), jnp.float32), 0.5, 1.5)
    query_weight = bell_draw(key_list[5], (D, D), (D // 2) ** -0.5, 0.25, ((0, 2),), jnp.float32)
    query_bias = bell_draw(key_list[6], (D,), 0.5, 3.0, ((0, 2),), jnp.float32)
    key_weight = bell_draw(key_list[7], (D, D), D ** -0.5, 0.15625, ((0, 2),), jnp.float32)
    value_weight = bell_draw(key_list[8], (D, D), D ** -0.5, 0.15625, ((0, 2),), jnp.float32)
    value_bias = bell_draw(key_list[9], (D,), 0.5, 3.0, ((0, 2),), jnp.float32)
    query_scale = jnp.clip(-0.5 + 2.0 * jax.random.uniform(key_list[10], (HD,), jnp.float32) ** block_scale(key_list[10], (HD,), ((0, 2),), -0.2, 0.2), -0.5, 1.5)
    proj_weight = bell_draw(key_list[11], (D, D), (D // 16) ** -0.5, 0.625, ((0, 2),), jnp.float32)
    gain_ffn = jnp.clip(1.0 + 0.1 * jax.random.normal(key_list[12], (D,), jnp.float32), 0.5, 1.5)
    up_weight = bell_draw(key_list[13], (D, FF), D ** -0.5, 0.15625, ((0, 2),), jnp.float32)
    down_weight = bell_draw(key_list[14], (FF, D), FF ** -0.5, 0.15625, ((0, 2),), jnp.float32)
    return dict(tokens=tokens, cotangent=cotangent, lengths=lengths, deal=deal, gain_attn=gain_attn, query_weight=query_weight, query_bias=query_bias, key_weight=key_weight, value_weight=value_weight, value_bias=value_bias, query_scale=query_scale, proj_weight=proj_weight, gain_ffn=gain_ffn, up_weight=up_weight, down_weight=down_weight)


EPS = 1e-06
LOG2E = 1.442695041
NEG = -1e+30

@jax.custom_vjp
def low(v):
    return lax.optimization_barrier(v.astype(jnp.bfloat16)).astype(jnp.float32)

@jax.custom_vjp
def low_back(v):
    return v

def low_keep(v):
    return (low(v), None)

def low_pass(kept, grad):
    return (grad,)

def back_keep(v):
    return (v, None)

def back_low(kept, grad):
    return (low(grad),)
low.defvjp(low_keep, low_pass)
low_back.defvjp(back_keep, back_low)

def matmul(left, right):
    return jnp.dot(left, right, precision=lax.Precision.HIGHEST)

def rms_scale(values):
    return lax.rsqrt(lax.optimization_barrier(jnp.mean(values * values, axis=-1, keepdims=True)) + EPS)

def softplus(values):
    return jnp.log(1.0 + jnp.exp(values))

def attention(queries, key_heads, value_heads, position, segment):
    row_count = queries.shape[0]
    block_rows = min(512, row_count)

    def per_block(block_id):
        first_row = (block_id * block_rows).astype(jnp.int32)
        query_blk = lax.dynamic_slice_in_dim(queries, first_row, block_rows, 0)
        query_pos = lax.dynamic_slice_in_dim(position, first_row, block_rows, 0)
        query_seg = lax.dynamic_slice_in_dim(segment, first_row, block_rows, 0)
        scores = low_back(jnp.einsum('qhd,khd->hqk', query_blk, key_heads, precision=lax.Precision.HIGHEST))
        visible = (query_seg[:, None] == segment[None, :]) & (position[None, :] <= query_pos[:, None])
        scores = jnp.where(visible[None], scores, NEG)
        row_max = lax.optimization_barrier(jnp.max(scores, axis=-1, keepdims=True))
        exponent = jnp.exp(scores - row_max)
        weights = exponent / lax.optimization_barrier(jnp.sum(exponent, axis=-1, keepdims=True))
        return jnp.einsum('hqk,khd->qhd', low(weights), value_heads, precision=lax.Precision.HIGHEST)
    block_ids = jnp.arange(row_count // block_rows).astype(jnp.int32)
    result = lax.map(jax.checkpoint(per_block), block_ids)
    return result.reshape(row_count, H * HD)

def group_forward(tokens_nat, lengths_row, masters):
    gain_a, w_query, b_query, w_key, w_value, b_value, q_param, w_proj, gain_f, w_up, w_down = [low(item) for item in masters]
    row_count = tokens_nat.shape[0]
    position = jnp.arange(row_count).astype(jnp.int32)
    seq_ends = jnp.cumsum(lengths_row).astype(jnp.int32)
    segment = lax.optimization_barrier(jnp.sum((position[:, None] >= seq_ends[None, :]).astype(jnp.int32), axis=1)).astype(jnp.int32)
    normed = low(tokens_nat * rms_scale(tokens_nat) * gain_a)
    factor = jnp.tile(softplus(q_param) * (LOG2E / math.sqrt(HD)), H)
    queries = low(low_back(matmul(normed, w_query) + b_query) * factor)
    key_rows = low_back(low(matmul(normed, w_key)))
    value_rows = low_back(low(matmul(normed, w_value) + b_value))
    mixed = attention(queries.reshape(row_count, H, HD), key_rows.reshape(row_count, H, HD), value_rows.reshape(row_count, H, HD), position, segment)
    mixed = low_back(low(mixed))
    hidden = tokens_nat + low_back(matmul(mixed, w_proj))
    normed_ff = low(hidden * rms_scale(hidden) * gain_f)
    up_proj = low_back(matmul(normed_ff, w_up))
    activated = low(up_proj * jax.nn.sigmoid(up_proj))
    return hidden + matmul(activated, w_down)

def reference(tokens, cotangent, lengths, deal, gain_attn, query_weight, query_bias, key_weight, value_weight, value_bias, query_scale, proj_weight, gain_ffn, up_weight, down_weight):
    inverse = jnp.argsort(deal).astype(jnp.int32)
    deal_idx = deal.astype(jnp.int32)

    def to_natural(row_data):
        return row_data.reshape(NB, BLK, -1)[inverse].reshape(GROUP, -1)

    def to_dealt(row_data):
        return row_data.reshape(NB, BLK, -1)[deal_idx].reshape(GROUP, -1)
    masters = (gain_attn, query_weight, query_bias, key_weight, value_weight, value_bias, query_scale, proj_weight, gain_ffn, up_weight, down_weight)
    inputs = tuple((to_natural(tokens[group_id].astype(jnp.float32)) for group_id in range(N_FSDP)))

    def forward(group_inputs, weights):
        return tuple((group_forward(group_inputs[group_id], lengths[group_id], weights) for group_id in range(N_FSDP)))
    outputs, pullback = jax.vjp(forward, inputs, masters)
    cot_rows = tuple((to_natural(cotangent[group_id].astype(jnp.float32)) for group_id in range(N_FSDP)))
    grad_inputs, grad_masters = pullback(cot_rows)
    layer_out = jnp.stack([to_dealt(item) for item in outputs]).astype(jnp.bfloat16)
    grad_tokens = jnp.stack([to_dealt(item) for item in grad_inputs])
    return (layer_out, grad_tokens, grad_masters[0], grad_masters[1], grad_masters[2], grad_masters[3], grad_masters[4], grad_masters[5], grad_masters[6], grad_masters[7], grad_masters[8], grad_masters[9], grad_masters[10])
```

```python
import functools
import math

import jax
import jax.numpy as jnp
from jax import lax
from jax.experimental import pallas as pl
from jax.experimental.pallas import tpu as pltpu
from jax.sharding import PartitionSpec as P

H = 16
HD = 80
BLK = 128
D = 1280
EPS = 1e-06
LOG2E = 1.442695041
NEG = -1e30
MESH = pl.DeviceIdType.MESH
F32 = jnp.float32
BF16 = jnp.bfloat16
VMEM = pltpu.VMEM
MIB = 1 << 20

NN = (((1,), (0,)), ((), ()))
NT = (((1,), (1,)), ((), ()))
TN = (((0,), (0,)), ((), ()))


def dot(left, right, dims=NN):
    return lax.dot_general(left, right, dims, preferred_element_type=F32)


def al(value, multiple):
    return pl.multiple_of(value, multiple)


def in_vmem():
    return pl.BlockSpec(memory_space=pltpu.VMEM)


def in_smem():
    return pl.BlockSpec(memory_space=pltpu.SMEM)


def in_any():
    return pl.BlockSpec(memory_space=pl.ANY)


def gather_kernel(
    n, nf, x_ref, wh_ref, vec_ref, wo_ref, w1_ref, w2_ref,
    a_out, qkv_out, mats_out, vecs_out,
    abuf, whbuf, wht, vecbuf, stage, wcast,
    ag_send, ag_recv, wh_send, wh_recv, vec_send, vec_recv,
    ld_sem, own_sem, mx_send, mx_recv, ms_send, ms_recv, a_sem,
):
    c = lax.axis_index("ctx")
    f = lax.axis_index("fsdp")
    rows = wh_ref.shape[0]
    part = rows // 2
    zlen = n // 4
    z, y, core = c // 4, (c // 2) % 2, c % 2

    def idx(zz, yy, cc):
        return (zz * 2 + yy) * 2 + cc

    up, down = idx(z + 1, y, core), idx(z - 1, y, core)
    ypeer, twin = idx(z, 1 - y, core), idx(z, y, 1 - core)
    has_up, has_down = z < zlen - 1, z > 0
    targets = (up, down, ypeer, twin)
    guards = (has_up, has_down, None, None)
    fpeers = [(f + s) % nf for s in range(1, nf)]

    barrier = pltpu.get_barrier_semaphore()
    for target, guard in zip(targets, guards):
        def greet(target=target):
            pl.semaphore_signal(barrier, inc=1, device_id=(target, f), device_id_type=MESH)
        if guard is None:
            greet()
        else:
            pl.when(guard)(greet)
    for peer in fpeers:
        pl.semaphore_signal(barrier, inc=1, device_id=(c, peer), device_id_type=MESH)
    pl.semaphore_wait(barrier, 1 + nf + jnp.minimum(z, 1) + jnp.minimum(zlen - 1 - z, 1))

    def ag_copy(way, origin, i):
        return pltpu.make_async_remote_copy(
            src_ref=abuf.at[origin, i], dst_ref=abuf.at[origin, i],
            send_sem=ag_send.at[way, origin, i], recv_sem=ag_recv.at[origin, i],
            device_id=(targets[way], f), device_id_type=MESH,
        )

    def send(way, origin, i, guard=None):
        guards_here = [g for g in (guards[way], guard) if g is not None]
        def go():
            ag_copy(way, origin, i).start()
        if guards_here:
            pl.when(functools.reduce(jnp.logical_and, guards_here))(go)
        else:
            go()

    def arrive(origin, i):
        ag_copy(3, origin, i).wait_recv()

    for i in range(2):
        x = x_ref[pl.ds(i * BLK, BLK), :].astype(F32)
        scale = lax.rsqrt(jnp.mean(x * x, axis=-1, keepdims=True) + EPS)
        abuf[c, i] = (x * scale).astype(BF16)
        for way in range(4):
            send(way, c, i)

    def wh_copy(s, peer):
        return pltpu.make_async_remote_copy(
            src_ref=wh_ref, dst_ref=whbuf.at[pl.ds(al(f * rows, 16), rows)],
            send_sem=wh_send.at[s], recv_sem=wh_recv.at[s],
            device_id=(c, peer), device_id_type=MESH,
        )

    def vec_copy(s, peer):
        return pltpu.make_async_remote_copy(
            src_ref=vec_ref, dst_ref=vecbuf.at[f],
            send_sem=vec_send.at[s], recv_sem=vec_recv.at[s],
            device_id=(c, peer), device_id_type=MESH,
        )

    for s, peer in enumerate(fpeers):
        wh_copy(s, peer).start()
        vec_copy(s, peer).start()
    whbuf[pl.ds(al(f * rows, 16), rows), :] = wh_ref[...]
    vecbuf[f] = vec_ref[...]

    shards = (wo_ref, w1_ref, w2_ref)
    steps = [(m, h) for h in range(2) for m in range(3)]

    def half_of(h):
        return (core + h) % 2

    def load(step):
        m, h = steps[step]
        return pltpu.make_async_copy(
            shards[m].at[pl.ds(al(half_of(h) * part, 16), part)],
            stage.at[step % 2], ld_sem.at[step % 2],
        )

    def mx_copy(m, s, peer, source):
        return pltpu.make_async_remote_copy(
            src_ref=wcast.at[m, pl.ds(al(core * part, 16), part)],
            dst_ref=mats_out.at[m, pl.ds(al(source * rows + core * part, 16), part)],
            send_sem=mx_send.at[m, s], recv_sem=mx_recv.at[m, s],
            device_id=(c, peer), device_id_type=MESH,
        )

    def own_copy(m):
        return pltpu.make_async_copy(
            wcast.at[m], mats_out.at[m, pl.ds(al(f * rows, 16), rows)], own_sem.at[m]
        )

    load(0).start()
    for step, (m, h) in enumerate(steps):
        if step + 1 < len(steps):
            load(step + 1).start()
        load(step).wait()
        chunk = part // 4 if part % 64 == 0 else part
        @pl.loop(0, part // chunk)
        def _(t, m=m, h=h, step=step):
            wcast[m, pl.ds(al(half_of(h) * part + t * chunk, 16), chunk), :] = stage[
                step % 2, pl.ds(al(t * chunk, 16), chunk), :
            ].astype(BF16)
        if h == 0:
            for s, peer in enumerate(fpeers):
                mx_copy(m, s, peer, f).start()
        else:
            own_copy(m).start()

    for s, peer in enumerate(fpeers):
        wh_copy(s, peer).wait_recv()
        vec_copy(s, peer).wait_recv()
    wht[...] = whbuf[...].astype(F32).T.astype(BF16)
    vecs_out[...] = vecbuf[...]

    def a_copy(origin):
        return pltpu.make_async_copy(abuf.at[origin], a_out.at[origin], a_sem.at[origin])

    def project(origin):
        block = abuf[origin].reshape(2 * BLK, D)
        qkv_out[origin] = dot(wht[: 3 * HD, :], block, NT)
        a_copy(origin).start()

    def level(k):
        if k == 0:
            return [(z, None)]
        return [(z + k, z + k < zlen), (z - k, z - k >= 0)]

    def when(guard, body):
        if guard is None:
            body()
        else:
            pl.when(guard)(body)

    def pair_arrivals(k, i):
        for zz, guard in level(k):
            def body(zz=zz):
                origin = idx(zz, 1 - y, core)
                arrive(origin, i)
                send(3, origin, i)
            when(guard, body)

    def compute(k):
        for zz, guard in level(k):
            def body(zz=zz):
                for yy in (y, 1 - y):
                    for i in range(2):
                        arrive(idx(zz, yy, 1 - core), i)
                @pl.loop(0, 4)
                def _(t):
                    project(zz * 4 + t)
            when(guard, body)

    def ms_copy(m, s, source):
        where = pl.ds(al(source * rows + core * part, 16), part)
        return pltpu.make_async_remote_copy(
            src_ref=mats_out.at[m, where], dst_ref=mats_out.at[m, where],
            send_sem=ms_send.at[m, s], recv_sem=ms_recv.at[m, s],
            device_id=(twin, f), device_id_type=MESH,
        )

    def pass_matrix(m):
        for s, peer in enumerate(fpeers):
            source = (f + nf - 1 - s) % nf
            mx_copy(m, s, peer, source).wait_recv()
            ms_copy(m, s, source).start()

    for k in range(1, zlen):
        for i in range(2):
            for sign, (zz, guard) in zip((1, -1), level(k)):
                def body(zz=zz, sign=sign):
                    origin = idx(zz, y, core)
                    arrive(origin, i)
                    send(1 if sign == 1 else 0, origin, i)
                    send(2, origin, i)
                    send(3, origin, i)
                when(guard, body)
            pair_arrivals(k - 1, i)
        compute(k - 1)
        if k == 2:
            pass_matrix(0)
    for i in range(2):
        pair_arrivals(zlen - 1, i)
    pass_matrix(1)
    compute(zlen - 1)
    pass_matrix(2)

    for m in range(3):
        own_copy(m).wait()
        for s, peer in enumerate(fpeers):
            source = (f + nf - 1 - s) % nf
            mx_copy(m, s, peer, f).wait_send()
            ms_copy(m, s, source).wait_send()
            other = pl.ds(al(source * rows + (1 - core) * part, 16), part)
            pltpu.make_async_remote_copy(
                src_ref=mats_out.at[m, other], dst_ref=mats_out.at[m, other],
                send_sem=ms_send.at[m, s], recv_sem=ms_recv.at[m, s],
                device_id=(twin, f), device_id_type=MESH,
            ).wait_recv()
    for s, peer in enumerate(fpeers):
        wh_copy(s, peer).wait_send()
        vec_copy(s, peer).wait_send()
    for i in range(2):
        for way in range(4):
            when(guards[way], lambda way=way, i=i: ag_copy(way, c, i).wait_send())
        for k in range(zlen):
            for sign, (zz, guard) in zip((1, -1), level(k)):
                def body(zz=zz, sign=sign, k=k, i=i):
                    if k:
                        origin = idx(zz, y, core)
                        back = 1 if sign == 1 else 0
                        when(guards[back], lambda: ag_copy(back, origin, i).wait_send())
                        ag_copy(2, origin, i).wait_send()
                        ag_copy(3, origin, i).wait_send()
                    ag_copy(3, idx(zz, 1 - y, core), i).wait_send()
                when(guard, body)
    @pl.loop(0, n)
    def _(o):
        a_copy(o).wait()


def gather(n, nf, x, wh, vec, wo, w1, w2):
    rows = wh.shape[0]
    dma = pltpu.SemaphoreType.DMA
    peers = max(nf - 1, 1)
    return pl.pallas_call(
        functools.partial(gather_kernel, n, nf),
        out_shape=(
            jax.ShapeDtypeStruct((n, 2, BLK, D), BF16),
            jax.ShapeDtypeStruct((n, 3 * HD, 2 * BLK), F32),
            jax.ShapeDtypeStruct((3, nf * rows, D), BF16),
            jax.ShapeDtypeStruct((nf,) + vec.shape, F32),
        ),
        in_specs=[in_vmem(), in_vmem(), in_vmem(), in_any(), in_any(), in_any()],
        out_specs=(in_any(), in_vmem(), in_any(), in_vmem()),
        scratch_shapes=[
            VMEM((n, 2, BLK, D), BF16),
            VMEM((nf * rows, 256), BF16),
            VMEM((256, nf * rows), BF16),
            VMEM((nf,) + vec.shape, F32),
            VMEM((2, rows // 2, D), F32),
            VMEM((3, rows, D), BF16),
            dma((4, n, 2)), dma((n, 2)), dma((peers,)), dma((peers,)), dma((peers,)), dma((peers,)),
            dma((2,)), dma((3,)), dma((3, peers)), dma((3, peers)), dma((3, peers)), dma((3, peers)),
            dma((n,)),
        ],
        compiler_params=pltpu.CompilerParams(
            collective_id=0, has_side_effects=True, vmem_limit_bytes=56 * MIB
        ),
        name="gather_tokens",
    )(x, wh, vec, wo, w1, w2)


def swap_kernel(n, src, dst, send_sem, recv_sem, own_sem):
    c = lax.axis_index("ctx")
    f = lax.axis_index("fsdp")
    barrier = pltpu.get_barrier_semaphore()
    for s in range(1, n):
        pl.semaphore_signal(barrier, inc=1, device_id=((c + s) % n, f), device_id_type=MESH)
    pl.semaphore_wait(barrier, n - 1)

    def copy(s, block):
        return pltpu.make_async_remote_copy(
            src_ref=src.at[(c + s) % n], dst_ref=dst.at[block],
            send_sem=send_sem.at[s], recv_sem=recv_sem.at[s],
            device_id=((c + s) % n, f), device_id_type=MESH,
        )

    for s in range(1, n):
        copy(s, c).start()
    own = pltpu.make_async_copy(src.at[c], dst.at[c], own_sem)
    own.start()
    own.wait()
    for s in range(1, n):
        copy(s, (c + n - s) % n).wait_recv()
    for s in range(1, n):
        copy(s, c).wait_send()


def swap(n, blocks, collective):
    dma = pltpu.SemaphoreType.DMA
    return pl.pallas_call(
        functools.partial(swap_kernel, n),
        out_shape=jax.ShapeDtypeStruct(blocks.shape, blocks.dtype),
        in_specs=[in_vmem()],
        out_specs=in_vmem(),
        scratch_shapes=[dma((n,)), dma((n,)), dma],
        compiler_params=pltpu.CompilerParams(
            collective_id=collective, has_side_effects=True, vmem_limit_bytes=32 * MIB
        ),
        name=f"swap_{collective}",
    )(blocks)


def seq_start(ends, base, token):
    start = jnp.zeros_like(token)
    for e in ends:
        start = jnp.where(e - base <= token, jnp.maximum(start, e - base), start)
    return start


def read_ends(lengths_ref):
    ends, total = [], jnp.int32(0)
    for i in range(lengths_ref.shape[1]):
        total = total + lengths_ref[0, i]
        ends.append(total)
    return ends


def pad_rows(block):
    return jnp.concatenate([block, jnp.zeros((BLK - HD, block.shape[1]), block.dtype)], axis=0)


class Layout:
    def __init__(self, n, total_blocks):
        self.n = n
        self.hpd = 2 * H // n
        self.half_blocks = total_blocks // 2
        self.size = self.half_blocks * BLK
        self.rows = self.hpd * self.size
        self.tile = 512

    def half(self, i):
        return i if self.hpd == 2 else lax.axis_index("ctx") % 2

    def nat(self, deal_ref, d, i):
        half = self.half(i)
        block = deal_ref[2 * d + half]
        if self.hpd == 1:
            block = block - half * self.half_blocks
        return al(block * BLK, BLK)

    def base(self, unit):
        return self.half(unit) * self.size if self.hpd == 1 else unit * self.size


def fwd_kernel(
    lay, deal_ref, len_ref, qkv_ref, bias_ref, c_ref,
    ot_out, qraw, qst, kt, vt, kn, ot, lse,
    m_ref, l_ref, acc_ref,
):
    tile = lay.tile

    @pl.loop(0, lay.n)
    def _(d):
        for i in range(lay.hpd):
            nat = lay.nat(deal_ref, d, i)
            cols = pl.ds(nat, BLK)
            half = lay.half(i)
            src = pl.ds(half * BLK if lay.hpd == 2 else al(half * BLK, BLK), BLK)
            block = qkv_ref[d, :, src] + bias_ref[...]
            qr, kr, vr = block[:HD], block[HD : 2 * HD], block[2 * HD :]
            qraw[:, cols] = qr
            qst[:, cols] = pad_rows(qr * c_ref[...]).astype(BF16)
            kt[:, cols] = kr.astype(BF16)
            vt[:, cols] = vr.astype(BF16)
            kn[cols, :] = pad_rows(kr).T.astype(BF16)

    ends = read_ends(len_ref)
    for unit in range(lay.hpd):
        base = lay.base(unit)
        row0 = unit * lay.size

        @pl.loop(0, lay.size // tile)
        def _(qi):
            cols = pl.ds(al(row0 + qi * tile, tile), tile)
            t_row = qi * tile + lax.broadcasted_iota(jnp.int32, (1, tile), 1)
            start = seq_start(ends, base, t_row)
            low = seq_start(ends, base, qi * tile) // tile
            m_ref[...] = jnp.full_like(m_ref, NEG)
            l_ref[...] = jnp.zeros_like(l_ref)
            acc_ref[...] = jnp.zeros_like(acc_ref)

            def visit(j, diagonal):
                keys = pl.ds(al(row0 + j * tile, tile), tile)
                s = dot(kn[keys, :], qst[:, cols])
                u = j * tile + lax.broadcasted_iota(jnp.int32, (tile, 1), 0)
                seen = u >= start
                if diagonal:
                    seen = seen & (u <= t_row)
                s = jnp.where(seen, s, NEG)
                m_old = m_ref[...]
                m_new = jnp.maximum(m_old, jnp.max(s, axis=0, keepdims=True))
                p = jnp.exp(s - m_new)
                shrink = jnp.exp(m_old - m_new)
                m_ref[...] = m_new
                l_ref[...] = l_ref[...] * shrink + jnp.sum(p, axis=0, keepdims=True)
                acc_ref[...] = acc_ref[...] * shrink + dot(vt[:, keys], p.astype(BF16))

            @pl.loop(low, qi)
            def _(j):
                visit(j, False)

            visit(qi, True)
            ot[:, cols] = acc_ref[...] / l_ref[...]
            lse[:, cols] = m_ref[...] + jnp.log(l_ref[...])

    @pl.loop(0, lay.n)
    def _(d):
        for i in range(lay.hpd):
            ot_out[d, i] = ot[:, pl.ds(lay.nat(deal_ref, d, i), BLK)].astype(BF16)


def attend(lay, deal, lengths, qkv, bias, factor):
    rows = lay.rows
    return pl.pallas_call(
        functools.partial(fwd_kernel, lay),
        out_shape=(
            jax.ShapeDtypeStruct((lay.n, lay.hpd, HD, BLK), BF16),
            jax.ShapeDtypeStruct((HD, rows), F32),
            jax.ShapeDtypeStruct((BLK, rows), BF16),
            jax.ShapeDtypeStruct((HD, rows), BF16),
            jax.ShapeDtypeStruct((HD, rows), BF16),
            jax.ShapeDtypeStruct((rows, BLK), BF16),
            jax.ShapeDtypeStruct((HD, rows), F32),
            jax.ShapeDtypeStruct((1, rows), F32),
        ),
        in_specs=[in_smem(), in_smem()] + [in_vmem()] * 3,
        out_specs=tuple([in_vmem()] * 8),
        scratch_shapes=[
            VMEM((1, lay.tile), F32), VMEM((1, lay.tile), F32), VMEM((HD, lay.tile), F32),
        ],
        compiler_params=pltpu.CompilerParams(vmem_limit_bytes=56 * MIB),
        name="attend",
    )(deal, lengths, qkv, bias, factor)


def bwd_kernel(
    lay, deal_ref, len_ref, dot_ref, qraw, qst, kt, vt, kn, ot, lse, c_ref, a_ref,
    msg_out, small_out, dw_out,
    qn, vn, don, dost, delta, dk, dv, dqt,
):
    tile = lay.tile

    @pl.loop(0, lay.n)
    def _(d):
        for i in range(lay.hpd):
            cols = pl.ds(lay.nat(deal_ref, d, i), BLK)
            block = dot_ref[d, i].astype(F32)
            delta[:, cols] = jnp.sum(block * ot[:, cols], axis=0, keepdims=True)
            block = pad_rows(block)
            dost[:, cols] = block.astype(BF16)
            don[cols, :] = block.T.astype(BF16)

    @pl.loop(0, lay.rows // BLK)
    def _(t):
        cols = pl.ds(al(t * BLK, BLK), BLK)
        qn[cols, :] = qst[:, cols].astype(F32).T.astype(BF16)
        vn[cols, :] = pad_rows(vt[:, cols].astype(F32)).T.astype(BF16)
        dk[cols, :] = jnp.zeros((BLK, BLK), F32)
        dv[cols, :] = jnp.zeros((BLK, BLK), F32)

    ends = read_ends(len_ref)
    for unit in range(lay.hpd):
        base = lay.base(unit)
        row0 = unit * lay.size

        @pl.loop(0, lay.size // tile)
        def _(qi):
            cols = pl.ds(al(row0 + qi * tile, tile), tile)
            t_row = qi * tile + lax.broadcasted_iota(jnp.int32, (1, tile), 1)
            start = seq_start(ends, base, t_row)
            low = seq_start(ends, base, qi * tile) // tile
            dqt[:, cols] = jnp.zeros((HD, tile), F32)

            def visit(j, diagonal):
                keys = pl.ds(al(row0 + j * tile, tile), tile)
                s = dot(kn[keys, :], qst[:, cols])
                u = j * tile + lax.broadcasted_iota(jnp.int32, (tile, 1), 0)
                seen = u >= start
                if diagonal:
                    seen = seen & (u <= t_row)
                p = jnp.exp(jnp.where(seen, s - lse[:, cols], NEG))
                dp = dot(vn[keys, :], dost[:, cols])
                ds = (p * (dp - delta[:, cols])).astype(BF16)
                dv[keys, :] += dot(p.astype(BF16), don[cols, :])
                dk[keys, :] += dot(ds, qn[cols, :])
                dqt[:, cols] += dot(kt[:, keys], ds)

            @pl.loop(low, qi)
            def _(j):
                visit(j, False)

            visit(qi, True)

    small_out[...] = jnp.zeros_like(small_out)

    @pl.loop(0, lay.n)
    def _(d):
        for i in range(lay.hpd):
            cols = pl.ds(lay.nat(deal_ref, d, i), BLK)
            dqs = dqt[:, cols]
            dq = (dqs * c_ref[...]).astype(BF16)
            dkt = dk[cols, :].T[:HD].astype(BF16)
            dvt = dv[cols, :].T[:HD].astype(BF16)
            msg_out[d, 0, i] = dq
            msg_out[d, 1, i] = dkt
            msg_out[d, 2, i] = dvt
            small_out[0] += dqs * qraw[:, cols]
            small_out[1] += dq.astype(F32)
            small_out[2] += dvt.astype(F32)

    dw_out[...] = jnp.zeros_like(dw_out)

    @pl.loop(0, lay.n)
    def _(d):
        if lay.hpd == 2:
            left = jnp.concatenate(
                [msg_out[d, :, 0].reshape(3 * HD, BLK), msg_out[d, :, 1].reshape(3 * HD, BLK)], axis=1
            )
            right = a_ref[d].reshape(2 * BLK, D)
        else:
            left = msg_out[d, :, 0].reshape(3 * HD, BLK)
            right = a_ref[d, lay.half(0)]
        dw_out[...] += dot(left, right)


def attend_back(lay, deal, lengths, grad_t, kept, factor, tokens):
    rows = lay.rows
    return pl.pallas_call(
        functools.partial(bwd_kernel, lay),
        out_shape=(
            jax.ShapeDtypeStruct((lay.n, 3, lay.hpd, HD, BLK), BF16),
            jax.ShapeDtypeStruct((3, HD, BLK), F32),
            jax.ShapeDtypeStruct((3 * HD, D), F32),
        ),
        in_specs=[in_smem(), in_smem()] + [in_vmem()] * 10,
        out_specs=tuple([in_vmem()] * 3),
        scratch_shapes=[
            VMEM((rows, BLK), BF16), VMEM((rows, BLK), BF16), VMEM((rows, BLK), BF16),
            VMEM((BLK, rows), BF16), VMEM((1, rows), F32),
            VMEM((rows, BLK), F32), VMEM((rows, BLK), F32), VMEM((HD, rows), F32),
        ],
        compiler_params=pltpu.CompilerParams(vmem_limit_bytes=58 * MIB),
        name="attend_back",
    )(deal, lengths, grad_t, *kept, factor, tokens)


WIDE = 256


def over_columns(body):
    @pl.loop(0, D // WIDE)
    def _(j):
        body(pl.ds(al(j * WIDE, WIDE), WIDE))


def ffn_kernel(
    x_ref, cot_ref, ot_ref, g2_ref, mats_ref,
    out_ref, dh_ref, gt_ref, dwo_ref, dw1_ref, dw2_ref, dg2_ref,
    ot, o_rows, hidden, nh, b, up, z, du, db, gb, wide,
):
    tok = x_ref.shape[0]
    wo, w1, w2 = mats_ref.at[0], mats_ref.at[1], mats_ref.at[2]
    for i in range(2):
        for h in range(H):
            ot[pl.ds(h * HD, HD), pl.ds(i * BLK, BLK)] = ot_ref[h, i]
    @pl.loop(0, D // WIDE)
    def _(j):
        sl = pl.ds(al(j * WIDE, WIDE), WIDE)
        o_rows[:, sl] = ot[sl, :].astype(F32).T.astype(BF16)

    def body(sl):
        hidden[:, sl] = x_ref[:, sl].astype(F32) + dot(o_rows[...], wo[:, sl])
    over_columns(body)
    hid = hidden[...]
    r2 = lax.rsqrt(jnp.mean(hid * hid, axis=-1, keepdims=True) + EPS)
    nh[...] = hid * r2
    b[...] = (nh[...] * g2_ref[...]).astype(BF16)

    def body(sl):
        u = dot(b[...], w1[:, sl])
        up[:, sl] = u
        z[:, sl] = (u * jax.nn.sigmoid(u)).astype(BF16)
    over_columns(body)

    def body(sl):
        out_ref[:, sl] = (hidden[:, sl] + dot(z[...], w2[:, sl])).astype(BF16)
        dz = dot(cot_ref[...], w2[sl, :], NT)
        u = up[:, sl]
        sig = jax.nn.sigmoid(u)
        du[:, sl] = (dz * sig * (1.0 + u * (1.0 - sig))).astype(BF16)
    over_columns(body)

    def body(sl):
        g = dot(du[...], w1[sl, :], NT)
        db[:, sl] = g * g2_ref[:, sl]
        dg2_ref[:, sl] = jnp.sum(g * nh[:, sl], axis=0, keepdims=True)
    over_columns(body)
    scaled = db[...]
    mean = jnp.mean(scaled * nh[...], axis=-1, keepdims=True)
    dh = cot_ref[...].astype(F32) + r2 * (scaled - nh[...] * mean)
    dh_ref[...] = dh
    gb[...] = dh.astype(BF16)

    @pl.loop(0, D // WIDE)
    def _(j):
        sl = pl.ds(al(j * WIDE, WIDE), WIDE)
        wide[sl, :] = dot(wo[sl, :], gb[...], NT).astype(BF16)
    for i in range(2):
        for h in range(H):
            gt_ref[h, i] = wide[pl.ds(h * HD, HD), pl.ds(i * BLK, BLK)]

    def body(sl):
        dwo_ref[sl, :] = dot(ot[sl, :], gb[...]).astype(BF16)
        dw1_ref[sl, :] = dot(b[:, sl], du[...], TN).astype(BF16)
        dw2_ref[sl, :] = dot(z[:, sl], cot_ref[...], TN).astype(BF16)
    over_columns(body)


def ffn(x, cot, ot, g2, mats):
    tok = x.shape[0]
    grad = jax.ShapeDtypeStruct((D, D), BF16)
    return pl.pallas_call(
        ffn_kernel,
        out_shape=(
            jax.ShapeDtypeStruct((tok, D), BF16),
            jax.ShapeDtypeStruct((tok, D), F32),
            jax.ShapeDtypeStruct((H, 2, HD, BLK), BF16),
            grad, grad, grad,
            jax.ShapeDtypeStruct((1, D), F32),
        ),
        in_specs=[in_vmem()] * 5,
        out_specs=tuple([in_vmem()] * 7),
        scratch_shapes=[
            VMEM((D, tok), BF16), VMEM((tok, D), BF16), VMEM((tok, D), F32), VMEM((tok, D), F32),
            VMEM((tok, D), BF16), VMEM((tok, D), F32), VMEM((tok, D), BF16), VMEM((tok, D), BF16),
            VMEM((tok, D), F32), VMEM((tok, D), BF16), VMEM((D, tok), BF16),
        ],
        compiler_params=pltpu.CompilerParams(vmem_limit_bytes=56 * MIB),
        name="feed_forward",
    )(x, cot, ot, g2, mats)


def input_grad_kernel(x_ref, dh_ref, msg_ref, g1_ref, wq, wk, wv, out_ref, dg1_ref, wide, dat):
    mats = (wq, wk, wv)
    for p in range(3):
        for i in range(2):
            for h in range(H):
                wide[p, pl.ds(h * HD, HD), pl.ds(i * BLK, BLK)] = msg_ref[h, p, i]

    @pl.loop(0, D // WIDE)
    def _(j):
        sl = pl.ds(al(j * WIDE, WIDE), WIDE)
        total = dot(wq[sl, :], wide[0]) + dot(wk[sl, :], wide[1]) + dot(wv[sl, :], wide[2])
        dat[:, sl] = total.T
    x = x_ref[...].astype(F32)
    r1 = lax.rsqrt(jnp.mean(x * x, axis=-1, keepdims=True) + EPS)
    na = x * r1
    da = dat[...]
    dg1_ref[...] = jnp.sum(da * na, axis=0, keepdims=True)
    scaled = da * g1_ref[...]
    mean = jnp.mean(scaled * na, axis=-1, keepdims=True)
    out_ref[...] = dh_ref[...] + r1 * (scaled - na * mean)


def input_grad(x, dh, msg, g1, wq, wk, wv):
    tok = x.shape[0]
    return pl.pallas_call(
        input_grad_kernel,
        out_shape=(
            jax.ShapeDtypeStruct((tok, D), F32),
            jax.ShapeDtypeStruct((1, D), F32),
        ),
        in_specs=[in_vmem()] * 7,
        out_specs=(in_vmem(), in_vmem()),
        scratch_shapes=[VMEM((3, D, tok), BF16), VMEM((tok, D), F32)],
        compiler_params=pltpu.CompilerParams(vmem_limit_bytes=48 * MIB),
        name="input_grad",
    )(x, dh, msg, g1, wq, wk, wv)


def local(
    n, nf, tokens, cotangent, lengths, deal, gain_attn, query_weight, query_bias, key_weight,
    value_weight, value_bias, query_scale, proj_weight, gain_ffn, up_weight, down_weight,
):
    c = lax.axis_index("ctx")
    f = lax.axis_index("fsdp")
    lay = Layout(n, deal.shape[0])
    head = c * lay.hpd // 2
    rows = query_weight.shape[0]
    x, cot = tokens[0], cotangent[0]

    def low(v):
        return v.astype(BF16).astype(F32)

    g1_own = low(gain_attn)
    slices = [
        lax.dynamic_slice(w, (0, head * HD), (rows, HD)) for w in (query_weight, key_weight, value_weight)
    ]
    wh = jnp.concatenate(slices, axis=1).astype(BF16).astype(F32) * g1_own[:, None]
    wh = jnp.pad(wh, ((0, 0), (0, 256 - 3 * HD))).astype(BF16)
    vec = jnp.stack([g1_own, low(query_bias), low(value_bias), low(gain_ffn)])
    vec = jnp.concatenate([vec, jnp.pad(low(query_scale), (0, rows - query_scale.shape[0]))[None]])
    vec = jnp.pad(vec, ((0, 3), (0, -rows % 128)))

    a_all, qkv, mats, vecs = gather(n, nf, x, wh, vec, proj_weight, up_weight, down_weight)
    whole = jnp.swapaxes(vecs[:, :5, :rows], 0, 1).reshape(5, nf * rows)
    g1, bq, bv, g2 = whole[0], whole[1], whole[2], whole[3]
    q_param = vecs[:, 4, : query_scale.shape[0]].reshape(HD)
    factor = jnp.log(1.0 + jnp.exp(q_param)) * (LOG2E / math.sqrt(HD))
    bias = jnp.concatenate([
        lax.dynamic_slice(bq, (head * HD,), (HD,)), jnp.zeros((HD,), F32),
        lax.dynamic_slice(bv, (head * HD,), (HD,)),
    ])
    bias = jnp.broadcast_to(bias[:, None], (3 * HD, BLK))
    factor_col = jnp.broadcast_to(factor[:, None], (HD, BLK))

    core = c % 2
    part = rows // 2
    pairs = [(i, i ^ 1) for i in range(n)]
    stacked = jnp.stack([query_weight, key_weight, value_weight])
    mine = lax.dynamic_slice(stacked, (0, core * part, 0), (3, part, D)).astype(BF16)
    mine = lax.all_gather(mine, "fsdp", axis=1)
    other = lax.ppermute(mine, "ctx", pairs)
    first = jnp.where(core == 0, mine, other)
    second = jnp.where(core == 0, other, mine)
    proj = jnp.concatenate([first, second], axis=2).reshape(3, nf * rows, D)

    ot, *kept = attend(lay, deal, lengths, qkv, bias, factor_col)
    ot = swap(n, ot, 1).reshape(H, 2, HD, BLK)
    layer_out, dh, gt, dwo, dw1, dw2, dg2 = ffn(x, cot, ot, g2[None], mats)

    grads = lax.psum_scatter(jnp.stack([dwo, dw1, dw2]), "fsdp", scatter_dimension=1, tiled=True)
    grads = lax.psum(grads, "ctx").astype(F32)

    gt = swap(n, gt.reshape(n, lay.hpd, HD, BLK), 2)
    msg, small, dw = attend_back(lay, deal, lengths, gt, kept, factor_col, a_all)
    back = swap(n, msg, 3)
    if lay.hpd == 1:
        back = back.reshape(H, 2, 3, HD, BLK).transpose(0, 2, 1, 3, 4)
    grad_x, dg1 = input_grad(x, dh, back, g1[None], proj[0], proj[1], proj[2])

    dw = lax.psum_scatter(dw.astype(BF16), "fsdp", scatter_dimension=1, tiled=True)
    dw = lax.all_gather(dw, "ctx").astype(F32)
    dw = dw.reshape(H, 2 // lay.hpd, 3, HD, rows).sum(axis=1)
    dw = dw.transpose(1, 0, 2, 3).reshape(3, D, rows)
    dw = dw.transpose(0, 2, 1) * g1_own[None, :, None]

    small = jnp.sum(small, axis=-1)
    bias_part = jnp.zeros((2, H, HD), F32)
    bias_part = lax.dynamic_update_slice(bias_part, small[1:][:, None], (0, head, 0)).reshape(2, D)
    vectors = jnp.concatenate([dg1.reshape(D), dg2.reshape(D), bias_part.reshape(2 * D), small[0]])
    vectors = lax.psum(vectors, ("ctx", "fsdp"))

    def own(v):
        size = v.shape[0] // nf
        return lax.dynamic_slice(v, (f * size,), (size,))

    grad_scale = vectors[4 * D :] * jax.nn.sigmoid(q_param) * (LOG2E / math.sqrt(HD))
    return (
        layer_out[None],
        grad_x[None],
        own(vectors[:D]),
        dw[0],
        own(vectors[2 * D : 3 * D]),
        dw[1],
        dw[2],
        own(vectors[3 * D : 4 * D]),
        own(grad_scale),
        grads[0],
        own(vectors[D : 2 * D]),
        grads[1],
        grads[2],
    )


def solution(mesh):
    whole, vector, matrix = P("fsdp", "ctx", None), P("fsdp"), P("fsdp", None)
    return jax.shard_map(
        functools.partial(local, mesh.shape["ctx"], mesh.shape["fsdp"]),
        mesh=mesh,
        in_specs=(
            whole, whole, matrix, P(), vector, matrix, vector, matrix, matrix, vector, vector,
            matrix, vector, matrix, matrix,
        ),
        out_specs=(
            whole, whole, vector, matrix, vector, matrix, matrix, vector, vector, matrix, vector,
            matrix, matrix,
        ),
        check_vma=False,
    )
```

```python
import functools
import math

import jax
import jax.numpy as jnp
from jax import lax
from jax.experimental import pallas as pl
from jax.experimental.pallas import tpu as pltpu
from jax.sharding import PartitionSpec as P

H = 16
HD = 80
BLK = 128
D = 1280
EPS = 1e-06
LOG2E = 1.442695041
NEG = -1e30
MESH = pl.DeviceIdType.MESH
F32 = jnp.float32
BF16 = jnp.bfloat16
VMEM = pltpu.VMEM
MIB = 1 << 20

NN = (((1,), (0,)), ((), ()))
NT = (((1,), (1,)), ((), ()))
TN = (((0,), (0,)), ((), ()))


def dot(left, right, dims=NN):
    return lax.dot_general(left, right, dims, preferred_element_type=F32)


def al(value, multiple):
    return pl.multiple_of(value, multiple)


def in_vmem():
    return pl.BlockSpec(memory_space=pltpu.VMEM)


def in_smem():
    return pl.BlockSpec(memory_space=pltpu.SMEM)


def in_any():
    return pl.BlockSpec(memory_space=pl.ANY)


def cost(microseconds):
    return pl.CostEstimate(flops=0, bytes_accessed=int(microseconds * 3.0e6), transcendentals=0)


class Place:
    def __init__(self, n, nf):
        self.n, self.nf = n, nf
        self.c = lax.axis_index("ctx")
        self.f = lax.axis_index("fsdp")
        self.zlen = n // 4
        self.z, self.y, self.core = self.c // 4, (self.c // 2) % 2, self.c % 2
        self.twin = self.idx(self.z, self.y, 1 - self.core)
        self.ypeer = self.idx(self.z, 1 - self.y, self.core)
        self.targets = (
            self.idx(self.z + 1, self.y, self.core), self.idx(self.z - 1, self.y, self.core),
            self.ypeer, self.twin,
        )
        self.guards = (self.z < self.zlen - 1, self.z > 0, None, None)
        self.fpeers = [(self.f + s) % nf for s in range(1, nf)]
        self.fsources = [(self.f + nf - s) % nf for s in range(1, nf)]

    def idx(self, z, y, core):
        return (z * 2 + y) * 2 + core

    def level(self, k):
        if k == 0:
            return [(self.z, None, 0)]
        return [
            (self.z + k, self.z + k < self.zlen, 1),
            (self.z - k, self.z - k >= 0, -1),
        ]

    def greet_neighbours(self):
        barrier = pltpu.get_barrier_semaphore()
        for target, guard in zip(self.targets, self.guards):
            when(guard, lambda target=target: pl.semaphore_signal(
                barrier, inc=1, device_id=(target, self.f), device_id_type=MESH))
        for peer in self.fpeers:
            pl.semaphore_signal(barrier, inc=1, device_id=(self.c, peer), device_id_type=MESH)
        ends = jnp.minimum(self.z, 1) + jnp.minimum(self.zlen - 1 - self.z, 1)
        pl.semaphore_wait(barrier, 1 + self.nf + ends)

    def greet_all(self, with_fsdp):
        barrier = pltpu.get_barrier_semaphore()
        for s in range(1, self.n):
            pl.semaphore_signal(
                barrier, inc=1, device_id=((self.c + s) % self.n, self.f), device_id_type=MESH)
        if with_fsdp:
            for peer in self.fpeers:
                pl.semaphore_signal(barrier, inc=1, device_id=(self.c, peer), device_id_type=MESH)
        pl.semaphore_wait(barrier, self.n - 1 + (self.nf - 1 if with_fsdp else 0))


def when(guard, body):
    if guard is None:
        body()
    else:
        pl.when(guard)(body)


class Spread:
    def __init__(self, place, buf, send_sem, recv_sem, pieces):
        self.p, self.buf, self.send_sem, self.recv_sem, self.pieces = place, buf, send_sem, recv_sem, pieces

    def copy(self, way, origin, i):
        where = self.buf.at[origin, i] if self.pieces > 1 else self.buf.at[origin]
        return pltpu.make_async_remote_copy(
            src_ref=where, dst_ref=where,
            send_sem=self.send_sem.at[way, origin, i], recv_sem=self.recv_sem.at[origin, i],
            device_id=(self.p.targets[way], self.p.f), device_id_type=MESH,
        )

    def send(self, way, origin, i):
        when(self.p.guards[way], lambda: self.copy(way, origin, i).start())

    def arrive(self, origin, i):
        self.copy(3, origin, i).wait_recv()

    def start(self, i):
        for way in range(4):
            self.send(way, self.p.c, i)

    def chain(self, k, i):
        p = self.p
        for zz, guard, sign in p.level(k):
            def body(zz=zz, sign=sign):
                origin = p.idx(zz, p.y, p.core)
                self.arrive(origin, i)
                self.send(1 if sign == 1 else 0, origin, i)
                self.send(2, origin, i)
                self.send(3, origin, i)
            when(guard, body)

    def pair(self, k, i):
        p = self.p
        for zz, guard, _ in p.level(k):
            def body(zz=zz):
                origin = p.idx(zz, 1 - p.y, p.core)
                self.arrive(origin, i)
                self.send(3, origin, i)
            when(guard, body)

    def from_twin(self, zz):
        p = self.p
        for yy in (p.y, 1 - p.y):
            for i in range(self.pieces):
                self.arrive(p.idx(zz, yy, 1 - p.core), i)

    def drain(self):
        p = self.p
        for i in range(self.pieces):
            for way in range(4):
                when(p.guards[way], lambda way=way, i=i: self.copy(way, p.c, i).wait_send())
            for k in range(p.zlen):
                for zz, guard, sign in p.level(k):
                    def body(zz=zz, sign=sign, k=k, i=i):
                        if k:
                            origin = p.idx(zz, p.y, p.core)
                            on = 1 if sign == 1 else 0
                            when(p.guards[on], lambda: self.copy(on, origin, i).wait_send())
                            self.copy(2, origin, i).wait_send()
                            self.copy(3, origin, i).wait_send()
                        self.copy(3, p.idx(zz, 1 - p.y, p.core), i).wait_send()
                    when(guard, body)


class Reduce:
    def __init__(self, place, mine, result, acc, xrecv, yrecv, urecv, drecv, sems):
        self.p, self.mine, self.result, self.acc = place, mine, result, acc
        self.xrecv, self.yrecv, self.urecv, self.drecv = xrecv, yrecv, urecv, drecv
        (self.xs, self.xr, self.ys, self.yr, self.us, self.ur, self.ds, self.dr) = sems
        self.height = acc.shape[0] // place.zlen
        self.width = D // 2
        zlen = place.zlen
        ends = []
        for k in range(zlen // 2):
            ends += [zlen - 1 - k, k]
        self.order = ends

    @staticmethod
    def scratch(nf, zlen, height):
        dma = pltpu.SemaphoreType.DMA
        peers = max(nf - 1, 1)
        piece = VMEM((zlen, height // zlen, D // 2), BF16)
        return [
            VMEM((height // zlen, D // 2), BF16), VMEM((height, D), BF16), VMEM((peers, height, D), BF16),
            piece, piece, piece,
            dma((peers, zlen, 2)), dma((peers, zlen, 2)), dma((zlen,)), dma((zlen,)),
            dma((zlen,)), dma((zlen,)), dma((zlen,)), dma((zlen,)),
        ]

    def at(self, piece, side):
        return (
            pl.ds(al(piece * self.height, 16), self.height),
            pl.ds(al(side * self.width, 128), self.width),
        )

    def remote(self, src, dst, send, recv, c, f):
        return pltpu.make_async_remote_copy(
            src_ref=src, dst_ref=dst, send_sem=send, recv_sem=recv,
            device_id=(c, f), device_id_type=MESH,
        )

    def x_copy(self, s, peer, piece, turn):
        side = (self.p.y + 1 + turn) % 2
        where = self.at(piece, side)
        return self.remote(
            self.mine.at[peer].at[where], self.xrecv.at[s].at[where],
            self.xs.at[s, piece, turn], self.xr.at[s, piece, turn], self.p.c, peer,
        )

    def start_x(self):
        for piece in self.order:
            for turn in range(2):
                for s, peer in enumerate(self.p.fpeers):
                    self.x_copy(s, peer, piece, turn).start()

    def add(self, dst, terms):
        step = 48 if self.height % 48 == 0 else 16
        @pl.loop(0, self.height // step)
        def _(t):
            at = pl.ds(al(t * step, 16), step)
            total = terms[0][at, :].astype(F32)
            for term in terms[1:]:
                total = total + term[at, :].astype(F32)
            dst[at, :] = total.astype(BF16)

    def sum_x(self, piece, turn):
        side = (self.p.y + 1 + turn) % 2
        where = self.at(piece, side)
        terms = [self.mine.at[self.p.f].at[where]]
        for s, peer in enumerate(self.p.fpeers):
            self.x_copy(s, peer, piece, turn).wait_recv()
            terms.append(self.xrecv.at[s].at[where])
        self.add(self.acc.at[where], terms)

    def y_copy(self, piece):
        src = self.acc.at[self.at(piece, 1 - self.p.y)]
        return self.remote(
            src, self.yrecv.at[piece], self.ys.at[piece], self.yr.at[piece], self.p.ypeer, self.p.f)

    def u_copy(self, piece):
        src = self.acc.at[self.at(piece, self.p.y)]
        return self.remote(
            src, self.urecv.at[piece], self.us.at[piece], self.ur.at[piece], self.p.targets[0], self.p.f)

    def d_copy(self, piece):
        src = self.acc.at[self.at(piece, self.p.y)]
        return self.remote(
            src, self.drecv.at[piece], self.ds.at[piece], self.dr.at[piece], self.p.targets[1], self.p.f)

    def mine_of(self, piece):
        return self.acc.at[self.at(piece, self.p.y)]

    def xy(self, t):
        piece = self.order[t]
        self.sum_x(piece, 0)
        self.y_copy(piece).start()
        self.sum_x(piece, 1)

    def after_y(self, t):
        piece = self.order[t]
        self.y_copy(piece).wait_recv()
        self.add(self.mine_of(piece), [self.mine_of(piece), self.yrecv.at[piece]])

    def chain(self, t, hop):
        p, piece = self.p, self.order[t]
        if hop < piece:
            @pl.when(p.z == hop)
            def _():
                if hop:
                    self.u_copy(piece).wait_recv()
                    self.add(self.mine_of(piece), [self.mine_of(piece), self.urecv.at[piece]])
                self.u_copy(piece).start()
        if p.zlen - 1 - hop > piece:
            @pl.when(p.z == p.zlen - 1 - hop)
            def _():
                if hop:
                    self.d_copy(piece).wait_recv()
                    self.add(self.mine_of(piece), [self.mine_of(piece), self.drecv.at[piece]])
                self.d_copy(piece).start()

    def last(self):
        p = self.p
        @pl.when(p.z > 0)
        def _():
            self.u_copy(p.z).wait_recv()
            self.add(self.mine_of(p.z), [self.mine_of(p.z), self.urecv.at[p.z]])
        @pl.when(p.z < p.zlen - 1)
        def _():
            self.d_copy(p.z).wait_recv()
            self.add(self.mine_of(p.z), [self.mine_of(p.z), self.drecv.at[p.z]])
        self.add(self.result, [self.mine_of(p.z)])

    def drain(self):
        p = self.p
        for piece in self.order:
            for turn in range(2):
                for s, peer in enumerate(p.fpeers):
                    self.x_copy(s, peer, piece, turn).wait_send()
            self.y_copy(piece).wait_send()
            pl.when(p.z < piece)(lambda piece=piece: self.u_copy(piece).wait_send())
            pl.when(p.z > piece)(lambda piece=piece: self.d_copy(piece).wait_send())


def gather_kernel(
    n, nf, x_ref, wh_ref, vec_ref, wo_ref, w1_ref, w2_ref, wq_ref, wk_ref, wv_ref,
    a_out, qkv_out, mats_out, vecs_out, mine_out, other_out,
    abuf, norm, whbuf, wht, vecbuf, g1_ref, stage, wcast,
    ag_send, ag_recv, wh_send, wh_recv, vec_send, vec_recv,
    ld_sem, own_sem, mx_send, mx_recv, ms_send, ms_recv, a_sem, keep_sem,
):
    p = Place(n, nf)
    c, f, core, zlen = p.c, p.f, p.core, p.zlen
    rows = wh_ref.shape[0]
    part = rows // 2
    p.greet_neighbours()
    spread = Spread(p, abuf, ag_send, ag_recv, 2)

    for i in range(2):
        abuf[c, i] = x_ref[pl.ds(i * BLK, BLK), :]
        spread.start(i)

    def wh_copy(s, peer):
        return pltpu.make_async_remote_copy(
            src_ref=wh_ref, dst_ref=whbuf.at[pl.ds(al(f * rows, 16), rows)],
            send_sem=wh_send.at[s], recv_sem=wh_recv.at[s],
            device_id=(c, peer), device_id_type=MESH,
        )

    def vec_copy(s, peer):
        return pltpu.make_async_remote_copy(
            src_ref=vec_ref, dst_ref=vecbuf.at[f],
            send_sem=vec_send.at[s], recv_sem=vec_recv.at[s],
            device_id=(c, peer), device_id_type=MESH,
        )

    for s, peer in enumerate(p.fpeers):
        vec_copy(s, peer).start()
        wh_copy(s, peer).start()
    whbuf[pl.ds(al(f * rows, 16), rows), :] = wh_ref[...]
    vecbuf[f] = vec_ref[...]

    shards = (wo_ref, w1_ref, w2_ref, wq_ref, wk_ref, wv_ref)
    steps = [(m, h) for h in range(2) for m in range(3)] + [(m, h) for h in range(2) for m in range(3, 6)]

    def half_of(h):
        return (core + h) % 2

    def load(step):
        m, h = steps[step]
        return pltpu.make_async_copy(
            shards[m].at[pl.ds(al(half_of(h) * part, 16), part)],
            stage.at[step % 2], ld_sem.at[step % 2],
        )

    def mx_copy(m, s, peer, source):
        return pltpu.make_async_remote_copy(
            src_ref=wcast.at[m, core],
            dst_ref=mats_out.at[m, pl.ds(al(source * rows + core * part, 16), part)],
            send_sem=mx_send.at[m, s], recv_sem=mx_recv.at[m, s],
            device_id=(c, peer), device_id_type=MESH,
        )

    def keep_copies(m):
        if m < 3:
            return [
                pltpu.make_async_copy(
                    wcast.at[m, h], mats_out.at[m, pl.ds(al(f * rows + h * part, 16), part)],
                    keep_sem.at[m, h],
                ) for h in range(2)
            ]
        return [
            pltpu.make_async_copy(wcast.at[m, half_of(h)], out.at[m - 3], keep_sem.at[m, h])
            for h, out in enumerate((mine_out, other_out))
        ]

    def cast(step):
        m, h = steps[step]
        if step + 1 < len(steps):
            load(step + 1).start()
        load(step).wait()
        chunk = part // 4 if part % 64 == 0 else part
        @pl.loop(0, part // chunk)
        def _(t):
            wcast[m, half_of(h), pl.ds(al(t * chunk, 16), chunk), :] = stage[
                step % 2, pl.ds(al(t * chunk, 16), chunk), :
            ].astype(BF16)
        if h == 0 and m < 3:
            for s, peer in enumerate(p.fpeers):
                mx_copy(m, s, peer, f).start()
        if h == 1:
            for copy in keep_copies(m):
                copy.start()

    load(0).start()
    for step in range(len(steps)):
        cast(step)

    for s, peer in enumerate(p.fpeers):
        wh_copy(s, peer).wait_recv()
        vec_copy(s, peer).wait_recv()
    wht[...] = whbuf[...].astype(F32).T.astype(BF16)
    vecs_out[...] = vecbuf[...]
    for source in range(nf):
        g1_ref[:, pl.ds(source * rows, rows)] = vecbuf[source, 0:1, 0:rows]

    def a_copy(slot, origin):
        return pltpu.make_async_copy(norm.at[slot], a_out.at[origin], a_sem.at[slot])

    def project(slot, origin):
        for i in range(2):
            x = abuf[origin, i].astype(F32)
            scale = lax.rsqrt(jnp.mean(x * x, axis=-1, keepdims=True) + EPS)
            norm[slot, i] = (x * scale * g1_ref[...]).astype(BF16)
        a_copy(slot, origin).start()
        block = norm[slot].reshape(2 * BLK, D)
        qkv_out[origin] = dot(wht[: 3 * HD, :], block, NT)

    def compute(k):
        for zz, guard, _ in p.level(k):
            def body(zz=zz):
                spread.from_twin(zz)
                @pl.loop(0, 4)
                def _(t):
                    if k:
                        a_copy(t, zz * 4 + t).wait()
                    project(t, zz * 4 + t)
            when(guard, body)

    def ms_copy(m, s, source, half):
        where = mats_out.at[m, pl.ds(al(source * rows + half * part, 16), part)]
        return pltpu.make_async_remote_copy(
            src_ref=where, dst_ref=where,
            send_sem=ms_send.at[m, s], recv_sem=ms_recv.at[m, s],
            device_id=(p.twin, f), device_id_type=MESH,
        )

    def pass_matrix(m):
        for s, (peer, source) in enumerate(zip(p.fpeers, p.fsources)):
            mx_copy(m, s, peer, source).wait_recv()
            ms_copy(m, s, source, core).start()

    for k in range(1, zlen):
        for i in range(2):
            spread.chain(k, i)
            spread.pair(k - 1, i)
        compute(k - 1)
        if k == 2:
            pass_matrix(0)
    for i in range(2):
        spread.pair(zlen - 1, i)
    pass_matrix(1)
    compute(zlen - 1)
    pass_matrix(2)

    for m in range(6):
        for copy in keep_copies(m):
            copy.wait()
    for m in range(3):
        for s, (peer, source) in enumerate(zip(p.fpeers, p.fsources)):
            mx_copy(m, s, peer, f).wait_send()
            ms_copy(m, s, source, core).wait_send()
            ms_copy(m, s, source, 1 - core).wait_recv()
    for s, peer in enumerate(p.fpeers):
        wh_copy(s, peer).wait_send()
        vec_copy(s, peer).wait_send()
    spread.drain()
    for slot in range(4):
        a_copy(slot, slot).wait()


def gather(n, nf, x, wh, vec, mats):
    rows = wh.shape[0]
    dma = pltpu.SemaphoreType.DMA
    peers = max(nf - 1, 1)
    half = jax.ShapeDtypeStruct((3, rows // 2, D), BF16)
    return pl.pallas_call(
        functools.partial(gather_kernel, n, nf),
        out_shape=(
            jax.ShapeDtypeStruct((n, 2, BLK, D), BF16),
            jax.ShapeDtypeStruct((n, 3 * HD, 2 * BLK), F32),
            jax.ShapeDtypeStruct((3, nf * rows, D), BF16),
            jax.ShapeDtypeStruct((nf,) + vec.shape, F32),
            half, half,
        ),
        in_specs=[in_vmem(), in_vmem(), in_vmem()] + [in_any()] * 6,
        out_specs=(in_any(), in_vmem(), in_any(), in_vmem(), in_any(), in_any()),
        scratch_shapes=[
            VMEM((n, 2, BLK, D), BF16),
            VMEM((4, 2, BLK, D), BF16),
            VMEM((nf * rows, 256), BF16),
            VMEM((256, nf * rows), BF16),
            VMEM((nf,) + vec.shape, F32),
            VMEM((1, nf * rows), F32),
            VMEM((2, rows // 2, D), F32),
            VMEM((6, 2, rows // 2, D), BF16),
            dma((4, n, 2)), dma((n, 2)), dma((peers,)), dma((peers,)), dma((peers,)), dma((peers,)),
            dma((2,)), dma((3,)), dma((3, peers)), dma((3, peers)), dma((3, peers)), dma((3, peers)),
            dma((4,)), dma((6, 2)),
        ],
        compiler_params=pltpu.CompilerParams(
            collective_id=0, has_side_effects=True, vmem_limit_bytes=56 * MIB
        ),
        cost_estimate=cost(60),
        name="gather_tokens",
    )(x, wh, vec, *mats)


class Swap:
    def __init__(self, place, src, dst, send_sem, recv_sem, own_sem):
        self.p, self.src, self.dst = place, src, dst
        self.send_sem, self.recv_sem, self.own_sem = send_sem, recv_sem, own_sem

    def copy(self, s, block):
        p = self.p
        return pltpu.make_async_remote_copy(
            src_ref=self.src.at[(p.c + s) % p.n], dst_ref=self.dst.at[block],
            send_sem=self.send_sem.at[s], recv_sem=self.recv_sem.at[s],
            device_id=((p.c + s) % p.n, p.f), device_id_type=MESH,
        )

    def own(self):
        return pltpu.make_async_copy(self.src.at[self.p.c], self.dst.at[self.p.c], self.own_sem)

    def start(self):
        for s in range(1, self.p.n):
            self.copy(s, self.p.c).start()
        self.own().start()

    def wait(self):
        self.own().wait()
        for s in range(1, self.p.n):
            self.copy(s, (self.p.c + self.p.n - s) % self.p.n).wait_recv()

    def drain(self):
        for s in range(1, self.p.n):
            self.copy(s, self.p.c).wait_send()


def swap_kernel(n, nf, src, dst, send_sem, recv_sem, own_sem):
    p = Place(n, nf)
    p.greet_all(False)
    swap = Swap(p, src, dst, send_sem, recv_sem, own_sem)
    swap.start()
    swap.wait()
    swap.drain()


def swap_out(n, nf, blocks):
    dma = pltpu.SemaphoreType.DMA
    return pl.pallas_call(
        functools.partial(swap_kernel, n, nf),
        out_shape=jax.ShapeDtypeStruct(blocks.shape, blocks.dtype),
        in_specs=[in_vmem()],
        out_specs=in_vmem(),
        scratch_shapes=[dma((n,)), dma((n,)), dma],
        compiler_params=pltpu.CompilerParams(
            collective_id=1, has_side_effects=True, vmem_limit_bytes=32 * MIB
        ),
        cost_estimate=cost(15),
        name="swap_out",
    )(blocks)


def swap_grad_kernel(
    n, nf, src, ot, bt, zt, gb, du, cot,
    dst, sum_out,
    mine, theirs, got, send_sem, recv_sem, own_sem, tw_send, tw_recv, out_sem,
):
    p = Place(n, nf)
    p.greet_all(False)
    swap = Swap(p, src, dst, send_sem, recv_sem, own_sem)
    swap.start()
    part = mine.shape[2]
    rows = 2 * part
    pairs = ((ot, gb), (bt, du), (zt, cot))

    def twin_copy(m):
        return pltpu.make_async_remote_copy(
            src_ref=theirs.at[:, m], dst_ref=got.at[:, m],
            send_sem=tw_send.at[m], recv_sem=tw_recv.at[m],
            device_id=(p.twin, p.f), device_id_type=MESH,
        )

    def out_copy(m):
        return pltpu.make_async_copy(mine.at[:, m], sum_out.at[:, m], out_sem.at[m])

    for half, keep in ((1 - p.core, theirs), (p.core, mine)):
        for m, (left, right) in enumerate(pairs):
            @pl.loop(0, D // WIDE)
            def _(j):
                sl = pl.ds(al(j * WIDE, WIDE), WIDE)
                for source in range(nf):
                    where = pl.ds(al(source * rows + half * part, 16), part)
                    keep[source, m, :, sl] = dot(left[where, :], right[:, sl]).astype(BF16)
            if keep is theirs:
                twin_copy(m).start()
    for m in range(3):
        twin_copy(m).wait_recv()
        for source in range(nf):
            chunk = part // 4 if part % 64 == 0 else part
            @pl.loop(0, part // chunk)
            def _(t):
                where = pl.ds(al(t * chunk, 16), chunk)
                mine[source, m, where, :] = (
                    mine[source, m, where, :].astype(F32) + got[source, m, where, :].astype(F32)
                ).astype(BF16)
        out_copy(m).start()
    swap.wait()
    swap.drain()
    for m in range(3):
        twin_copy(m).wait_send()
        out_copy(m).wait()


def swap_grad(n, nf, blocks, ot, bt, zt, gb, du, cot):
    dma = pltpu.SemaphoreType.DMA
    part = D // nf // 2
    shape = (nf, 3, part, D)
    return pl.pallas_call(
        functools.partial(swap_grad_kernel, n, nf),
        out_shape=(
            jax.ShapeDtypeStruct(blocks.shape, blocks.dtype),
            jax.ShapeDtypeStruct(shape, BF16),
        ),
        in_specs=[in_vmem()] * 7,
        out_specs=(in_vmem(), in_any()),
        scratch_shapes=[
            VMEM(shape, BF16), VMEM(shape, BF16), VMEM(shape, BF16),
            dma((n,)), dma((n,)), dma, dma((3,)), dma((3,)), dma((3,)),
        ],
        compiler_params=pltpu.CompilerParams(
            collective_id=2, has_side_effects=True, vmem_limit_bytes=48 * MIB
        ),
        cost_estimate=cost(18),
        name="swap_grad",
    )(blocks, ot, bt, zt, gb, du, cot)


def seq_start(ends, base, token):
    start = jnp.zeros_like(token)
    for e in ends:
        start = jnp.where(e - base <= token, jnp.maximum(start, e - base), start)
    return start


def read_ends(lengths_ref):
    ends, total = [], jnp.int32(0)
    for i in range(lengths_ref.shape[1]):
        total = total + lengths_ref[0, i]
        ends.append(total)
    return ends


def pad_rows(block):
    return jnp.concatenate([block, jnp.zeros((BLK - HD, block.shape[1]), block.dtype)], axis=0)


class Layout:
    def __init__(self, n, total_blocks):
        self.n = n
        self.hpd = 2 * H // n
        self.half_blocks = total_blocks // 2
        self.size = self.half_blocks * BLK
        self.rows = self.hpd * self.size
        self.tile = 512

    def half(self, i):
        return i if self.hpd == 2 else lax.axis_index("ctx") % 2

    def nat(self, deal_ref, d, i):
        half = self.half(i)
        block = deal_ref[2 * d + half]
        if self.hpd == 1:
            block = block - half * self.half_blocks
        return al(block * BLK, BLK)

    def base(self, unit):
        return self.half(unit) * self.size if self.hpd == 1 else unit * self.size


def fwd_kernel(
    lay, deal_ref, len_ref, qkv_ref, bias_ref, c_ref,
    ot_out, qraw, qst, kt, vt, kn, ot, lse,
    m_ref, l_ref, acc_ref,
):
    tile = lay.tile

    @pl.loop(0, lay.n)
    def _(d):
        for i in range(lay.hpd):
            nat = lay.nat(deal_ref, d, i)
            cols = pl.ds(nat, BLK)
            half = lay.half(i)
            src = pl.ds(half * BLK if lay.hpd == 2 else al(half * BLK, BLK), BLK)
            block = qkv_ref[d, :, src] + bias_ref[...]
            qr, kr, vr = block[:HD], block[HD : 2 * HD], block[2 * HD :]
            qraw[:, cols] = qr
            qst[:, cols] = pad_rows(qr * c_ref[...]).astype(BF16)
            kt[:, cols] = kr.astype(BF16)
            vt[:, cols] = vr.astype(BF16)
            kn[cols, :] = pad_rows(kr).T.astype(BF16)

    ends = read_ends(len_ref)
    for unit in range(lay.hpd):
        base = lay.base(unit)
        row0 = unit * lay.size

        @pl.loop(0, lay.size // tile)
        def _(qi):
            cols = pl.ds(al(row0 + qi * tile, tile), tile)
            t_row = qi * tile + lax.broadcasted_iota(jnp.int32, (1, tile), 1)
            start = seq_start(ends, base, t_row)
            low = seq_start(ends, base, qi * tile) // tile
            m_ref[...] = jnp.full_like(m_ref, NEG)
            l_ref[...] = jnp.zeros_like(l_ref)
            acc_ref[...] = jnp.zeros_like(acc_ref)

            def visit(j, diagonal):
                keys = pl.ds(al(row0 + j * tile, tile), tile)
                s = dot(kn[keys, :], qst[:, cols])
                u = j * tile + lax.broadcasted_iota(jnp.int32, (tile, 1), 0)
                seen = u >= start
                if diagonal:
                    seen = seen & (u <= t_row)
                s = jnp.where(seen, s, NEG)
                m_old = m_ref[...]
                m_new = jnp.maximum(m_old, jnp.max(s, axis=0, keepdims=True))
                p = jnp.exp(s - m_new)
                shrink = jnp.exp(m_old - m_new)
                m_ref[...] = m_new
                l_ref[...] = l_ref[...] * shrink + jnp.sum(p, axis=0, keepdims=True)
                acc_ref[...] = acc_ref[...] * shrink + dot(vt[:, keys], p.astype(BF16))

            @pl.loop(low, qi)
            def _(j):
                visit(j, False)

            visit(qi, True)
            ot[:, cols] = acc_ref[...] / l_ref[...]
            lse[:, cols] = m_ref[...] + jnp.log(l_ref[...])

    @pl.loop(0, lay.n)
    def _(d):
        for i in range(lay.hpd):
            ot_out[d, i] = ot[:, pl.ds(lay.nat(deal_ref, d, i), BLK)].astype(BF16)


def attend(lay, deal, lengths, qkv, bias, factor):
    rows = lay.rows
    return pl.pallas_call(
        functools.partial(fwd_kernel, lay),
        out_shape=(
            jax.ShapeDtypeStruct((lay.n, lay.hpd, HD, BLK), BF16),
            jax.ShapeDtypeStruct((HD, rows), F32),
            jax.ShapeDtypeStruct((BLK, rows), BF16),
            jax.ShapeDtypeStruct((HD, rows), BF16),
            jax.ShapeDtypeStruct((HD, rows), BF16),
            jax.ShapeDtypeStruct((rows, BLK), BF16),
            jax.ShapeDtypeStruct((HD, rows), F32),
            jax.ShapeDtypeStruct((1, rows), F32),
        ),
        in_specs=[in_smem(), in_smem()] + [in_vmem()] * 3,
        out_specs=tuple([in_vmem()] * 8),
        scratch_shapes=[
            VMEM((1, lay.tile), F32), VMEM((1, lay.tile), F32), VMEM((HD, lay.tile), F32),
        ],
        compiler_params=pltpu.CompilerParams(vmem_limit_bytes=56 * MIB),
        cost_estimate=cost(19),
        name="attend",
    )(deal, lengths, qkv, bias, factor)


def bwd_kernel(
    lay, deal_ref, len_ref, dot_ref, qraw, qst, kt, vt, kn, ot, lse, c_ref,
    msg_out, small_out,
    qn, vn, don, dost, delta, dk, dv, dqt, sums,
):
    tile = lay.tile

    @pl.loop(0, lay.n)
    def _(d):
        for i in range(lay.hpd):
            cols = pl.ds(lay.nat(deal_ref, d, i), BLK)
            block = dot_ref[d, i].astype(F32)
            delta[:, cols] = jnp.sum(block * ot[:, cols], axis=0, keepdims=True)
            block = pad_rows(block)
            dost[:, cols] = block.astype(BF16)
            don[cols, :] = block.T.astype(BF16)

    @pl.loop(0, lay.rows // BLK)
    def _(t):
        cols = pl.ds(al(t * BLK, BLK), BLK)
        qn[cols, :] = qst[:, cols].astype(F32).T.astype(BF16)
        vn[cols, :] = pad_rows(vt[:, cols].astype(F32)).T.astype(BF16)
        dk[cols, :] = jnp.zeros((BLK, BLK), F32)
        dv[cols, :] = jnp.zeros((BLK, BLK), F32)

    ends = read_ends(len_ref)
    for unit in range(lay.hpd):
        base = lay.base(unit)
        row0 = unit * lay.size

        @pl.loop(0, lay.size // tile)
        def _(qi):
            cols = pl.ds(al(row0 + qi * tile, tile), tile)
            t_row = qi * tile + lax.broadcasted_iota(jnp.int32, (1, tile), 1)
            start = seq_start(ends, base, t_row)
            low = seq_start(ends, base, qi * tile) // tile
            dqt[:, cols] = jnp.zeros((HD, tile), F32)

            def visit(j, diagonal):
                keys = pl.ds(al(row0 + j * tile, tile), tile)
                s = dot(kn[keys, :], qst[:, cols])
                u = j * tile + lax.broadcasted_iota(jnp.int32, (tile, 1), 0)
                seen = u >= start
                if diagonal:
                    seen = seen & (u <= t_row)
                p = jnp.exp(jnp.where(seen, s - lse[:, cols], NEG))
                dp = dot(vn[keys, :], dost[:, cols])
                ds = (p * (dp - delta[:, cols])).astype(BF16)
                dv[keys, :] += dot(p.astype(BF16), don[cols, :])
                dk[keys, :] += dot(ds, qn[cols, :])
                dqt[:, cols] += dot(kt[:, keys], ds)

            @pl.loop(low, qi)
            def _(j):
                visit(j, False)

            visit(qi, True)

    sums[...] = jnp.zeros_like(sums)

    @pl.loop(0, lay.n)
    def _(d):
        for i in range(lay.hpd):
            cols = pl.ds(lay.nat(deal_ref, d, i), BLK)
            dqs = dqt[:, cols]
            dq = (dqs * c_ref[...]).astype(BF16)
            dkt = dk[cols, :].T[:HD].astype(BF16)
            dvt = dv[cols, :].T[:HD].astype(BF16)
            msg_out[d, 0, i] = dq
            msg_out[d, 1, i] = dkt
            msg_out[d, 2, i] = dvt
            sums[0, :HD] += dqs * qraw[:, cols]
            sums[1, :HD] += dq.astype(F32)
            sums[2, :HD] += dvt.astype(F32)

    small_out[...] = jnp.zeros_like(small_out)
    for r in range(3):
        small_out[r : r + 1, :] = jnp.sum(sums[r].T, axis=0, keepdims=True)


def attend_back(lay, deal, lengths, grad_t, kept, factor):
    rows = lay.rows
    return pl.pallas_call(
        functools.partial(bwd_kernel, lay),
        out_shape=(
            jax.ShapeDtypeStruct((lay.n, 3, lay.hpd, HD, BLK), BF16),
            jax.ShapeDtypeStruct((8, BLK), F32),
        ),
        in_specs=[in_smem(), in_smem()] + [in_vmem()] * 9,
        out_specs=tuple([in_vmem()] * 2),
        scratch_shapes=[
            VMEM((rows, BLK), BF16), VMEM((rows, BLK), BF16), VMEM((rows, BLK), BF16),
            VMEM((BLK, rows), BF16), VMEM((1, rows), F32),
            VMEM((rows, BLK), F32), VMEM((rows, BLK), F32), VMEM((HD, rows), F32),
            VMEM((3, BLK, BLK), F32),
        ],
        compiler_params=pltpu.CompilerParams(vmem_limit_bytes=58 * MIB),
        cost_estimate=cost(25),
        name="attend_back",
    )(deal, lengths, grad_t, *kept, factor)


WIDE = 256


def over_columns(body):
    @pl.loop(0, D // WIDE)
    def _(j):
        body(pl.ds(al(j * WIDE, WIDE), WIDE))


def ffn_kernel(
    x_ref, cot_ref, ot_ref, g2_ref, mats_ref,
    out_ref, dh_ref, gt_ref, ot, bt, zt, gb, du, dg2_ref,
    o_rows, hidden, nh, b, up, z, db, wide,
):
    tok = x_ref.shape[0]
    wo, w1, w2 = mats_ref.at[0], mats_ref.at[1], mats_ref.at[2]
    for i in range(2):
        for h in range(H):
            ot[pl.ds(h * HD, HD), pl.ds(i * BLK, BLK)] = ot_ref[h, i]
    @pl.loop(0, D // WIDE)
    def _(j):
        sl = pl.ds(al(j * WIDE, WIDE), WIDE)
        o_rows[:, sl] = ot[sl, :].astype(F32).T.astype(BF16)

    def body(sl):
        hidden[:, sl] = x_ref[:, sl].astype(F32) + dot(o_rows[...], wo[:, sl])
    over_columns(body)
    hid = hidden[...]
    r2 = lax.rsqrt(jnp.mean(hid * hid, axis=-1, keepdims=True) + EPS)
    nh[...] = hid * r2
    b[...] = (nh[...] * g2_ref[...]).astype(BF16)

    def body(sl):
        u = dot(b[...], w1[:, sl])
        up[:, sl] = u
        z[:, sl] = (u * jax.nn.sigmoid(u)).astype(BF16)
    over_columns(body)

    def body(sl):
        out_ref[:, sl] = (hidden[:, sl] + dot(z[...], w2[:, sl])).astype(BF16)
        dz = dot(cot_ref[...], w2[sl, :], NT)
        u = up[:, sl]
        sig = jax.nn.sigmoid(u)
        du[:, sl] = (dz * sig * (1.0 + u * (1.0 - sig))).astype(BF16)
    over_columns(body)

    def body(sl):
        g = dot(du[...], w1[sl, :], NT)
        db[:, sl] = g * g2_ref[:, sl]
        dg2_ref[:, sl] = jnp.sum(g * nh[:, sl], axis=0, keepdims=True)
    over_columns(body)
    scaled = db[...]
    mean = jnp.mean(scaled * nh[...], axis=-1, keepdims=True)
    dh = cot_ref[...].astype(F32) + r2 * (scaled - nh[...] * mean)
    dh_ref[...] = dh
    gb[...] = dh.astype(BF16)

    @pl.loop(0, D // WIDE)
    def _(j):
        sl = pl.ds(al(j * WIDE, WIDE), WIDE)
        wide[sl, :] = dot(wo[sl, :], gb[...], NT).astype(BF16)
    for i in range(2):
        for h in range(H):
            gt_ref[h, i] = wide[pl.ds(h * HD, HD), pl.ds(i * BLK, BLK)]

    @pl.loop(0, D // WIDE)
    def _(j):
        sl = pl.ds(al(j * WIDE, WIDE), WIDE)
        bt[sl, :] = b[:, sl].astype(F32).T.astype(BF16)
        zt[sl, :] = z[:, sl].astype(F32).T.astype(BF16)


def ffn(x, cot, ot, g2, mats):
    tok = x.shape[0]
    turned = jax.ShapeDtypeStruct((D, tok), BF16)
    plain = jax.ShapeDtypeStruct((tok, D), BF16)
    return pl.pallas_call(
        ffn_kernel,
        out_shape=(
            plain,
            jax.ShapeDtypeStruct((tok, D), F32),
            jax.ShapeDtypeStruct((H, 2, HD, BLK), BF16),
            turned, turned, turned, plain, plain,
            jax.ShapeDtypeStruct((1, D), F32),
        ),
        in_specs=[in_vmem()] * 5,
        out_specs=tuple([in_vmem()] * 9),
        scratch_shapes=[
            VMEM((tok, D), BF16), VMEM((tok, D), F32), VMEM((tok, D), F32),
            VMEM((tok, D), BF16), VMEM((tok, D), F32), VMEM((tok, D), BF16),
            VMEM((tok, D), F32), VMEM((D, tok), BF16),
        ],
        compiler_params=pltpu.CompilerParams(vmem_limit_bytes=56 * MIB),
        cost_estimate=cost(20),
        name="feed_forward",
    )(x, cot, ot, g2, mats)


VEC_ROWS = 24


def finish_kernel(
    n, nf, hpd, msg, a_ref, sums_ref, mine_ref, other_ref, got_ref, tgot_ref,
    x_ref, dh_ref, g1_ref, dg2_ref, small_ref,
    gx_out, dw_out, fw_out, vec_out,
    back, abuf, left, dw, dwsend, dwrecv, dwown, w, wide, dat, vx, vsum, vall,
    sw_send, sw_recv, sw_own, a_sem, w_sem, x_send, x_recv, own_sem, ag_send, ag_recv, v_send, v_recv, u_send, u_recv,
    fg_send, fg_recv, sums_sem, sums, *reduce_scratch,
):
    p = Place(n, nf)
    c, f = p.c, p.f
    rows = dwsend.shape[2]
    part = rows // 2
    load = pltpu.make_async_copy(sums_ref, sums, sums_sem)
    load.start()
    p.greet_all(True)
    swap = Swap(p, msg, back, sw_send, sw_recv, sw_own)
    swap.start()
    result = reduce_scratch[0]
    reduce = Reduce(p, sums, *reduce_scratch[:6], reduce_scratch[6:])
    load.wait()
    reduce.start_x()

    if hpd == 2:
        a_copy = pltpu.make_async_copy(a_ref, abuf, a_sem)
    else:
        a_copy = pltpu.make_async_copy(a_ref.at[:, pl.ds(c % 2, 1)], abuf, a_sem)
    a_copy.start()
    w_copies = []
    for m in range(3):
        def put(src, source, half):
            at = pl.ds(al(source * rows + half * part, 16), part)
            w_copies.append(pltpu.make_async_copy(src, w.at[m, at], w_sem.at[len(w_copies)]))
        put(mine_ref.at[m], f, p.core)
        put(other_ref.at[m], f, 1 - p.core)
        for s, source in enumerate(p.fsources):
            put(got_ref.at[s, m], source, p.core)
            put(tgot_ref.at[s, m], source, 1 - p.core)
    for copy in w_copies:
        copy.start()

    for d in range(n):
        for i in range(hpd):
            left[:, pl.ds((d * hpd + i) * BLK, BLK)] = msg[d, :, i].reshape(3 * HD, BLK)
    a_copy.wait()
    depth = n * hpd * BLK
    @pl.loop(0, D // WIDE)
    def _(j):
        sl = pl.ds(al(j * WIDE, WIDE), WIDE)
        dw[:, sl] = dot(left[...], abuf[:, :, :, sl].reshape(depth, WIDE))
    for source in range(nf):
        dwsend[source] = dw[:, source * rows : (source + 1) * rows].astype(BF16)

    def x_copy(s, peer):
        return pltpu.make_async_remote_copy(
            src_ref=dwsend.at[peer], dst_ref=dwrecv.at[s],
            send_sem=x_send.at[s], recv_sem=x_recv.at[s],
            device_id=(c, peer), device_id_type=MESH,
        )

    for s, peer in enumerate(p.fpeers):
        x_copy(s, peer).start()
    total = dwsend[f].astype(F32)
    for s, peer in enumerate(p.fpeers):
        x_copy(s, peer).wait_recv()
        total = total + dwrecv[s].astype(F32)
    dwown[...] = total.astype(BF16)
    own = pltpu.make_async_copy(dwown, dw_out.at[c], own_sem)
    own.start()
    own.wait()
    spread = Spread(p, dw_out, ag_send, ag_recv, 1)
    spread.start(0)

    zlen = p.zlen
    for t in range(2 * zlen - 1):
        if t < zlen:
            reduce.xy(t)
        if 1 <= t <= zlen:
            reduce.after_y(t - 1)
            reduce.chain(t - 1, 0)
        for hop in range(1, zlen - 1):
            if 0 <= t - 1 - hop < zlen:
                reduce.chain(t - 1 - hop, hop)
        if 1 <= t < zlen:
            spread.chain(t, 0)
            spread.pair(t - 1, 0)
    reduce.last()
    own = pltpu.make_async_copy(result, fw_out.at[c], own_sem)
    own.start()
    own.wait()
    spread2 = Spread(p, fw_out, fg_send, fg_recv, 1)
    spread2.start(0)

    swap.wait()
    for m in range(3):
        for i in range(2):
            for h in range(H):
                block = back[h, m, i] if hpd == 2 else back[2 * h + i, m, 0]
                wide[m, pl.ds(h * HD, HD), pl.ds(i * BLK, BLK)] = block
    for copy in w_copies:
        copy.wait()

    @pl.loop(0, D // WIDE)
    def _(j):
        sl = pl.ds(al(j * WIDE, WIDE), WIDE)
        total = dot(w[0, sl, :], wide[0]) + dot(w[1, sl, :], wide[1]) + dot(w[2, sl, :], wide[2])
        dat[:, sl] = total.T
    x = x_ref[...].astype(F32)
    r1 = lax.rsqrt(jnp.mean(x * x, axis=-1, keepdims=True) + EPS)
    na = x * r1
    da = dat[...]
    dg1 = jnp.sum(da * na, axis=0, keepdims=True)
    for r in range(D // BLK):
        vx[f, r : r + 1, :] = dg1[:, r * BLK : (r + 1) * BLK]
        vx[f, D // BLK + r : D // BLK + r + 1, :] = dg2_ref[:, r * BLK : (r + 1) * BLK]
    vx[f, 20:24, :] = small_ref[0:4, :]

    def v_copy(s, peer, source):
        return pltpu.make_async_remote_copy(
            src_ref=vx.at[f], dst_ref=vx.at[source],
            send_sem=v_send.at[s], recv_sem=v_recv.at[s],
            device_id=(c, peer), device_id_type=MESH,
        )

    for s, peer in enumerate(p.fpeers):
        v_copy(s, peer, f).start()
    scaled = da * g1_ref[...]
    mean = jnp.mean(scaled * na, axis=-1, keepdims=True)
    gx_out[...] = dh_ref[...] + r1 * (scaled - na * mean)
    for s, (peer, source) in enumerate(zip(p.fpeers, p.fsources)):
        v_copy(s, peer, source).wait_recv()
    vsum[...] = jnp.sum(vx[...], axis=0)
    vall[c] = vsum[...]

    def u_copy(s, block):
        return pltpu.make_async_remote_copy(
            src_ref=vsum, dst_ref=vall.at[block],
            send_sem=u_send.at[s], recv_sem=u_recv.at[s],
            device_id=((c + s) % n, f), device_id_type=MESH,
        )

    for s in range(1, n):
        u_copy(s, c).start()
    spread.pair(p.zlen - 1, 0)
    for k in range(1, zlen):
        spread2.chain(k, 0)
        spread2.pair(k - 1, 0)
    spread2.pair(zlen - 1, 0)
    for k in range(p.zlen):
        for zz, guard, _ in p.level(k):
            when(guard, lambda zz=zz: spread.from_twin(zz))
            when(guard, lambda zz=zz: spread2.from_twin(zz))
    for s in range(1, n):
        u_copy(s, (c + n - s) % n).wait_recv()
    vec_out[...] = vall[...]
    swap.drain()
    spread.drain()
    spread2.drain()
    reduce.drain()
    for s, peer in enumerate(p.fpeers):
        x_copy(s, peer).wait_send()
        v_copy(s, peer, f).wait_send()
    for s in range(1, n):
        u_copy(s, c).wait_send()


def finish(n, nf, hpd, msg, tokens, sums, mine, other, got, tgot, x, dh, g1, dg2, small):
    dma = pltpu.SemaphoreType.DMA
    rows = D // nf
    peers = max(nf - 1, 1)
    tok = x.shape[0]
    return pl.pallas_call(
        functools.partial(finish_kernel, n, nf, hpd),
        out_shape=(
            jax.ShapeDtypeStruct((tok, D), F32),
            jax.ShapeDtypeStruct((n, 3 * HD, rows), BF16),
            jax.ShapeDtypeStruct((n, sums.shape[1] * 4 // n, D // 2), BF16),
            jax.ShapeDtypeStruct((n, VEC_ROWS, BLK), F32),
        ),
        in_specs=[in_vmem()] + [in_any()] * 6 + [in_vmem()] * 5,
        out_specs=(in_vmem(), in_any(), in_any(), in_vmem()),
        scratch_shapes=[
            VMEM(msg.shape, BF16), VMEM((n, hpd, BLK, D), BF16), VMEM((3 * HD, n * hpd * BLK), BF16),
            VMEM((3 * HD, D), F32), VMEM((nf, 3 * HD, rows), BF16), VMEM((peers, 3 * HD, rows), BF16),
            VMEM((3 * HD, rows), BF16), VMEM((3, D, D), BF16), VMEM((3, D, tok), BF16), VMEM((tok, D), F32),
            VMEM((nf, VEC_ROWS, BLK), F32), VMEM((VEC_ROWS, BLK), F32), VMEM((n, VEC_ROWS, BLK), F32),
            dma((n,)), dma((n,)), dma, dma, dma((6 * nf,)), dma((peers,)), dma((peers,)), dma,
            dma((4, n, 1)), dma((n, 1)), dma((peers,)), dma((peers,)), dma((n,)), dma((n,)),
            dma((4, n, 1)), dma((n, 1)), dma, VMEM(sums.shape, BF16),
        ] + Reduce.scratch(nf, n // 4, sums.shape[1]),
        compiler_params=pltpu.CompilerParams(
            collective_id=3, has_side_effects=True, vmem_limit_bytes=60 * MIB
        ),
        cost_estimate=cost(60),
        name="finish",
    )(msg, tokens, sums, mine, other, got, tgot, x, dh, g1, dg2, small)


def turn_kernel(hpd, dw_ref, q_ref, k_ref, v_ref, wide):
    j = pl.program_id(0)

    @pl.when(j == 0)
    def _():
        for m in range(3):
            for h in range(H):
                at = pl.ds(m * HD, HD)
                if hpd == 2:
                    block = dw_ref[h, at, :].astype(F32)
                else:
                    block = dw_ref[2 * h, at, :].astype(F32) + dw_ref[2 * h + 1, at, :].astype(F32)
                wide[m, pl.ds(h * HD, HD), :] = block

    for m, out in enumerate((q_ref, k_ref, v_ref)):
        out[...] = wide[m, pl.ds(al(j * WIDE, WIDE), WIDE), :].T


def turn(hpd, dw):
    n, _, rows = dw.shape
    spec = pl.BlockSpec((rows, WIDE), lambda j: (0, j))
    return pl.pallas_call(
        functools.partial(turn_kernel, hpd),
        grid=(D // WIDE,),
        out_shape=tuple([jax.ShapeDtypeStruct((rows, D), F32)] * 3),
        in_specs=[pl.BlockSpec((n, 3 * HD, rows), lambda j: (0, 0, 0))],
        out_specs=(spec, spec, spec),
        scratch_shapes=[VMEM((3, D, rows), F32)],
        compiler_params=pltpu.CompilerParams(vmem_limit_bytes=48 * MIB),
        cost_estimate=cost(6),
        name="turn",
    )(dw)


def widen_kernel(zlen, part, in_ref, o_ref, u_ref, d_ref):
    j, y = pl.program_id(0), pl.program_id(1)
    height = in_ref.shape[3]
    for m, out in enumerate((o_ref, u_ref, d_ref)):
        for z in range(zlen):
            first, last = max(m * part, z * height), min((m + 1) * part, (z + 1) * height)
            if first < last:
                out[first - m * part : last - m * part, :] = in_ref[
                    z, y, j, first - z * height : last - z * height, :
                ].astype(F32)


def widen(zlen, part, pieces):
    height, half = pieces.shape[1:]
    spec = pl.BlockSpec((part, half), lambda j, y: (j, y))
    return pl.pallas_call(
        functools.partial(widen_kernel, zlen, part),
        grid=(2, 2),
        out_shape=tuple([jax.ShapeDtypeStruct((2 * part, D), F32)] * 3),
        in_specs=[pl.BlockSpec((zlen, 2, 2, height, half), lambda j, y: (0, 0, 0, 0, 0))],
        out_specs=(spec, spec, spec),
        compiler_params=pltpu.CompilerParams(vmem_limit_bytes=48 * MIB),
        cost_estimate=cost(5),
        name="widen",
    )(pieces.reshape(zlen, 2, 2, height, half))


def local(
    n, nf, tokens, cotangent, lengths, deal, gain_attn, query_weight, query_bias, key_weight,
    value_weight, value_bias, query_scale, proj_weight, gain_ffn, up_weight, down_weight,
):
    c = lax.axis_index("ctx")
    f = lax.axis_index("fsdp")
    lay = Layout(n, deal.shape[0])
    head = c * lay.hpd // 2
    rows = query_weight.shape[0]
    x, cot = tokens[0], cotangent[0]

    def low(v):
        return v.astype(BF16).astype(F32)

    g1_own = low(gain_attn)
    slices = [
        lax.dynamic_slice(w, (0, head * HD), (rows, HD)) for w in (query_weight, key_weight, value_weight)
    ]
    wh = jnp.pad(jnp.concatenate(slices, axis=1), ((0, 0), (0, 256 - 3 * HD))).astype(BF16)
    vec = jnp.stack([g1_own, low(query_bias), low(value_bias), low(gain_ffn)])
    vec = jnp.concatenate([vec, jnp.pad(low(query_scale), (0, rows - query_scale.shape[0]))[None]])
    vec = jnp.pad(vec, ((0, 3), (0, -rows % 128)))

    a_all, qkv, mats, vecs, mine, other = gather(
        n, nf, x, wh, vec, (proj_weight, up_weight, down_weight, query_weight, key_weight, value_weight)
    )
    whole = jnp.swapaxes(vecs[:, :5, :rows], 0, 1).reshape(5, nf * rows)
    g1, bq, bv, g2 = whole[0], whole[1], whole[2], whole[3]
    q_param = vecs[:, 4, : query_scale.shape[0]].reshape(HD)
    factor = jnp.log(1.0 + jnp.exp(q_param)) * (LOG2E / math.sqrt(HD))
    bias = jnp.concatenate([
        lax.dynamic_slice(bq, (head * HD,), (HD,)), jnp.zeros((HD,), F32),
        lax.dynamic_slice(bv, (head * HD,), (HD,)),
    ])
    bias = jnp.broadcast_to(bias[:, None], (3 * HD, BLK))
    factor_col = jnp.broadcast_to(factor[:, None], (HD, BLK))

    twins = [(i, i ^ 1) for i in range(n)]
    got = jnp.stack([
        lax.ppermute(mine, "fsdp", [(i, (i + s) % nf) for i in range(nf)]) for s in range(1, nf)
    ])
    tgot = lax.ppermute(got, "ctx", twins)

    ot, *kept = attend(lay, deal, lengths, qkv, bias, factor_col)
    ot = swap_out(n, nf, ot).reshape(H, 2, HD, BLK)
    layer_out, dh, gt, ott, bt, zt, gb, du, dg2 = ffn(x, cot, ot, g2[None], mats)
    gt, sums = swap_grad(n, nf, gt.reshape(n, lay.hpd, HD, BLK), ott, bt, zt, gb, du, cot)

    part = rows // 2
    zlen = n // 4
    sums = jnp.pad(sums.reshape(nf, 3 * part, D), ((0, 0), (0, -3 * part % (16 * zlen)), (0, 0)))

    msg, small = attend_back(lay, deal, lengths, gt, kept, factor_col)
    grad_x, dw, pieces, vectors = finish(
        n, nf, lay.hpd, msg, a_all, sums, mine, other, got, tgot, x, dh, g1[None], dg2, small
    )
    dwq, dwk, dwv = turn(lay.hpd, dw)
    grads = widen(zlen, part, pieces)

    def own(v):
        size = v.shape[0] // nf
        return lax.dynamic_slice(v, (f * size,), (size,))

    def of_heads(r):
        return vectors[:, r, :HD].reshape(H, 2 // lay.hpd, HD).sum(axis=1).reshape(D)

    gains = jnp.sum(vectors[:, : 2 * D // BLK], axis=0).reshape(2, D)
    grad_scale = jnp.sum(vectors[:, 20, :HD], axis=0) * jax.nn.sigmoid(q_param) * (LOG2E / math.sqrt(HD))
    return (
        layer_out[None],
        grad_x[None],
        own(gains[0]),
        dwq,
        own(of_heads(21)),
        dwk,
        dwv,
        own(of_heads(22)),
        own(grad_scale),
        grads[0],
        own(gains[1]),
        grads[1],
        grads[2],
    )


def solution(mesh):
    whole, vector, matrix = P("fsdp", "ctx", None), P("fsdp"), P("fsdp", None)
    return jax.shard_map(
        functools.partial(local, mesh.shape["ctx"], mesh.shape["fsdp"]),
        mesh=mesh,
        in_specs=(
            whole, whole, matrix, P(), vector, matrix, vector, matrix, matrix, vector, vector,
            matrix, vector, matrix, matrix,
        ),
        out_specs=(
            whole, whole, vector, matrix, vector, matrix, matrix, vector, vector, matrix, vector,
            matrix, matrix,
        ),
        check_vma=False,
    )
```

```python
import functools
import math

import jax
import jax.numpy as jnp
from jax import lax
from jax.experimental import pallas as pl
from jax.experimental.pallas import tpu as pltpu
from jax.sharding import PartitionSpec as P

H = 16
HD = 80
BLK = 128
D = 1280
EPS = 1e-06
LOG2E = 1.442695041
NEG = -1e30
MESH = pl.DeviceIdType.MESH
F32 = jnp.float32
BF16 = jnp.bfloat16
VMEM = pltpu.VMEM
MIB = 1 << 20

NN = (((1,), (0,)), ((), ()))
NT = (((1,), (1,)), ((), ()))
TN = (((0,), (0,)), ((), ()))


def dot(left, right, dims=NN):
    return lax.dot_general(left, right, dims, preferred_element_type=F32)


def al(value, multiple):
    return pl.multiple_of(value, multiple)


def in_vmem():
    return pl.BlockSpec(memory_space=pltpu.VMEM)


def in_smem():
    return pl.BlockSpec(memory_space=pltpu.SMEM)


def in_any():
    return pl.BlockSpec(memory_space=pl.ANY)


def cost(microseconds):
    return pl.CostEstimate(flops=0, bytes_accessed=int(microseconds * 3.0e6), transcendentals=0)


class Place:
    def __init__(self, n, nf):
        self.n, self.nf = n, nf
        self.c = lax.axis_index("ctx")
        self.f = lax.axis_index("fsdp")
        self.zlen = n // 4
        self.z, self.y, self.core = self.c // 4, (self.c // 2) % 2, self.c % 2
        self.twin = self.idx(self.z, self.y, 1 - self.core)
        self.ypeer = self.idx(self.z, 1 - self.y, self.core)
        self.targets = (
            self.idx(self.z + 1, self.y, self.core), self.idx(self.z - 1, self.y, self.core),
            self.ypeer, self.twin,
        )
        self.guards = (self.z < self.zlen - 1, self.z > 0, None, None)
        self.fpeers = [(self.f + s) % nf for s in range(1, nf)]
        self.fsources = [(self.f + nf - s) % nf for s in range(1, nf)]

    def idx(self, z, y, core):
        return (z * 2 + y) * 2 + core

    def level(self, k):
        if k == 0:
            return [(self.z, None, 0)]
        return [
            (self.z + k, self.z + k < self.zlen, 1),
            (self.z - k, self.z - k >= 0, -1),
        ]

    def greet_neighbours(self):
        barrier = pltpu.get_barrier_semaphore()
        for target, guard in zip(self.targets, self.guards):
            when(guard, lambda target=target: pl.semaphore_signal(
                barrier, inc=1, device_id=(target, self.f), device_id_type=MESH))
        for peer in self.fpeers:
            pl.semaphore_signal(barrier, inc=1, device_id=(self.c, peer), device_id_type=MESH)
        ends = jnp.minimum(self.z, 1) + jnp.minimum(self.zlen - 1 - self.z, 1)
        pl.semaphore_wait(barrier, 1 + self.nf + ends)

    def greet_all(self, with_fsdp):
        barrier = pltpu.get_barrier_semaphore()
        for s in range(1, self.n):
            pl.semaphore_signal(
                barrier, inc=1, device_id=((self.c + s) % self.n, self.f), device_id_type=MESH)
        if with_fsdp:
            for peer in self.fpeers:
                pl.semaphore_signal(barrier, inc=1, device_id=(self.c, peer), device_id_type=MESH)
        pl.semaphore_wait(barrier, self.n - 1 + (self.nf - 1 if with_fsdp else 0))


def when(guard, body):
    if guard is None:
        body()
    else:
        pl.when(guard)(body)


class Spread:
    def __init__(self, place, buf, send_sem, recv_sem, pieces):
        self.p, self.buf, self.send_sem, self.recv_sem, self.pieces = place, buf, send_sem, recv_sem, pieces

    def copy(self, way, origin, i):
        where = self.buf.at[origin, i]
        return pltpu.make_async_remote_copy(
            src_ref=where, dst_ref=where,
            send_sem=self.send_sem.at[way, origin, i], recv_sem=self.recv_sem.at[origin, i],
            device_id=(self.p.targets[way], self.p.f), device_id_type=MESH,
        )

    def send(self, way, origin, i):
        when(self.p.guards[way], lambda: self.copy(way, origin, i).start())

    def arrive(self, origin, i):
        self.copy(3, origin, i).wait_recv()

    def start(self, i):
        for way in range(4):
            self.send(way, self.p.c, i)

    def chain(self, k, i):
        p = self.p
        for zz, guard, sign in p.level(k):
            def body(zz=zz, sign=sign):
                origin = p.idx(zz, p.y, p.core)
                self.arrive(origin, i)
                self.send(1 if sign == 1 else 0, origin, i)
                self.send(2, origin, i)
                self.send(3, origin, i)
            when(guard, body)

    def pair(self, k, i):
        p = self.p
        for zz, guard, _ in p.level(k):
            def body(zz=zz):
                origin = p.idx(zz, 1 - p.y, p.core)
                self.arrive(origin, i)
                self.send(3, origin, i)
            when(guard, body)

    def from_twin(self, zz):
        p = self.p
        for yy in (p.y, 1 - p.y):
            for i in range(self.pieces):
                self.arrive(p.idx(zz, yy, 1 - p.core), i)

    def drain(self):
        p = self.p
        for i in range(self.pieces):
            for way in range(4):
                when(p.guards[way], lambda way=way, i=i: self.copy(way, p.c, i).wait_send())
            for k in range(p.zlen):
                for zz, guard, sign in p.level(k):
                    def body(zz=zz, sign=sign, k=k, i=i):
                        if k:
                            origin = p.idx(zz, p.y, p.core)
                            on = 1 if sign == 1 else 0
                            when(p.guards[on], lambda: self.copy(on, origin, i).wait_send())
                            self.copy(2, origin, i).wait_send()
                            self.copy(3, origin, i).wait_send()
                        self.copy(3, p.idx(zz, 1 - p.y, p.core), i).wait_send()
                    when(guard, body)


class Reduce:
    def __init__(self, place, mine, result, acc, xrecv, yrecv, urecv, drecv, sems):
        self.p, self.mine, self.result, self.acc = place, mine, result, acc
        self.xrecv, self.yrecv, self.urecv, self.drecv = xrecv, yrecv, urecv, drecv
        (self.xs, self.xr, self.ys, self.yr, self.us, self.ur, self.ds, self.dr) = sems
        self.height = acc.shape[0] // place.zlen
        self.width = D // 2
        zlen = place.zlen
        ends = []
        for k in range(zlen // 2):
            ends += [zlen - 1 - k, k]
        self.order = ends

    @staticmethod
    def scratch(nf, zlen, height):
        dma = pltpu.SemaphoreType.DMA
        peers = max(nf - 1, 1)
        piece = VMEM((zlen, height // zlen, D // 2), BF16)
        return [
            VMEM((height // zlen, D // 2), BF16), VMEM((height, D), BF16), VMEM((peers, height, D), BF16),
            piece, piece, piece,
            dma((peers, zlen, 2)), dma((peers, zlen, 2)), dma((zlen,)), dma((zlen,)),
            dma((zlen,)), dma((zlen,)), dma((zlen,)), dma((zlen,)),
        ]

    def at(self, piece, side):
        return (
            pl.ds(al(piece * self.height, 16), self.height),
            pl.ds(al(side * self.width, 128), self.width),
        )

    def remote(self, src, dst, send, recv, c, f):
        return pltpu.make_async_remote_copy(
            src_ref=src, dst_ref=dst, send_sem=send, recv_sem=recv,
            device_id=(c, f), device_id_type=MESH,
        )

    def x_copy(self, s, peer, piece, turn):
        side = (self.p.y + 1 + turn) % 2
        where = self.at(piece, side)
        return self.remote(
            self.mine.at[peer].at[where], self.xrecv.at[s].at[where],
            self.xs.at[s, piece, turn], self.xr.at[s, piece, turn], self.p.c, peer,
        )

    def start_x(self, t):
        for turn in range(2):
            for s, peer in enumerate(self.p.fpeers):
                self.x_copy(s, peer, self.order[t], turn).start()

    def add(self, dst, terms, count=None):
        count = count or self.height
        step = 48 if count % 48 == 0 else 16
        @pl.loop(0, count // step)
        def _(t):
            at = pl.ds(al(t * step, 16), step)
            total = terms[0][at, :].astype(F32)
            for term in terms[1:]:
                total = total + term[at, :].astype(F32)
            dst[at, :] = total.astype(BF16)

    def sum_x(self, piece, turn):
        side = (self.p.y + 1 + turn) % 2
        where = self.at(piece, side)
        terms = [self.mine.at[self.p.f].at[where]]
        for s, peer in enumerate(self.p.fpeers):
            self.x_copy(s, peer, piece, turn).wait_recv()
            terms.append(self.xrecv.at[s].at[where])
        self.add(self.acc.at[where], terms)

    def y_copy(self, piece):
        src = self.acc.at[self.at(piece, 1 - self.p.y)]
        return self.remote(
            src, self.yrecv.at[piece], self.ys.at[piece], self.yr.at[piece], self.p.ypeer, self.p.f)

    def u_copy(self, piece):
        src = self.acc.at[self.at(piece, self.p.y)]
        return self.remote(
            src, self.urecv.at[piece], self.us.at[piece], self.ur.at[piece], self.p.targets[0], self.p.f)

    def d_copy(self, piece):
        src = self.acc.at[self.at(piece, self.p.y)]
        return self.remote(
            src, self.drecv.at[piece], self.ds.at[piece], self.dr.at[piece], self.p.targets[1], self.p.f)

    def mine_of(self, piece):
        return self.acc.at[self.at(piece, self.p.y)]

    def xy(self, t):
        piece = self.order[t]
        self.sum_x(piece, 0)
        self.y_copy(piece).start()
        self.sum_x(piece, 1)

    def after_y(self, t):
        piece = self.order[t]
        self.y_copy(piece).wait_recv()
        self.add(self.mine_of(piece), [self.mine_of(piece), self.yrecv.at[piece]])

    def chain(self, t, hop):
        p, piece = self.p, self.order[t]
        if hop < piece:
            @pl.when(p.z == hop)
            def _():
                if hop:
                    self.u_copy(piece).wait_recv()
                    self.add(self.mine_of(piece), [self.mine_of(piece), self.urecv.at[piece]])
                self.u_copy(piece).start()
        if p.zlen - 1 - hop > piece:
            @pl.when(p.z == p.zlen - 1 - hop)
            def _():
                if hop:
                    self.d_copy(piece).wait_recv()
                    self.add(self.mine_of(piece), [self.mine_of(piece), self.drecv.at[piece]])
                self.d_copy(piece).start()

    def last(self):
        p = self.p
        @pl.when(p.z > 0)
        def _():
            self.u_copy(p.z).wait_recv()
            self.add(self.mine_of(p.z), [self.mine_of(p.z), self.urecv.at[p.z]])
        @pl.when(p.z < p.zlen - 1)
        def _():
            self.d_copy(p.z).wait_recv()
            self.add(self.mine_of(p.z), [self.mine_of(p.z), self.drecv.at[p.z]])
        self.add(self.result, [self.mine_of(p.z)])

    def drain(self):
        p = self.p
        for piece in self.order:
            for turn in range(2):
                for s, peer in enumerate(p.fpeers):
                    self.x_copy(s, peer, piece, turn).wait_send()
            self.y_copy(piece).wait_send()
            pl.when(p.z < piece)(lambda piece=piece: self.u_copy(piece).wait_send())
            pl.when(p.z > piece)(lambda piece=piece: self.d_copy(piece).wait_send())


def gather_kernel(
    n, nf, x_ref, wh_ref, vec_ref, wo_ref, w1_ref, w2_ref, wq_ref, wk_ref, wv_ref,
    a_out, qkv_out, mats_out, vecs_out, mine_out, other_out,
    abuf, norm, whbuf, wht, vecbuf, g1_ref, stage, wcast,
    ag_send, ag_recv, wh_send, wh_recv, vec_send, vec_recv,
    ld_sem, own_sem, mx_send, mx_recv, ms_send, ms_recv, a_sem, keep_sem,
):
    p = Place(n, nf)
    c, f, core, zlen = p.c, p.f, p.core, p.zlen
    rows = wh_ref.shape[0]
    part = rows // 2
    p.greet_neighbours()
    spread = Spread(p, abuf, ag_send, ag_recv, 2)

    for i in range(2):
        abuf[c, i] = x_ref[pl.ds(i * BLK, BLK), :]
        spread.start(i)

    def wh_copy(s, peer):
        return pltpu.make_async_remote_copy(
            src_ref=wh_ref, dst_ref=whbuf.at[pl.ds(al(f * rows, 16), rows)],
            send_sem=wh_send.at[s], recv_sem=wh_recv.at[s],
            device_id=(c, peer), device_id_type=MESH,
        )

    def vec_copy(s, peer):
        return pltpu.make_async_remote_copy(
            src_ref=vec_ref, dst_ref=vecbuf.at[f],
            send_sem=vec_send.at[s], recv_sem=vec_recv.at[s],
            device_id=(c, peer), device_id_type=MESH,
        )

    for s, peer in enumerate(p.fpeers):
        vec_copy(s, peer).start()
        wh_copy(s, peer).start()
    whbuf[pl.ds(al(f * rows, 16), rows), :] = wh_ref[...]
    vecbuf[f] = vec_ref[...]

    shards = (wo_ref, w1_ref, w2_ref, wq_ref, wk_ref, wv_ref)
    steps = [(m, h) for h in range(2) for m in range(3)] + [(m, h) for h in range(2) for m in range(3, 6)]

    def half_of(h):
        return (core + h) % 2

    def load(step):
        m, h = steps[step]
        return pltpu.make_async_copy(
            shards[m].at[pl.ds(al(half_of(h) * part, 16), part)],
            stage.at[step % 2], ld_sem.at[step % 2],
        )

    def mx_copy(m, s, peer, source):
        return pltpu.make_async_remote_copy(
            src_ref=wcast.at[m, core],
            dst_ref=mats_out.at[m, pl.ds(al(source * rows + core * part, 16), part)],
            send_sem=mx_send.at[m, s], recv_sem=mx_recv.at[m, s],
            device_id=(c, peer), device_id_type=MESH,
        )

    def keep_copies(m):
        if m < 3:
            return [
                pltpu.make_async_copy(
                    wcast.at[m, h], mats_out.at[m, pl.ds(al(f * rows + h * part, 16), part)],
                    keep_sem.at[m, h],
                ) for h in range(2)
            ]
        return [
            pltpu.make_async_copy(wcast.at[m, half_of(h)], out.at[m - 3], keep_sem.at[m, h])
            for h, out in enumerate((mine_out, other_out))
        ]

    def cast(step):
        m, h = steps[step]
        if step + 1 < len(steps):
            load(step + 1).start()
        load(step).wait()
        chunk = part // 4 if part % 64 == 0 else part
        @pl.loop(0, part // chunk)
        def _(t):
            wcast[m, half_of(h), pl.ds(al(t * chunk, 16), chunk), :] = stage[
                step % 2, pl.ds(al(t * chunk, 16), chunk), :
            ].astype(BF16)
        if h == 0 and m < 3:
            for s, peer in enumerate(p.fpeers):
                mx_copy(m, s, peer, f).start()
        if h == 1:
            for copy in keep_copies(m):
                copy.start()

    load(0).start()
    for step in range(len(steps)):
        cast(step)

    for s, peer in enumerate(p.fpeers):
        wh_copy(s, peer).wait_recv()
        vec_copy(s, peer).wait_recv()
    wht[...] = whbuf[...].astype(F32).T.astype(BF16)
    vecs_out[...] = vecbuf[...]
    for source in range(nf):
        g1_ref[:, pl.ds(source * rows, rows)] = vecbuf[source, 0:1, 0:rows]

    def a_copy(slot, origin):
        return pltpu.make_async_copy(norm.at[slot], a_out.at[origin], a_sem.at[slot])

    def project(slot, origin):
        for i in range(2):
            x = abuf[origin, i].astype(F32)
            scale = lax.rsqrt(jnp.mean(x * x, axis=-1, keepdims=True) + EPS)
            norm[slot, i] = (x * scale * g1_ref[...]).astype(BF16)
        a_copy(slot, origin).start()
        block = norm[slot].reshape(2 * BLK, D)
        qkv_out[origin] = dot(wht[: 3 * HD, :], block, NT)

    def compute(k):
        for zz, guard, _ in p.level(k):
            def body(zz=zz):
                spread.from_twin(zz)
                @pl.loop(0, 4)
                def _(t):
                    if k:
                        a_copy(t, zz * 4 + t).wait()
                    project(t, zz * 4 + t)
            when(guard, body)

    def ms_copy(m, s, source, half):
        where = mats_out.at[m, pl.ds(al(source * rows + half * part, 16), part)]
        return pltpu.make_async_remote_copy(
            src_ref=where, dst_ref=where,
            send_sem=ms_send.at[m, s], recv_sem=ms_recv.at[m, s],
            device_id=(p.twin, f), device_id_type=MESH,
        )

    def pass_matrix(m):
        for s, (peer, source) in enumerate(zip(p.fpeers, p.fsources)):
            mx_copy(m, s, peer, source).wait_recv()
            ms_copy(m, s, source, core).start()

    for k in range(1, zlen):
        for i in range(2):
            spread.chain(k, i)
            spread.pair(k - 1, i)
        compute(k - 1)
        if k == 2:
            pass_matrix(0)
    for i in range(2):
        spread.pair(zlen - 1, i)
    pass_matrix(1)
    compute(zlen - 1)
    pass_matrix(2)

    for m in range(6):
        for copy in keep_copies(m):
            copy.wait()
    for m in range(3):
        for s, (peer, source) in enumerate(zip(p.fpeers, p.fsources)):
            mx_copy(m, s, peer, f).wait_send()
            ms_copy(m, s, source, core).wait_send()
            ms_copy(m, s, source, 1 - core).wait_recv()
    for s, peer in enumerate(p.fpeers):
        wh_copy(s, peer).wait_send()
        vec_copy(s, peer).wait_send()
    spread.drain()
    for slot in range(4):
        a_copy(slot, slot).wait()


def gather(n, nf, x, wh, vec, mats):
    rows = wh.shape[0]
    dma = pltpu.SemaphoreType.DMA
    peers = max(nf - 1, 1)
    half = jax.ShapeDtypeStruct((3, rows // 2, D), BF16)
    return pl.pallas_call(
        functools.partial(gather_kernel, n, nf),
        out_shape=(
            jax.ShapeDtypeStruct((n, 2, BLK, D), BF16),
            jax.ShapeDtypeStruct((n, 3 * HD, 2 * BLK), F32),
            jax.ShapeDtypeStruct((3, nf * rows, D), BF16),
            jax.ShapeDtypeStruct((nf,) + vec.shape, F32),
            half, half,
        ),
        in_specs=[in_vmem(), in_vmem(), in_vmem()] + [in_any()] * 6,
        out_specs=(in_any(), in_vmem(), in_any(), in_vmem(), in_any(), in_any()),
        scratch_shapes=[
            VMEM((n, 2, BLK, D), BF16),
            VMEM((4, 2, BLK, D), BF16),
            VMEM((nf * rows, 256), BF16),
            VMEM((256, nf * rows), BF16),
            VMEM((nf,) + vec.shape, F32),
            VMEM((1, nf * rows), F32),
            VMEM((2, rows // 2, D), F32),
            VMEM((6, 2, rows // 2, D), BF16),
            dma((4, n, 2)), dma((n, 2)), dma((peers,)), dma((peers,)), dma((peers,)), dma((peers,)),
            dma((2,)), dma((3,)), dma((3, peers)), dma((3, peers)), dma((3, peers)), dma((3, peers)),
            dma((4,)), dma((6, 2)),
        ],
        compiler_params=pltpu.CompilerParams(
            collective_id=0, has_side_effects=True, vmem_limit_bytes=60 * MIB
        ),
        cost_estimate=cost(60),
        name="gather_tokens",
    )(x, wh, vec, *mats)


class Swap:
    def __init__(self, place, src, dst, send_sem, recv_sem, own_sem):
        self.p, self.src, self.dst = place, src, dst
        self.send_sem, self.recv_sem, self.own_sem = send_sem, recv_sem, own_sem

    def copy(self, s, block):
        p = self.p
        return pltpu.make_async_remote_copy(
            src_ref=self.src((p.c + s) % p.n), dst_ref=self.dst(block),
            send_sem=self.send_sem.at[s], recv_sem=self.recv_sem.at[s],
            device_id=((p.c + s) % p.n, p.f), device_id_type=MESH,
        )

    def own(self):
        return pltpu.make_async_copy(self.src(self.p.c), self.dst(self.p.c), self.own_sem)

    def start(self):
        for s in range(1, self.p.n):
            self.copy(s, self.p.c).start()
        self.own().start()

    def wait(self):
        self.own().wait()
        for s in range(1, self.p.n):
            self.copy(s, (self.p.c + self.p.n - s) % self.p.n).wait_recv()

    def drain(self):
        for s in range(1, self.p.n):
            self.copy(s, self.p.c).wait_send()


def swap_kernel(n, nf, src, dst, send_sem, recv_sem, own_sem):
    p = Place(n, nf)
    p.greet_all(False)
    swap = Swap(p, lambda d: src.at[d], lambda d: dst.at[d], send_sem, recv_sem, own_sem)
    swap.start()
    swap.wait()
    swap.drain()


def swap_out(n, nf, blocks):
    dma = pltpu.SemaphoreType.DMA
    return pl.pallas_call(
        functools.partial(swap_kernel, n, nf),
        out_shape=jax.ShapeDtypeStruct(blocks.shape, blocks.dtype),
        in_specs=[in_vmem()],
        out_specs=in_vmem(),
        scratch_shapes=[dma((n,)), dma((n,)), dma],
        compiler_params=pltpu.CompilerParams(
            collective_id=1, has_side_effects=True, vmem_limit_bytes=60 * MIB
        ),
        cost_estimate=cost(15),
        name="swap_out",
    )(blocks)


def seq_start(ends, base, token):
    start = jnp.zeros_like(token)
    for e in ends:
        start = jnp.where(e - base <= token, jnp.maximum(start, e - base), start)
    return start


def read_ends(lengths_ref):
    ends, total = [], jnp.int32(0)
    for i in range(lengths_ref.shape[1]):
        total = total + lengths_ref[0, i]
        ends.append(total)
    return ends


def pad_rows(block):
    return jnp.concatenate([block, jnp.zeros((BLK - HD, block.shape[1]), block.dtype)], axis=0)


class Layout:
    def __init__(self, n, total_blocks):
        self.n = n
        self.hpd = 2 * H // n
        self.half_blocks = total_blocks // 2
        self.size = self.half_blocks * BLK
        self.rows = self.hpd * self.size
        self.tile = 512

    def half(self, i):
        return i if self.hpd == 2 else lax.axis_index("ctx") % 2

    def nat(self, deal_ref, d, i):
        half = self.half(i)
        block = deal_ref[2 * d + half]
        if self.hpd == 1:
            block = block - half * self.half_blocks
        return al(block * BLK, BLK)

    def base(self, unit):
        return self.half(unit) * self.size if self.hpd == 1 else unit * self.size


def fwd_kernel(
    lay, deal_ref, len_ref, qkv_ref, bias_ref, c_ref,
    ot_out, qraw, qst, kt, vt, kn, ot, lse,
    m_ref, l_ref, acc_ref,
):
    tile = lay.tile

    @pl.loop(0, lay.n)
    def _(d):
        for i in range(lay.hpd):
            nat = lay.nat(deal_ref, d, i)
            cols = pl.ds(nat, BLK)
            half = lay.half(i)
            src = pl.ds(half * BLK if lay.hpd == 2 else al(half * BLK, BLK), BLK)
            block = qkv_ref[d, :, src] + bias_ref[...]
            qr, kr, vr = block[:HD], block[HD : 2 * HD], block[2 * HD :]
            qraw[:, cols] = qr
            qst[:, cols] = pad_rows(qr * c_ref[...]).astype(BF16)
            kt[:, cols] = kr.astype(BF16)
            vt[:, cols] = vr.astype(BF16)
            kn[cols, :] = pad_rows(kr).T.astype(BF16)

    ends = read_ends(len_ref)
    for unit in range(lay.hpd):
        base = lay.base(unit)
        row0 = unit * lay.size

        @pl.loop(0, lay.size // tile)
        def _(qi):
            cols = pl.ds(al(row0 + qi * tile, tile), tile)
            t_row = qi * tile + lax.broadcasted_iota(jnp.int32, (1, tile), 1)
            start = seq_start(ends, base, t_row)
            low = seq_start(ends, base, qi * tile) // tile
            m_ref[...] = jnp.full_like(m_ref, NEG)
            l_ref[...] = jnp.zeros_like(l_ref)
            acc_ref[...] = jnp.zeros_like(acc_ref)

            def visit(j, diagonal):
                keys = pl.ds(al(row0 + j * tile, tile), tile)
                s = dot(kn[keys, :], qst[:, cols])
                u = j * tile + lax.broadcasted_iota(jnp.int32, (tile, 1), 0)
                seen = u >= start
                if diagonal:
                    seen = seen & (u <= t_row)
                s = jnp.where(seen, s, NEG)
                m_old = m_ref[...]
                m_new = jnp.maximum(m_old, jnp.max(s, axis=0, keepdims=True))
                p = jnp.exp(s - m_new)
                shrink = jnp.exp(m_old - m_new)
                m_ref[...] = m_new
                l_ref[...] = l_ref[...] * shrink + jnp.sum(p, axis=0, keepdims=True)
                acc_ref[...] = acc_ref[...] * shrink + dot(vt[:, keys], p.astype(BF16))

            @pl.loop(low, qi)
            def _(j):
                visit(j, False)

            visit(qi, True)
            ot[:, cols] = acc_ref[...] / l_ref[...]
            lse[:, cols] = m_ref[...] + jnp.log(l_ref[...])

    @pl.loop(0, lay.n)
    def _(d):
        for i in range(lay.hpd):
            ot_out[d, i] = ot[:, pl.ds(lay.nat(deal_ref, d, i), BLK)].astype(BF16)


def attend(lay, deal, lengths, qkv, bias, factor):
    rows = lay.rows
    return pl.pallas_call(
        functools.partial(fwd_kernel, lay),
        out_shape=(
            jax.ShapeDtypeStruct((lay.n, lay.hpd, HD, BLK), BF16),
            jax.ShapeDtypeStruct((HD, rows), F32),
            jax.ShapeDtypeStruct((BLK, rows), BF16),
            jax.ShapeDtypeStruct((HD, rows), BF16),
            jax.ShapeDtypeStruct((HD, rows), BF16),
            jax.ShapeDtypeStruct((rows, BLK), BF16),
            jax.ShapeDtypeStruct((HD, rows), F32),
            jax.ShapeDtypeStruct((1, rows), F32),
        ),
        in_specs=[in_smem(), in_smem()] + [in_vmem()] * 3,
        out_specs=tuple([in_vmem()] * 8),
        scratch_shapes=[
            VMEM((1, lay.tile), F32), VMEM((1, lay.tile), F32), VMEM((HD, lay.tile), F32),
        ],
        compiler_params=pltpu.CompilerParams(vmem_limit_bytes=60 * MIB),
        cost_estimate=cost(19),
        name="attend",
    )(deal, lengths, qkv, bias, factor)


WIDE = 256


def over_columns(body):
    @pl.loop(0, D // WIDE)
    def _(j):
        body(pl.ds(al(j * WIDE, WIDE), WIDE))


def ffn_kernel(
    x_ref, cot_ref, ot_ref, g2_ref, mats_ref,
    out_ref, dh_ref, gt_ref, ot, bt, zt, gb, du, dg2_ref,
    o_rows, hidden, nh, b, up, z, db, wide,
):
    tok = x_ref.shape[0]
    wo, w1, w2 = mats_ref.at[0], mats_ref.at[1], mats_ref.at[2]
    for i in range(2):
        for h in range(H):
            ot[pl.ds(h * HD, HD), pl.ds(i * BLK, BLK)] = ot_ref[h, i]
    @pl.loop(0, D // WIDE)
    def _(j):
        sl = pl.ds(al(j * WIDE, WIDE), WIDE)
        o_rows[:, sl] = ot[sl, :].astype(F32).T.astype(BF16)

    def body(sl):
        hidden[:, sl] = x_ref[:, sl].astype(F32) + dot(o_rows[...], wo[:, sl])
    over_columns(body)
    hid = hidden[...]
    r2 = lax.rsqrt(jnp.mean(hid * hid, axis=-1, keepdims=True) + EPS)
    nh[...] = hid * r2
    b[...] = (nh[...] * g2_ref[...]).astype(BF16)

    def body(sl):
        u = dot(b[...], w1[:, sl])
        up[:, sl] = u
        z[:, sl] = (u * jax.nn.sigmoid(u)).astype(BF16)
    over_columns(body)

    def body(sl):
        out_ref[:, sl] = (hidden[:, sl] + dot(z[...], w2[:, sl])).astype(BF16)
        dz = dot(cot_ref[...], w2[sl, :], NT)
        u = up[:, sl]
        sig = jax.nn.sigmoid(u)
        du[:, sl] = (dz * sig * (1.0 + u * (1.0 - sig))).astype(BF16)
    over_columns(body)

    def body(sl):
        g = dot(du[...], w1[sl, :], NT)
        db[:, sl] = g * g2_ref[:, sl]
        dg2_ref[:, sl] = jnp.sum(g * nh[:, sl], axis=0, keepdims=True)
    over_columns(body)
    scaled = db[...]
    mean = jnp.mean(scaled * nh[...], axis=-1, keepdims=True)
    dh = cot_ref[...].astype(F32) + r2 * (scaled - nh[...] * mean)
    dh_ref[...] = dh
    gb[...] = dh.astype(BF16)

    @pl.loop(0, D // WIDE)
    def _(j):
        sl = pl.ds(al(j * WIDE, WIDE), WIDE)
        wide[sl, :] = dot(wo[sl, :], gb[...], NT).astype(BF16)
    for i in range(2):
        for h in range(H):
            gt_ref[h, i] = wide[pl.ds(h * HD, HD), pl.ds(i * BLK, BLK)]

    @pl.loop(0, D // WIDE)
    def _(j):
        sl = pl.ds(al(j * WIDE, WIDE), WIDE)
        bt[sl, :] = b[:, sl].astype(F32).T.astype(BF16)
        zt[sl, :] = z[:, sl].astype(F32).T.astype(BF16)


def ffn(x, cot, ot, g2, mats):
    tok = x.shape[0]
    turned = jax.ShapeDtypeStruct((D, tok), BF16)
    plain = jax.ShapeDtypeStruct((tok, D), BF16)
    return pl.pallas_call(
        ffn_kernel,
        out_shape=(
            plain,
            jax.ShapeDtypeStruct((tok, D), F32),
            jax.ShapeDtypeStruct((H, 2, HD, BLK), BF16),
            turned, turned, turned, plain, plain,
            jax.ShapeDtypeStruct((1, D), F32),
        ),
        in_specs=[in_vmem()] * 5,
        out_specs=tuple([in_vmem()] * 9),
        scratch_shapes=[
            VMEM((tok, D), BF16), VMEM((tok, D), F32), VMEM((tok, D), F32),
            VMEM((tok, D), BF16), VMEM((tok, D), F32), VMEM((tok, D), BF16),
            VMEM((tok, D), F32), VMEM((D, tok), BF16),
        ],
        compiler_params=pltpu.CompilerParams(vmem_limit_bytes=60 * MIB),
        cost_estimate=cost(20),
        name="feed_forward",
    )(x, cot, ot, g2, mats)


VEC_ROWS = 24


class Loads:
    def __init__(self, sems):
        self.sems, self.count = sems, 0

    def start(self, src, dst):
        copy = pltpu.make_async_copy(src, dst, self.sems.at[self.count])
        self.count += 1
        copy.start()
        return copy


def backward_kernel(
    lay, n, nf,
    rel_ref, inv_ref, len_ref, gt, c_ref, g1_ref, dg2_ref,
    ot_t_in, bt_in, zt_in, gb_in, du_in, cot_in,
    qraw_in, qst_in, kt_in, vt_in, kn_in, ot_in, lse_in,
    a_ref, mine_ref, other_ref, got_ref, x_in, dh_in,
    gx_out, dw_out, fw_out, vec_out, tg_out,
    big, sums, wide, abuf, qraw, qst, kt, vt, kn, ot, lse, x_ref, dh_ref,
    qn, vn, don, dost, delta, dk, dv, dqt, natural, part_sums, left, back, dw, dwsend, dwrecv, dwown, vx, vsum, vall,
    ld_sem, do_send, do_recv, do_own, dq_send, dq_recv, dq_own, tw_send, tw_recv, tg_send, tg_recv, a_sem,
    x_send, x_recv, own_sem, ag_send, ag_recv, fg_send, fg_recv, v_send, v_recv, u_send, u_recv,
    *rest,
):
    p = Place(n, nf)
    c, f, zlen, hpd, tile = p.c, p.f, p.zlen, lay.hpd, lay.tile
    dob, reduce_scratch = rest[:hpd], rest[hpd:]
    rows = D // nf
    part = rows // 2
    loads = Loads(ld_sem)
    ffn_rows = [abuf.at[1, pl.ds(i * 2 * BLK, 2 * BLK)] for i in range(3)]
    ffn_loads = [loads.start(src, wide.at[m]) for m, src in enumerate((ot_t_in, bt_in, zt_in))]
    ffn_loads += [loads.start(src, dst) for src, dst in zip((gb_in, du_in, cot_in), ffn_rows)]
    att_loads = [
        loads.start(src, dst) for src, dst in zip(
            (qraw_in, qst_in, kt_in, vt_in, kn_in, ot_in, lse_in), (qraw, qst, kt, vt, kn, ot, lse))
    ]
    row_loads = [loads.start(x_in, x_ref), loads.start(dh_in, dh_ref)]
    p.greet_all(True)

    do_swaps = [
        Swap(p, lambda d, u=u: gt.at[d, u], lambda d, u=u: dob[u].at[d],
             do_send.at[u], do_recv.at[u], do_own.at[u])
        for u in range(hpd)
    ]
    for swap in do_swaps:
        swap.start()

    def tg_copy(s):
        return pltpu.make_async_remote_copy(
            src_ref=got_ref.at[s], dst_ref=tg_out.at[s], send_sem=tg_send.at[s], recv_sem=tg_recv.at[s],
            device_id=(p.twin, f), device_id_type=MESH,
        )

    for s in range(nf - 1):
        tg_copy(s).start()

    height = sums.shape[1]
    flat = 3 * part
    if height > flat:
        for source in range(nf):
            sums[source, flat:, :] = jnp.zeros((height - flat, D), BF16)
    for copy in ffn_loads:
        copy.wait()
    theirs = lambda source: pl.ds(al(source * flat, 16), flat)
    got = lambda source: pl.ds(al((nf + source) * flat, 16), flat)

    def weight_grads(source, half, put):
        for m in range(3):
            @pl.loop(0, D // WIDE)
            def _(j):
                sl = pl.ds(al(j * WIDE, WIDE), WIDE)
                where = pl.ds(al(source * rows + half * part, 16), part)
                put(m, sl, dot(wide[m, where, :], ffn_rows[m][:, sl]).astype(BF16))

    def twin_copy(s, source):
        return pltpu.make_async_remote_copy(
            src_ref=big.at[theirs(source)], dst_ref=big.at[got(source)],
            send_sem=tw_send.at[s], recv_sem=tw_recv.at[s],
            device_id=(p.twin, f), device_id_type=MESH,
        )

    shards = list(enumerate(p.fpeers)) + [(nf - 1, f)]
    for s, source in shards:
        def put(m, sl, value, source=source):
            big[pl.ds(al(source * flat + m * part, 16), part), sl] = value
        weight_grads(source, 1 - p.core, put)
        twin_copy(s, source).start()
    reduce = Reduce(p, sums, *reduce_scratch[:6], reduce_scratch[6:])
    for s, source in shards:
        def put(m, sl, value, source=source):
            sums[source, pl.ds(m * part, part), sl] = value
        weight_grads(source, p.core, put)
        twin_copy(s, source).wait_recv()
        reduce.add(
            sums.at[source, pl.ds(0, flat)],
            [sums.at[source, pl.ds(0, flat)], big.at[got(source)]], flat)
        if s == max(nf - 2, 0):
            for t in range(zlen - 1):
                reduce.start_x(t)
    for s, source in shards:
        twin_copy(s, source).wait_send()

    for s in range(nf - 1):
        tg_copy(s).wait_recv()
    w_loads = []
    for m in range(3):
        def load_w(src, source, half, m=m):
            at = pl.ds(al(m * D + source * rows + half * part, 16), part)
            w_loads.append(loads.start(src, big.at[at]))
        load_w(mine_ref.at[m], f, p.core)
        load_w(other_ref.at[m], f, 1 - p.core)
        for s, source in enumerate(p.fsources):
            load_w(got_ref.at[s, m], source, p.core)
            load_w(tg_out.at[s, m], source, 1 - p.core)

    for copy in att_loads:
        copy.wait()
    ends = read_ends(len_ref)
    part_sums[...] = jnp.zeros_like(part_sums)
    step = 8
    steps = [(u, q) for u in range(hpd) for q in range(n // step)]

    def a_copy(k):
        u, q = steps[k]
        half = lay.half(u)
        return pltpu.make_async_copy(
            a_ref.at[pl.ds(q * step, step), half], abuf.at[k % 2].reshape(step, BLK, D), a_sem.at[k % 2])

    def weights_of_head(k):
        u, q = steps[k]
        a_copy(k).wait()
        if k + 1 < len(steps):
            a_copy(k + 1).start()
        @pl.loop(0, D // WIDE)
        def _(j):
            sl = pl.ds(al(j * WIDE, WIDE), WIDE)
            term = dot(left[u, :, q * step * BLK : (q + 1) * step * BLK], abuf[k % 2, :, sl])
            dw[:, sl] = term if k == 0 else dw[:, sl] + term

    def gradient_swap(u):
        return Swap(
            p, lambda d: left.at[u, :, pl.ds(al(d * BLK, BLK), BLK)], lambda d: back.at[u, d],
            dq_send.at[u], dq_recv.at[u], dq_own.at[u])

    a_copy(0).start()
    for u in range(hpd):
        base = lay.base(u)
        row0 = u * lay.size
        do_swaps[u].wait()

        @pl.loop(0, lay.half_blocks)
        def _(b):
            cols = pl.ds(al(b * BLK, BLK), BLK)
            here = pl.ds(al(row0 + b * BLK, BLK), BLK)
            block = dob[u][inv_ref[b + lay.half(u) * lay.half_blocks]].astype(F32)
            delta[:, cols] = jnp.sum(block * ot[:, here], axis=0, keepdims=True)
            block = pad_rows(block)
            dost[:, cols] = block.astype(BF16)
            don[cols, :] = block.T.astype(BF16)
            qn[cols, :] = qst[:, here].astype(F32).T.astype(BF16)
            vn[cols, :] = pad_rows(vt[:, here].astype(F32)).T.astype(BF16)
            dk[cols, :] = jnp.zeros((BLK, BLK), F32)
            dv[cols, :] = jnp.zeros((BLK, BLK), F32)

        @pl.loop(0, lay.size // tile)
        def _(qi):
            cols = pl.ds(al(qi * tile, tile), tile)
            here = pl.ds(al(row0 + qi * tile, tile), tile)
            t_row = qi * tile + lax.broadcasted_iota(jnp.int32, (1, tile), 1)
            start = seq_start(ends, base, t_row)
            dqt[:, cols] = jnp.zeros((HD, tile), F32)

            @pl.loop(0, qi + 1)
            def _(j):
                keys = pl.ds(al(j * tile, tile), tile)
                keys_here = pl.ds(al(row0 + j * tile, tile), tile)
                s = dot(kn[keys_here, :], qst[:, here])
                token = j * tile + lax.broadcasted_iota(jnp.int32, (tile, 1), 0)
                seen = (token >= start) & (token <= t_row)
                prob = jnp.exp(jnp.where(seen, s - lse[:, here], NEG))
                dp = dot(vn[keys, :], dost[:, cols])
                ds = (prob * (dp - delta[:, cols])).astype(BF16)
                dv[keys, :] += dot(prob.astype(BF16), don[cols, :])
                dk[keys, :] += dot(ds, qn[cols, :])
                dqt[:, cols] += dot(kt[:, keys_here], ds)

            if u == hpd - 1:
                @pl.when(qi == lay.size // tile // 2 - 1)
                def _():
                    if hpd == 1:
                        reduce.xy(0)
                    reduce.after_y(0)
                    reduce.chain(0, 0)

        @pl.loop(0, lay.half_blocks)
        def _(b):
            cols = pl.ds(al(b * BLK, BLK), BLK)
            here = pl.ds(al(row0 + b * BLK, BLK), BLK)
            dqs = dqt[:, cols]
            dq = (dqs * c_ref[...]).astype(BF16)
            dkt = dk[cols, :].T[:HD].astype(BF16)
            dvt = dv[cols, :].T[:HD].astype(BF16)
            natural[b, 0:HD] = dq
            natural[b, HD : 2 * HD] = dkt
            natural[b, 2 * HD : 3 * HD] = dvt
            part_sums[0, :HD] += dqs * qraw[:, here]
            part_sums[1, :HD] += dq.astype(F32)
            part_sums[2, :HD] += dvt.astype(F32)

        @pl.loop(0, n)
        def _(d):
            left[u, :, pl.ds(al(d * BLK, BLK), BLK)] = natural[rel_ref[2 * d + lay.half(u)]]

        gradient_swap(u).start()
        if u < hpd - 1:
            reduce.xy(0)
            for k, (unit, _) in enumerate(steps):
                if unit == u:
                    weights_of_head(k)
    reduce.xy(1)

    for k, (unit, _) in enumerate(steps):
        if unit == hpd - 1:
            weights_of_head(k)
    for source in range(nf):
        dwsend[source] = dw[:, source * rows : (source + 1) * rows].astype(BF16)

    def x_copy(s, peer):
        return pltpu.make_async_remote_copy(
            src_ref=dwsend.at[peer], dst_ref=dwrecv.at[s],
            send_sem=x_send.at[s], recv_sem=x_recv.at[s],
            device_id=(c, peer), device_id_type=MESH,
        )

    for s, peer in enumerate(p.fpeers):
        x_copy(s, peer).start()
    reduce.start_x(zlen - 1)

    spread = Spread(p, dw_out, ag_send, ag_recv, 3)
    spread2 = Spread(p, fw_out, fg_send, fg_recv, fw_out.shape[1])

    def start_spread():
        total = dwsend[f].astype(F32)
        for s, peer in enumerate(p.fpeers):
            x_copy(s, peer).wait_recv()
            total = total + dwrecv[s].astype(F32)
        for i in range(3):
            dwown[i] = total[i * HD : (i + 1) * HD].astype(BF16)
        own = pltpu.make_async_copy(dwown, dw_out.at[c], own_sem)
        own.start()
        own.wait()
        for i in range(3):
            spread.start(i)

    for t in range(2, 2 * zlen - 1):
        if t < zlen:
            reduce.xy(t)
        if t <= zlen:
            reduce.after_y(t - 1)
            reduce.chain(t - 1, 0)
        for hop in range(1, zlen - 1):
            if 0 <= t - 1 - hop < zlen:
                reduce.chain(t - 1 - hop, hop)
        if t == 2:
            start_spread()
        if 1 <= t - 2 < zlen:
            for i in range(3):
                spread.chain(t - 2, i)
                spread.pair(t - 3, i)
    reduce.last()
    result = reduce_scratch[0]
    pieces = fw_out.shape[1]
    own = [
        pltpu.make_async_copy(result.at[pl.ds(i * (height // zlen // pieces), height // zlen // pieces)],
                              fw_out.at[c, i], own_sem)
        for i in range(pieces)
    ]
    for i in range(pieces):
        own[i].start()
        own[i].wait()
        spread2.start(i)
    done = max(2 * zlen - 4, 0)
    for k in range(1, zlen):
        if k > min(done, zlen - 1):
            for i in range(3):
                spread.chain(k, i)
                spread.pair(k - 1, i)

    for u in range(hpd):
        gradient_swap(u).wait()
    for m in range(3):
        for i in range(2):
            for h in range(H):
                block = back[i, h] if hpd == 2 else back[0, 2 * h + i]
                wide[m, pl.ds(h * HD, HD), pl.ds(i * BLK, BLK)] = block[m * HD : (m + 1) * HD]
    for copy in w_loads:
        copy.wait()

    @pl.loop(0, D // WIDE)
    def _(j):
        def rows_of(m):
            return big[pl.ds(al(m * D + j * WIDE, WIDE), WIDE), :]
        total = dot(rows_of(0), wide[0]) + dot(rows_of(1), wide[1]) + dot(rows_of(2), wide[2])
        gx_out[:, pl.ds(al(j * WIDE, WIDE), WIDE)] = total.T

    for i in range(3):
        spread.pair(zlen - 1, i)
    for i in range(pieces):
        spread2.chain(1, i)
        spread2.pair(0, i)
    for copy in row_loads:
        copy.wait()
    x = x_ref[...].astype(F32)
    r1 = lax.rsqrt(jnp.mean(x * x, axis=-1, keepdims=True) + EPS)
    na = x * r1
    da = gx_out[...]
    dg1 = jnp.sum(da * na, axis=0, keepdims=True)
    for r in range(D // BLK):
        vx[f, r : r + 1, :] = dg1[:, r * BLK : (r + 1) * BLK]
        vx[f, D // BLK + r : D // BLK + r + 1, :] = dg2_ref[:, r * BLK : (r + 1) * BLK]
    for r in range(3):
        vx[f, 20 + r : 21 + r, :] = jnp.sum(part_sums[r].T, axis=0, keepdims=True)
    vx[f, 23:24, :] = jnp.zeros((1, BLK), F32)

    def v_copy(s, peer, source):
        return pltpu.make_async_remote_copy(
            src_ref=vx.at[f], dst_ref=vx.at[source],
            send_sem=v_send.at[s], recv_sem=v_recv.at[s],
            device_id=(c, peer), device_id_type=MESH,
        )

    for s, peer in enumerate(p.fpeers):
        v_copy(s, peer, f).start()
    scaled = da * g1_ref[...]
    mean = jnp.mean(scaled * na, axis=-1, keepdims=True)
    gx_out[...] = dh_ref[...] + r1 * (scaled - na * mean)
    for s, (peer, source) in enumerate(zip(p.fpeers, p.fsources)):
        v_copy(s, peer, source).wait_recv()
    vsum[...] = jnp.sum(vx[...], axis=0)
    vall[c] = vsum[...]

    def u_copy(s, block):
        return pltpu.make_async_remote_copy(
            src_ref=vsum, dst_ref=vall.at[block],
            send_sem=u_send.at[s], recv_sem=u_recv.at[s],
            device_id=((c + s) % n, f), device_id_type=MESH,
        )

    for s in range(1, n):
        u_copy(s, c).start()
    for k in range(2, zlen):
        for i in range(pieces):
            spread2.chain(k, i)
            spread2.pair(k - 1, i)
    for i in range(pieces):
        spread2.pair(zlen - 1, i)
    for k in range(zlen):
        for zz, guard, _ in p.level(k):
            when(guard, lambda zz=zz: spread.from_twin(zz))
            when(guard, lambda zz=zz: spread2.from_twin(zz))
    for s in range(1, n):
        u_copy(s, (c + n - s) % n).wait_recv()
    vec_out[...] = vall[...]

    for u in range(hpd):
        do_swaps[u].drain()
        gradient_swap(u).drain()
    spread.drain()
    spread2.drain()
    reduce.drain()
    for s, peer in enumerate(p.fpeers):
        tg_copy(s).wait_send()
        x_copy(s, peer).wait_send()
        v_copy(s, peer, f).wait_send()
    for s in range(1, n):
        u_copy(s, c).wait_send()


def backward(lay, nf, within, inverse, lengths, gt, factor, g1, dg2, ffn_parts, cot, kept, tokens, mine, other, got, x, dh):
    n, hpd, rows, size = lay.n, lay.hpd, lay.rows, lay.size
    dma = pltpu.SemaphoreType.DMA
    shard = D // nf
    part = shard // 2
    zlen = n // 4
    height = -(-3 * part // (16 * zlen)) * 16 * zlen
    piece = height // zlen
    pieces = 3 if piece % 48 == 0 else 1
    peers = max(nf - 1, 1)
    tok = x.shape[0]
    return pl.pallas_call(
        functools.partial(backward_kernel, lay, n, nf),
        out_shape=(
            jax.ShapeDtypeStruct((tok, D), F32),
            jax.ShapeDtypeStruct((n, 3, HD, shard), BF16),
            jax.ShapeDtypeStruct((n, pieces, piece // pieces, D // 2), BF16),
            jax.ShapeDtypeStruct((n, VEC_ROWS, BLK), F32),
            jax.ShapeDtypeStruct((peers, 3, part, D), BF16),
        ),
        in_specs=[in_smem()] * 3 + [in_vmem()] * 4 + [in_any()] * 19,
        out_specs=(in_vmem(), in_any(), in_any(), in_vmem(), in_any()),
        scratch_shapes=[
            VMEM((3 * D, D), BF16), VMEM((nf, height, D), BF16), VMEM((3, D, tok), BF16),
            VMEM((2, 8 * BLK, D), BF16),
            VMEM((HD, rows), F32), VMEM((BLK, rows), BF16), VMEM((HD, rows), BF16), VMEM((HD, rows), BF16),
            VMEM((rows, BLK), BF16), VMEM((HD, rows), F32), VMEM((1, rows), F32),
            VMEM((tok, D), BF16), VMEM((tok, D), F32),
            VMEM((size, BLK), BF16), VMEM((size, BLK), BF16), VMEM((size, BLK), BF16), VMEM((BLK, size), BF16),
            VMEM((1, size), F32), VMEM((size, BLK), F32), VMEM((size, BLK), F32), VMEM((HD, size), F32),
            VMEM((size // BLK, 3 * HD, BLK), BF16), VMEM((3, BLK, BLK), F32), VMEM((hpd, 3 * HD, n * BLK), BF16),
            VMEM((hpd, n, 3 * HD, BLK), BF16), VMEM((3 * HD, D), F32), VMEM((nf, 3 * HD, shard), BF16),
            VMEM((peers, 3 * HD, shard), BF16), VMEM((3, HD, shard), BF16),
            VMEM((nf, VEC_ROWS, BLK), F32), VMEM((VEC_ROWS, BLK), F32), VMEM((n, VEC_ROWS, BLK), F32),
            dma((15 + 6 * nf,)), dma((hpd, n)), dma((hpd, n)), dma((hpd,)), dma((hpd, n)), dma((hpd, n)), dma((hpd,)),
            dma((nf,)), dma((nf,)), dma((peers,)), dma((peers,)), dma((2,)),
            dma((peers,)), dma((peers,)), dma, dma((4, n, 3)), dma((n, 3)), dma((4, n, pieces)), dma((n, pieces)),
            dma((peers,)), dma((peers,)), dma((n,)), dma((n,)),
        ] + [VMEM((n, HD, BLK), BF16)] * hpd + Reduce.scratch(nf, zlen, height),
        compiler_params=pltpu.CompilerParams(
            collective_id=2, has_side_effects=True, vmem_limit_bytes=62 * MIB
        ),
        cost_estimate=cost(130),
        name="backward",
    )(within, inverse, lengths, gt, factor, g1, dg2, *ffn_parts, cot, *kept, tokens, mine, other, got, x, dh)


def turn_kernel(hpd, dw_ref, q_ref, k_ref, v_ref, wide):
    j = pl.program_id(0)

    @pl.when(j == 0)
    def _():
        for m in range(3):
            for h in range(H):
                if hpd == 2:
                    block = dw_ref[h, m].astype(F32)
                else:
                    block = dw_ref[2 * h, m].astype(F32) + dw_ref[2 * h + 1, m].astype(F32)
                wide[m, pl.ds(h * HD, HD), :] = block

    for m, out in enumerate((q_ref, k_ref, v_ref)):
        out[...] = wide[m, pl.ds(al(j * WIDE, WIDE), WIDE), :].T


def turn(hpd, dw):
    n, _, _, rows = dw.shape
    spec = pl.BlockSpec((rows, WIDE), lambda j: (0, j))
    return pl.pallas_call(
        functools.partial(turn_kernel, hpd),
        grid=(D // WIDE,),
        out_shape=tuple([jax.ShapeDtypeStruct((rows, D), F32)] * 3),
        in_specs=[pl.BlockSpec((n, 3, HD, rows), lambda j: (0, 0, 0, 0))],
        out_specs=(spec, spec, spec),
        scratch_shapes=[VMEM((3, D, rows), F32)],
        compiler_params=pltpu.CompilerParams(vmem_limit_bytes=60 * MIB),
        cost_estimate=cost(6),
        name="turn",
    )(dw)


def widen_kernel(zlen, part, in_ref, o_ref, u_ref, d_ref):
    j, y = pl.program_id(0), pl.program_id(1)
    height = in_ref.shape[3]
    for m, out in enumerate((o_ref, u_ref, d_ref)):
        for z in range(zlen):
            first, last = max(m * part, z * height), min((m + 1) * part, (z + 1) * height)
            if first < last:
                out[first - m * part : last - m * part, :] = in_ref[
                    z, y, j, first - z * height : last - z * height, :
                ].astype(F32)


def widen(zlen, part, pieces):
    half = pieces.shape[-1]
    height = pieces.shape[1] * pieces.shape[2]
    spec = pl.BlockSpec((part, half), lambda j, y: (j, y))
    return pl.pallas_call(
        functools.partial(widen_kernel, zlen, part),
        grid=(2, 2),
        out_shape=tuple([jax.ShapeDtypeStruct((2 * part, D), F32)] * 3),
        in_specs=[pl.BlockSpec((zlen, 2, 2, height, half), lambda j, y: (0, 0, 0, 0, 0))],
        out_specs=(spec, spec, spec),
        compiler_params=pltpu.CompilerParams(vmem_limit_bytes=60 * MIB),
        cost_estimate=cost(5),
        name="widen",
    )(pieces.reshape(zlen, 2, 2, height, half))


def local(
    n, nf, tokens, cotangent, lengths, deal, gain_attn, query_weight, query_bias, key_weight,
    value_weight, value_bias, query_scale, proj_weight, gain_ffn, up_weight, down_weight,
):
    c = lax.axis_index("ctx")
    f = lax.axis_index("fsdp")
    lay = Layout(n, deal.shape[0])
    head = c * lay.hpd // 2
    rows = query_weight.shape[0]
    x, cot = tokens[0], cotangent[0]

    def low(v):
        return v.astype(BF16).astype(F32)

    g1_own = low(gain_attn)
    slices = [
        lax.dynamic_slice(w, (0, head * HD), (rows, HD)) for w in (query_weight, key_weight, value_weight)
    ]
    wh = jnp.pad(jnp.concatenate(slices, axis=1), ((0, 0), (0, 256 - 3 * HD))).astype(BF16)
    vec = jnp.stack([g1_own, low(query_bias), low(value_bias), low(gain_ffn)])
    vec = jnp.concatenate([vec, jnp.pad(low(query_scale), (0, rows - query_scale.shape[0]))[None]])
    vec = jnp.pad(vec, ((0, 3), (0, -rows % 128)))

    a_all, qkv, mats, vecs, mine, other = gather(
        n, nf, x, wh, vec, (proj_weight, up_weight, down_weight, query_weight, key_weight, value_weight)
    )
    whole = jnp.swapaxes(vecs[:, :5, :rows], 0, 1).reshape(5, nf * rows)
    g1, bq, bv, g2 = whole[0], whole[1], whole[2], whole[3]
    q_param = vecs[:, 4, : query_scale.shape[0]].reshape(HD)
    factor = jnp.log(1.0 + jnp.exp(q_param)) * (LOG2E / math.sqrt(HD))
    bias = jnp.concatenate([
        lax.dynamic_slice(bq, (head * HD,), (HD,)), jnp.zeros((HD,), F32),
        lax.dynamic_slice(bv, (head * HD,), (HD,)),
    ])
    bias = jnp.broadcast_to(bias[:, None], (3 * HD, BLK))
    factor_col = jnp.broadcast_to(factor[:, None], (HD, BLK))

    got = jnp.stack([
        lax.ppermute(mine, "fsdp", [(i, (i + s) % nf) for i in range(nf)]) for s in range(1, nf)
    ])

    ot, *kept = attend(lay, deal, lengths, qkv, bias, factor_col)
    ot = swap_out(n, nf, ot).reshape(H, 2, HD, BLK)
    layer_out, dh, gt, ott, bt, zt, gb, du, dg2 = ffn(x, cot, ot, g2[None], mats)
    part = rows // 2
    zlen = n // 4
    blocks = jnp.arange(deal.shape[0], dtype=jnp.int32)
    inverse = jnp.sum(jnp.where(deal[None, :] == blocks[:, None], blocks[None, :] // 2, 0), axis=1, dtype=jnp.int32)
    grad_x, dw, pieces, vectors, _ = backward(
        lay, nf, deal % lay.half_blocks, inverse, lengths, gt.reshape(n, lay.hpd, HD, BLK), factor_col, g1[None], dg2,
        (ott, bt, zt, gb, du), cot, kept, a_all, mine, other, got, x, dh,
    )
    dwq, dwk, dwv = turn(lay.hpd, dw)
    grads = widen(zlen, part, pieces)

    def own(v):
        size = v.shape[0] // nf
        return lax.dynamic_slice(v, (f * size,), (size,))

    def of_heads(r):
        return vectors[:, r, :HD].reshape(H, 2 // lay.hpd, HD).sum(axis=1).reshape(D)

    gains = jnp.sum(vectors[:, : 2 * D // BLK], axis=0).reshape(2, D)
    grad_scale = jnp.sum(vectors[:, 20, :HD], axis=0) * jax.nn.sigmoid(q_param) * (LOG2E / math.sqrt(HD))
    return (
        layer_out[None],
        grad_x[None],
        own(gains[0]),
        dwq,
        own(of_heads(21)),
        dwk,
        dwv,
        own(of_heads(22)),
        own(grad_scale),
        grads[0],
        own(gains[1]),
        grads[1],
        grads[2],
    )


def solution(mesh):
    whole, vector, matrix = P("fsdp", "ctx", None), P("fsdp"), P("fsdp", None)
    return jax.shard_map(
        functools.partial(local, mesh.shape["ctx"], mesh.shape["fsdp"]),
        mesh=mesh,
        in_specs=(
            whole, whole, matrix, P(), vector, matrix, vector, matrix, matrix, vector, vector,
            matrix, vector, matrix, matrix,
        ),
        out_specs=(
            whole, whole, vector, matrix, vector, matrix, matrix, vector, vector, matrix, vector,
            matrix, matrix,
        ),
        check_vma=False,
    )
```

```python
import functools
import math

import jax
import jax.numpy as jnp
from jax import lax
from jax.experimental import pallas as pl
from jax.experimental.pallas import tpu as pltpu
from jax.sharding import PartitionSpec as P

H = 16
HD = 80
BLK = 128
D = 1280
EPS = 1e-06
LOG2E = 1.442695041
NEG = -1e30
MESH = pl.DeviceIdType.MESH
F32 = jnp.float32
BF16 = jnp.bfloat16
VMEM = pltpu.VMEM
MIB = 1 << 20

NN = (((1,), (0,)), ((), ()))
NT = (((1,), (1,)), ((), ()))
TN = (((0,), (0,)), ((), ()))


def dot(left, right, dims=NN):
    return lax.dot_general(left, right, dims, preferred_element_type=F32)


def al(value, multiple):
    return pl.multiple_of(value, multiple)


def in_vmem():
    return pl.BlockSpec(memory_space=pltpu.VMEM)


def in_smem():
    return pl.BlockSpec(memory_space=pltpu.SMEM)


def in_any():
    return pl.BlockSpec(memory_space=pl.ANY)


def cost(microseconds):
    return pl.CostEstimate(flops=0, bytes_accessed=int(microseconds * 3.0e6), transcendentals=0)


class Place:
    def __init__(self, n, nf):
        self.n, self.nf = n, nf
        self.c = lax.axis_index("ctx")
        self.f = lax.axis_index("fsdp")
        self.zlen = n // 4
        self.z, self.y, self.core = self.c // 4, (self.c // 2) % 2, self.c % 2
        self.twin = self.idx(self.z, self.y, 1 - self.core)
        self.ypeer = self.idx(self.z, 1 - self.y, self.core)
        self.targets = (
            self.idx(self.z + 1, self.y, self.core), self.idx(self.z - 1, self.y, self.core),
            self.ypeer, self.twin,
        )
        self.guards = (self.z < self.zlen - 1, self.z > 0, None, None)
        self.fpeers = [(self.f + s) % nf for s in range(1, nf)]
        self.fsources = [(self.f + nf - s) % nf for s in range(1, nf)]

    def idx(self, z, y, core):
        return (z * 2 + y) * 2 + core

    def level(self, k):
        if k == 0:
            return [(self.z, None, 0)]
        return [
            (self.z + k, self.z + k < self.zlen, 1),
            (self.z - k, self.z - k >= 0, -1),
        ]

    def greet_neighbours(self):
        barrier = pltpu.get_barrier_semaphore()
        for target, guard in zip(self.targets, self.guards):
            when(guard, lambda target=target: pl.semaphore_signal(
                barrier, inc=1, device_id=(target, self.f), device_id_type=MESH))
        for peer in self.fpeers:
            pl.semaphore_signal(barrier, inc=1, device_id=(self.c, peer), device_id_type=MESH)
        ends = jnp.minimum(self.z, 1) + jnp.minimum(self.zlen - 1 - self.z, 1)
        pl.semaphore_wait(barrier, 1 + self.nf + ends)

    def greet_all(self, with_fsdp):
        barrier = pltpu.get_barrier_semaphore()
        for s in range(1, self.n):
            pl.semaphore_signal(
                barrier, inc=1, device_id=((self.c + s) % self.n, self.f), device_id_type=MESH)
        if with_fsdp:
            for peer in self.fpeers:
                pl.semaphore_signal(barrier, inc=1, device_id=(self.c, peer), device_id_type=MESH)
        pl.semaphore_wait(barrier, self.n - 1 + (self.nf - 1 if with_fsdp else 0))


def when(guard, body):
    if guard is None:
        body()
    else:
        pl.when(guard)(body)


class Spread:
    def __init__(self, place, buf, send_sem, recv_sem, pieces):
        self.p, self.buf, self.send_sem, self.recv_sem, self.pieces = place, buf, send_sem, recv_sem, pieces

    def copy(self, way, origin, i):
        where = self.buf.at[origin, i]
        return pltpu.make_async_remote_copy(
            src_ref=where, dst_ref=where,
            send_sem=self.send_sem.at[way, origin, i], recv_sem=self.recv_sem.at[origin, i],
            device_id=(self.p.targets[way], self.p.f), device_id_type=MESH,
        )

    def send(self, way, origin, i):
        when(self.p.guards[way], lambda: self.copy(way, origin, i).start())

    def arrive(self, origin, i):
        self.copy(3, origin, i).wait_recv()

    def start(self, i):
        for way in range(4):
            self.send(way, self.p.c, i)

    def chain(self, k, i):
        p = self.p
        for zz, guard, sign in p.level(k):
            def body(zz=zz, sign=sign):
                origin = p.idx(zz, p.y, p.core)
                self.arrive(origin, i)
                self.send(1 if sign == 1 else 0, origin, i)
                self.send(2, origin, i)
                self.send(3, origin, i)
            when(guard, body)

    def pair(self, k, i):
        p = self.p
        for zz, guard, _ in p.level(k):
            def body(zz=zz):
                origin = p.idx(zz, 1 - p.y, p.core)
                self.arrive(origin, i)
                self.send(3, origin, i)
            when(guard, body)

    def from_twin(self, zz, pieces=None):
        p = self.p
        for yy in (p.y, 1 - p.y):
            for i in range(self.pieces) if pieces is None else pieces:
                self.arrive(p.idx(zz, yy, 1 - p.core), i)

    def drain(self):
        p = self.p
        for i in range(self.pieces):
            for way in range(4):
                when(p.guards[way], lambda way=way, i=i: self.copy(way, p.c, i).wait_send())
            for k in range(p.zlen):
                for zz, guard, sign in p.level(k):
                    def body(zz=zz, sign=sign, k=k, i=i):
                        if k:
                            origin = p.idx(zz, p.y, p.core)
                            on = 1 if sign == 1 else 0
                            when(p.guards[on], lambda: self.copy(on, origin, i).wait_send())
                            self.copy(2, origin, i).wait_send()
                            self.copy(3, origin, i).wait_send()
                        self.copy(3, p.idx(zz, 1 - p.y, p.core), i).wait_send()
                    when(guard, body)


class Reduce:
    def __init__(self, place, mine, result, acc, xrecv, yrecv, urecv, drecv, sems):
        self.p, self.mine, self.result, self.acc = place, mine, result, acc
        self.xrecv, self.yrecv, self.urecv, self.drecv = xrecv, yrecv, urecv, drecv
        (self.xs, self.xr, self.ys, self.yr, self.us, self.ur, self.ds, self.dr) = sems
        self.height = acc.shape[0] // place.zlen
        self.width = D // 2
        zlen = place.zlen
        ends = []
        for k in range(zlen // 2):
            ends += [zlen - 1 - k, k]
        self.order = ends

    @staticmethod
    def scratch(nf, zlen, height):
        dma = pltpu.SemaphoreType.DMA
        peers = max(nf - 1, 1)
        piece = VMEM((zlen, height // zlen, D // 2), BF16)
        return [
            VMEM((height // zlen, D // 2), BF16), VMEM((height, D), BF16), VMEM((peers, height, D), BF16),
            piece, piece, piece,
            dma((peers, zlen, 2)), dma((peers, zlen, 2)), dma((zlen,)), dma((zlen,)),
            dma((zlen,)), dma((zlen,)), dma((zlen,)), dma((zlen,)),
        ]

    def at(self, piece, side):
        return (
            pl.ds(al(piece * self.height, 16), self.height),
            pl.ds(al(side * self.width, 128), self.width),
        )

    def remote(self, src, dst, send, recv, c, f):
        return pltpu.make_async_remote_copy(
            src_ref=src, dst_ref=dst, send_sem=send, recv_sem=recv,
            device_id=(c, f), device_id_type=MESH,
        )

    def x_copy(self, s, peer, piece, turn):
        side = (self.p.y + 1 + turn) % 2
        where = self.at(piece, side)
        return self.remote(
            self.mine.at[peer].at[where], self.xrecv.at[s].at[where],
            self.xs.at[s, piece, turn], self.xr.at[s, piece, turn], self.p.c, peer,
        )

    def start_x(self, t):
        for turn in range(2):
            for s, peer in enumerate(self.p.fpeers):
                self.x_copy(s, peer, self.order[t], turn).start()

    def add(self, dst, terms, count=None):
        count = count or self.height
        step = 48 if count % 48 == 0 else 16
        @pl.loop(0, count // step)
        def _(t):
            at = pl.ds(al(t * step, 16), step)
            total = terms[0][at, :].astype(F32)
            for term in terms[1:]:
                total = total + term[at, :].astype(F32)
            dst[at, :] = total.astype(BF16)

    def sum_x(self, piece, turn):
        side = (self.p.y + 1 + turn) % 2
        where = self.at(piece, side)
        terms = [self.mine.at[self.p.f].at[where]]
        for s, peer in enumerate(self.p.fpeers):
            self.x_copy(s, peer, piece, turn).wait_recv()
            terms.append(self.xrecv.at[s].at[where])
        self.add(self.acc.at[where], terms)

    def y_copy(self, piece):
        src = self.acc.at[self.at(piece, 1 - self.p.y)]
        return self.remote(
            src, self.yrecv.at[piece], self.ys.at[piece], self.yr.at[piece], self.p.ypeer, self.p.f)

    def u_copy(self, piece):
        src = self.acc.at[self.at(piece, self.p.y)]
        return self.remote(
            src, self.urecv.at[piece], self.us.at[piece], self.ur.at[piece], self.p.targets[0], self.p.f)

    def d_copy(self, piece):
        src = self.acc.at[self.at(piece, self.p.y)]
        return self.remote(
            src, self.drecv.at[piece], self.ds.at[piece], self.dr.at[piece], self.p.targets[1], self.p.f)

    def mine_of(self, piece):
        return self.acc.at[self.at(piece, self.p.y)]

    def xy(self, t):
        piece = self.order[t]
        self.sum_x(piece, 0)
        self.y_copy(piece).start()
        self.sum_x(piece, 1)

    def after_y(self, t):
        piece = self.order[t]
        self.y_copy(piece).wait_recv()
        self.add(self.mine_of(piece), [self.mine_of(piece), self.yrecv.at[piece]])

    def chain(self, t, hop):
        p, piece = self.p, self.order[t]
        if hop < piece:
            @pl.when(p.z == hop)
            def _():
                if hop:
                    self.u_copy(piece).wait_recv()
                    self.add(self.mine_of(piece), [self.mine_of(piece), self.urecv.at[piece]])
                self.u_copy(piece).start()
        if p.zlen - 1 - hop > piece:
            @pl.when(p.z == p.zlen - 1 - hop)
            def _():
                if hop:
                    self.d_copy(piece).wait_recv()
                    self.add(self.mine_of(piece), [self.mine_of(piece), self.drecv.at[piece]])
                self.d_copy(piece).start()

    def last(self):
        p = self.p
        @pl.when(p.z > 0)
        def _():
            self.u_copy(p.z).wait_recv()
            self.add(self.mine_of(p.z), [self.mine_of(p.z), self.urecv.at[p.z]])
        @pl.when(p.z < p.zlen - 1)
        def _():
            self.d_copy(p.z).wait_recv()
            self.add(self.mine_of(p.z), [self.mine_of(p.z), self.drecv.at[p.z]])
        self.add(self.result, [self.mine_of(p.z)])

    def drain(self):
        p = self.p
        for piece in self.order:
            for turn in range(2):
                for s, peer in enumerate(p.fpeers):
                    self.x_copy(s, peer, piece, turn).wait_send()
            self.y_copy(piece).wait_send()
            pl.when(p.z < piece)(lambda piece=piece: self.u_copy(piece).wait_send())
            pl.when(p.z > piece)(lambda piece=piece: self.d_copy(piece).wait_send())


class Loads:
    def __init__(self, sems):
        self.sems, self.copies = sems, []

    def start(self, src, dst):
        copy = pltpu.make_async_copy(src, dst, self.sems.at[len(self.copies)])
        self.copies.append(copy)
        copy.start()
        return copy

    def wait(self):
        for copy in self.copies:
            copy.wait()


class Swap:
    def __init__(self, place, src, dst, send_sem, recv_sem, own_sem):
        self.p, self.src, self.dst = place, src, dst
        self.send_sem, self.recv_sem, self.own_sem = send_sem, recv_sem, own_sem

    def copy(self, s, block):
        p = self.p
        return pltpu.make_async_remote_copy(
            src_ref=self.src((p.c + s) % p.n), dst_ref=self.dst(block),
            send_sem=self.send_sem.at[s], recv_sem=self.recv_sem.at[s],
            device_id=((p.c + s) % p.n, p.f), device_id_type=MESH,
        )

    def own(self):
        return pltpu.make_async_copy(self.src(self.p.c), self.dst(self.p.c), self.own_sem)

    def start(self):
        for s in range(1, self.p.n):
            self.copy(s, self.p.c).start()
        self.own().start()

    def wait(self):
        self.own().wait()
        for s in range(1, self.p.n):
            self.copy(s, (self.p.c + self.p.n - s) % self.p.n).wait_recv()

    def drain(self):
        for s in range(1, self.p.n):
            self.copy(s, self.p.c).wait_send()


def seq_start(ends, base, token):
    start = jnp.zeros_like(token)
    for e in ends:
        start = jnp.where(e - base <= token, jnp.maximum(start, e - base), start)
    return start


def read_ends(lengths_ref):
    ends, total = [], jnp.int32(0)
    for i in range(lengths_ref.shape[1]):
        total = total + lengths_ref[0, i]
        ends.append(total)
    return ends


def pad_rows(block):
    return jnp.concatenate([block, jnp.zeros((BLK - HD, block.shape[1]), block.dtype)], axis=0)


class Layout:
    def __init__(self, n, total_blocks):
        self.n = n
        self.hpd = 2 * H // n
        self.half_blocks = total_blocks // 2
        self.size = self.half_blocks * BLK
        self.rows = self.hpd * self.size
        self.tile = 512

    def half(self, i):
        return i if self.hpd == 2 else lax.axis_index("ctx") % 2

    def base(self, unit):
        return self.half(unit) * self.size if self.hpd == 1 else unit * self.size


WIDE = 256


def over_columns(body):
    @pl.loop(0, D // WIDE)
    def _(j):
        body(pl.ds(al(j * WIDE, WIDE), WIDE))


def token_rows(
    x_ref, cot_ref, oswap, rows_ref, weights, w_loads,
    out_ref, dh_ref, gt_ref, ot, bt, zt, gb, du, dg2_ref,
    o_rows, hidden, nh, b, up, z, db, wide,
):
    wo, w1, w2 = weights
    hpd = oswap.shape[1]
    for i in range(2):
        for h in range(H):
            ot[pl.ds(h * HD, HD), pl.ds(i * BLK, BLK)] = oswap[h, i] if hpd == 2 else oswap[2 * h + i, 0]
    @pl.loop(0, D // WIDE)
    def _(j):
        sl = pl.ds(al(j * WIDE, WIDE), WIDE)
        o_rows[:, sl] = ot[sl, :].astype(F32).T.astype(BF16)

    def body(sl):
        hidden[:, sl] = x_ref[:, sl].astype(F32) + dot(o_rows[...], wo[:, sl])
    over_columns(body)
    hid = hidden[...]
    r2 = lax.rsqrt(jnp.mean(hid * hid, axis=-1, keepdims=True) + EPS)
    nh[...] = hid * r2
    b[...] = (nh[...] * rows_ref[3:4, :]).astype(BF16)
    w_loads[1].wait()

    def body(sl):
        u = dot(b[...], w1[:, sl])
        up[:, sl] = u
        z[:, sl] = (u * jax.nn.sigmoid(u)).astype(BF16)
    over_columns(body)

    w_loads[2].wait()

    def body(sl):
        out_ref[:, sl] = (hidden[:, sl] + dot(z[...], w2[:, sl])).astype(BF16)
        dz = dot(cot_ref[...], w2[sl, :], NT)
        u = up[:, sl]
        sig = jax.nn.sigmoid(u)
        du[:, sl] = (dz * sig * (1.0 + u * (1.0 - sig))).astype(BF16)
    over_columns(body)

    def body(sl):
        g = dot(du[...], w1[sl, :], NT)
        db[:, sl] = g * rows_ref[3:4, sl]
        dg2_ref[:, sl] = jnp.sum(g * nh[:, sl], axis=0, keepdims=True)
    over_columns(body)
    scaled = db[...]
    mean = jnp.mean(scaled * nh[...], axis=-1, keepdims=True)
    dh = cot_ref[...].astype(F32) + r2 * (scaled - nh[...] * mean)
    dh_ref[...] = dh
    gb[...] = dh.astype(BF16)

    @pl.loop(0, D // WIDE)
    def _(j):
        sl = pl.ds(al(j * WIDE, WIDE), WIDE)
        wide[sl, :] = dot(wo[sl, :], gb[...], NT).astype(BF16)
    for i in range(2):
        for h in range(H):
            gt_ref[h, i] = wide[pl.ds(h * HD, HD), pl.ds(i * BLK, BLK)]

    @pl.loop(0, D // WIDE)
    def _(j):
        sl = pl.ds(al(j * WIDE, WIDE), WIDE)
        bt[sl, :] = b[:, sl].astype(F32).T.astype(BF16)
        zt[sl, :] = z[:, sl].astype(F32).T.astype(BF16)


def forward_kernel(
    lay, n, nf,
    rel_ref, inv_ref, len_ref, x_ref, cot_ref, wh_ref, vec_ref, *rest,
):
    mat_refs, rest = rest[:6], rest[6:]
    (a_out, mats_out, mine_out, other_out, rows_out, factor_out, dg2_out, *stored) = rest[: 7 + 15]
    (abuf, norm, whbuf, wht, vecbuf, vcol, stage, wcast, qkv, osend, onat, oswap,
     qraw, qst, kt, vt, kn, ot, lse, layer, dh, gt, ot_t, bt, zt, gb, du,
     o_rows, hidden, nh, b_rows, up, z, db, wide, m_ref, l_ref, acc_ref,
     ag_send, ag_recv, wh_send, wh_recv, vec_send, vec_recv,
     ld_sem, mx_send, mx_recv, ms_send, ms_recv, a_sem, keep_sem, o_send, o_recv, o_own,
     st_sem, w_sem) = rest[7 + 15 :]
    kept = (qraw, qst, kt, vt, kn, ot, lse)
    made = (layer, dh, gt, ot_t, bt, zt, gb, du)
    stores = Loads(st_sem)
    p = Place(n, nf)
    c, f, core, zlen, hpd, tile = p.c, p.f, p.core, p.zlen, lay.hpd, lay.tile
    rows = wh_ref.shape[0]
    part = rows // 2
    p.greet_all(True)
    spread = Spread(p, abuf, ag_send, ag_recv, 2)

    for i in range(2):
        abuf[c, i] = x_ref[pl.ds(i * BLK, BLK), :]
    spread.start(0)

    def wh_copy(s, peer):
        return pltpu.make_async_remote_copy(
            src_ref=wh_ref, dst_ref=whbuf.at[pl.ds(al(f * rows, 16), rows)],
            send_sem=wh_send.at[s], recv_sem=wh_recv.at[s],
            device_id=(c, peer), device_id_type=MESH,
        )

    def vec_copy(s, peer):
        return pltpu.make_async_remote_copy(
            src_ref=vec_ref, dst_ref=vecbuf.at[f],
            send_sem=vec_send.at[s], recv_sem=vec_recv.at[s],
            device_id=(c, peer), device_id_type=MESH,
        )

    for s, peer in enumerate(p.fpeers):
        vec_copy(s, peer).start()
        wh_copy(s, peer).start()
    whbuf[pl.ds(al(f * rows, 16), rows), :] = wh_ref[...]
    vecbuf[f] = vec_ref[...]

    shards = mat_refs
    moved = len(mat_refs) - 1
    steps = [(m, 0) for m in range(moved)] + [(m, 1) for m in range(moved)] + [(moved, 0), (moved, 1)]

    def half_of(h):
        return (core + h) % 2

    def load(step):
        m, h = steps[step]
        return pltpu.make_async_copy(
            shards[m].at[pl.ds(al(half_of(h) * part, 16), part)],
            stage.at[step % 2], ld_sem.at[step % 2],
        )

    def mx_copy(m, s, peer, source):
        return pltpu.make_async_remote_copy(
            src_ref=wcast.at[m, core],
            dst_ref=mats_out.at[m, pl.ds(al(source * rows + core * part, 16), part)],
            send_sem=mx_send.at[m, s], recv_sem=mx_recv.at[m, s],
            device_id=(c, peer), device_id_type=MESH,
        )

    def keep_copies(m):
        if m < moved:
            return [
                pltpu.make_async_copy(
                    wcast.at[m, h], mats_out.at[m, pl.ds(al(f * rows + h * part, 16), part)],
                    keep_sem.at[m, h],
                ) for h in range(2)
            ]
        return [
            pltpu.make_async_copy(wcast.at[m, half_of(h)], out, keep_sem.at[m, h])
            for h, out in enumerate((mine_out, other_out))
        ]

    def cast(step):
        m, h = steps[step]
        if step + 1 < len(steps):
            load(step + 1).start()
        load(step).wait()
        chunk = part // 4 if part % 64 == 0 else part
        @pl.loop(0, part // chunk)
        def _(t):
            wcast[m, half_of(h), pl.ds(al(t * chunk, 16), chunk), :] = stage[
                step % 2, pl.ds(al(t * chunk, 16), chunk), :
            ].astype(BF16)
        if h == 0 and m < moved:
            for s, peer in enumerate(p.fpeers):
                mx_copy(m, s, peer, f).start()
        if h == 1:
            for copy in keep_copies(m):
                copy.start()

    load(0).start()
    for step in range(len(steps)):
        cast(step)

    def ms_copy(m, s, source, half):
        where = mats_out.at[m, pl.ds(al(source * rows + half * part, 16), part)]
        return pltpu.make_async_remote_copy(
            src_ref=where, dst_ref=where,
            send_sem=ms_send.at[m, s], recv_sem=ms_recv.at[m, s],
            device_id=(p.twin, f), device_id_type=MESH,
        )

    def pass_matrix(m):
        for s, (peer, source) in enumerate(zip(p.fpeers, p.fsources)):
            mx_copy(m, s, peer, source).wait_recv()
            ms_copy(m, s, source, core).start()

    for s, peer in enumerate(p.fpeers):
        vec_copy(s, peer).wait_recv()
        wh_copy(s, peer).wait_recv()
    wht[...] = whbuf[...].astype(F32).T.astype(BF16)
    for source in range(nf):
        rows_out[:, pl.ds(source * rows, rows)] = vecbuf[source, :, 0:rows]
    for r in (4, 5):
        shares = vecbuf[0, r : r + 1, 0:BLK]
        for source in range(1, nf):
            shares = shares + vecbuf[source, r : r + 1, 0:BLK]
        rows_out[r : r + 1, 0:BLK] = shares
    vcol[...] = rows_out[...].T
    head = c * hpd // 2
    here = pl.ds(al(head * HD, 16), HD)
    bias_q, bias_v = vcol[here, 1:2], vcol[here, 2:3]
    factor = vcol[0:HD, 4:5]
    factor_out[...] = jnp.broadcast_to(factor, (HD, BLK))

    def a_copy(slot, origin, half):
        return pltpu.make_async_copy(norm.at[slot], a_out.at[pl.ds(origin, 2), half], a_sem.at[slot])

    def project(u, k, first=False):
        half = lay.half(u)
        for zz, guard, _ in p.level(k):
            def body(zz=zz):
                spread.from_twin(zz, [u] if hpd == 2 else range(2))
                for t in range(2):
                    origin = zz * 4 + 2 * t
                    if not first:
                        a_copy(t, origin, half).wait()
                    for i in range(2):
                        x = abuf[origin + i, half].astype(F32)
                        scale = lax.rsqrt(jnp.mean(x * x, axis=-1, keepdims=True) + EPS)
                        norm[t, i] = (x * scale * rows_out[0:1, :]).astype(BF16)
                    a_copy(t, origin, half).start()
                    value = dot(wht[: 3 * HD, :], norm[t].reshape(2 * BLK, D), NT)
                    qkv[origin] = value[:, :BLK]
                    qkv[origin + 1] = value[:, BLK:]
            when(guard, body)

    ends = read_ends(len_ref)

    def attend(u, during):
        base, row0 = lay.base(u), u * lay.size

        @pl.loop(0, lay.half_blocks)
        def _(b):
            cols = pl.ds(al(row0 + b * BLK, BLK), BLK)
            block = qkv[inv_ref[b + lay.half(u) * lay.half_blocks]]
            qr, kr, vr = block[:HD] + bias_q, block[HD : 2 * HD], block[2 * HD :] + bias_v
            qraw[:, cols] = qr
            qst[:, cols] = pad_rows(qr * factor).astype(BF16)
            kt[:, cols] = kr.astype(BF16)
            vt[:, cols] = vr.astype(BF16)
            kn[cols, :] = pad_rows(kr).T.astype(BF16)

        @pl.loop(0, lay.size // tile)
        def _(qi):
            cols = pl.ds(al(row0 + qi * tile, tile), tile)
            t_row = qi * tile + lax.broadcasted_iota(jnp.int32, (1, tile), 1)
            start = seq_start(ends, base, t_row)
            m_ref[...] = jnp.full_like(m_ref, NEG)
            l_ref[...] = jnp.zeros_like(l_ref)
            acc_ref[...] = jnp.zeros_like(acc_ref)

            @pl.loop(0, qi + 1)
            def _(j):
                keys = pl.ds(al(row0 + j * tile, tile), tile)
                s = dot(kn[keys, :], qst[:, cols])
                token = j * tile + lax.broadcasted_iota(jnp.int32, (tile, 1), 0)
                s = jnp.where((token >= start) & (token <= t_row), s, NEG)
                m_old = m_ref[...]
                m_new = jnp.maximum(m_old, jnp.max(s, axis=0, keepdims=True))
                prob = jnp.exp(s - m_new)
                shrink = jnp.exp(m_old - m_new)
                m_ref[...] = m_new
                l_ref[...] = l_ref[...] * shrink + jnp.sum(prob, axis=0, keepdims=True)
                acc_ref[...] = acc_ref[...] * shrink + dot(vt[:, keys], prob.astype(BF16))

            out = acc_ref[...] / l_ref[...]
            ot[:, cols] = out
            lse[:, cols] = m_ref[...] + jnp.log(l_ref[...])
            for b in range(tile // BLK):
                onat[qi * (tile // BLK) + b] = out[:, b * BLK : (b + 1) * BLK].astype(BF16)
            for at, event in during:
                pl.when(qi == at)(event)

        @pl.loop(0, n)
        def _(d):
            osend[u, d] = onat[rel_ref[2 * d + lay.half(u)]]

        o_swaps[u].start()

    o_swaps = [
        Swap(p, lambda d, u=u: osend.at[u, d], lambda d, u=u: oswap.at[d, u],
             o_send.at[u], o_recv.at[u], o_own.at[u])
        for u in range(hpd)
    ]

    def gather_events(i, first, last):
        for k in range(first, last):
            if k < zlen:
                spread.chain(k, i)
            spread.pair(k - 1, i)

    later = min(2, zlen - 1)
    for k in range(1, zlen + 1):
        gather_events(0, k, k + 1)
        if k == later:
            spread.start(1)
        if hpd == 2:
            project(0, k - 1, first=k == 1)
    pass_matrix(0)
    if hpd == 2:
        gather_events(1, 1, 2)
        attend(0, [(lay.size // tile // 2, lambda: gather_events(1, 2, 3))])
        pass_matrix(1)
        for k in range(3, zlen + 1):
            gather_events(1, k, k + 1)
            project(1, k - 3)
        for k in range(zlen - 2, zlen):
            project(1, k)
        attend(1, [])
    else:
        for k in range(1, zlen + 1):
            gather_events(1, k, k + 1)
            project(0, k - 1, first=k == 1)
        attend(0, [])
        pass_matrix(1)
    pass_matrix(2)
    for src, dst in zip(kept, stored[: len(kept)]):
        stores.start(src, dst)

    def handed(m):
        for s, (peer, source) in enumerate(zip(p.fpeers, p.fsources)):
            ms_copy(m, s, source, 1 - core).wait_recv()
    for m in range(3):
        for copy in keep_copies(m):
            copy.wait()
        handed(m)
    spread.drain()
    weights = [abuf.at[pl.ds(5 * m, 5)].reshape(5 * 2 * BLK, D) for m in range(3)]
    w_loads = [
        pltpu.make_async_copy(mats_out.at[m], weights[m], w_sem.at[m]) for m in range(3)
    ]
    for copy in w_loads:
        copy.start()
    for u in range(hpd):
        o_swaps[u].wait()
    w_loads[0].wait()
    token_rows(
        x_ref, cot_ref, oswap, rows_out, weights, w_loads,
        layer, dh, gt, ot_t, bt, zt, gb, du, dg2_out, o_rows, hidden, nh, b_rows, up, z, db, wide)
    for src, dst in zip(made, stored[len(kept) :]):
        stores.start(src, dst)

    for m in range(3, moved):
        pass_matrix(m)
    for m in range(3, moved):
        for copy in keep_copies(m):
            copy.wait()
        handed(m)
    for copy in keep_copies(moved):
        copy.wait()
    for m in range(moved):
        for s, (peer, source) in enumerate(zip(p.fpeers, p.fsources)):
            mx_copy(m, s, peer, f).wait_send()
            ms_copy(m, s, source, core).wait_send()
    for s, peer in enumerate(p.fpeers):
        wh_copy(s, peer).wait_send()
        vec_copy(s, peer).wait_send()
    for u in range(hpd):
        o_swaps[u].drain()
    for slot in range(2):
        a_copy(slot, 2 * slot, lay.half(0)).wait()
    stores.wait()


def forward(lay, nf, within, inverse, lengths, x, cot, wh, vec, mats):
    n, hpd, total = lay.n, lay.hpd, lay.rows
    rows, tok, count = wh.shape[0], x.shape[0], len(mats)
    dma = pltpu.SemaphoreType.DMA
    peers = max(nf - 1, 1)
    half = ((rows // 2, D), BF16)
    kept = [
        ((HD, total), F32), ((BLK, total), BF16), ((HD, total), BF16), ((HD, total), BF16), ((total, BLK), BF16),
        ((HD, total), F32), ((1, total), F32),
    ]
    plain, turned, wide = ((tok, D), BF16), ((D, tok), BF16), ((tok, D), F32)
    made = [plain, wide, ((H, 2, HD, BLK), BF16), turned, turned, turned, plain, plain]
    outs = [
        ((n, 2, BLK, D), BF16), ((count - 1, nf * rows, D), BF16), half, half,
        ((8, D), F32), ((HD, BLK), F32), ((1, D), F32),
    ] + kept + made
    places = [in_any()] * 4 + [in_vmem()] * 3 + [in_any()] * (len(kept) + len(made))
    moves = dma((count - 1, peers))
    return pl.pallas_call(
        functools.partial(forward_kernel, lay, n, nf),
        out_shape=tuple(jax.ShapeDtypeStruct(*out) for out in outs),
        in_specs=[in_smem()] * 3 + [in_vmem()] * 4 + [in_any()] * count,
        out_specs=tuple(places),
        scratch_shapes=[
            VMEM((n, 2, BLK, D), BF16),
            VMEM((2, 2, BLK, D), BF16),
            VMEM((nf * rows, 256), BF16),
            VMEM((256, nf * rows), BF16),
            VMEM((nf,) + vec.shape, F32),
            VMEM((D, 8), F32),
            VMEM((2, rows // 2, D), F32),
            VMEM((count, 2, rows // 2, D), BF16),
            VMEM((n, 3 * HD, BLK), F32),
            VMEM((hpd, n, HD, BLK), BF16),
            VMEM((lay.half_blocks, HD, BLK), BF16),
            VMEM((n, hpd, HD, BLK), BF16),
        ] + [VMEM(*item) for item in kept + made] + [
            VMEM(*plain), VMEM(*wide), VMEM(*wide), VMEM(*plain), VMEM(*wide), VMEM(*plain), VMEM(*wide),
            VMEM(*turned),
            VMEM((1, lay.tile), F32), VMEM((1, lay.tile), F32), VMEM((HD, lay.tile), F32),
            dma((4, n, 2)), dma((n, 2)), dma((peers,)), dma((peers,)), dma((peers,)), dma((peers,)),
            dma((2,)), moves, moves, moves, moves,
            dma((2,)), dma((count, 2)), dma((hpd, n)), dma((hpd, n)), dma((hpd,)),
            dma((len(kept) + len(made),)), dma((3,)),
        ],
        compiler_params=pltpu.CompilerParams(
            collective_id=0, has_side_effects=True, vmem_limit_bytes=61 * MIB
        ),
        cost_estimate=cost(100),
        name="forward",
    )(within, inverse, lengths, x, cot, wh, vec, *mats)


VEC_ROWS = 24


def backward_kernel(
    lay, n, nf,
    rel_ref, inv_ref, len_ref, gt, c_ref, g1_ref, dg2_ref,
    ot_t_in, bt_in, zt_in, gb_in, du_in, cot_in,
    qraw_in, qst_in, kt_in, vt_in, kn_in, ot_in, lse_in,
    a_ref, mats_ref, mine_ref, other_ref, x_in, dh_in,
    gx_out, dw_out, fw_out, vec_out, xw_out, tw_out,
    big, sums, wide, abuf, qraw, qst, kt, vt, kn, ot, lse, x_ref, dh_ref,
    qn, vn, don, dost, delta, dk, dv, dqt, natural, part_sums, left, back, dw, dwsend, dwrecv, dwown, vx, vsum, vall,
    ld_sem, do_send, do_recv, do_own, dq_send, dq_recv, dq_own, tw_send, tw_recv, xw_send, xw_recv, tg_send, tg_recv, a_sem,
    x_send, x_recv, own_sem, ag_send, ag_recv, fg_send, fg_recv, v_send, v_recv, u_send, u_recv,
    *rest,
):
    p = Place(n, nf)
    c, f, zlen, hpd, tile = p.c, p.f, p.zlen, lay.hpd, lay.tile
    dob, reduce_scratch = rest[:hpd], rest[hpd:]
    rows = D // nf
    part = rows // 2
    loads = Loads(ld_sem)
    ffn_rows = [abuf.at[1, pl.ds(i * 2 * BLK, 2 * BLK)] for i in range(3)]
    ffn_loads = [loads.start(src, wide.at[m]) for m, src in enumerate((ot_t_in, bt_in, zt_in))]
    ffn_loads += [loads.start(src, dst) for src, dst in zip((gb_in, du_in, cot_in), ffn_rows)]
    att_loads = [
        loads.start(src, dst) for src, dst in zip(
            (qraw_in, qst_in, kt_in, vt_in, kn_in, ot_in, lse_in), (qraw, qst, kt, vt, kn, ot, lse))
    ]
    row_loads = [loads.start(x_in, x_ref), loads.start(dh_in, dh_ref)]
    p.greet_all(True)

    do_swaps = [
        Swap(p, lambda d, u=u: gt.at[d, u], lambda d, u=u: dob[u].at[d],
             do_send.at[u], do_recv.at[u], do_own.at[u])
        for u in range(hpd)
    ]
    for swap in do_swaps:
        swap.start()

    def xw_copy(s, peer):
        return pltpu.make_async_remote_copy(
            src_ref=mine_ref, dst_ref=xw_out.at[s], send_sem=xw_send.at[s], recv_sem=xw_recv.at[s],
            device_id=(c, peer), device_id_type=MESH,
        )

    def tg_copy(s):
        return pltpu.make_async_remote_copy(
            src_ref=xw_out.at[s], dst_ref=tw_out.at[s], send_sem=tg_send.at[s], recv_sem=tg_recv.at[s],
            device_id=(p.twin, f), device_id_type=MESH,
        )

    height = sums.shape[1]
    flat = 3 * part
    if height > flat:
        for source in range(nf):
            sums[source, flat:, :] = jnp.zeros((height - flat, D), BF16)
    for copy in ffn_loads:
        copy.wait()
    theirs = lambda source: pl.ds(al(source * flat, 16), flat)
    got = lambda source: pl.ds(al((nf + source) * flat, 16), flat)

    def weight_grads(source, half, put):
        for m in range(3):
            @pl.loop(0, D // WIDE)
            def _(j):
                sl = pl.ds(al(j * WIDE, WIDE), WIDE)
                where = pl.ds(al(source * rows + half * part, 16), part)
                put(m, sl, dot(wide[m, where, :], ffn_rows[m][:, sl]).astype(BF16))

    def twin_copy(s, source):
        return pltpu.make_async_remote_copy(
            src_ref=big.at[theirs(source)], dst_ref=big.at[got(source)],
            send_sem=tw_send.at[s], recv_sem=tw_recv.at[s],
            device_id=(p.twin, f), device_id_type=MESH,
        )

    shards = list(enumerate(p.fpeers)) + [(nf - 1, f)]
    for s, source in shards:
        def put(m, sl, value, source=source):
            big[pl.ds(al(source * flat + m * part, 16), part), sl] = value
        weight_grads(source, 1 - p.core, put)
        twin_copy(s, source).start()
    reduce = Reduce(p, sums, *reduce_scratch[:6], reduce_scratch[6:])
    for s, source in shards:
        def put(m, sl, value, source=source):
            sums[source, pl.ds(m * part, part), sl] = value
        weight_grads(source, p.core, put)
        twin_copy(s, source).wait_recv()
        reduce.add(
            sums.at[source, pl.ds(0, flat)],
            [sums.at[source, pl.ds(0, flat)], big.at[got(source)]], flat)
        if s == max(nf - 2, 0):
            for t in range(zlen - 1):
                reduce.start_x(t)
    for s, source in shards:
        twin_copy(s, source).wait_send()

    w_loads = [loads.start(mats_ref.at[3 + m], big.at[pl.ds(m * D, D)]) for m in range(2)]

    def load_w(src, source, half):
        at = pl.ds(al(2 * D + source * rows + half * part, 16), part)
        w_loads.append(loads.start(src, big.at[at]))

    load_w(mine_ref, f, p.core)
    load_w(other_ref, f, 1 - p.core)

    for copy in att_loads:
        copy.wait()
    ends = read_ends(len_ref)
    part_sums[...] = jnp.zeros_like(part_sums)
    step = 8
    steps = [(u, q) for u in range(hpd) for q in range(n // step)]

    def a_copy(k):
        u, q = steps[k]
        half = lay.half(u)
        return pltpu.make_async_copy(
            a_ref.at[pl.ds(q * step, step), half], abuf.at[k % 2].reshape(step, BLK, D), a_sem.at[k % 2])

    def weights_of_head(k):
        u, q = steps[k]
        a_copy(k).wait()
        if k + 1 < len(steps):
            a_copy(k + 1).start()
        @pl.loop(0, D // WIDE)
        def _(j):
            sl = pl.ds(al(j * WIDE, WIDE), WIDE)
            term = dot(left[u, :, q * step * BLK : (q + 1) * step * BLK], abuf[k % 2, :, sl])
            dw[:, sl] = term if k == 0 else dw[:, sl] + term

    def gradient_swap(u):
        return Swap(
            p, lambda d: left.at[u, :, pl.ds(al(d * BLK, BLK), BLK)], lambda d: back.at[u, d],
            dq_send.at[u], dq_recv.at[u], dq_own.at[u])

    a_copy(0).start()
    for u in range(hpd):
        base = lay.base(u)
        row0 = u * lay.size
        do_swaps[u].wait()

        @pl.loop(0, lay.half_blocks)
        def _(b):
            cols = pl.ds(al(b * BLK, BLK), BLK)
            here = pl.ds(al(row0 + b * BLK, BLK), BLK)
            block = dob[u][inv_ref[b + lay.half(u) * lay.half_blocks]].astype(F32)
            delta[:, cols] = jnp.sum(block * ot[:, here], axis=0, keepdims=True)
            block = pad_rows(block)
            dost[:, cols] = block.astype(BF16)
            don[cols, :] = block.T.astype(BF16)
            qn[cols, :] = qst[:, here].astype(F32).T.astype(BF16)
            vn[cols, :] = pad_rows(vt[:, here].astype(F32)).T.astype(BF16)
            dk[cols, :] = jnp.zeros((BLK, BLK), F32)
            dv[cols, :] = jnp.zeros((BLK, BLK), F32)

        @pl.loop(0, lay.size // tile)
        def _(qi):
            cols = pl.ds(al(qi * tile, tile), tile)
            here = pl.ds(al(row0 + qi * tile, tile), tile)
            t_row = qi * tile + lax.broadcasted_iota(jnp.int32, (1, tile), 1)
            start = seq_start(ends, base, t_row)
            dqt[:, cols] = jnp.zeros((HD, tile), F32)

            @pl.loop(0, qi + 1)
            def _(j):
                keys = pl.ds(al(j * tile, tile), tile)
                keys_here = pl.ds(al(row0 + j * tile, tile), tile)
                s = dot(kn[keys_here, :], qst[:, here])
                token = j * tile + lax.broadcasted_iota(jnp.int32, (tile, 1), 0)
                seen = (token >= start) & (token <= t_row)
                prob = jnp.exp(jnp.where(seen, s - lse[:, here], NEG))
                dp = dot(vn[keys, :], dost[:, cols])
                ds = (prob * (dp - delta[:, cols])).astype(BF16)
                dv[keys, :] += dot(prob.astype(BF16), don[cols, :])
                dk[keys, :] += dot(ds, qn[cols, :])
                dqt[:, cols] += dot(kt[:, keys_here], ds)

            if u == hpd - 1:
                @pl.when(qi == lay.size // tile // 2 - 1)
                def _():
                    if hpd == 1:
                        reduce.xy(0)
                    reduce.after_y(0)
                    reduce.chain(0, 0)

        @pl.loop(0, lay.half_blocks)
        def _(b):
            cols = pl.ds(al(b * BLK, BLK), BLK)
            here = pl.ds(al(row0 + b * BLK, BLK), BLK)
            dqs = dqt[:, cols]
            dq = (dqs * c_ref[...]).astype(BF16)
            dkt = dk[cols, :].T[:HD].astype(BF16)
            dvt = dv[cols, :].T[:HD].astype(BF16)
            natural[b, 0:HD] = dq
            natural[b, HD : 2 * HD] = dkt
            natural[b, 2 * HD : 3 * HD] = dvt
            part_sums[0, :HD] += dqs * qraw[:, here]
            part_sums[1, :HD] += dq.astype(F32)
            part_sums[2, :HD] += dvt.astype(F32)

        @pl.loop(0, n)
        def _(d):
            left[u, :, pl.ds(al(d * BLK, BLK), BLK)] = natural[rel_ref[2 * d + lay.half(u)]]

        gradient_swap(u).start()
        if u < hpd - 1:
            reduce.xy(0)
            for k, (unit, _) in enumerate(steps):
                if unit == u:
                    weights_of_head(k)
    reduce.xy(1)

    for k, (unit, _) in enumerate(steps):
        if unit == hpd - 1:
            weights_of_head(k)
    for source in range(nf):
        dwsend[source] = dw[:, source * rows : (source + 1) * rows].astype(BF16)

    def x_copy(s, peer):
        return pltpu.make_async_remote_copy(
            src_ref=dwsend.at[peer], dst_ref=dwrecv.at[s],
            send_sem=x_send.at[s], recv_sem=x_recv.at[s],
            device_id=(c, peer), device_id_type=MESH,
        )

    for s, peer in enumerate(p.fpeers):
        x_copy(s, peer).start()
    reduce.start_x(zlen - 1)
    for s, peer in enumerate(p.fpeers):
        xw_copy(s, peer).start()

    spread = Spread(p, dw_out, ag_send, ag_recv, 3)
    spread2 = Spread(p, fw_out, fg_send, fg_recv, fw_out.shape[1])

    def start_spread():
        total = dwsend[f].astype(F32)
        for s, peer in enumerate(p.fpeers):
            x_copy(s, peer).wait_recv()
            total = total + dwrecv[s].astype(F32)
        for i in range(3):
            dwown[i] = total[i * HD : (i + 1) * HD].astype(BF16)
        own = pltpu.make_async_copy(dwown, dw_out.at[c], own_sem)
        own.start()
        own.wait()
        for i in range(3):
            spread.start(i)

    for t in range(2, 2 * zlen - 1):
        if t < zlen:
            reduce.xy(t)
        if t <= zlen:
            reduce.after_y(t - 1)
            reduce.chain(t - 1, 0)
        for hop in range(1, zlen - 1):
            if 0 <= t - 1 - hop < zlen:
                reduce.chain(t - 1 - hop, hop)
        if t == 2:
            start_spread()
        if 1 <= t - 2 < zlen:
            for i in range(3):
                spread.chain(t - 2, i)
                spread.pair(t - 3, i)
    reduce.last()
    result = reduce_scratch[0]
    pieces = fw_out.shape[1]
    own = [
        pltpu.make_async_copy(result.at[pl.ds(i * (height // zlen // pieces), height // zlen // pieces)],
                              fw_out.at[c, i], own_sem)
        for i in range(pieces)
    ]
    for i in range(pieces):
        own[i].start()
        own[i].wait()
        spread2.start(i)
    done = max(2 * zlen - 4, 0)
    for k in range(1, zlen):
        if k > min(done, zlen - 1):
            for i in range(3):
                spread.chain(k, i)
                spread.pair(k - 1, i)

    for s, (peer, source) in enumerate(zip(p.fpeers, p.fsources)):
        xw_copy(s, peer).wait_recv()
        tg_copy(s).start()
        load_w(xw_out.at[s], source, p.core)

    for u in range(hpd):
        gradient_swap(u).wait()
    for m in range(3):
        for i in range(2):
            for h in range(H):
                block = back[i, h] if hpd == 2 else back[0, 2 * h + i]
                wide[m, pl.ds(h * HD, HD), pl.ds(i * BLK, BLK)] = block[m * HD : (m + 1) * HD]
    for s, source in enumerate(p.fsources):
        tg_copy(s).wait_recv()
        load_w(tw_out.at[s], source, 1 - p.core)
    for copy in w_loads:
        copy.wait()

    @pl.loop(0, D // WIDE)
    def _(j):
        def rows_of(m):
            return big[pl.ds(al(m * D + j * WIDE, WIDE), WIDE), :]
        total = dot(rows_of(0), wide[0]) + dot(rows_of(1), wide[1]) + dot(rows_of(2), wide[2])
        gx_out[:, pl.ds(al(j * WIDE, WIDE), WIDE)] = total.T

    for i in range(3):
        spread.pair(zlen - 1, i)
    for i in range(pieces):
        spread2.chain(1, i)
        spread2.pair(0, i)
    for copy in row_loads:
        copy.wait()
    x = x_ref[...].astype(F32)
    r1 = lax.rsqrt(jnp.mean(x * x, axis=-1, keepdims=True) + EPS)
    na = x * r1
    da = gx_out[...]
    dg1 = jnp.sum(da * na, axis=0, keepdims=True)
    for r in range(D // BLK):
        vx[f, r : r + 1, :] = dg1[:, r * BLK : (r + 1) * BLK]
        vx[f, D // BLK + r : D // BLK + r + 1, :] = dg2_ref[:, r * BLK : (r + 1) * BLK]
    for r in range(3):
        vx[f, 20 + r : 21 + r, :] = jnp.sum(part_sums[r].T, axis=0, keepdims=True)
    vx[f, 23:24, :] = jnp.zeros((1, BLK), F32)

    def v_copy(s, peer, source):
        return pltpu.make_async_remote_copy(
            src_ref=vx.at[f], dst_ref=vx.at[source],
            send_sem=v_send.at[s], recv_sem=v_recv.at[s],
            device_id=(c, peer), device_id_type=MESH,
        )

    for s, peer in enumerate(p.fpeers):
        v_copy(s, peer, f).start()
    scaled = da * g1_ref[...]
    mean = jnp.mean(scaled * na, axis=-1, keepdims=True)
    gx_out[...] = dh_ref[...] + r1 * (scaled - na * mean)
    for s, (peer, source) in enumerate(zip(p.fpeers, p.fsources)):
        v_copy(s, peer, source).wait_recv()
    vsum[...] = jnp.sum(vx[...], axis=0)
    vall[c] = vsum[...]

    def u_copy(s, block):
        return pltpu.make_async_remote_copy(
            src_ref=vsum, dst_ref=vall.at[block],
            send_sem=u_send.at[s], recv_sem=u_recv.at[s],
            device_id=((c + s) % n, f), device_id_type=MESH,
        )

    for s in range(1, n):
        u_copy(s, c).start()
    for k in range(2, zlen):
        for i in range(pieces):
            spread2.chain(k, i)
            spread2.pair(k - 1, i)
    for i in range(pieces):
        spread2.pair(zlen - 1, i)
    for k in range(zlen):
        for zz, guard, _ in p.level(k):
            when(guard, lambda zz=zz: spread.from_twin(zz))
            when(guard, lambda zz=zz: spread2.from_twin(zz))
    for s in range(1, n):
        u_copy(s, (c + n - s) % n).wait_recv()
    vec_out[...] = vall[...]

    for u in range(hpd):
        do_swaps[u].drain()
        gradient_swap(u).drain()
    spread.drain()
    spread2.drain()
    reduce.drain()
    for s, peer in enumerate(p.fpeers):
        xw_copy(s, peer).wait_send()
        tg_copy(s).wait_send()
        x_copy(s, peer).wait_send()
        v_copy(s, peer, f).wait_send()
    for s in range(1, n):
        u_copy(s, c).wait_send()


def backward(lay, nf, within, inverse, lengths, gt, factor, g1, dg2, ffn_parts, cot, kept, tokens, mats, mine, other, x, dh):
    n, hpd, rows, size = lay.n, lay.hpd, lay.rows, lay.size
    dma = pltpu.SemaphoreType.DMA
    shard = D // nf
    part = shard // 2
    zlen = n // 4
    height = -(-3 * part // (16 * zlen)) * 16 * zlen
    piece = height // zlen
    pieces = 3 if piece % 48 == 0 else 1
    peers = max(nf - 1, 1)
    tok = x.shape[0]
    return pl.pallas_call(
        functools.partial(backward_kernel, lay, n, nf),
        out_shape=(
            jax.ShapeDtypeStruct((tok, D), F32),
            jax.ShapeDtypeStruct((n, 3, HD, shard), BF16),
            jax.ShapeDtypeStruct((n, pieces, piece // pieces, D // 2), BF16),
            jax.ShapeDtypeStruct((n, VEC_ROWS, BLK), F32),
            jax.ShapeDtypeStruct((peers, part, D), BF16),
            jax.ShapeDtypeStruct((peers, part, D), BF16),
        ),
        in_specs=[in_smem()] * 3 + [in_vmem()] * 4 + [in_any()] * 19,
        out_specs=(in_vmem(), in_any(), in_any(), in_vmem(), in_any(), in_any()),
        scratch_shapes=[
            VMEM((3 * D, D), BF16), VMEM((nf, height, D), BF16), VMEM((3, D, tok), BF16),
            VMEM((2, 8 * BLK, D), BF16),
            VMEM((HD, rows), F32), VMEM((BLK, rows), BF16), VMEM((HD, rows), BF16), VMEM((HD, rows), BF16),
            VMEM((rows, BLK), BF16), VMEM((HD, rows), F32), VMEM((1, rows), F32),
            VMEM((tok, D), BF16), VMEM((tok, D), F32),
            VMEM((size, BLK), BF16), VMEM((size, BLK), BF16), VMEM((size, BLK), BF16), VMEM((BLK, size), BF16),
            VMEM((1, size), F32), VMEM((size, BLK), F32), VMEM((size, BLK), F32), VMEM((HD, size), F32),
            VMEM((size // BLK, 3 * HD, BLK), BF16), VMEM((3, BLK, BLK), F32), VMEM((hpd, 3 * HD, n * BLK), BF16),
            VMEM((hpd, n, 3 * HD, BLK), BF16), VMEM((3 * HD, D), F32), VMEM((nf, 3 * HD, shard), BF16),
            VMEM((peers, 3 * HD, shard), BF16), VMEM((3, HD, shard), BF16),
            VMEM((nf, VEC_ROWS, BLK), F32), VMEM((VEC_ROWS, BLK), F32), VMEM((n, VEC_ROWS, BLK), F32),
            dma((15 + 6 * nf,)), dma((hpd, n)), dma((hpd, n)), dma((hpd,)), dma((hpd, n)), dma((hpd, n)), dma((hpd,)),
            dma((nf,)), dma((nf,)), dma((peers,)), dma((peers,)), dma((peers,)), dma((peers,)), dma((2,)),
            dma((peers,)), dma((peers,)), dma, dma((4, n, 3)), dma((n, 3)), dma((4, n, pieces)), dma((n, pieces)),
            dma((peers,)), dma((peers,)), dma((n,)), dma((n,)),
        ] + [VMEM((n, HD, BLK), BF16)] * hpd + Reduce.scratch(nf, zlen, height),
        compiler_params=pltpu.CompilerParams(
            collective_id=2, has_side_effects=True, vmem_limit_bytes=62 * MIB
        ),
        cost_estimate=cost(130),
        name="backward",
    )(within, inverse, lengths, gt, factor, g1, dg2, *ffn_parts, cot, *kept, tokens, mats, mine, other, x, dh)


def turn_kernel(hpd, dw_ref, q_ref, k_ref, v_ref, wide):
    j = pl.program_id(0)

    @pl.when(j == 0)
    def _():
        for m in range(3):
            for h in range(H):
                if hpd == 2:
                    block = dw_ref[h, m].astype(F32)
                else:
                    block = dw_ref[2 * h, m].astype(F32) + dw_ref[2 * h + 1, m].astype(F32)
                wide[m, pl.ds(h * HD, HD), :] = block

    for m, out in enumerate((q_ref, k_ref, v_ref)):
        out[...] = wide[m, pl.ds(al(j * WIDE, WIDE), WIDE), :].T


def turn(hpd, dw):
    n, _, _, rows = dw.shape
    spec = pl.BlockSpec((rows, WIDE), lambda j: (0, j))
    return pl.pallas_call(
        functools.partial(turn_kernel, hpd),
        grid=(D // WIDE,),
        out_shape=tuple([jax.ShapeDtypeStruct((rows, D), F32)] * 3),
        in_specs=[pl.BlockSpec((n, 3, HD, rows), lambda j: (0, 0, 0, 0))],
        out_specs=(spec, spec, spec),
        scratch_shapes=[VMEM((3, D, rows), F32)],
        compiler_params=pltpu.CompilerParams(vmem_limit_bytes=60 * MIB),
        cost_estimate=cost(6),
        name="turn",
    )(dw)


def widen_kernel(zlen, part, in_ref, o_ref, u_ref, d_ref):
    j, y = pl.program_id(0), pl.program_id(1)
    height = in_ref.shape[3]
    for m, out in enumerate((o_ref, u_ref, d_ref)):
        for z in range(zlen):
            first, last = max(m * part, z * height), min((m + 1) * part, (z + 1) * height)
            if first < last:
                out[first - m * part : last - m * part, :] = in_ref[
                    z, y, j, first - z * height : last - z * height, :
                ].astype(F32)


def widen(zlen, part, pieces):
    half = pieces.shape[-1]
    height = pieces.shape[1] * pieces.shape[2]
    spec = pl.BlockSpec((part, half), lambda j, y: (j, y))
    return pl.pallas_call(
        functools.partial(widen_kernel, zlen, part),
        grid=(2, 2),
        out_shape=tuple([jax.ShapeDtypeStruct((2 * part, D), F32)] * 3),
        in_specs=[pl.BlockSpec((zlen, 2, 2, height, half), lambda j, y: (0, 0, 0, 0, 0))],
        out_specs=(spec, spec, spec),
        compiler_params=pltpu.CompilerParams(vmem_limit_bytes=60 * MIB),
        cost_estimate=cost(5),
        name="widen",
    )(pieces.reshape(zlen, 2, 2, height, half))


def local(
    n, nf, tokens, cotangent, lengths, deal, gain_attn, query_weight, query_bias, key_weight,
    value_weight, value_bias, query_scale, proj_weight, gain_ffn, up_weight, down_weight,
):
    c = lax.axis_index("ctx")
    f = lax.axis_index("fsdp")
    lay = Layout(n, deal.shape[0])
    head = c * lay.hpd // 2
    rows = query_weight.shape[0]
    x, cot = tokens[0], cotangent[0]

    def low(v):
        return lax.reduce_precision(v, exponent_bits=8, mantissa_bits=7)

    g1_own = low(gain_attn)
    slices = [
        lax.dynamic_slice(w, (0, head * HD), (rows, HD)) for w in (query_weight, key_weight, value_weight)
    ]
    wh = jnp.pad(jnp.concatenate(slices, axis=1), ((0, 0), (0, 256 - 3 * HD))).astype(BF16)
    scale = low(query_scale)
    factor = jnp.log(1.0 + jnp.exp(scale)) * (LOG2E / math.sqrt(HD))
    shares = lax.dynamic_update_slice(
        jnp.zeros((2, rows), F32), jnp.stack([factor, scale]), (0, f * query_scale.shape[0]))
    vec = jnp.concatenate(
        [jnp.stack([g1_own, low(query_bias), low(value_bias), low(gain_ffn)]), shares])
    vec = jnp.pad(vec, ((0, 2), (0, -rows % 128)))
    blocks = jnp.arange(deal.shape[0], dtype=jnp.int32)
    inverse = jnp.sum(jnp.where(deal[None, :] == blocks[:, None], blocks[None, :] // 2, 0), axis=1, dtype=jnp.int32)
    within = deal % lay.half_blocks

    a_all, mats, mine, other, whole, factor_col, dg2, *stored = forward(
        lay, nf, within, inverse, lengths, x, cot, wh, vec,
        (proj_weight, up_weight, down_weight, query_weight, key_weight, value_weight),
    )
    kept, (layer_out, dh, gt, ott, bt, zt, gb, du) = stored[:7], stored[7:]
    g1 = whole[0:1]
    q_param = whole[5, :HD]

    grad_x, dw, pieces, vectors, *_ = backward(
        lay, nf, within, inverse, lengths, gt.reshape(n, lay.hpd, HD, BLK), factor_col, g1, dg2,
        (ott, bt, zt, gb, du), cot, kept, a_all, mats, mine, other, x, dh,
    )
    dwq, dwk, dwv = turn(lay.hpd, dw)
    grads = widen(n // 4, rows // 2, pieces)

    def own(v):
        size = v.shape[0] // nf
        return lax.dynamic_slice(v, (f * size,), (size,))

    def of_heads(r):
        return vectors[:, r, :HD].reshape(H, 2 // lay.hpd, HD).sum(axis=1).reshape(D)

    gains = jnp.sum(vectors[:, : 2 * D // BLK], axis=0).reshape(2, D)
    grad_scale = jnp.sum(vectors[:, 20, :HD], axis=0) * jax.nn.sigmoid(q_param) * (LOG2E / math.sqrt(HD))
    return (
        layer_out[None],
        grad_x[None],
        own(gains[0]),
        dwq,
        own(of_heads(21)),
        dwk,
        dwv,
        own(of_heads(22)),
        own(grad_scale),
        grads[0],
        own(gains[1]),
        grads[1],
        grads[2],
    )


def solution(mesh):
    whole, vector, matrix = P("fsdp", "ctx", None), P("fsdp"), P("fsdp", None)
    return jax.shard_map(
        functools.partial(local, mesh.shape["ctx"], mesh.shape["fsdp"]),
        mesh=mesh,
        in_specs=(
            whole, whole, matrix, P(), vector, matrix, vector, matrix, matrix, vector, vector,
            matrix, vector, matrix, matrix,
        ),
        out_specs=(
            whole, whole, vector, matrix, vector, matrix, matrix, vector, vector, matrix, vector,
            matrix, matrix,
        ),
        check_vma=False,
    )
```

```python
import functools
import math

import jax
import jax.numpy as jnp
from jax import lax
from jax.experimental import pallas as pl
from jax.experimental.pallas import tpu as pltpu
from jax.sharding import PartitionSpec as P

H = 16
HD = 80
BLK = 128
D = 1280
EPS = 1e-06
LOG2E = 1.442695041
NEG = -1e30
MESH = pl.DeviceIdType.MESH
F32 = jnp.float32
BF16 = jnp.bfloat16
VMEM = pltpu.VMEM
MIB = 1 << 20

NN = (((1,), (0,)), ((), ()))
NT = (((1,), (1,)), ((), ()))
TN = (((0,), (0,)), ((), ()))


def dot(left, right, dims=NN):
    return lax.dot_general(left, right, dims, preferred_element_type=F32)


def al(value, multiple):
    return pl.multiple_of(value, multiple)


def in_vmem():
    return pl.BlockSpec(memory_space=pltpu.VMEM)


def in_smem():
    return pl.BlockSpec(memory_space=pltpu.SMEM)


def in_any():
    return pl.BlockSpec(memory_space=pl.ANY)


def cost(microseconds):
    return pl.CostEstimate(flops=0, bytes_accessed=int(microseconds * 3.0e6), transcendentals=0)


class Place:
    def __init__(self, n, nf):
        self.n, self.nf = n, nf
        self.c = lax.axis_index("ctx")
        self.f = lax.axis_index("fsdp")
        self.zlen = n // 4
        self.z, self.y, self.core = self.c // 4, (self.c // 2) % 2, self.c % 2
        self.twin = self.idx(self.z, self.y, 1 - self.core)
        self.ypeer = self.idx(self.z, 1 - self.y, self.core)
        self.targets = (
            self.idx(self.z + 1, self.y, self.core), self.idx(self.z - 1, self.y, self.core),
            self.ypeer, self.twin,
        )
        self.guards = (self.z < self.zlen - 1, self.z > 0, None, None)
        self.fpeers = [(self.f + s) % nf for s in range(1, nf)]
        self.fsources = [(self.f + nf - s) % nf for s in range(1, nf)]

    def idx(self, z, y, core):
        return (z * 2 + y) * 2 + core

    def level(self, k):
        if k == 0:
            return [(self.z, None, 0)]
        return [
            (self.z + k, self.z + k < self.zlen, 1),
            (self.z - k, self.z - k >= 0, -1),
        ]

    def greet_neighbours(self):
        barrier = pltpu.get_barrier_semaphore()
        for target, guard in zip(self.targets, self.guards):
            when(guard, lambda target=target: pl.semaphore_signal(
                barrier, inc=1, device_id=(target, self.f), device_id_type=MESH))
        for peer in self.fpeers:
            pl.semaphore_signal(barrier, inc=1, device_id=(self.c, peer), device_id_type=MESH)
        ends = jnp.minimum(self.z, 1) + jnp.minimum(self.zlen - 1 - self.z, 1)
        pl.semaphore_wait(barrier, 1 + self.nf + ends)

    def greet_all(self, with_fsdp):
        barrier = pltpu.get_barrier_semaphore()
        for s in range(1, self.n):
            pl.semaphore_signal(
                barrier, inc=1, device_id=(self.c ^ s, self.f), device_id_type=MESH)
        if with_fsdp:
            for peer in self.fpeers:
                pl.semaphore_signal(barrier, inc=1, device_id=(self.c, peer), device_id_type=MESH)
        pl.semaphore_wait(barrier, self.n - 1 + (self.nf - 1 if with_fsdp else 0))


def when(guard, body):
    if guard is None:
        body()
    else:
        pl.when(guard)(body)


class Spread:
    def __init__(self, place, buf, send_sem, recv_sem, pieces, own=None, own_sem=None):
        self.p, self.buf, self.send_sem, self.recv_sem, self.pieces = place, buf, send_sem, recv_sem, pieces
        self.own, self.own_sem = own, own_sem

    def copy(self, way, origin, i, src=None):
        where = self.buf.at[origin, i]
        return pltpu.make_async_remote_copy(
            src_ref=where if src is None else src, dst_ref=where,
            send_sem=self.send_sem.at[way, origin, i], recv_sem=self.recv_sem.at[origin, i],
            device_id=(self.p.targets[way], self.p.f), device_id_type=MESH,
        )

    def send(self, way, origin, i):
        when(self.p.guards[way], lambda: self.copy(way, origin, i).start())

    def arrive(self, origin, i):
        self.copy(3, origin, i).wait_recv()

    def keep(self, i):
        return pltpu.make_async_copy(self.own(i), self.buf.at[self.p.c, i], self.own_sem.at[i])

    def start(self, i):
        src = self.own(i) if self.own else None
        for way in range(4):
            when(self.p.guards[way], lambda way=way: self.copy(way, self.p.c, i, src).start())
        if self.own:
            self.keep(i).start()

    def chain(self, k, i):
        p = self.p
        for zz, guard, sign in p.level(k):
            def body(zz=zz, sign=sign):
                origin = p.idx(zz, p.y, p.core)
                self.arrive(origin, i)
                self.send(1 if sign == 1 else 0, origin, i)
                self.send(2, origin, i)
                self.send(3, origin, i)
            when(guard, body)

    def pair(self, k, i):
        p = self.p
        for zz, guard, _ in p.level(k):
            def body(zz=zz):
                origin = p.idx(zz, 1 - p.y, p.core)
                self.arrive(origin, i)
                self.send(3, origin, i)
            when(guard, body)

    def from_twin(self, zz, pieces=None):
        p = self.p
        for yy in (p.y, 1 - p.y):
            for i in range(self.pieces) if pieces is None else pieces:
                self.arrive(p.idx(zz, yy, 1 - p.core), i)

    def drain(self):
        p = self.p
        for i in range(self.pieces):
            if self.own:
                self.keep(i).wait()
            for way in range(4):
                when(p.guards[way], lambda way=way, i=i: self.copy(way, p.c, i).wait_send())
            for k in range(p.zlen):
                for zz, guard, sign in p.level(k):
                    def body(zz=zz, sign=sign, k=k, i=i):
                        if k:
                            origin = p.idx(zz, p.y, p.core)
                            on = 1 if sign == 1 else 0
                            when(p.guards[on], lambda: self.copy(on, origin, i).wait_send())
                            self.copy(2, origin, i).wait_send()
                            self.copy(3, origin, i).wait_send()
                        self.copy(3, p.idx(zz, 1 - p.y, p.core), i).wait_send()
                    when(guard, body)


class Reduce:
    def __init__(self, place, mine, result, acc, xrecv, yrecv, zsend, zrecv, sems):
        self.p, self.mine, self.result, self.acc = place, mine, result, acc
        self.xrecv, self.yrecv, self.zsend, self.zrecv = xrecv, yrecv, zsend, zrecv
        (self.xs, self.xr, self.ys, self.yr, self.zs, self.zr) = sems
        self.height = acc.shape[0] // place.zlen
        self.width = D // 2
        zlen = place.zlen
        ends = []
        for k in range(zlen // 2):
            ends += [zlen - 1 - k, k]
        self.order = ends

    @staticmethod
    def scratch(nf, zlen, height):
        dma = pltpu.SemaphoreType.DMA
        peers = max(nf - 1, 1)
        piece = VMEM((zlen, height // zlen, D // 2), BF16)
        return [
            VMEM((height // zlen, D // 2), BF16), VMEM((height, D), BF16), VMEM((peers, height, D), BF16),
            piece, piece, piece,
            dma((peers, zlen, 2)), dma((peers, zlen, 2)), dma((zlen,)), dma((zlen,)),
            dma((zlen,)), dma((zlen,)),
        ]

    def at(self, piece, side):
        return (
            pl.ds(al(piece * self.height, 16), self.height),
            pl.ds(al(side * self.width, 128), self.width),
        )

    def remote(self, src, dst, send, recv, c, f):
        return pltpu.make_async_remote_copy(
            src_ref=src, dst_ref=dst, send_sem=send, recv_sem=recv,
            device_id=(c, f), device_id_type=MESH,
        )

    def x_copy(self, s, peer, piece, turn):
        side = (self.p.y + 1 + turn) % 2
        where = self.at(piece, side)
        return self.remote(
            self.mine.at[peer].at[where], self.xrecv.at[s].at[where],
            self.xs.at[s, piece, turn], self.xr.at[s, piece, turn], self.p.c, peer,
        )

    def start_x(self, t):
        for turn in range(2):
            for s, peer in enumerate(self.p.fpeers):
                self.x_copy(s, peer, self.order[t], turn).start()

    def add(self, dst, terms, count=None):
        count = count or self.height
        step = 48 if count % 48 == 0 else 16
        @pl.loop(0, count // step)
        def _(t):
            at = pl.ds(al(t * step, 16), step)
            total = terms[0][at, :].astype(F32)
            for term in terms[1:]:
                total = total + term[at, :].astype(F32)
            dst[at, :] = total.astype(BF16)

    def sum_x(self, piece, turn):
        side = (self.p.y + 1 + turn) % 2
        where = self.at(piece, side)
        terms = [self.mine.at[self.p.f].at[where]]
        for s, peer in enumerate(self.p.fpeers):
            self.x_copy(s, peer, piece, turn).wait_recv()
            terms.append(self.xrecv.at[s].at[where])
        self.add(self.acc.at[where], terms)

    def y_copy(self, piece):
        src = self.acc.at[self.at(piece, 1 - self.p.y)]
        return self.remote(
            src, self.yrecv.at[piece], self.ys.at[piece], self.yr.at[piece], self.p.ypeer, self.p.f)

    def z_copy(self, piece, slot):
        p = self.p
        return self.remote(
            self.zsend.at[piece], self.zrecv.at[slot], self.zs.at[piece], self.zr.at[slot],
            p.idx(piece, p.y, p.core), p.f)

    def xy(self, t):
        piece = self.order[t]
        self.sum_x(piece, 0)
        self.y_copy(piece).start()
        self.sum_x(piece, 1)

    def after_y(self, t):
        p, piece = self.p, self.order[t]
        self.y_copy(piece).wait_recv()
        self.add(self.zsend.at[piece], [self.acc.at[self.at(piece, p.y)], self.yrecv.at[piece]])
        pl.when(p.z != piece)(lambda: self.z_copy(piece, p.z).start())

    def last(self):
        p = self.p
        terms = [self.zsend.at[p.z]]
        for k in range(1, p.zlen):
            other = lax.rem(p.z + k, p.zlen)
            self.z_copy(0, other).wait_recv()
            terms.append(self.zrecv.at[other])
        self.add(self.result, terms)

    def drain(self):
        p = self.p
        for piece in self.order:
            for turn in range(2):
                for s, peer in enumerate(p.fpeers):
                    self.x_copy(s, peer, piece, turn).wait_send()
            self.y_copy(piece).wait_send()
            pl.when(p.z != piece)(lambda piece=piece: self.z_copy(piece, p.z).wait_send())


class Loads:
    def __init__(self, sems):
        self.sems, self.copies = sems, []

    def start(self, src, dst):
        copy = pltpu.make_async_copy(src, dst, self.sems.at[len(self.copies)])
        self.copies.append(copy)
        copy.start()
        return copy

    def wait(self):
        for copy in self.copies:
            copy.wait()


class Swap:
    def __init__(self, place, src, dst, send_sem, recv_sem, own_sem):
        self.p, self.src, self.dst = place, src, dst
        self.send_sem, self.recv_sem, self.own_sem = send_sem, recv_sem, own_sem

    def copy(self, s, block):
        p = self.p
        return pltpu.make_async_remote_copy(
            src_ref=self.src(p.c ^ s), dst_ref=self.dst(block),
            send_sem=self.send_sem.at[s], recv_sem=self.recv_sem.at[s],
            device_id=(p.c ^ s, p.f), device_id_type=MESH,
        )

    def own(self):
        return pltpu.make_async_copy(self.src(self.p.c), self.dst(self.p.c), self.own_sem)

    def start(self):
        for s in range(1, self.p.n):
            self.copy(s, self.p.c).start()
        self.own().start()

    def wait(self):
        self.own().wait()
        for s in range(1, self.p.n):
            self.copy(s, self.p.c ^ s).wait_recv()

    def drain(self):
        for s in range(1, self.p.n):
            self.copy(s, self.p.c).wait_send()


def seq_start(ends, base, token):
    start = jnp.zeros_like(token)
    for e in ends:
        start = jnp.where(e - base <= token, jnp.maximum(start, e - base), start)
    return start


def read_ends(lengths_ref):
    ends, total = [], jnp.int32(0)
    for i in range(lengths_ref.shape[1]):
        total = total + lengths_ref[0, i]
        ends.append(total)
    return ends


def pad_rows(block):
    return jnp.concatenate([block, jnp.zeros((BLK - HD, block.shape[1]), block.dtype)], axis=0)


class Layout:
    def __init__(self, n, total_blocks):
        self.n = n
        self.hpd = 2 * H // n
        self.half_blocks = total_blocks // 2
        self.size = self.half_blocks * BLK
        self.rows = self.hpd * self.size
        self.tile = 512

    def half(self, i):
        return i if self.hpd == 2 else lax.axis_index("ctx") % 2

    def within(self, deal_ref, d, u):
        return deal_ref[2 * d + self.half(u)] & (self.half_blocks - 1)

    def base(self, unit):
        return self.half(unit) * self.size if self.hpd == 1 else unit * self.size


WIDE = 256


def over_columns(body):
    @pl.loop(0, D // WIDE)
    def _(j):
        body(pl.ds(al(j * WIDE, WIDE), WIDE))


def token_rows(
    x_ref, cot_ref, oswap, rows_ref, weights, w_loads,
    out_ref, dh_ref, gt_ref, ot, bt, zt, gb, du, dg2_ref,
    o_rows, hidden, nh, b, up, z, db, wide, stage,
):
    wo, w1, w2 = weights
    hpd = oswap.shape[1]
    for i in range(2):
        for h in range(H):
            ot[pl.ds(h * HD, HD), pl.ds(i * BLK, BLK)] = oswap[h, i] if hpd == 2 else oswap[2 * h + i, 0]
    @pl.loop(0, D // WIDE)
    def _(j):
        sl = pl.ds(al(j * WIDE, WIDE), WIDE)
        o_rows[:, sl] = ot[sl, :].astype(F32).T.astype(BF16)
    stage("ot")

    def body(sl):
        hidden[:, sl] = x_ref[:, sl].astype(F32) + dot(o_rows[...], wo[:, sl])
    over_columns(body)
    hid = hidden[...]
    r2 = lax.rsqrt(jnp.mean(hid * hid, axis=-1, keepdims=True) + EPS)
    nh[...] = hid * r2
    b[...] = (nh[...] * rows_ref[3:4, :]).astype(BF16)
    w_loads[1].wait()

    def body(sl):
        u = dot(b[...], w1[:, sl])
        up[:, sl] = u
        act = u * jax.nn.sigmoid(u)
        z[:, sl] = act.astype(BF16)
        zt[sl, :] = act.T.astype(BF16)
        bt[sl, :] = b[:, sl].astype(F32).T.astype(BF16)
    over_columns(body)
    stage("z")
    stage("b")

    w_loads[2].wait()

    def body(sl):
        out_ref[:, sl] = (hidden[:, sl] + dot(z[...], w2[:, sl])).astype(BF16)
        dz = dot(cot_ref[...], w2[sl, :], NT)
        u = up[:, sl]
        sig = jax.nn.sigmoid(u)
        du[:, sl] = (dz * sig * (1.0 + u * (1.0 - sig))).astype(BF16)
    over_columns(body)
    stage("out")
    stage("du")

    def body(sl):
        g = dot(du[...], w1[sl, :], NT)
        db[:, sl] = g * rows_ref[3:4, sl]
        dg2_ref[:, sl] = jnp.sum(g * nh[:, sl], axis=0, keepdims=True)
    over_columns(body)
    scaled = db[...]
    mean = jnp.mean(scaled * nh[...], axis=-1, keepdims=True)
    dh = cot_ref[...].astype(F32) + r2 * (scaled - nh[...] * mean)
    dh_ref[...] = dh
    gb[...] = dh.astype(BF16)
    stage("gb")

    @pl.loop(0, D // WIDE)
    def _(j):
        sl = pl.ds(al(j * WIDE, WIDE), WIDE)
        wide[sl, :] = dot(wo[sl, :], gb[...], NT).astype(BF16)
    for i in range(2):
        for h in range(H):
            gt_ref[h, i] = wide[pl.ds(h * HD, HD), pl.ds(i * BLK, BLK)]
    stage("gt")


def forward_kernel(
    lay, n, nf,
    deal_ref, inv_ref, len_ref, x_ref, cot_ref, *rest,
):
    row_refs, mat_refs, rest = rest[:5], rest[5:11], rest[11:]
    (a_out, mats_out, mine_out, other_out, twin_t, twin_r, rows_out, factor_out, dg2_out, *stored) = rest[: 9 + 12]
    (abuf, norm, windows, wh_ref, whbuf, wht, vec_ref, vecbuf, vcol, stage, wcast, qkv, osend, onat, oswap,
     qraw, qst, kt, vt, kn, ot, lse, layer, dh, gt, ot_t, bt, zt, gb, du,
     o_rows, hidden, nh, b_rows, up, z, db, wide, m_ref, l_ref, acc_ref,
     ag_send, ag_recv, wh_send, wh_recv, vec_send, vec_recv,
     ld_sem, mx_send, mx_recv, ms_send, ms_recv, a_sem, keep_sem, o_send, o_recv, o_own,
     st_sem, w_sem, tt_send, tt_recv, tr_send, tr_recv, win_sem) = rest[9 + 12 :]
    kept = (qraw, qst, kt, vt, kn, ot, lse)
    stores = Loads(st_sem)
    p = Place(n, nf)
    c, f, core, zlen, hpd, tile = p.c, p.f, p.core, p.zlen, lay.hpd, lay.tile
    rows = wh_ref.shape[0]
    part = rows // 2

    head = c * hpd // 2
    first = jnp.minimum(head * HD // BLK * BLK, D - 2 * BLK)
    window_loads = [
        pltpu.make_async_copy(
            mat_refs[3 + m].at[:, pl.ds(al(first, BLK), 2 * BLK)], windows.at[m], win_sem.at[m])
        for m in range(3)
    ]
    for copy in window_loads:
        copy.start()
    vec_ref[...] = jnp.zeros_like(vec_ref)
    for r, ref in enumerate(row_refs):
        for k in range(ref.shape[0]):
            vec_ref[r : r + 1, k * BLK : (k + 1) * BLK] = ref[k : k + 1, :]
    p.greet_all(True)
    spread = Spread(p, abuf, ag_send, ag_recv, 2)

    for i in range(2):
        abuf[c, i] = x_ref[pl.ds(i * BLK, BLK), :]
    spread.start(0)

    def wh_copy(s, peer):
        return pltpu.make_async_remote_copy(
            src_ref=wh_ref, dst_ref=whbuf.at[pl.ds(al(f * rows, 16), rows)],
            send_sem=wh_send.at[s], recv_sem=wh_recv.at[s],
            device_id=(c, peer), device_id_type=MESH,
        )

    def vec_copy(s, peer):
        return pltpu.make_async_remote_copy(
            src_ref=vec_ref, dst_ref=vecbuf.at[f],
            send_sem=vec_send.at[s], recv_sem=vec_recv.at[s],
            device_id=(c, peer), device_id_type=MESH,
        )

    for s, peer in enumerate(p.fpeers):
        vec_copy(s, peer).start()
    for copy in window_loads:
        copy.wait()
    strip = 128 if rows % 128 == 0 else 32

    @pl.loop(0, rows // strip)
    def _(t):
        at = pl.ds(al(t * strip, 32), strip)
        lane = lax.broadcasted_iota(jnp.int32, (strip, 2 * BLK), 1)
        value = jnp.zeros((strip, 2 * BLK), F32)
        for m in range(3):
            turned = pltpu.roll(windows[m, at, :], lax.rem(m * HD + 2 * BLK - (head * HD - first), 2 * BLK), 1)
            value = jnp.where((lane >= m * HD) & (lane < (m + 1) * HD), turned, value)
        wh_ref[at, :] = value.astype(BF16)

    for s, peer in enumerate(p.fpeers):
        wh_copy(s, peer).start()
    whbuf[pl.ds(al(f * rows, 16), rows), :] = wh_ref[...]
    vecbuf[f] = vec_ref[...]

    shards = mat_refs
    moved = len(mat_refs) - 1
    steps = [(m, 0) for m in range(moved)] + [(m, 1) for m in range(moved)] + [(moved, 0), (moved, 1)]

    def half_of(h):
        return (core + h) % 2

    def load(step):
        m, h = steps[step]
        return pltpu.make_async_copy(
            shards[m].at[pl.ds(al(half_of(h) * part, 16), part)],
            stage.at[step % 2], ld_sem.at[step % 2],
        )

    def mx_copy(m, s, peer, source):
        return pltpu.make_async_remote_copy(
            src_ref=wcast.at[m, core],
            dst_ref=mats_out.at[m, pl.ds(al(source * rows + core * part, 16), part)],
            send_sem=mx_send.at[m, s], recv_sem=mx_recv.at[m, s],
            device_id=(c, peer), device_id_type=MESH,
        )

    def keep_copies(m):
        if m < moved:
            return [
                pltpu.make_async_copy(
                    wcast.at[m, h], mats_out.at[m, pl.ds(al(f * rows + h * part, 16), part)],
                    keep_sem.at[m, h],
                ) for h in range(2)
            ]
        return [
            pltpu.make_async_copy(wcast.at[m, half_of(h)], out, keep_sem.at[m, h])
            for h, out in enumerate((mine_out, other_out))
        ]

    def cast(step):
        m, h = steps[step]
        if step + 1 < len(steps):
            load(step + 1).start()
        load(step).wait()
        chunk = part // 4 if part % 64 == 0 else part
        @pl.loop(0, part // chunk)
        def _(t):
            wcast[m, half_of(h), pl.ds(al(t * chunk, 16), chunk), :] = stage[
                step % 2, pl.ds(al(t * chunk, 16), chunk), :
            ].astype(BF16)
        if h == 0 and m < moved:
            for s, peer in enumerate(p.fpeers):
                mx_copy(m, s, peer, f).start()
        if h == 1:
            for copy in keep_copies(m):
                copy.start()

    load(0).start()
    done = [0]

    def casts(count):
        for step in range(done[0], min(done[0] + count, len(steps))):
            cast(step)
        done[0] += count

    casts(2)

    def gather_events(i, first, last):
        for k in range(first, last):
            if k < zlen:
                spread.chain(k, i)
            spread.pair(k - 1, i)

    def ms_copy(m, s, source, half):
        where = mats_out.at[m, pl.ds(al(source * rows + half * part, 16), part)]
        return pltpu.make_async_remote_copy(
            src_ref=where, dst_ref=where,
            send_sem=ms_send.at[m, s], recv_sem=ms_recv.at[m, s],
            device_id=(p.twin, f), device_id_type=MESH,
        )

    def pass_matrix(m):
        for s, (peer, source) in enumerate(zip(p.fpeers, p.fsources)):
            mx_copy(m, s, peer, source).wait_recv()
            ms_copy(m, s, source, core).start()

    def t_copy(m, source):
        mat = (ot_t, bt, zt)[m]
        return pltpu.make_async_remote_copy(
            src_ref=mat.at[pl.ds(al(source * rows + (1 - core) * part, 16), part)],
            dst_ref=twin_t.at[m, pl.ds(source * part, part)],
            send_sem=tt_send.at[m, source], recv_sem=tt_recv.at[m, source],
            device_id=(p.twin, f), device_id_type=MESH,
        )

    def r_copy(m):
        return pltpu.make_async_remote_copy(
            src_ref=(gb, du, cot_ref)[m], dst_ref=twin_r.at[m], send_sem=tr_send.at[m], recv_sem=tr_recv.at[m],
            device_id=(p.twin, f), device_id_type=MESH,
        )

    own_t, own_r = stored[10], stored[11]

    def to_twin(m, src):
        for source in range(nf):
            t_copy(m, source).start()
            stores.start(
                src.at[pl.ds(al(source * rows + core * part, 16), part)], own_t.at[m, pl.ds(source * part, part)])

    r_copy(2).start()
    gather_events(0, 1, 2)
    casts(1)

    for s, peer in enumerate(p.fpeers):
        vec_copy(s, peer).wait_recv()
        wh_copy(s, peer).wait_recv()
    wht[...] = whbuf[...].astype(F32).T.astype(BF16)
    for source in range(nf):
        rows_out[:, pl.ds(source * rows, rows)] = vecbuf[source, :, 0:rows].astype(BF16).astype(F32)
    share = HD // nf
    shares = [vecbuf[source, 4:5, 0:share].astype(BF16).astype(F32) for source in range(nf)]
    for source in range(nf):
        rows_out[4:5, source * share : (source + 1) * share] = shares[source]
    vcol[...] = rows_out[...].T
    here = pl.ds(al(head * HD, 16), HD)
    bias_q, bias_v = vcol[here, 1:2], vcol[here, 2:3]
    factor = jnp.log(1.0 + jnp.exp(vcol[0:HD, 4:5])) * (LOG2E / math.sqrt(HD))
    factor_out[...] = jnp.broadcast_to(factor, (HD, BLK))

    def a_copy(slot, origin, half):
        return pltpu.make_async_copy(norm.at[slot], a_out.at[pl.ds(origin, 2), half], a_sem.at[slot])

    def project(u, k, first=False):
        half = lay.half(u)
        for zz, guard, _ in p.level(k):
            def body(zz=zz):
                spread.from_twin(zz, [u] if hpd == 2 else range(2))
                for t in range(2):
                    origin = zz * 4 + 2 * t
                    if not first:
                        a_copy(t, origin, half).wait()
                    for i in range(2):
                        x = abuf[origin + i, half].astype(F32)
                        scale = lax.rsqrt(jnp.mean(x * x, axis=-1, keepdims=True) + EPS)
                        norm[t, i] = (x * scale * rows_out[0:1, :]).astype(BF16)
                    a_copy(t, origin, half).start()
                    value = dot(wht[: 3 * HD, :], norm[t].reshape(2 * BLK, D), NT)
                    qkv[origin] = value[:, :BLK]
                    qkv[origin + 1] = value[:, BLK:]
            when(guard, body)

    ends = read_ends(len_ref)

    def attend(u, during):
        base, row0 = lay.base(u), u * lay.size

        @pl.loop(0, lay.half_blocks)
        def _(b):
            cols = pl.ds(al(row0 + b * BLK, BLK), BLK)
            block = qkv[inv_ref[b + lay.half(u) * lay.half_blocks]]
            qr, kr, vr = block[:HD] + bias_q, block[HD : 2 * HD], block[2 * HD :] + bias_v
            qraw[:, cols] = qr
            qst[:, cols] = pad_rows(qr * factor).astype(BF16)
            kt[:, cols] = kr.astype(BF16)
            vt[:, cols] = vr.astype(BF16)
            kn[cols, :] = pad_rows(kr).T.astype(BF16)

        @pl.loop(0, lay.size // tile)
        def _(qi):
            cols = pl.ds(al(row0 + qi * tile, tile), tile)
            t_row = qi * tile + lax.broadcasted_iota(jnp.int32, (1, tile), 1)
            start = seq_start(ends, base, t_row)
            m_ref[...] = jnp.full_like(m_ref, NEG)
            l_ref[...] = jnp.zeros_like(l_ref)
            acc_ref[...] = jnp.zeros_like(acc_ref)

            @pl.loop(0, qi + 1)
            def _(j):
                keys = pl.ds(al(row0 + j * tile, tile), tile)
                s = dot(kn[keys, :], qst[:, cols])
                token = j * tile + lax.broadcasted_iota(jnp.int32, (tile, 1), 0)
                s = jnp.where((token >= start) & (token <= t_row), s, NEG)
                m_old = m_ref[...]
                m_new = jnp.maximum(m_old, jnp.max(s, axis=0, keepdims=True))
                prob = jnp.exp(s - m_new)
                shrink = jnp.exp(m_old - m_new)
                m_ref[...] = m_new
                l_ref[...] = l_ref[...] * shrink + jnp.sum(prob, axis=0, keepdims=True)
                acc_ref[...] = acc_ref[...] * shrink + dot(vt[:, keys], prob.astype(BF16))

            out = acc_ref[...] / l_ref[...]
            ot[:, cols] = out
            lse[:, cols] = m_ref[...] + jnp.log(l_ref[...])
            for b in range(tile // BLK):
                onat[qi * (tile // BLK) + b] = out[:, b * BLK : (b + 1) * BLK].astype(BF16)
            for at, event in during:
                pl.when(qi == at)(event)

        @pl.loop(0, n)
        def _(d):
            osend[u, d] = onat[lay.within(deal_ref, d, u)]

        o_swaps[u].start()

    o_swaps = [
        Swap(p, lambda d, u=u: osend.at[u, d], lambda d, u=u: oswap.at[d, u],
             o_send.at[u], o_recv.at[u], o_own.at[u])
        for u in range(hpd)
    ]

    def handed(m):
        for s, (peer, source) in enumerate(zip(p.fpeers, p.fsources)):
            ms_copy(m, s, source, 1 - core).wait_recv()
        for copy in keep_copies(m):
            copy.wait()

    weights = [abuf.at[pl.ds(5 * m, 5)].reshape(5 * 2 * BLK, D) for m in range(3)]
    w_loads = [
        pltpu.make_async_copy(mats_out.at[m], weights[m], w_sem.at[m]) for m in range(3)
    ]

    if hpd == 2:
        project(0, 0, first=True)
        for k in range(2, zlen + 1):
            gather_events(0, k, k + 1)
            if k == 2:
                spread.start(1)
            casts(2)
            project(0, k - 1)
        pass_matrix(0)
        gather_events(1, 1, 2)
        attend(0, [(lay.size // tile // 2, lambda: gather_events(1, 2, 3))])
        pass_matrix(1)
        casts(len(steps))
        project(1, 0)
        for k in range(3, zlen + 1):
            gather_events(1, k, k + 1)
            project(1, k - 2)
        project(1, zlen - 1)
    else:
        spread.start(1)
        casts(len(steps))
        for k in range(1, zlen + 1):
            if k > 1:
                gather_events(0, k, k + 1)
            gather_events(1, k, k + 1)
            project(0, k - 1, first=k == 1)
        pass_matrix(0)
        pass_matrix(1)
    spread.drain()
    for m in range(2):
        handed(m)
        w_loads[m].start()
    attend(hpd - 1, [])
    for src, dst in zip(kept, stored):
        stores.start(src, dst)
    pass_matrix(2)
    handed(2)
    w_loads[2].start()
    for u in range(hpd):
        o_swaps[u].wait()
    w_loads[0].wait()

    def stage(name):
        if name == "ot":
            to_twin(0, ot_t)
        elif name == "z":
            to_twin(2, zt)
        elif name == "b":
            to_twin(1, bt)
        elif name == "out":
            stores.start(layer, stored[7])
        elif name == "du":
            r_copy(1).start()
            stores.start(du, own_r.at[1])
        elif name == "gb":
            r_copy(0).start()
            stores.start(gb, own_r.at[0])
            stores.start(dh, stored[8])
        elif name == "gt":
            stores.start(gt, stored[9])

    token_rows(
        x_ref, cot_ref, oswap, rows_out, weights, w_loads,
        layer, dh, gt, ot_t, bt, zt, gb, du, dg2_out, o_rows, hidden, nh, b_rows, up, z, db, wide, stage)

    for m in range(3, moved):
        pass_matrix(m)
    for m in range(3, moved):
        handed(m)
    for copy in keep_copies(moved):
        copy.wait()
    for m in range(moved):
        for s, (peer, source) in enumerate(zip(p.fpeers, p.fsources)):
            mx_copy(m, s, peer, f).wait_send()
            ms_copy(m, s, source, core).wait_send()
    for m in range(3):
        r_copy(m).wait()
        for source in range(nf):
            t_copy(m, source).wait()
    for s, peer in enumerate(p.fpeers):
        wh_copy(s, peer).wait_send()
        vec_copy(s, peer).wait_send()
    for u in range(hpd):
        o_swaps[u].drain()
    for slot in range(2):
        a_copy(slot, 2 * slot, lay.half(0)).wait()
    stores.wait()


def forward(lay, nf, deal, inverse, lengths, x, cot, vectors, mats):
    n, hpd, total = lay.n, lay.hpd, lay.rows
    rows, tok, count = mats[0].shape[0], x.shape[0], len(mats)
    dma = pltpu.SemaphoreType.DMA
    peers = max(nf - 1, 1)
    half = ((rows // 2, D), BF16)
    kept = [
        ((HD, total), F32), ((BLK, total), BF16), ((HD, total), BF16), ((HD, total), BF16), ((total, BLK), BF16),
        ((HD, total), F32), ((1, total), F32),
    ]
    plain, turned, wide = ((tok, D), BF16), ((D, tok), BF16), ((tok, D), F32)
    made = [plain, wide, ((H, 2, HD, BLK), BF16), turned, turned, turned, plain, plain]
    shared = ((3, D // 2, tok), BF16)
    results = made[:3] + [shared, ((2, tok, D), BF16)]
    outs = [
        ((n, 2, BLK, D), BF16), ((count - 1, nf * rows, D), BF16), half, half, shared, ((3, tok, D), BF16),
        ((8, D), F32), ((HD, BLK), F32), ((1, D), F32),
    ] + kept + results
    places = [in_any()] * 6 + [in_vmem()] * 3 + [in_any()] * (len(kept) + len(results))
    moves = dma((count - 1, peers))
    return pl.pallas_call(
        functools.partial(forward_kernel, lay, n, nf),
        out_shape=tuple(jax.ShapeDtypeStruct(*out) for out in outs),
        in_specs=[in_smem()] * 3 + [in_vmem()] * (2 + len(vectors)) + [in_any()] * count,
        out_specs=tuple(places),
        scratch_shapes=[
            VMEM((n, 2, BLK, D), BF16),
            VMEM((2, 2, BLK, D), BF16),
            VMEM((3, rows, 2 * BLK), F32),
            VMEM((rows, 2 * BLK), BF16),
            VMEM((nf * rows, 2 * BLK), BF16),
            VMEM((2 * BLK, nf * rows), BF16),
            VMEM((8, -(-rows // BLK) * BLK), F32),
            VMEM((nf, 8, -(-rows // BLK) * BLK), F32),
            VMEM((D, 8), F32),
            VMEM((2, rows // 2, D), F32),
            VMEM((count, 2, rows // 2, D), BF16),
            VMEM((n, 3 * HD, BLK), F32),
            VMEM((hpd, n, HD, BLK), BF16),
            VMEM((lay.half_blocks, HD, BLK), BF16),
            VMEM((n, hpd, HD, BLK), BF16),
        ] + [VMEM(*item) for item in kept + made] + [
            VMEM(*plain), VMEM(*wide), VMEM(*wide), VMEM(*plain), VMEM(*wide), VMEM(*plain), VMEM(*wide),
            VMEM(*turned),
            VMEM((1, lay.tile), F32), VMEM((1, lay.tile), F32), VMEM((HD, lay.tile), F32),
            dma((4, n, 2)), dma((n, 2)), dma((peers,)), dma((peers,)), dma((peers,)), dma((peers,)),
            dma((2,)), moves, moves, moves, moves,
            dma((2,)), dma((count, 2)), dma((hpd, n)), dma((hpd, n)), dma((hpd,)),
            dma((len(kept) + 6 + 3 * nf,)), dma((3,)), dma((3, nf)), dma((3, nf)), dma((3,)), dma((3,)),
            dma((3,)),
        ],
        compiler_params=pltpu.CompilerParams(
            collective_id=0, has_side_effects=True, vmem_limit_bytes=61 * MIB
        ),
        cost_estimate=cost(100),
        name="forward",
    )(deal, inverse, lengths, x, cot, *vectors, *mats)


VEC_ROWS = 24


def backward_kernel(
    lay, n, nf,
    deal_ref, inv_ref, len_ref, gt, c_ref, g1_ref, dg2_ref,
    own_t, own_r, twin_t, twin_r, cot_in,
    qraw_in, qst_in, kt_in, vt_in, kn_in, ot_in, lse_in,
    a_ref, mats_ref, mine_ref, other_ref, x_in, dh_in,
    gx_out, dw_out, fw_out, vec_out, xw_out, tw_out,
    big, sums, wide, abuf, qraw, qst, kt, vt, kn, ot, lse, x_ref, dh_ref,
    qn, vn, don, dost, delta, dk, dv, dqt, natural, part_sums, left, back, dw, dwsend, dwrecv, dwown, vx, vsum, vall,
    ld_sem, do_send, do_recv, do_own, dq_send, dq_recv, dq_own, xw_send, xw_recv, tg_send, tg_recv, a_sem,
    x_send, x_recv, own_sem, ag_send, ag_recv, fg_send, fg_recv, v_send, v_recv, u_send, u_recv,
    *rest,
):
    p = Place(n, nf)
    c, f, zlen, hpd, tile = p.c, p.f, p.zlen, lay.hpd, lay.tile
    dob, reduce_scratch = rest[:hpd], rest[hpd:]
    rows = D // nf
    part = rows // 2
    loads = Loads(ld_sem)
    flat = 3 * part
    deep = 4 * BLK

    def left_rows(m, source):
        return pl.ds(al(3 * deep + m * nf * part + source * part, 16), part)

    def right_rows(m):
        return pl.ds(m * deep, deep)

    ffn_loads = []
    for m in range(3):
        at = pl.ds(3 * deep + m * nf * part, nf * part)
        ffn_loads += [
            loads.start(own_t.at[m], big.at[at, pl.ds(0, 2 * BLK)]),
            loads.start(twin_t.at[m], big.at[at, pl.ds(2 * BLK, 2 * BLK)]),
            loads.start(own_r.at[m] if m < 2 else cot_in, big.at[pl.ds(m * deep, 2 * BLK)]),
            loads.start(twin_r.at[m], big.at[pl.ds(m * deep + 2 * BLK, 2 * BLK)]),
        ]
    att_loads = [
        loads.start(src, dst) for src, dst in zip(
            (qraw_in, qst_in, kt_in, vt_in, kn_in, ot_in, lse_in), (qraw, qst, kt, vt, kn, ot, lse))
    ]
    row_loads = [loads.start(x_in, x_ref), loads.start(dh_in, dh_ref)]
    p.greet_all(True)

    do_swaps = [
        Swap(p, lambda d, u=u: gt.at[d, u], lambda d, u=u: dob[u].at[d],
             do_send.at[u], do_recv.at[u], do_own.at[u])
        for u in range(hpd)
    ]
    for swap in do_swaps:
        swap.start()

    def xw_copy(s, peer):
        return pltpu.make_async_remote_copy(
            src_ref=mine_ref, dst_ref=xw_out.at[s], send_sem=xw_send.at[s], recv_sem=xw_recv.at[s],
            device_id=(c, peer), device_id_type=MESH,
        )

    def tg_copy(s):
        return pltpu.make_async_remote_copy(
            src_ref=xw_out.at[s], dst_ref=tw_out.at[s], send_sem=tg_send.at[s], recv_sem=tg_recv.at[s],
            device_id=(p.twin, f), device_id_type=MESH,
        )

    height = sums.shape[1]
    if height > flat:
        for source in range(nf):
            sums[source, flat:, :] = jnp.zeros((height - flat, D), BF16)
    for copy in ffn_loads:
        copy.wait()
    reduce = Reduce(p, sums, *reduce_scratch[:6], reduce_scratch[6:])

    def weight_grads(source):
        for m in range(3):
            @pl.loop(0, D // WIDE)
            def _(j):
                sl = pl.ds(al(j * WIDE, WIDE), WIDE)
                sums[source, pl.ds(m * part, part), sl] = dot(
                    big[left_rows(m, source), 0:deep], big[right_rows(m), sl]).astype(BF16)

    for peer in p.fpeers:
        weight_grads(peer)
    reduce.start_x(0)
    reduce.start_x(1)

    w_loads = []


    def load_w(src, source, half):
        at = pl.ds(al(2 * D + source * rows + half * part, 16), part)
        w_loads.append(loads.start(src, big.at[at]))

    def own_weight_grads():
        weight_grads(f)
        for m in range(2):
            w_loads.append(loads.start(mats_ref.at[3 + m], big.at[pl.ds(m * D, D)]))
        load_w(mine_ref, f, p.core)
        load_w(other_ref, f, 1 - p.core)

    for copy in att_loads:
        copy.wait()
    ends = read_ends(len_ref)
    part_sums[...] = jnp.zeros_like(part_sums)
    step = 8
    steps = [(u, q) for u in range(hpd) for q in range(n // step)]

    def a_copy(k):
        u, q = steps[k]
        half = lay.half(u)
        return pltpu.make_async_copy(
            a_ref.at[pl.ds(q * step, step), half], abuf.at[k % 2].reshape(step, BLK, D), a_sem.at[k % 2])

    def weights_of_head(k):
        u, q = steps[k]
        a_copy(k).wait()
        if k + 1 < len(steps):
            a_copy(k + 1).start()
        @pl.loop(0, D // WIDE)
        def _(j):
            sl = pl.ds(al(j * WIDE, WIDE), WIDE)
            term = dot(left[u, :, q * step * BLK : (q + 1) * step * BLK], abuf[k % 2, :, sl])
            dw[:, sl] = term if k == 0 else dw[:, sl] + term

    def gradient_swap(u):
        return Swap(
            p, lambda d: left.at[u, :, pl.ds(al(d * BLK, BLK), BLK)], lambda d: back.at[u, d],
            dq_send.at[u], dq_recv.at[u], dq_own.at[u])

    a_copy(0).start()
    for u in range(hpd):
        base = lay.base(u)
        row0 = u * lay.size

        @pl.loop(0, lay.half_blocks)
        def _(b):
            cols = pl.ds(al(b * BLK, BLK), BLK)
            here = pl.ds(al(row0 + b * BLK, BLK), BLK)
            qn[cols, :] = qst[:, here].astype(F32).T.astype(BF16)
            vn[cols, :] = pad_rows(vt[:, here].astype(F32)).T.astype(BF16)
            dk[cols, :] = jnp.zeros((BLK, BLK), F32)
            dv[cols, :] = jnp.zeros((BLK, BLK), F32)

        do_swaps[u].wait()

        @pl.loop(0, lay.half_blocks)
        def _(b):
            cols = pl.ds(al(b * BLK, BLK), BLK)
            here = pl.ds(al(row0 + b * BLK, BLK), BLK)
            block = dob[u][inv_ref[b + lay.half(u) * lay.half_blocks]].astype(F32)
            delta[:, cols] = jnp.sum(block * ot[:, here], axis=0, keepdims=True)
            block = pad_rows(block)
            dost[:, cols] = block.astype(BF16)
            don[cols, :] = block.T.astype(BF16)

        @pl.loop(0, lay.size // tile)
        def _(qi):
            cols = pl.ds(al(qi * tile, tile), tile)
            here = pl.ds(al(row0 + qi * tile, tile), tile)
            t_row = qi * tile + lax.broadcasted_iota(jnp.int32, (1, tile), 1)
            start = seq_start(ends, base, t_row)
            dqt[:, cols] = jnp.zeros((HD, tile), F32)

            @pl.loop(0, qi + 1)
            def _(j):
                keys = pl.ds(al(j * tile, tile), tile)
                keys_here = pl.ds(al(row0 + j * tile, tile), tile)
                s = dot(kn[keys_here, :], qst[:, here])
                token = j * tile + lax.broadcasted_iota(jnp.int32, (tile, 1), 0)
                seen = (token >= start) & (token <= t_row)
                prob = jnp.exp(jnp.where(seen, s - lse[:, here], NEG))
                dp = dot(vn[keys, :], dost[:, cols])
                ds = (prob * (dp - delta[:, cols])).astype(BF16)
                dv[keys, :] += dot(prob.astype(BF16), don[cols, :])
                dk[keys, :] += dot(ds, qn[cols, :])
                dqt[:, cols] += dot(kt[:, keys_here], ds)

            if u == hpd - 1:
                @pl.when(qi == lay.size // tile // 2 - 1)
                def _():
                    if hpd == 2:
                        reduce.xy(1)
                        reduce.after_y(0)

        @pl.loop(0, lay.half_blocks)
        def _(b):
            cols = pl.ds(al(b * BLK, BLK), BLK)
            here = pl.ds(al(row0 + b * BLK, BLK), BLK)
            dqs = dqt[:, cols]
            dq = (dqs * c_ref[...]).astype(BF16)
            dkt = dk[cols, :].T[:HD].astype(BF16)
            dvt = dv[cols, :].T[:HD].astype(BF16)
            natural[b, 0:HD] = dq
            natural[b, HD : 2 * HD] = dkt
            natural[b, 2 * HD : 3 * HD] = dvt
            part_sums[0, :HD] += dqs * qraw[:, here]
            part_sums[1, :HD] += dq.astype(F32)
            part_sums[2, :HD] += dvt.astype(F32)

        @pl.loop(0, n)
        def _(d):
            left[u, :, pl.ds(al(d * BLK, BLK), BLK)] = natural[lay.within(deal_ref, d, u)]

        if u == 0:
            own_weight_grads()
        if u < hpd - 1:
            reduce.xy(0)
            reduce.start_x(2)
        gradient_swap(u).start()
        if u < hpd - 1:
            for k, (unit, _) in enumerate(steps):
                if unit == u:
                    weights_of_head(k)
    if hpd == 1:
        reduce.xy(0)
        reduce.xy(1)
        reduce.start_x(2)
        reduce.after_y(0)

    for k, (unit, _) in enumerate(steps):
        if unit == hpd - 1:
            weights_of_head(k)
    for source in range(nf):
        dwsend[source] = dw[:, source * rows : (source + 1) * rows].astype(BF16)

    def x_copy(s, peer):
        return pltpu.make_async_remote_copy(
            src_ref=dwsend.at[peer], dst_ref=dwrecv.at[s],
            send_sem=x_send.at[s], recv_sem=x_recv.at[s],
            device_id=(c, peer), device_id_type=MESH,
        )

    for s, peer in enumerate(p.fpeers):
        x_copy(s, peer).start()
    for t in range(3, zlen):
        reduce.start_x(t)
    for s, peer in enumerate(p.fpeers):
        xw_copy(s, peer).start()

    pieces = fw_out.shape[1]
    result = reduce_scratch[0]
    cut = height // zlen // pieces
    spread = Spread(p, dw_out, ag_send, ag_recv, 3, lambda i: dwown.at[i], own_sem.at[0])
    spread2 = Spread(
        p, fw_out, fg_send, fg_recv, pieces, lambda i: result.at[pl.ds(i * cut, cut)], own_sem.at[1])

    def start_spread():
        total = dwsend[f].astype(F32)
        for s, peer in enumerate(p.fpeers):
            x_copy(s, peer).wait_recv()
            total = total + dwrecv[s].astype(F32)
        for i in range(3):
            dwown[i] = total[i * HD : (i + 1) * HD].astype(BF16)
            spread.start(i)

    def spread_events(k):
        if 1 <= k < zlen:
            for i in range(3):
                spread.chain(k, i)
                spread.pair(k - 1, i)

    def gather_rows():
        for u in range(hpd):
            gradient_swap(u).wait()
        for m in range(3):
            for i in range(2):
                for h in range(H):
                    block = back[i, h] if hpd == 2 else back[0, 2 * h + i]
                    wide[m, pl.ds(h * HD, HD), pl.ds(i * BLK, BLK)] = block[m * HD : (m + 1) * HD]
        for copy in w_loads[:2]:
            copy.wait()

    def row_grads(mats, more):
        @pl.loop(0, D // WIDE)
        def _(j):
            at = pl.ds(al(j * WIDE, WIDE), WIDE)
            total = None
            for m in mats:
                term = dot(big[pl.ds(al(m * D + j * WIDE, WIDE), WIDE), :], wide[m])
                total = term if total is None else total + term
            total = total.T
            gx_out[:, at] = gx_out[:, at] + total if more else total

    for t in range(2, zlen):
        reduce.after_y(t - 1)
        reduce.xy(t)
        if t == 2:
            start_spread()
        else:
            spread_events(t - 2)
    gather_rows()
    row_grads((0, 1), False)
    reduce.after_y(zlen - 1)
    for k in range(zlen - 2, zlen):
        spread_events(k)
    reduce.last()
    for i in range(pieces):
        spread2.start(i)
    for i in range(3):
        spread.pair(zlen - 1, i)

    for s, (peer, source) in enumerate(zip(p.fpeers, p.fsources)):
        xw_copy(s, peer).wait_recv()
        tg_copy(s).start()
        load_w(xw_out.at[s], source, p.core)
    for copy in row_loads:
        copy.wait()
    for s, source in enumerate(p.fsources):
        tg_copy(s).wait_recv()
        load_w(tw_out.at[s], source, 1 - p.core)
    for copy in w_loads[2:]:
        copy.wait()
    row_grads((2,), True)
    for i in range(pieces):
        spread2.chain(1, i)
        spread2.pair(0, i)
    x = x_ref[...].astype(F32)
    r1 = lax.rsqrt(jnp.mean(x * x, axis=-1, keepdims=True) + EPS)
    na = x * r1
    da = gx_out[...]
    dg1 = jnp.sum(da * na, axis=0, keepdims=True)
    for r in range(D // BLK):
        vx[f, r : r + 1, :] = dg1[:, r * BLK : (r + 1) * BLK]
        vx[f, D // BLK + r : D // BLK + r + 1, :] = dg2_ref[:, r * BLK : (r + 1) * BLK]
    for r in range(3):
        vx[f, 20 + r : 21 + r, :] = jnp.sum(part_sums[r].T, axis=0, keepdims=True)
    vx[f, 23:24, :] = jnp.zeros((1, BLK), F32)

    def v_copy(s, peer, source):
        return pltpu.make_async_remote_copy(
            src_ref=vx.at[f], dst_ref=vx.at[source],
            send_sem=v_send.at[s], recv_sem=v_recv.at[s],
            device_id=(c, peer), device_id_type=MESH,
        )

    for s, peer in enumerate(p.fpeers):
        v_copy(s, peer, f).start()
    scaled = da * g1_ref[0:1, :]
    mean = jnp.mean(scaled * na, axis=-1, keepdims=True)
    gx_out[...] = dh_ref[...] + r1 * (scaled - na * mean)
    for s, (peer, source) in enumerate(zip(p.fpeers, p.fsources)):
        v_copy(s, peer, source).wait_recv()
    vsum[...] = jnp.sum(vx[...], axis=0)
    vall[c] = vsum[...]

    def u_copy(s, block):
        return pltpu.make_async_remote_copy(
            src_ref=vsum, dst_ref=vall.at[block],
            send_sem=u_send.at[s], recv_sem=u_recv.at[s],
            device_id=(c ^ s, f), device_id_type=MESH,
        )

    for s in range(1, n):
        u_copy(s, c).start()
    for k in range(2, zlen):
        for i in range(pieces):
            spread2.chain(k, i)
            spread2.pair(k - 1, i)
    for i in range(pieces):
        spread2.pair(zlen - 1, i)
    for k in range(zlen):
        for zz, guard, _ in p.level(k):
            when(guard, lambda zz=zz: spread.from_twin(zz))
            when(guard, lambda zz=zz: spread2.from_twin(zz))
    for s in range(1, n):
        u_copy(s, c ^ s).wait_recv()
    vec_out[...] = vall[...]

    for u in range(hpd):
        do_swaps[u].drain()
        gradient_swap(u).drain()
    spread.drain()
    spread2.drain()
    reduce.drain()
    for s, peer in enumerate(p.fpeers):
        xw_copy(s, peer).wait_send()
        tg_copy(s).wait_send()
        x_copy(s, peer).wait_send()
        v_copy(s, peer, f).wait_send()
    for s in range(1, n):
        u_copy(s, c).wait_send()


def backward(lay, nf, deal, inverse, lengths, gt, factor, g1, dg2, ffn_parts, cot, kept, tokens, mats, mine, other, x, dh):
    n, hpd, rows, size = lay.n, lay.hpd, lay.rows, lay.size
    dma = pltpu.SemaphoreType.DMA
    shard = D // nf
    part = shard // 2
    zlen = n // 4
    height = -(-3 * part // (16 * zlen)) * 16 * zlen
    piece = height // zlen
    pieces = 3 if piece % 48 == 0 else 1
    peers = max(nf - 1, 1)
    tok = x.shape[0]
    return pl.pallas_call(
        functools.partial(backward_kernel, lay, n, nf),
        out_shape=(
            jax.ShapeDtypeStruct((tok, D), F32),
            jax.ShapeDtypeStruct((n, 3, HD, shard), BF16),
            jax.ShapeDtypeStruct((n, pieces, piece // pieces, D // 2), BF16),
            jax.ShapeDtypeStruct((n, VEC_ROWS, BLK), F32),
            jax.ShapeDtypeStruct((peers, part, D), BF16),
            jax.ShapeDtypeStruct((peers, part, D), BF16),
        ),
        in_specs=[in_smem()] * 3 + [in_vmem()] * 4 + [in_any()] * 18,
        out_specs=(in_vmem(), in_any(), in_any(), in_vmem(), in_any(), in_any()),
        scratch_shapes=[
            VMEM((3 * D, D), BF16), VMEM((nf, height, D), BF16), VMEM((3, D, tok), BF16),
            VMEM((2, 8 * BLK, D), BF16),
            VMEM((HD, rows), F32), VMEM((BLK, rows), BF16), VMEM((HD, rows), BF16), VMEM((HD, rows), BF16),
            VMEM((rows, BLK), BF16), VMEM((HD, rows), F32), VMEM((1, rows), F32),
            VMEM((tok, D), BF16), VMEM((tok, D), F32),
            VMEM((size, BLK), BF16), VMEM((size, BLK), BF16), VMEM((size, BLK), BF16), VMEM((BLK, size), BF16),
            VMEM((1, size), F32), VMEM((size, BLK), F32), VMEM((size, BLK), F32), VMEM((HD, size), F32),
            VMEM((size // BLK, 3 * HD, BLK), BF16), VMEM((3, BLK, BLK), F32), VMEM((hpd, 3 * HD, n * BLK), BF16),
            VMEM((hpd, n, 3 * HD, BLK), BF16), VMEM((3 * HD, D), F32), VMEM((nf, 3 * HD, shard), BF16),
            VMEM((peers, 3 * HD, shard), BF16), VMEM((3, HD, shard), BF16),
            VMEM((nf, VEC_ROWS, BLK), F32), VMEM((VEC_ROWS, BLK), F32), VMEM((n, VEC_ROWS, BLK), F32),
            dma((25 + 2 * nf,)), dma((hpd, n)), dma((hpd, n)), dma((hpd,)), dma((hpd, n)), dma((hpd, n)), dma((hpd,)),
            dma((peers,)), dma((peers,)), dma((peers,)), dma((peers,)), dma((2,)),
            dma((peers,)), dma((peers,)), dma((2, 3)), dma((4, n, 3)), dma((n, 3)), dma((4, n, pieces)), dma((n, pieces)),
            dma((peers,)), dma((peers,)), dma((n,)), dma((n,)),
        ] + [VMEM((n, HD, BLK), BF16)] * hpd + Reduce.scratch(nf, zlen, height),
        compiler_params=pltpu.CompilerParams(
            collective_id=2, has_side_effects=True, vmem_limit_bytes=62 * MIB
        ),
        cost_estimate=cost(130),
        name="backward",
    )(deal, inverse, lengths, gt, factor, g1, dg2, *ffn_parts, cot, *kept, tokens, mats, mine, other, x, dh)


def results_kernel(
    n, nf, hpd,
    dw_in, pieces_in, vec_ref, scale_ref,
    q_out, k_out, v_out, o_out, u_out, d_out, ga_out, bq_out, bv_out, gf_out, sc_out,
    dw, pieces, wide, full, tail, ld_sem, st_sem,
):
    f = lax.axis_index("fsdp")
    rows = dw.shape[3]
    part = rows // 2
    zlen, height = pieces.shape[0], pieces.shape[3]
    loads = Loads(ld_sem)
    piece_load = loads.start(pieces_in, pieces)
    dw_load = loads.start(dw_in, dw)
    stores = Loads(st_sem)

    piece_load.wait()
    for m, out in enumerate((o_out, u_out, d_out)):
        for core in range(2):
            for y in range(2):
                for z in range(zlen):
                    first, last = max(m * part, z * height), min((m + 1) * part, (z + 1) * height)
                    if first < last:
                        at = core * part + first - m * part
                        full[m, at : at + last - first, y * (D // 2) : (y + 1) * (D // 2)] = pieces[
                            z, y, core, first - z * height : last - z * height, :
                        ].astype(F32)
        stores.start(full.at[m], out)

    dw_load.wait()
    for m, out in enumerate((q_out, k_out, v_out)):
        for h in range(H):
            if hpd == 2:
                block = dw[h, m].astype(F32)
            else:
                block = dw[2 * h, m].astype(F32) + dw[2 * h + 1, m].astype(F32)
            wide[pl.ds(h * HD, HD), :] = block
        for j in range(D // WIDE):
            full[3 + m, :, j * WIDE : (j + 1) * WIDE] = wide[j * WIDE : (j + 1) * WIDE, :].T
        stores.start(full.at[3 + m], out)

    tail[...] = jnp.zeros_like(tail)
    total = jnp.sum(vec_ref[...], axis=0)
    for r in range(D // BLK):
        tail[0:1, r * BLK : (r + 1) * BLK] = total[r : r + 1]
        tail[1:2, r * BLK : (r + 1) * BLK] = total[D // BLK + r : D // BLK + r + 1]
    for r in (21, 22):
        for h in range(H):
            if hpd == 2:
                row = vec_ref[h, r : r + 1, 0:HD]
            else:
                row = vec_ref[2 * h, r : r + 1, 0:HD] + vec_ref[2 * h + 1, r : r + 1, 0:HD]
            tail[r - 19 : r - 18, h * HD : (h + 1) * HD] = row
    scale = scale_ref[4:5, 0:BLK]
    tail[4:5, 0:BLK] = total[20:21] * (1.0 / (1.0 + jnp.exp(-scale))) * (LOG2E / math.sqrt(HD))
    share = HD // nf
    for source in range(nf):
        @pl.when(f == source)
        def _():
            for r, out in enumerate((ga_out, gf_out, bq_out, bv_out)):
                for k in range(out.shape[0]):
                    at = source * rows + k * BLK
                    out[k : k + 1, :] = tail[r : r + 1, at : at + BLK]
            sc_out[...] = tail[4:5, source * share : source * share + BLK]
    stores.wait()


def results(n, nf, hpd, dw, pieces, vectors, scale):
    rows = dw.shape[3]
    zlen = n // 4
    height = pieces.shape[1] * pieces.shape[2]
    pieces = pieces.reshape(zlen, 2, 2, height, D // 2)
    dma = pltpu.SemaphoreType.DMA
    mat, row = jax.ShapeDtypeStruct((rows, D), F32), jax.ShapeDtypeStruct((-(-rows // BLK), BLK), F32)
    return pl.pallas_call(
        functools.partial(results_kernel, n, nf, hpd),
        out_shape=(mat,) * 6 + (row,) * 4 + (jax.ShapeDtypeStruct((1, BLK), F32),),
        in_specs=[in_any(), in_any(), in_vmem(), in_vmem()],
        out_specs=(in_any(),) * 6 + (in_vmem(),) * 5,
        scratch_shapes=[
            VMEM(dw.shape, BF16), VMEM(pieces.shape, BF16), VMEM((D, rows), F32), VMEM((6, rows, D), F32),
            VMEM((8, D + 2 * BLK), F32), dma((2,)), dma((6,)),
        ],
        compiler_params=pltpu.CompilerParams(vmem_limit_bytes=60 * MIB),
        cost_estimate=cost(11),
        name="results",
    )(dw, pieces, vectors, scale)


def local(
    n, nf, tokens, cotangent, lengths, deal, gain_attn, query_weight, query_bias, key_weight,
    value_weight, value_bias, query_scale, proj_weight, gain_ffn, up_weight, down_weight,
):
    lay = Layout(n, deal.shape[0])
    rows = query_weight.shape[0]
    x, cot = tokens[0], cotangent[0]

    def in_rows(v):
        return jnp.pad(v, (0, -v.shape[0] % BLK)).reshape(-1, BLK)

    vectors = tuple(in_rows(v) for v in (gain_attn, query_bias, value_bias, gain_ffn, query_scale))
    blocks = jnp.arange(deal.shape[0], dtype=jnp.int32)
    inverse = jnp.sum(jnp.where(deal[None, :] == blocks[:, None], blocks[None, :] // 2, 0), axis=1, dtype=jnp.int32)

    a_all, mats, mine, other, twin_t, twin_r, whole, factor_col, dg2, *stored = forward(
        lay, nf, deal, inverse, lengths, x, cot, vectors,
        (proj_weight, up_weight, down_weight, query_weight, key_weight, value_weight),
    )
    kept, (layer_out, dh, gt, own_t, own_r) = stored[:7], stored[7:]
    grad_x, dw, pieces, sums, *_ = backward(
        lay, nf, deal, inverse, lengths, gt.reshape(n, lay.hpd, HD, BLK), factor_col, whole, dg2,
        (own_t, own_r, twin_t, twin_r), cot, kept, a_all, mats, mine, other, x, dh,
    )
    dwq, dwk, dwv, dwo, dw1, dw2, ga, bq, bv, gf, scale = results(
        n, nf, lay.hpd, dw, pieces, sums, whole)
    ga, bq, bv, gf = (v.reshape(-1)[:rows] for v in (ga, bq, bv, gf))
    scale = scale.reshape(-1)[: query_scale.shape[0]]
    return layer_out[None], grad_x[None], ga, dwq, bq, dwk, dwv, bv, scale, dwo, gf, dw1, dw2


def solution(mesh):
    whole, vector, matrix = P("fsdp", "ctx", None), P("fsdp"), P("fsdp", None)
    return jax.shard_map(
        functools.partial(local, mesh.shape["ctx"], mesh.shape["fsdp"]),
        mesh=mesh,
        in_specs=(
            whole, whole, matrix, P(), vector, matrix, vector, matrix, matrix, vector, vector,
            matrix, vector, matrix, matrix,
        ),
        out_specs=(
            whole, whole, vector, matrix, vector, matrix, matrix, vector, vector, matrix, vector,
            matrix, matrix,
        ),
        check_vma=False,
    )
```

```python
import functools
import math

import jax
import jax.numpy as jnp
from jax import lax
from jax.experimental import pallas as pl
from jax.experimental.pallas import tpu as pltpu
from jax.sharding import PartitionSpec as P

H = 16
HD = 80
BLK = 128
D = 1280
EPS = 1e-06
LOG2E = 1.442695041
NEG = -1e30
MESH = pl.DeviceIdType.MESH
F32 = jnp.float32
BF16 = jnp.bfloat16
VMEM = pltpu.VMEM
MIB = 1 << 20

NN = (((1,), (0,)), ((), ()))
NT = (((1,), (1,)), ((), ()))
TN = (((0,), (0,)), ((), ()))


def dot(left, right, dims=NN):
    return lax.dot_general(left, right, dims, preferred_element_type=F32)


def al(value, multiple):
    return pl.multiple_of(value, multiple)


def in_vmem():
    return pl.BlockSpec(memory_space=pltpu.VMEM)


def in_smem():
    return pl.BlockSpec(memory_space=pltpu.SMEM)


def in_any():
    return pl.BlockSpec(memory_space=pl.ANY)


def cost(microseconds):
    return pl.CostEstimate(flops=0, bytes_accessed=int(microseconds * 3.0e6), transcendentals=0)


class Place:
    def __init__(self, n, nf):
        self.n, self.nf = n, nf
        self.c = lax.axis_index("ctx")
        self.f = lax.axis_index("fsdp")
        self.zlen = n // 4
        self.z, self.y, self.core = self.c // 4, (self.c // 2) % 2, self.c % 2
        self.twin = self.idx(self.z, self.y, 1 - self.core)
        self.ypeer = self.idx(self.z, 1 - self.y, self.core)
        self.targets = (
            self.idx(self.z + 1, self.y, self.core), self.idx(self.z - 1, self.y, self.core),
            self.ypeer, self.twin,
        )
        self.guards = (self.z < self.zlen - 1, self.z > 0, None, None)
        self.fpeers = [(self.f + s) % nf for s in range(1, nf)]
        self.fsources = [(self.f + nf - s) % nf for s in range(1, nf)]

    def idx(self, z, y, core):
        return (z * 2 + y) * 2 + core

    def level(self, k):
        if k == 0:
            return [(self.z, None, 0)]
        return [
            (self.z + k, self.z + k < self.zlen, 1),
            (self.z - k, self.z - k >= 0, -1),
        ]

    def greet_neighbours(self):
        barrier = pltpu.get_barrier_semaphore()
        for target, guard in zip(self.targets, self.guards):
            when(guard, lambda target=target: pl.semaphore_signal(
                barrier, inc=1, device_id=(target, self.f), device_id_type=MESH))
        for peer in self.fpeers:
            pl.semaphore_signal(barrier, inc=1, device_id=(self.c, peer), device_id_type=MESH)
        ends = jnp.minimum(self.z, 1) + jnp.minimum(self.zlen - 1 - self.z, 1)
        pl.semaphore_wait(barrier, 1 + self.nf + ends)

    def greet_all(self, with_fsdp):
        barrier = pltpu.get_barrier_semaphore()
        for s in range(1, self.n):
            pl.semaphore_signal(
                barrier, inc=1, device_id=(self.c ^ s, self.f), device_id_type=MESH)
        if with_fsdp:
            for peer in self.fpeers:
                pl.semaphore_signal(barrier, inc=1, device_id=(self.c, peer), device_id_type=MESH)
        pl.semaphore_wait(barrier, self.n - 1 + (self.nf - 1 if with_fsdp else 0))


def when(guard, body):
    if guard is None:
        body()
    else:
        pl.when(guard)(body)


class Spread:
    def __init__(self, place, buf, send_sem, recv_sem, pieces, wide=(), own=None, own_sem=None):
        self.wide = wide
        self.p, self.buf, self.send_sem, self.recv_sem, self.pieces = place, buf, send_sem, recv_sem, pieces
        self.own, self.own_sem = own, own_sem

    def copy(self, way, origin, i, src=None):
        where = self.buf.at[origin, i]
        return pltpu.make_async_remote_copy(
            src_ref=where if src is None else src, dst_ref=where,
            send_sem=self.send_sem.at[way, origin, i], recv_sem=self.recv_sem.at[origin, i],
            device_id=(self.p.targets[way], self.p.f), device_id_type=MESH,
        )

    def send(self, way, origin, i):
        when(self.p.guards[way], lambda: self.copy(way, origin, i).start())

    def arrive(self, origin, i):
        self.copy(3, origin, i).wait_recv()

    def keep(self, i):
        return pltpu.make_async_copy(self.own(i), self.buf.at[self.p.c, i], self.own_sem.at[i])

    def start(self, i):
        src = self.own(i) if self.own else None
        for way in range(4):
            when(self.p.guards[way], lambda way=way: self.copy(way, self.p.c, i, src).start())
        if self.own:
            self.keep(i).start()

    def chain(self, k, i):
        p = self.p
        for zz, guard, sign in p.level(k):
            def body(zz=zz, sign=sign):
                origin = p.idx(zz, p.y, p.core)
                self.arrive(origin, i)
                self.send(1 if sign == 1 else 0, origin, i)
                when(self.crosses(zz, i), lambda: self.send(2, origin, i))
                self.send(3, origin, i)
            when(guard, body)

    def crosses(self, zz, i):
        return (zz > 0) & (zz < self.p.zlen - 1) if i in self.wide else None

    def both_chains(self, zz, sign, i, act):
        if i in self.wide:
            p, origin = self.p, self.p.idx(zz, 1 - self.p.y, self.p.core)
            for way, end, signs in ((0, 0, (0, -1)), (1, p.zlen - 1, (0, 1))):
                if sign in signs:
                    pl.when((zz == end) & p.guards[way])(lambda way=way: act(way, origin, i))

    def pair(self, k, i):
        p = self.p
        for zz, guard, sign in p.level(k):
            def body(zz=zz, sign=sign):
                origin = p.idx(zz, 1 - p.y, p.core)
                self.arrive(origin, i)
                self.both_chains(zz, sign, i, lambda way, o, i: self.copy(way, o, i).start())
                self.send(3, origin, i)
            when(guard, body)

    def from_twin(self, zz, pieces=None):
        p = self.p
        for yy in (p.y, 1 - p.y):
            for i in range(self.pieces) if pieces is None else pieces:
                self.arrive(p.idx(zz, yy, 1 - p.core), i)

    def drain(self):
        p = self.p
        for i in range(self.pieces):
            if self.own:
                self.keep(i).wait()
            for way in range(4):
                when(p.guards[way], lambda way=way, i=i: self.copy(way, p.c, i).wait_send())
            for k in range(p.zlen):
                for zz, guard, sign in p.level(k):
                    def body(zz=zz, sign=sign, k=k, i=i):
                        if k:
                            origin = p.idx(zz, p.y, p.core)
                            on = 1 if sign == 1 else 0
                            when(p.guards[on], lambda: self.copy(on, origin, i).wait_send())
                            when(self.crosses(zz, i), lambda: self.copy(2, origin, i).wait_send())
                            self.copy(3, origin, i).wait_send()
                        self.both_chains(zz, sign, i, lambda way, o, i: self.copy(way, o, i).wait_send())
                        self.copy(3, p.idx(zz, 1 - p.y, p.core), i).wait_send()
                    when(guard, body)


class Reduce:
    def __init__(self, place, mine, result, acc, xrecv, yrecv, zsend, zrecv, sems):
        self.p, self.mine, self.result, self.acc = place, mine, result, acc
        self.xrecv, self.yrecv, self.zsend, self.zrecv = xrecv, yrecv, zsend, zrecv
        (self.xs, self.xr, self.ys, self.yr, self.zs, self.zr) = sems
        self.height = acc.shape[0] // place.zlen
        self.width = D // 2
        zlen = place.zlen
        ends = []
        for k in range(zlen // 2):
            ends += [zlen - 1 - k, k]
        self.order = ends

    @staticmethod
    def scratch(nf, zlen, height):
        dma = pltpu.SemaphoreType.DMA
        peers = max(nf - 1, 1)
        piece = VMEM((zlen, height // zlen, D // 2), BF16)
        return [
            VMEM((height // zlen, D // 2), BF16), VMEM((height, D), BF16), VMEM((peers, height, D), BF16),
            piece, piece, piece,
            dma((peers, zlen, 2)), dma((peers, zlen, 2)), dma((zlen,)), dma((zlen,)),
            dma((zlen,)), dma((zlen,)),
        ]

    def at(self, piece, side):
        return (
            pl.ds(al(piece * self.height, 16), self.height),
            pl.ds(al(side * self.width, 128), self.width),
        )

    def remote(self, src, dst, send, recv, c, f):
        return pltpu.make_async_remote_copy(
            src_ref=src, dst_ref=dst, send_sem=send, recv_sem=recv,
            device_id=(c, f), device_id_type=MESH,
        )

    def x_copy(self, s, peer, piece, turn):
        side = (self.p.y + 1 + turn) % 2
        where = self.at(piece, side)
        return self.remote(
            self.mine.at[peer].at[where], self.xrecv.at[s].at[where],
            self.xs.at[s, piece, turn], self.xr.at[s, piece, turn], self.p.c, peer,
        )

    def start_x(self, t):
        for turn in range(2):
            for s, peer in enumerate(self.p.fpeers):
                self.x_copy(s, peer, self.order[t], turn).start()

    def add(self, dst, terms, count=None):
        count = count or self.height
        step = 48 if count % 48 == 0 else 16
        @pl.loop(0, count // step)
        def _(t):
            at = pl.ds(al(t * step, 16), step)
            total = terms[0][at, :].astype(F32)
            for term in terms[1:]:
                total = total + term[at, :].astype(F32)
            dst[at, :] = total.astype(BF16)

    def sum_x(self, piece, turn):
        side = (self.p.y + 1 + turn) % 2
        where = self.at(piece, side)
        terms = [self.mine.at[self.p.f].at[where]]
        for s, peer in enumerate(self.p.fpeers):
            self.x_copy(s, peer, piece, turn).wait_recv()
            terms.append(self.xrecv.at[s].at[where])
        self.add(self.acc.at[where], terms)

    def y_copy(self, piece):
        src = self.acc.at[self.at(piece, 1 - self.p.y)]
        return self.remote(
            src, self.yrecv.at[piece], self.ys.at[piece], self.yr.at[piece], self.p.ypeer, self.p.f)

    def z_copy(self, piece, slot):
        p = self.p
        return self.remote(
            self.zsend.at[piece], self.zrecv.at[slot], self.zs.at[piece], self.zr.at[slot],
            p.idx(piece, p.y, p.core), p.f)

    def xy(self, t):
        piece = self.order[t]
        self.sum_x(piece, 0)
        self.y_copy(piece).start()
        self.sum_x(piece, 1)

    def after_y(self, t):
        p, piece = self.p, self.order[t]
        self.y_copy(piece).wait_recv()
        self.add(self.zsend.at[piece], [self.acc.at[self.at(piece, p.y)], self.yrecv.at[piece]])
        pl.when(p.z != piece)(lambda: self.z_copy(piece, p.z).start())

    def last(self):
        p = self.p
        terms = [self.zsend.at[p.z]]
        for k in range(1, p.zlen):
            other = lax.rem(p.z + k, p.zlen)
            self.z_copy(0, other).wait_recv()
            terms.append(self.zrecv.at[other])
        self.add(self.result, terms)

    def drain(self):
        p = self.p
        for piece in self.order:
            for turn in range(2):
                for s, peer in enumerate(p.fpeers):
                    self.x_copy(s, peer, piece, turn).wait_send()
            self.y_copy(piece).wait_send()
            pl.when(p.z != piece)(lambda piece=piece: self.z_copy(piece, p.z).wait_send())


class Loads:
    def __init__(self, sems):
        self.sems, self.copies = sems, []

    def start(self, src, dst):
        copy = pltpu.make_async_copy(src, dst, self.sems.at[len(self.copies)])
        self.copies.append(copy)
        copy.start()
        return copy

    def wait(self):
        for copy in self.copies:
            copy.wait()


class Swap:
    def __init__(self, place, src, dst, send_sem, recv_sem, own_sem):
        self.p, self.src, self.dst = place, src, dst
        self.send_sem, self.recv_sem, self.own_sem = send_sem, recv_sem, own_sem

    def copy(self, s, block):
        p = self.p
        return pltpu.make_async_remote_copy(
            src_ref=self.src(p.c ^ s), dst_ref=self.dst(block),
            send_sem=self.send_sem.at[s], recv_sem=self.recv_sem.at[s],
            device_id=(p.c ^ s, p.f), device_id_type=MESH,
        )

    def own(self):
        return pltpu.make_async_copy(self.src(self.p.c), self.dst(self.p.c), self.own_sem)

    def start(self):
        for s in range(1, self.p.n):
            self.copy(s, self.p.c).start()
        self.own().start()

    def wait(self):
        self.own().wait()
        for s in range(1, self.p.n):
            self.copy(s, self.p.c ^ s).wait_recv()

    def drain(self):
        for s in range(1, self.p.n):
            self.copy(s, self.p.c).wait_send()


def seq_start(ends, base, token):
    start = jnp.zeros_like(token)
    for e in ends:
        start = jnp.where(e - base <= token, jnp.maximum(start, e - base), start)
    return start


def read_ends(lengths_ref):
    ends, total = [], jnp.int32(0)
    for i in range(lengths_ref.shape[1]):
        total = total + lengths_ref[0, i]
        ends.append(total)
    return ends


def pad_rows(block):
    return jnp.concatenate([block, jnp.zeros((BLK - HD, block.shape[1]), block.dtype)], axis=0)


class Layout:
    def __init__(self, n, total_blocks):
        self.n = n
        self.hpd = 2 * H // n
        self.half_blocks = total_blocks // 2
        self.size = self.half_blocks * BLK
        self.rows = self.hpd * self.size
        self.tile = 512

    def half(self, i):
        return i if self.hpd == 2 else lax.axis_index("ctx") % 2

    def within(self, deal_ref, d, u):
        return deal_ref[2 * d + self.half(u)] & (self.half_blocks - 1)

    def base(self, unit):
        return self.half(unit) * self.size if self.hpd == 1 else unit * self.size


WIDE = 256


def over_columns(body):
    @pl.loop(0, D // WIDE)
    def _(j):
        body(pl.ds(al(j * WIDE, WIDE), WIDE))


def token_rows(
    x_ref, cot_ref, oswap, rows_ref, weights, w_loads,
    out_ref, dh_ref, gt_ref, ot, bt, zt, gb, du, dg2_ref,
    o_rows, hidden, nh, b, up, z, db, wide, stage,
):
    wo, w1, w2 = weights
    hpd = oswap.shape[1]
    for i in range(2):
        for h in range(H):
            ot[pl.ds(h * HD, HD), pl.ds(i * BLK, BLK)] = oswap[h, i] if hpd == 2 else oswap[2 * h + i, 0]
    @pl.loop(0, D // WIDE)
    def _(j):
        sl = pl.ds(al(j * WIDE, WIDE), WIDE)
        o_rows[:, sl] = ot[sl, :].astype(F32).T.astype(BF16)
    stage("ot")

    def body(sl):
        hidden[:, sl] = x_ref[:, sl].astype(F32) + dot(o_rows[...], wo[:, sl])
    over_columns(body)
    hid = hidden[...]
    r2 = lax.rsqrt(jnp.mean(hid * hid, axis=-1, keepdims=True) + EPS)
    nh[...] = hid * r2
    b[...] = (nh[...] * rows_ref[3:4, :]).astype(BF16)
    w_loads[1].wait()

    def body(sl):
        u = dot(b[...], w1[:, sl])
        up[:, sl] = u
        act = u * jax.nn.sigmoid(u)
        z[:, sl] = act.astype(BF16)
        zt[sl, :] = act.T.astype(BF16)
        bt[sl, :] = b[:, sl].astype(F32).T.astype(BF16)
    over_columns(body)
    stage("z")
    stage("b")

    w_loads[2].wait()

    def body(sl):
        out_ref[:, sl] = (hidden[:, sl] + dot(z[...], w2[:, sl])).astype(BF16)
        dz = dot(cot_ref[...], w2[sl, :], NT)
        u = up[:, sl]
        sig = jax.nn.sigmoid(u)
        du[:, sl] = (dz * sig * (1.0 + u * (1.0 - sig))).astype(BF16)
    over_columns(body)
    stage("out")
    stage("du")

    def body(sl):
        g = dot(du[...], w1[sl, :], NT)
        db[:, sl] = g * rows_ref[3:4, sl]
        dg2_ref[:, sl] = jnp.sum(g * nh[:, sl], axis=0, keepdims=True)
    over_columns(body)
    scaled = db[...]
    mean = jnp.mean(scaled * nh[...], axis=-1, keepdims=True)
    dh = cot_ref[...].astype(F32) + r2 * (scaled - nh[...] * mean)
    dh_ref[...] = dh
    gb[...] = dh.astype(BF16)
    stage("gb")

    @pl.loop(0, D // WIDE)
    def _(j):
        sl = pl.ds(al(j * WIDE, WIDE), WIDE)
        wide[sl, :] = dot(wo[sl, :], gb[...], NT).astype(BF16)
    for i in range(2):
        for h in range(H):
            gt_ref[h, i] = wide[pl.ds(h * HD, HD), pl.ds(i * BLK, BLK)]
    stage("gt")


def forward_kernel(
    lay, n, nf,
    deal_ref, inv_ref, len_ref, x_ref, cot_ref, *rest,
):
    row_refs, mat_refs, rest = rest[:5], rest[5:11], rest[11:]
    (a_out, mats_out, mine_out, other_out, twin_t, twin_r, rows_out, factor_out, dg2_out, *stored) = rest[: 9 + 12]
    (abuf, norm, windows, wh_ref, whbuf, wht, vec_ref, vecbuf, vcol, stage, wcast, qkv, osend, onat, oswap,
     qraw, qst, kt, vt, kn, ot, lse, layer, dh, gt, ot_t, bt, zt, gb, du,
     o_rows, hidden, nh, b_rows, up, z, db, wide, m_ref, l_ref, acc_ref,
     ag_send, ag_recv, wh_send, wh_recv, vec_send, vec_recv,
     ld_sem, mx_send, mx_recv, ms_send, ms_recv, a_sem, keep_sem, o_send, o_recv, o_own,
     st_sem, w_sem, tt_send, tt_recv, tr_send, tr_recv, win_sem) = rest[9 + 12 :]
    kept = (qraw, qst, kt, vt, kn, ot, lse)
    stores = Loads(st_sem)
    p = Place(n, nf)
    c, f, core, zlen, hpd, tile = p.c, p.f, p.core, p.zlen, lay.hpd, lay.tile
    rows = wh_ref.shape[0]
    part = rows // 2

    head = c * hpd // 2
    first = jnp.minimum(head * HD // BLK * BLK, D - 2 * BLK)
    window_loads = [
        pltpu.make_async_copy(
            mat_refs[3 + m].at[:, pl.ds(al(first, BLK), 2 * BLK)], windows.at[m], win_sem.at[m])
        for m in range(3)
    ]
    for copy in window_loads:
        copy.start()
    vec_ref[...] = jnp.zeros_like(vec_ref)
    vec_ref[4:5, 0 : row_refs[4].shape[0]] = row_refs[4][...].reshape(1, -1)
    for r, ref in enumerate(row_refs[:4]):
        for k in range(ref.shape[0]):
            vec_ref[r : r + 1, k * BLK : (k + 1) * BLK] = ref[k : k + 1, :]
    p.greet_all(True)
    spread = Spread(p, abuf, ag_send, ag_recv, 2)

    for i in range(2):
        abuf[c, i] = x_ref[pl.ds(i * BLK, BLK), :]
    spread.start(0)

    def wh_copy(s, peer):
        return pltpu.make_async_remote_copy(
            src_ref=wh_ref, dst_ref=whbuf.at[pl.ds(al(f * rows, 16), rows)],
            send_sem=wh_send.at[s], recv_sem=wh_recv.at[s],
            device_id=(c, peer), device_id_type=MESH,
        )

    def vec_copy(s, peer):
        return pltpu.make_async_remote_copy(
            src_ref=vec_ref, dst_ref=vecbuf.at[f],
            send_sem=vec_send.at[s], recv_sem=vec_recv.at[s],
            device_id=(c, peer), device_id_type=MESH,
        )

    for s, peer in enumerate(p.fpeers):
        vec_copy(s, peer).start()
    for copy in window_loads:
        copy.wait()
    strip = 128 if rows % 128 == 0 else 32

    @pl.loop(0, rows // strip)
    def _(t):
        at = pl.ds(al(t * strip, 32), strip)
        lane = lax.broadcasted_iota(jnp.int32, (strip, 2 * BLK), 1)
        value = jnp.zeros((strip, 2 * BLK), F32)
        for m in range(3):
            turned = pltpu.roll(windows[m, at, :], lax.rem(m * HD + 2 * BLK - (head * HD - first), 2 * BLK), 1)
            value = jnp.where((lane >= m * HD) & (lane < (m + 1) * HD), turned, value)
        wh_ref[at, :] = value.astype(BF16)

    for s, peer in enumerate(p.fpeers):
        wh_copy(s, peer).start()
    whbuf[pl.ds(al(f * rows, 16), rows), :] = wh_ref[...]
    vecbuf[f] = vec_ref[...]

    shards = mat_refs
    moved = len(mat_refs) - 1
    steps = [(m, 0) for m in range(moved)] + [(m, 1) for m in range(moved)] + [(moved, 0), (moved, 1)]

    def half_of(h):
        return (core + h) % 2

    def load(step):
        m, h = steps[step]
        return pltpu.make_async_copy(
            shards[m].at[pl.ds(al(half_of(h) * part, 16), part)],
            stage.at[step % 2], ld_sem.at[step % 2],
        )

    def mx_copy(m, s, peer, source):
        return pltpu.make_async_remote_copy(
            src_ref=wcast.at[m, core],
            dst_ref=mats_out.at[m, pl.ds(al(source * rows + core * part, 16), part)],
            send_sem=mx_send.at[m, s], recv_sem=mx_recv.at[m, s],
            device_id=(c, peer), device_id_type=MESH,
        )

    def keep_copies(m):
        if m < moved:
            return [
                pltpu.make_async_copy(
                    wcast.at[m, h], mats_out.at[m, pl.ds(al(f * rows + h * part, 16), part)],
                    keep_sem.at[m, h],
                ) for h in range(2)
            ]
        return [
            pltpu.make_async_copy(wcast.at[m, half_of(h)], out, keep_sem.at[m, h])
            for h, out in enumerate((mine_out, other_out))
        ]

    def cast(step):
        m, h = steps[step]
        if step + 1 < len(steps):
            load(step + 1).start()
        load(step).wait()
        chunk = part // 4 if part % 64 == 0 else part
        @pl.loop(0, part // chunk)
        def _(t):
            wcast[m, half_of(h), pl.ds(al(t * chunk, 16), chunk), :] = stage[
                step % 2, pl.ds(al(t * chunk, 16), chunk), :
            ].astype(BF16)
        if h == 0 and m < moved:
            for s, peer in enumerate(p.fpeers):
                mx_copy(m, s, peer, f).start()
        if h == 1:
            for copy in keep_copies(m):
                copy.start()

    load(0).start()
    done = [0]

    def casts(count):
        for step in range(done[0], min(done[0] + count, len(steps))):
            cast(step)
        done[0] += count

    casts(2)

    def gather_events(i, first, last):
        for k in range(first, last):
            if k < zlen:
                spread.chain(k, i)
            spread.pair(k - 1, i)

    def ms_copy(m, s, source, half):
        where = mats_out.at[m, pl.ds(al(source * rows + half * part, 16), part)]
        return pltpu.make_async_remote_copy(
            src_ref=where, dst_ref=where,
            send_sem=ms_send.at[m, s], recv_sem=ms_recv.at[m, s],
            device_id=(p.twin, f), device_id_type=MESH,
        )

    def pass_matrix(m):
        for s, (peer, source) in enumerate(zip(p.fpeers, p.fsources)):
            mx_copy(m, s, peer, source).wait_recv()
            ms_copy(m, s, source, core).start()

    def t_copy(m, source):
        mat = (ot_t, bt, zt)[m]
        return pltpu.make_async_remote_copy(
            src_ref=mat.at[pl.ds(al(source * rows + (1 - core) * part, 16), part)],
            dst_ref=twin_t.at[m, pl.ds(source * part, part)],
            send_sem=tt_send.at[m, source], recv_sem=tt_recv.at[m, source],
            device_id=(p.twin, f), device_id_type=MESH,
        )

    def r_copy(m):
        return pltpu.make_async_remote_copy(
            src_ref=(gb, du, cot_ref)[m], dst_ref=twin_r.at[m], send_sem=tr_send.at[m], recv_sem=tr_recv.at[m],
            device_id=(p.twin, f), device_id_type=MESH,
        )

    own_t, own_r = stored[10], stored[11]

    def to_twin(m, src):
        for source in range(nf):
            t_copy(m, source).start()
            stores.start(
                src.at[pl.ds(al(source * rows + core * part, 16), part)], own_t.at[m, pl.ds(source * part, part)])

    r_copy(2).start()
    gather_events(0, 1, 2)
    casts(1)

    for s, peer in enumerate(p.fpeers):
        vec_copy(s, peer).wait_recv()
        wh_copy(s, peer).wait_recv()
    wht[...] = whbuf[...].astype(F32).T.astype(BF16)
    for source in range(nf):
        rows_out[:, pl.ds(source * rows, rows)] = vecbuf[source, :, 0:rows].astype(BF16).astype(F32)
    share = HD // nf
    shares = [vecbuf[source, 4:5, 0:share].astype(BF16).astype(F32) for source in range(nf)]
    for source in range(nf):
        rows_out[4:5, source * share : (source + 1) * share] = shares[source]
    vcol[...] = rows_out[...].T
    here = pl.ds(al(head * HD, 16), HD)
    bias_q, bias_v = vcol[here, 1:2], vcol[here, 2:3]
    factor = jnp.log(1.0 + jnp.exp(vcol[0:HD, 4:5])) * (LOG2E / math.sqrt(HD))
    factor_out[...] = jnp.broadcast_to(factor, (HD, BLK))

    def a_copy(slot, origin, half):
        return pltpu.make_async_copy(norm.at[slot], a_out.at[pl.ds(origin, 2), half], a_sem.at[slot])

    def project(u, k, first=False):
        half = lay.half(u)
        for zz, guard, _ in p.level(k):
            def body(zz=zz):
                spread.from_twin(zz, [u] if hpd == 2 else range(2))
                for t in range(2):
                    origin = zz * 4 + 2 * t
                    if not first:
                        a_copy(t, origin, half).wait()
                    for i in range(2):
                        x = abuf[origin + i, half].astype(F32)
                        scale = lax.rsqrt(jnp.mean(x * x, axis=-1, keepdims=True) + EPS)
                        norm[t, i] = (x * scale * rows_out[0:1, :]).astype(BF16)
                    a_copy(t, origin, half).start()
                    value = dot(wht[: 3 * HD, :], norm[t].reshape(2 * BLK, D), NT)
                    qkv[origin] = value[:, :BLK]
                    qkv[origin + 1] = value[:, BLK:]
            when(guard, body)

    ends = read_ends(len_ref)

    def attend(u, during):
        base, row0 = lay.base(u), u * lay.size

        @pl.loop(0, lay.half_blocks)
        def _(b):
            cols = pl.ds(al(row0 + b * BLK, BLK), BLK)
            block = qkv[inv_ref[b + lay.half(u) * lay.half_blocks]]
            qr, kr, vr = block[:HD] + bias_q, block[HD : 2 * HD], block[2 * HD :] + bias_v
            qraw[:, cols] = qr
            qst[:, cols] = pad_rows(qr * factor).astype(BF16)
            kt[:, cols] = kr.astype(BF16)
            vt[:, cols] = vr.astype(BF16)
            kn[cols, :] = pad_rows(kr.astype(BF16)).T

        @pl.loop(0, lay.size // tile)
        def _(qi):
            cols = pl.ds(al(row0 + qi * tile, tile), tile)
            t_row = qi * tile + lax.broadcasted_iota(jnp.int32, (1, tile), 1)
            start = seq_start(ends, base, t_row)
            m_ref[...] = jnp.full_like(m_ref, NEG)
            l_ref[...] = jnp.zeros_like(l_ref)
            acc_ref[...] = jnp.zeros_like(acc_ref)

            def visit(key0, count, ahead, causal):
                keys = pl.ds(al(row0 + key0, count), count)
                side = slice(ahead, tile)
                s = dot(kn[keys, :], qst[:, pl.ds(al(row0 + qi * tile + ahead, BLK), tile - ahead)])
                token = key0 + lax.broadcasted_iota(jnp.int32, (count, 1), 0)
                seen = token >= start[:, side]
                if causal:
                    seen = seen & (token <= t_row[:, side])
                s = jnp.where(seen, s, NEG)
                m_old = m_ref[:, side]
                m_new = jnp.maximum(m_old, jnp.max(s, axis=0, keepdims=True))
                prob = jnp.exp(s - m_new)
                shrink = jnp.exp(m_old - m_new)
                m_ref[:, side] = m_new
                l_ref[:, side] = l_ref[:, side] * shrink + jnp.sum(prob, axis=0, keepdims=True)
                acc_ref[:, side] = acc_ref[:, side] * shrink + dot(vt[:, keys], prob.astype(BF16))

            @pl.loop(0, qi)
            def _(j):
                visit(j * tile, tile, 0, False)

            visit(qi * tile, tile // 2, 0, True)
            visit(qi * tile + tile // 2, tile // 2, tile // 2, True)

            out = acc_ref[...] / l_ref[...]
            ot[:, cols] = out
            lse[:, cols] = m_ref[...] + jnp.log(l_ref[...])
            for b in range(tile // BLK):
                onat[qi * (tile // BLK) + b] = out[:, b * BLK : (b + 1) * BLK].astype(BF16)
            for at, event in during:
                pl.when(qi == at)(event)

        @pl.loop(0, n)
        def _(d):
            osend[u, d] = onat[lay.within(deal_ref, d, u)]

        o_swaps[u].start()

    o_swaps = [
        Swap(p, lambda d, u=u: osend.at[u, d], lambda d, u=u: oswap.at[d, u],
             o_send.at[u], o_recv.at[u], o_own.at[u])
        for u in range(hpd)
    ]

    def handed(m):
        for s, (peer, source) in enumerate(zip(p.fpeers, p.fsources)):
            ms_copy(m, s, source, 1 - core).wait_recv()
        for copy in keep_copies(m):
            copy.wait()

    weights = [abuf.at[pl.ds(5 * m, 5)].reshape(5 * 2 * BLK, D) for m in range(3)]
    w_loads = [
        pltpu.make_async_copy(mats_out.at[m], weights[m], w_sem.at[m]) for m in range(3)
    ]

    if hpd == 2:
        project(0, 0, first=True)
        for k in range(2, zlen + 1):
            gather_events(0, k, k + 1)
            if k == 2:
                spread.start(1)
            casts(2)
            project(0, k - 1)
        pass_matrix(0)
        gather_events(1, 1, 2)
        attend(0, [(lay.size // tile // 2, lambda: gather_events(1, 2, 3))])
        pass_matrix(1)
        casts(len(steps))
        project(1, 0)
        for k in range(3, zlen + 1):
            gather_events(1, k, k + 1)
            project(1, k - 2)
        project(1, zlen - 1)
    else:
        spread.start(1)
        casts(len(steps))
        for k in range(1, zlen + 1):
            if k > 1:
                gather_events(0, k, k + 1)
            gather_events(1, k, k + 1)
            project(0, k - 1, first=k == 1)
        pass_matrix(0)
        pass_matrix(1)
    spread.drain()
    for m in range(2):
        handed(m)
        w_loads[m].start()
    attend(hpd - 1, [])
    for src, dst in zip(kept, stored):
        stores.start(src, dst)
    pass_matrix(2)
    handed(2)
    w_loads[2].start()
    for u in range(hpd):
        o_swaps[u].wait()
    w_loads[0].wait()

    def stage(name):
        if name == "ot":
            to_twin(0, ot_t)
        elif name == "z":
            to_twin(2, zt)
        elif name == "b":
            to_twin(1, bt)
        elif name == "out":
            stores.start(layer, stored[7])
        elif name == "du":
            r_copy(1).start()
            stores.start(du, own_r.at[1])
        elif name == "gb":
            r_copy(0).start()
            stores.start(gb, own_r.at[0])
            stores.start(dh, stored[8])
        elif name == "gt":
            stores.start(gt, stored[9])

    token_rows(
        x_ref, cot_ref, oswap, rows_out, weights, w_loads,
        layer, dh, gt, ot_t, bt, zt, gb, du, dg2_out, o_rows, hidden, nh, b_rows, up, z, db, wide, stage)

    for m in range(3, moved):
        pass_matrix(m)
    for m in range(3, moved):
        handed(m)
    for copy in keep_copies(moved):
        copy.wait()
    for m in range(moved):
        for s, (peer, source) in enumerate(zip(p.fpeers, p.fsources)):
            mx_copy(m, s, peer, f).wait_send()
            ms_copy(m, s, source, core).wait_send()
    for m in range(3):
        r_copy(m).wait()
        for source in range(nf):
            t_copy(m, source).wait()
    for s, peer in enumerate(p.fpeers):
        wh_copy(s, peer).wait_send()
        vec_copy(s, peer).wait_send()
    for u in range(hpd):
        o_swaps[u].drain()
    for slot in range(2):
        a_copy(slot, 2 * slot, lay.half(0)).wait()
    stores.wait()


def forward(lay, nf, deal, inverse, lengths, x, cot, vectors, mats):
    n, hpd, total = lay.n, lay.hpd, lay.rows
    rows, tok, count = mats[0].shape[0], x.shape[0], len(mats)
    dma = pltpu.SemaphoreType.DMA
    peers = max(nf - 1, 1)
    half = ((rows // 2, D), BF16)
    kept = [
        ((HD, total), F32), ((BLK, total), BF16), ((HD, total), BF16), ((HD, total), BF16), ((total, BLK), BF16),
        ((HD, total), F32), ((1, total), F32),
    ]
    plain, turned, wide = ((tok, D), BF16), ((D, tok), BF16), ((tok, D), F32)
    made = [plain, wide, ((H, 2, HD, BLK), BF16), turned, turned, turned, plain, plain]
    shared = ((3, D // 2, tok), BF16)
    results = made[:3] + [shared, ((2, tok, D), BF16)]
    outs = [
        ((n, 2, BLK, D), BF16), ((count - 1, nf * rows, D), BF16), half, half, shared, ((3, tok, D), BF16),
        ((8, D), F32), ((HD, BLK), F32), ((1, D), F32),
    ] + kept + results
    places = [in_any()] * 6 + [in_vmem()] * 3 + [in_any()] * (len(kept) + len(results))
    moves = dma((count - 1, peers))
    return pl.pallas_call(
        functools.partial(forward_kernel, lay, n, nf),
        out_shape=tuple(jax.ShapeDtypeStruct(*out) for out in outs),
        in_specs=[in_smem()] * 3 + [in_vmem()] * (2 + len(vectors)) + [in_any()] * count,
        out_specs=tuple(places),
        scratch_shapes=[
            VMEM((n, 2, BLK, D), BF16),
            VMEM((2, 2, BLK, D), BF16),
            VMEM((3, rows, 2 * BLK), F32),
            VMEM((rows, 2 * BLK), BF16),
            VMEM((nf * rows, 2 * BLK), BF16),
            VMEM((2 * BLK, nf * rows), BF16),
            VMEM((8, -(-rows // BLK) * BLK), F32),
            VMEM((nf, 8, -(-rows // BLK) * BLK), F32),
            VMEM((D, 8), F32),
            VMEM((2, rows // 2, D), F32),
            VMEM((count, 2, rows // 2, D), BF16),
            VMEM((n, 3 * HD, BLK), F32),
            VMEM((hpd, n, HD, BLK), BF16),
            VMEM((lay.half_blocks, HD, BLK), BF16),
            VMEM((n, hpd, HD, BLK), BF16),
        ] + [VMEM(*item) for item in kept + made] + [
            VMEM(*plain), VMEM(*wide), VMEM(*wide), VMEM(*plain), VMEM(*wide), VMEM(*plain), VMEM(*wide),
            VMEM(*turned),
            VMEM((1, lay.tile), F32), VMEM((1, lay.tile), F32), VMEM((HD, lay.tile), F32),
            dma((4, n, 2)), dma((n, 2)), dma((peers,)), dma((peers,)), dma((peers,)), dma((peers,)),
            dma((2,)), moves, moves, moves, moves,
            dma((2,)), dma((count, 2)), dma((hpd, n)), dma((hpd, n)), dma((hpd,)),
            dma((len(kept) + 6 + 3 * nf,)), dma((3,)), dma((3, nf)), dma((3, nf)), dma((3,)), dma((3,)),
            dma((3,)),
        ],
        compiler_params=pltpu.CompilerParams(
            collective_id=0, has_side_effects=True, vmem_limit_bytes=61 * MIB
        ),
        cost_estimate=cost(100),
        name="forward",
    )(deal, inverse, lengths, x, cot, *vectors, *mats)


VEC_ROWS = 24


def backward_kernel(
    lay, n, nf,
    deal_ref, inv_ref, len_ref, gt, c_ref, g1_ref, dg2_ref,
    own_t, own_r, twin_t, twin_r, cot_in,
    qraw_in, qst_in, kt_in, vt_in, kn_in, ot_in, lse_in,
    a_ref, mats_ref, mine_ref, other_ref, x_in, dh_in,
    gx_out, dw_out, fw_out, vec_out, xw_out, tw_out,
    big, sums, wide, abuf, qraw, qst, kt, vt, kn, ot, lse, x_ref, dh_ref,
    qn, vn, don, dost, delta, dk, dv, dqt, natural, part_sums, left, back, dw, dwsend, dwrecv, dwown, vx, vsum, vall,
    ld_sem, do_send, do_recv, do_own, dq_send, dq_recv, dq_own, xw_send, xw_recv, tg_send, tg_recv, a_sem,
    x_send, x_recv, own_sem, ag_send, ag_recv, fg_send, fg_recv, v_send, v_recv, u_send, u_recv,
    *rest,
):
    p = Place(n, nf)
    c, f, zlen, hpd, tile = p.c, p.f, p.zlen, lay.hpd, lay.tile
    dob, reduce_scratch = rest[:hpd], rest[hpd:]
    rows = D // nf
    part = rows // 2
    loads = Loads(ld_sem)
    flat = 3 * part
    deep = 4 * BLK

    def left_rows(m, source):
        return pl.ds(al(3 * deep + m * nf * part + source * part, 16), part)

    def right_rows(m):
        return pl.ds(m * deep, deep)

    ffn_loads = []
    for m in range(3):
        at = pl.ds(3 * deep + m * nf * part, nf * part)
        ffn_loads += [
            loads.start(own_t.at[m], big.at[at, pl.ds(0, 2 * BLK)]),
            loads.start(twin_t.at[m], big.at[at, pl.ds(2 * BLK, 2 * BLK)]),
            loads.start(own_r.at[m] if m < 2 else cot_in, big.at[pl.ds(m * deep, 2 * BLK)]),
            loads.start(twin_r.at[m], big.at[pl.ds(m * deep + 2 * BLK, 2 * BLK)]),
        ]
    att_loads = [
        loads.start(src, dst) for src, dst in zip(
            (qraw_in, qst_in, kt_in, vt_in, kn_in, ot_in, lse_in), (qraw, qst, kt, vt, kn, ot, lse))
    ]
    row_loads = [loads.start(x_in, x_ref), loads.start(dh_in, dh_ref)]
    p.greet_all(True)

    do_swaps = [
        Swap(p, lambda d, u=u: gt.at[d, u], lambda d, u=u: dob[u].at[d],
             do_send.at[u], do_recv.at[u], do_own.at[u])
        for u in range(hpd)
    ]
    for swap in do_swaps:
        swap.start()

    def xw_copy(s, peer):
        return pltpu.make_async_remote_copy(
            src_ref=mine_ref, dst_ref=xw_out.at[s], send_sem=xw_send.at[s], recv_sem=xw_recv.at[s],
            device_id=(c, peer), device_id_type=MESH,
        )

    def tg_copy(s):
        return pltpu.make_async_remote_copy(
            src_ref=xw_out.at[s], dst_ref=tw_out.at[s], send_sem=tg_send.at[s], recv_sem=tg_recv.at[s],
            device_id=(p.twin, f), device_id_type=MESH,
        )

    height = sums.shape[1]
    if height > flat:
        for source in range(nf):
            sums[source, flat:, :] = jnp.zeros((height - flat, D), BF16)
    for copy in ffn_loads:
        copy.wait()
    reduce = Reduce(p, sums, *reduce_scratch[:6], reduce_scratch[6:])

    def weight_grads(source):
        for m in range(3):
            @pl.loop(0, D // WIDE)
            def _(j):
                sl = pl.ds(al(j * WIDE, WIDE), WIDE)
                sums[source, pl.ds(m * part, part), sl] = dot(
                    big[left_rows(m, source), 0:deep], big[right_rows(m), sl]).astype(BF16)

    for peer in p.fpeers:
        weight_grads(peer)
    reduce.start_x(0)
    reduce.start_x(1)

    w_loads = []


    def load_w(src, source, half):
        at = pl.ds(al(2 * D + source * rows + half * part, 16), part)
        w_loads.append(loads.start(src, big.at[at]))

    def own_weight_grads():
        weight_grads(f)
        for m in range(2):
            w_loads.append(loads.start(mats_ref.at[3 + m], big.at[pl.ds(m * D, D)]))
        load_w(mine_ref, f, p.core)
        load_w(other_ref, f, 1 - p.core)

    for copy in att_loads:
        copy.wait()
    ends = read_ends(len_ref)
    part_sums[...] = jnp.zeros_like(part_sums)
    step = 8
    steps = [(u, q) for u in range(hpd) for q in range(n // step)]

    def a_copy(k):
        u, q = steps[k]
        half = lay.half(u)
        return pltpu.make_async_copy(
            a_ref.at[pl.ds(q * step, step), half], abuf.at[k % 2].reshape(step, BLK, D), a_sem.at[k % 2])

    def weights_of_head(k):
        u, q = steps[k]
        a_copy(k).wait()
        if k + 1 < len(steps):
            a_copy(k + 1).start()
        @pl.loop(0, D // WIDE)
        def _(j):
            sl = pl.ds(al(j * WIDE, WIDE), WIDE)
            term = dot(left[u, :, q * step * BLK : (q + 1) * step * BLK], abuf[k % 2, :, sl])
            dw[:, sl] = term if k == 0 else dw[:, sl] + term

    def gradient_swap(u):
        return Swap(
            p, lambda d: left.at[u, :, pl.ds(al(d * BLK, BLK), BLK)], lambda d: back.at[u, d],
            dq_send.at[u], dq_recv.at[u], dq_own.at[u])

    a_copy(0).start()
    for u in range(hpd):
        base = lay.base(u)
        row0 = u * lay.size

        @pl.loop(0, lay.half_blocks)
        def _(b):
            cols = pl.ds(al(b * BLK, BLK), BLK)
            here = pl.ds(al(row0 + b * BLK, BLK), BLK)
            qn[cols, :] = qst[:, here].T
            vn[cols, :] = pad_rows(vt[:, here]).T
            dk[cols, :] = jnp.zeros((BLK, BLK), F32)
            dv[cols, :] = jnp.zeros((BLK, BLK), F32)

        do_swaps[u].wait()

        @pl.loop(0, lay.half_blocks)
        def _(b):
            cols = pl.ds(al(b * BLK, BLK), BLK)
            here = pl.ds(al(row0 + b * BLK, BLK), BLK)
            block = dob[u][inv_ref[b + lay.half(u) * lay.half_blocks]].astype(F32)
            delta[:, cols] = jnp.sum(block * ot[:, here], axis=0, keepdims=True)
            block = pad_rows(block.astype(BF16))
            dost[:, cols] = block
            don[cols, :] = block.T

        @pl.loop(0, lay.size // tile)
        def _(qi):
            t_row = qi * tile + lax.broadcasted_iota(jnp.int32, (1, tile), 1)
            start = seq_start(ends, base, t_row)
            dqt[:, pl.ds(al(qi * tile, tile), tile)] = jnp.zeros((HD, tile), F32)

            def visit(key0, count, ahead, causal):
                side = slice(ahead, tile)
                cols = pl.ds(al(qi * tile + ahead, BLK), tile - ahead)
                here = pl.ds(al(row0 + qi * tile + ahead, BLK), tile - ahead)
                keys = pl.ds(al(key0, count), count)
                keys_here = pl.ds(al(row0 + key0, count), count)
                s = dot(kn[keys_here, :], qst[:, here])
                token = key0 + lax.broadcasted_iota(jnp.int32, (count, 1), 0)
                seen = token >= start[:, side]
                if causal:
                    seen = seen & (token <= t_row[:, side])
                prob = jnp.exp(jnp.where(seen, s - lse[:, here], NEG))
                dp = dot(vn[keys, :], dost[:, cols])
                ds = (prob * (dp - delta[:, cols])).astype(BF16)
                dv[keys, :] += dot(prob.astype(BF16), don[cols, :])
                dk[keys, :] += dot(ds, qn[cols, :])
                dqt[:, cols] += dot(kt[:, keys_here], ds)

            @pl.loop(0, qi)
            def _(j):
                visit(j * tile, tile, 0, False)

            visit(qi * tile, tile // 2, 0, True)
            visit(qi * tile + tile // 2, tile // 2, tile // 2, True)

            if u == hpd - 1:
                @pl.when(qi == lay.size // tile // 2 - 1)
                def _():
                    if hpd == 2:
                        reduce.xy(1)
                        reduce.after_y(0)

        @pl.loop(0, lay.half_blocks)
        def _(b):
            cols = pl.ds(al(b * BLK, BLK), BLK)
            here = pl.ds(al(row0 + b * BLK, BLK), BLK)
            dqs = dqt[:, cols]
            dq = (dqs * c_ref[...]).astype(BF16)
            dkt = dk[cols, :].astype(BF16).T[:HD]
            dvt = dv[cols, :].astype(BF16).T[:HD]
            natural[b, 0:HD] = dq
            natural[b, HD : 2 * HD] = dkt
            natural[b, 2 * HD : 3 * HD] = dvt
            part_sums[0, :HD] += dqs * qraw[:, here]
            part_sums[1, :HD] += dq.astype(F32)
            part_sums[2, :HD] += dvt.astype(F32)

        @pl.loop(0, n)
        def _(d):
            left[u, :, pl.ds(al(d * BLK, BLK), BLK)] = natural[lay.within(deal_ref, d, u)]

        if u == 0:
            own_weight_grads()
        if u < hpd - 1:
            reduce.xy(0)
            reduce.start_x(2)
        gradient_swap(u).start()
    if hpd == 1:
        reduce.xy(0)
        reduce.xy(1)
        reduce.start_x(2)
        reduce.after_y(0)

    for k in range(len(steps)):
        weights_of_head(k)
    for source in range(nf):
        dwsend[source] = dw[:, source * rows : (source + 1) * rows].astype(BF16)

    def x_copy(s, peer):
        return pltpu.make_async_remote_copy(
            src_ref=dwsend.at[peer], dst_ref=dwrecv.at[s],
            send_sem=x_send.at[s], recv_sem=x_recv.at[s],
            device_id=(c, peer), device_id_type=MESH,
        )

    for s, peer in enumerate(p.fpeers):
        x_copy(s, peer).start()
    for t in range(3, zlen):
        reduce.start_x(t)
    for s, peer in enumerate(p.fpeers):
        xw_copy(s, peer).start()

    pieces = fw_out.shape[1]
    result = reduce_scratch[0]
    cut = height // zlen // pieces
    spread = Spread(p, dw_out, ag_send, ag_recv, 3, (), lambda i: dwown.at[i], own_sem.at[0])
    spread2 = Spread(
        p, fw_out, fg_send, fg_recv, pieces, (0, 2), lambda i: result.at[pl.ds(i * cut, cut)], own_sem.at[1])

    def start_spread():
        total = dwsend[f].astype(F32)
        for s, peer in enumerate(p.fpeers):
            x_copy(s, peer).wait_recv()
            total = total + dwrecv[s].astype(F32)
        for i in range(3):
            dwown[i] = total[i * HD : (i + 1) * HD].astype(BF16)
            spread.start(i)

    def spread_events(k):
        if 1 <= k < zlen:
            for i in range(3):
                spread.chain(k, i)
                spread.pair(k - 1, i)

    def gather_rows():
        for u in range(hpd):
            gradient_swap(u).wait()
        for m in range(3):
            for i in range(2):
                for h in range(H):
                    block = back[i, h] if hpd == 2 else back[0, 2 * h + i]
                    wide[m, pl.ds(h * HD, HD), pl.ds(i * BLK, BLK)] = block[m * HD : (m + 1) * HD]
        for copy in w_loads[:2]:
            copy.wait()

    def row_grads(mats, more):
        @pl.loop(0, D // WIDE)
        def _(j):
            at = pl.ds(al(j * WIDE, WIDE), WIDE)
            total = None
            for m in mats:
                term = dot(big[pl.ds(al(m * D + j * WIDE, WIDE), WIDE), :], wide[m])
                total = term if total is None else total + term
            total = total.T
            gx_out[:, at] = gx_out[:, at] + total if more else total

    for t in range(2, zlen):
        reduce.after_y(t - 1)
        reduce.xy(t)
        if t == 2:
            start_spread()
        else:
            spread_events(t - 2)
    gather_rows()
    row_grads((0, 1), False)
    reduce.after_y(zlen - 1)
    for k in range(zlen - 2, zlen):
        spread_events(k)
    reduce.last()
    for i in range(pieces):
        spread2.start(i)
    for i in range(3):
        spread.pair(zlen - 1, i)

    for s, (peer, source) in enumerate(zip(p.fpeers, p.fsources)):
        xw_copy(s, peer).wait_recv()
        tg_copy(s).start()
        load_w(xw_out.at[s], source, p.core)
    for copy in row_loads:
        copy.wait()
    for s, source in enumerate(p.fsources):
        tg_copy(s).wait_recv()
        load_w(tw_out.at[s], source, 1 - p.core)
    for copy in w_loads[2:]:
        copy.wait()
    row_grads((2,), True)
    for i in range(pieces):
        spread2.chain(1, i)
        spread2.pair(0, i)
    x = x_ref[...].astype(F32)
    r1 = lax.rsqrt(jnp.mean(x * x, axis=-1, keepdims=True) + EPS)
    na = x * r1
    da = gx_out[...]
    dg1 = jnp.sum(da * na, axis=0, keepdims=True)
    for r in range(D // BLK):
        vx[f, r : r + 1, :] = dg1[:, r * BLK : (r + 1) * BLK]
        vx[f, D // BLK + r : D // BLK + r + 1, :] = dg2_ref[:, r * BLK : (r + 1) * BLK]
    for r in range(3):
        vx[f, 20 + r : 21 + r, :] = jnp.sum(part_sums[r].T, axis=0, keepdims=True)
    vx[f, 23:24, :] = jnp.zeros((1, BLK), F32)

    def v_copy(s, peer, source):
        return pltpu.make_async_remote_copy(
            src_ref=vx.at[f], dst_ref=vx.at[source],
            send_sem=v_send.at[s], recv_sem=v_recv.at[s],
            device_id=(c, peer), device_id_type=MESH,
        )

    for s, peer in enumerate(p.fpeers):
        v_copy(s, peer, f).start()
    scaled = da * g1_ref[0:1, :]
    mean = jnp.mean(scaled * na, axis=-1, keepdims=True)
    gx_out[...] = dh_ref[...] + r1 * (scaled - na * mean)
    for s, (peer, source) in enumerate(zip(p.fpeers, p.fsources)):
        v_copy(s, peer, source).wait_recv()
    vsum[...] = jnp.sum(vx[...], axis=0)
    vall[c] = vsum[...]

    def u_copy(s, block):
        return pltpu.make_async_remote_copy(
            src_ref=vsum, dst_ref=vall.at[block],
            send_sem=u_send.at[s], recv_sem=u_recv.at[s],
            device_id=(c ^ s, f), device_id_type=MESH,
        )

    for s in range(1, n):
        u_copy(s, c).start()
    for k in range(2, zlen):
        for i in range(pieces):
            spread2.chain(k, i)
            spread2.pair(k - 1, i)
    for i in range(pieces):
        spread2.pair(zlen - 1, i)
    for k in range(zlen):
        for zz, guard, _ in p.level(k):
            when(guard, lambda zz=zz: spread.from_twin(zz))
            when(guard, lambda zz=zz: spread2.from_twin(zz))
    for s in range(1, n):
        u_copy(s, c ^ s).wait_recv()
    vec_out[...] = vall[...]

    for u in range(hpd):
        do_swaps[u].drain()
        gradient_swap(u).drain()
    spread.drain()
    spread2.drain()
    reduce.drain()
    for s, peer in enumerate(p.fpeers):
        xw_copy(s, peer).wait_send()
        tg_copy(s).wait_send()
        x_copy(s, peer).wait_send()
        v_copy(s, peer, f).wait_send()
    for s in range(1, n):
        u_copy(s, c).wait_send()


def backward(lay, nf, deal, inverse, lengths, gt, factor, g1, dg2, ffn_parts, cot, kept, tokens, mats, mine, other, x, dh):
    n, hpd, rows, size = lay.n, lay.hpd, lay.rows, lay.size
    dma = pltpu.SemaphoreType.DMA
    shard = D // nf
    part = shard // 2
    zlen = n // 4
    height = -(-3 * part // (16 * zlen)) * 16 * zlen
    piece = height // zlen
    pieces = 3 if piece % 48 == 0 else 1
    peers = max(nf - 1, 1)
    tok = x.shape[0]
    return pl.pallas_call(
        functools.partial(backward_kernel, lay, n, nf),
        out_shape=(
            jax.ShapeDtypeStruct((tok, D), F32),
            jax.ShapeDtypeStruct((n, 3, HD, shard), BF16),
            jax.ShapeDtypeStruct((n, pieces, piece // pieces, D // 2), BF16),
            jax.ShapeDtypeStruct((n, VEC_ROWS, BLK), F32),
            jax.ShapeDtypeStruct((peers, part, D), BF16),
            jax.ShapeDtypeStruct((peers, part, D), BF16),
        ),
        in_specs=[in_smem()] * 3 + [in_vmem()] * 4 + [in_any()] * 18,
        out_specs=(in_vmem(), in_any(), in_any(), in_vmem(), in_any(), in_any()),
        scratch_shapes=[
            VMEM((3 * D, D), BF16), VMEM((nf, height, D), BF16), VMEM((3, D, tok), BF16),
            VMEM((2, 8 * BLK, D), BF16),
            VMEM((HD, rows), F32), VMEM((BLK, rows), BF16), VMEM((HD, rows), BF16), VMEM((HD, rows), BF16),
            VMEM((rows, BLK), BF16), VMEM((HD, rows), F32), VMEM((1, rows), F32),
            VMEM((tok, D), BF16), VMEM((tok, D), F32),
            VMEM((size, BLK), BF16), VMEM((size, BLK), BF16), VMEM((size, BLK), BF16), VMEM((BLK, size), BF16),
            VMEM((1, size), F32), VMEM((size, BLK), F32), VMEM((size, BLK), F32), VMEM((HD, size), F32),
            VMEM((size // BLK, 3 * HD, BLK), BF16), VMEM((3, BLK, BLK), F32), VMEM((hpd, 3 * HD, n * BLK), BF16),
            VMEM((hpd, n, 3 * HD, BLK), BF16), VMEM((3 * HD, D), F32), VMEM((nf, 3 * HD, shard), BF16),
            VMEM((peers, 3 * HD, shard), BF16), VMEM((3, HD, shard), BF16),
            VMEM((nf, VEC_ROWS, BLK), F32), VMEM((VEC_ROWS, BLK), F32), VMEM((n, VEC_ROWS, BLK), F32),
            dma((25 + 2 * nf,)), dma((hpd, n)), dma((hpd, n)), dma((hpd,)), dma((hpd, n)), dma((hpd, n)), dma((hpd,)),
            dma((peers,)), dma((peers,)), dma((peers,)), dma((peers,)), dma((2,)),
            dma((peers,)), dma((peers,)), dma((2, 3)), dma((4, n, 3)), dma((n, 3)), dma((4, n, pieces)), dma((n, pieces)),
            dma((peers,)), dma((peers,)), dma((n,)), dma((n,)),
        ] + [VMEM((n, HD, BLK), BF16)] * hpd + Reduce.scratch(nf, zlen, height),
        compiler_params=pltpu.CompilerParams(
            collective_id=2, has_side_effects=True, vmem_limit_bytes=62 * MIB
        ),
        cost_estimate=cost(130),
        name="backward",
    )(deal, inverse, lengths, gt, factor, g1, dg2, *ffn_parts, cot, *kept, tokens, mats, mine, other, x, dh)


def results_kernel(
    n, nf, hpd,
    dw_in, pieces_in, vec_ref, scale_ref,
    q_out, k_out, v_out, o_out, u_out, d_out, ga_out, bq_out, bv_out, gf_out, sc_out,
    dw, pieces, wide, full, tail, ld_sem, st_sem,
):
    f = lax.axis_index("fsdp")
    rows = dw.shape[3]
    part = rows // 2
    zlen, height = pieces.shape[0], pieces.shape[3]
    loads = Loads(ld_sem)
    piece_load = loads.start(pieces_in, pieces)
    dw_load = loads.start(dw_in, dw)
    stores = Loads(st_sem)

    piece_load.wait()
    for m, out in enumerate((o_out, u_out, d_out)):
        for core in range(2):
            for y in range(2):
                for z in range(zlen):
                    first, last = max(m * part, z * height), min((m + 1) * part, (z + 1) * height)
                    if first < last:
                        at = core * part + first - m * part
                        full[m, at : at + last - first, y * (D // 2) : (y + 1) * (D // 2)] = pieces[
                            z, y, core, first - z * height : last - z * height, :
                        ].astype(F32)
        stores.start(full.at[m], out)

    dw_load.wait()
    for m, out in enumerate((q_out, k_out, v_out)):
        for h in range(H):
            if hpd == 2:
                block = dw[h, m].astype(F32)
            else:
                block = dw[2 * h, m].astype(F32) + dw[2 * h + 1, m].astype(F32)
            wide[pl.ds(h * HD, HD), :] = block
        for j in range(D // WIDE):
            full[3 + m, :, j * WIDE : (j + 1) * WIDE] = wide[j * WIDE : (j + 1) * WIDE, :].T
        stores.start(full.at[3 + m], out)

    tail[...] = jnp.zeros_like(tail)
    total = jnp.sum(vec_ref[...], axis=0)
    for r in range(D // BLK):
        tail[0:1, r * BLK : (r + 1) * BLK] = total[r : r + 1]
        tail[1:2, r * BLK : (r + 1) * BLK] = total[D // BLK + r : D // BLK + r + 1]
    for r in (21, 22):
        for h in range(H):
            if hpd == 2:
                row = vec_ref[h, r : r + 1, 0:HD]
            else:
                row = vec_ref[2 * h, r : r + 1, 0:HD] + vec_ref[2 * h + 1, r : r + 1, 0:HD]
            tail[r - 19 : r - 18, h * HD : (h + 1) * HD] = row
    scale = scale_ref[4:5, 0:BLK]
    tail[4:5, 0:BLK] = total[20:21] * (1.0 / (1.0 + jnp.exp(-scale))) * (LOG2E / math.sqrt(HD))
    share = HD // nf
    for source in range(nf):
        @pl.when(f == source)
        def _():
            for r, out in enumerate((ga_out, gf_out, bq_out, bv_out)):
                for k in range(out.shape[0]):
                    at = source * rows + k * BLK
                    out[k : k + 1, :] = tail[r : r + 1, at : at + BLK]
            sc_out[...] = tail[4:5, source * share : (source + 1) * share].reshape(share)
    stores.wait()


def results(n, nf, hpd, dw, pieces, vectors, scale):
    rows = dw.shape[3]
    zlen = n // 4
    height = pieces.shape[1] * pieces.shape[2]
    pieces = pieces.reshape(zlen, 2, 2, height, D // 2)
    dma = pltpu.SemaphoreType.DMA
    mat, row = jax.ShapeDtypeStruct((rows, D), F32), jax.ShapeDtypeStruct((-(-rows // BLK), BLK), F32)
    return pl.pallas_call(
        functools.partial(results_kernel, n, nf, hpd),
        out_shape=(mat,) * 6 + (row,) * 4 + (jax.ShapeDtypeStruct((HD // nf,), F32),),
        in_specs=[in_any(), in_any(), in_vmem(), in_vmem()],
        out_specs=(in_any(),) * 6 + (in_vmem(),) * 5,
        scratch_shapes=[
            VMEM(dw.shape, BF16), VMEM(pieces.shape, BF16), VMEM((D, rows), F32), VMEM((6, rows, D), F32),
            VMEM((8, D + 2 * BLK), F32), dma((2,)), dma((6,)),
        ],
        compiler_params=pltpu.CompilerParams(vmem_limit_bytes=60 * MIB),
        cost_estimate=cost(11),
        name="results",
    )(dw, pieces, vectors, scale)


def local(
    n, nf, tokens, cotangent, lengths, deal, gain_attn, query_weight, query_bias, key_weight,
    value_weight, value_bias, query_scale, proj_weight, gain_ffn, up_weight, down_weight,
):
    lay = Layout(n, deal.shape[0])
    rows = query_weight.shape[0]
    x, cot = tokens[0], cotangent[0]

    def in_rows(v):
        return jnp.pad(v, (0, -v.shape[0] % BLK)).reshape(-1, BLK)

    vectors = tuple(in_rows(v) for v in (gain_attn, query_bias, value_bias, gain_ffn)) + (query_scale,)
    blocks = jnp.arange(deal.shape[0], dtype=jnp.int32)
    inverse = jnp.sum(jnp.where(deal[None, :] == blocks[:, None], blocks[None, :] // 2, 0), axis=1, dtype=jnp.int32)

    a_all, mats, mine, other, twin_t, twin_r, whole, factor_col, dg2, *stored = forward(
        lay, nf, deal, inverse, lengths, x, cot, vectors,
        (proj_weight, up_weight, down_weight, query_weight, key_weight, value_weight),
    )
    kept, (layer_out, dh, gt, own_t, own_r) = stored[:7], stored[7:]
    grad_x, dw, pieces, sums, *_ = backward(
        lay, nf, deal, inverse, lengths, gt.reshape(n, lay.hpd, HD, BLK), factor_col, whole, dg2,
        (own_t, own_r, twin_t, twin_r), cot, kept, a_all, mats, mine, other, x, dh,
    )
    dwq, dwk, dwv, dwo, dw1, dw2, ga, bq, bv, gf, scale = results(
        n, nf, lay.hpd, dw, pieces, sums, whole)
    ga, bq, bv, gf = (v.reshape(-1)[:rows] for v in (ga, bq, bv, gf))
    return layer_out[None], grad_x[None], ga, dwq, bq, dwk, dwv, bv, scale, dwo, gf, dw1, dw2


def solution(mesh):
    whole, vector, matrix = P("fsdp", "ctx", None), P("fsdp"), P("fsdp", None)
    return jax.shard_map(
        functools.partial(local, mesh.shape["ctx"], mesh.shape["fsdp"]),
        mesh=mesh,
        in_specs=(
            whole, whole, matrix, P(), vector, matrix, vector, matrix, matrix, vector, vector,
            matrix, vector, matrix, matrix,
        ),
        out_specs=(
            whole, whole, vector, matrix, vector, matrix, matrix, vector, vector, matrix, vector,
            matrix, matrix,
        ),
        check_vma=False,
    )
```

```python
import functools
import math

import jax
import jax.numpy as jnp
from jax import lax
from jax.experimental import pallas as pl
from jax.experimental.pallas import tpu as pltpu
from jax.sharding import PartitionSpec as P

H = 16
HD = 80
BLK = 128
D = 1280
EPS = 1e-06
LOG2E = 1.442695041
NEG = -1e30
MESH = pl.DeviceIdType.MESH
F32 = jnp.float32
BF16 = jnp.bfloat16
VMEM = pltpu.VMEM
MIB = 1 << 20

NN = (((1,), (0,)), ((), ()))
NT = (((1,), (1,)), ((), ()))
TN = (((0,), (0,)), ((), ()))


def dot(left, right, dims=NN):
    return lax.dot_general(left, right, dims, preferred_element_type=F32)


def al(value, multiple):
    return pl.multiple_of(value, multiple)


def in_vmem():
    return pl.BlockSpec(memory_space=pltpu.VMEM)


def in_smem():
    return pl.BlockSpec(memory_space=pltpu.SMEM)


def in_any():
    return pl.BlockSpec(memory_space=pl.ANY)


def cost(microseconds):
    return pl.CostEstimate(flops=0, bytes_accessed=int(microseconds * 3.0e6), transcendentals=0)


class Place:
    def __init__(self, n, nf):
        self.n, self.nf = n, nf
        self.c = lax.axis_index("ctx")
        self.f = lax.axis_index("fsdp")
        self.zlen = n // 4
        self.z, self.y, self.core = self.c // 4, (self.c // 2) % 2, self.c % 2
        self.twin = self.idx(self.z, self.y, 1 - self.core)
        self.ypeer = self.idx(self.z, 1 - self.y, self.core)
        self.targets = (
            self.idx(self.z + 1, self.y, self.core), self.idx(self.z - 1, self.y, self.core),
            self.ypeer, self.twin,
        )
        self.guards = (self.z < self.zlen - 1, self.z > 0, None, None)
        self.fpeers = [(self.f + s) % nf for s in range(1, nf)]
        self.fsources = [(self.f + nf - s) % nf for s in range(1, nf)]

    def idx(self, z, y, core):
        return (z * 2 + y) * 2 + core

    def level(self, k):
        if k == 0:
            return [(self.z, None, 0)]
        return [
            (self.z + k, self.z + k < self.zlen, 1),
            (self.z - k, self.z - k >= 0, -1),
        ]

    def greet_neighbours(self):
        barrier = pltpu.get_barrier_semaphore()
        for target, guard in zip(self.targets, self.guards):
            when(guard, lambda target=target: pl.semaphore_signal(
                barrier, inc=1, device_id=(target, self.f), device_id_type=MESH))
        for peer in self.fpeers:
            pl.semaphore_signal(barrier, inc=1, device_id=(self.c, peer), device_id_type=MESH)
        ends = jnp.minimum(self.z, 1) + jnp.minimum(self.zlen - 1 - self.z, 1)
        pl.semaphore_wait(barrier, 1 + self.nf + ends)

    def greet_all(self, with_fsdp):
        barrier = pltpu.get_barrier_semaphore()
        for s in range(1, self.n):
            pl.semaphore_signal(
                barrier, inc=1, device_id=(self.c ^ s, self.f), device_id_type=MESH)
        if with_fsdp:
            for peer in self.fpeers:
                pl.semaphore_signal(barrier, inc=1, device_id=(self.c, peer), device_id_type=MESH)
        pl.semaphore_wait(barrier, self.n - 1 + (self.nf - 1 if with_fsdp else 0))


def when(guard, body):
    if guard is None:
        body()
    else:
        pl.when(guard)(body)


class Spread:
    def __init__(self, place, buf, send_sem, recv_sem, pieces, wide=(), own=None, own_sem=None):
        self.wide = wide
        self.p, self.buf, self.send_sem, self.recv_sem, self.pieces = place, buf, send_sem, recv_sem, pieces
        self.own, self.own_sem = own, own_sem

    def copy(self, way, origin, i, src=None):
        where = self.buf.at[origin, i]
        return pltpu.make_async_remote_copy(
            src_ref=where if src is None else src, dst_ref=where,
            send_sem=self.send_sem.at[way, origin, i], recv_sem=self.recv_sem.at[origin, i],
            device_id=(self.p.targets[way], self.p.f), device_id_type=MESH,
        )

    def send(self, way, origin, i):
        when(self.p.guards[way], lambda: self.copy(way, origin, i).start())

    def arrive(self, origin, i):
        self.copy(3, origin, i).wait_recv()

    def keep(self, i):
        return pltpu.make_async_copy(self.own(i), self.buf.at[self.p.c, i], self.own_sem.at[i])

    def start(self, i):
        src = self.own(i) if self.own else None
        for way in range(4):
            when(self.p.guards[way], lambda way=way: self.copy(way, self.p.c, i, src).start())
        if self.own:
            self.keep(i).start()

    def chain(self, k, i):
        p = self.p
        for zz, guard, sign in p.level(k):
            def body(zz=zz, sign=sign):
                origin = p.idx(zz, p.y, p.core)
                self.arrive(origin, i)
                self.send(1 if sign == 1 else 0, origin, i)
                when(self.crosses(zz, i), lambda: self.send(2, origin, i))
                self.send(3, origin, i)
            when(guard, body)

    def crosses(self, zz, i):
        return (zz > 0) & (zz < self.p.zlen - 1) if i in self.wide else None

    def both_chains(self, zz, sign, i, act):
        if i in self.wide:
            p, origin = self.p, self.p.idx(zz, 1 - self.p.y, self.p.core)
            for way, end, signs in ((0, 0, (0, -1)), (1, p.zlen - 1, (0, 1))):
                if sign in signs:
                    pl.when((zz == end) & p.guards[way])(lambda way=way: act(way, origin, i))

    def pair(self, k, i):
        p = self.p
        for zz, guard, sign in p.level(k):
            def body(zz=zz, sign=sign):
                origin = p.idx(zz, 1 - p.y, p.core)
                self.arrive(origin, i)
                self.both_chains(zz, sign, i, lambda way, o, i: self.copy(way, o, i).start())
                self.send(3, origin, i)
            when(guard, body)

    def from_twin(self, zz, pieces=None):
        p = self.p
        for yy in (p.y, 1 - p.y):
            for i in range(self.pieces) if pieces is None else pieces:
                self.arrive(p.idx(zz, yy, 1 - p.core), i)

    def drain(self):
        p = self.p
        for i in range(self.pieces):
            if self.own:
                self.keep(i).wait()
            for way in range(4):
                when(p.guards[way], lambda way=way, i=i: self.copy(way, p.c, i).wait_send())
            for k in range(p.zlen):
                for zz, guard, sign in p.level(k):
                    def body(zz=zz, sign=sign, k=k, i=i):
                        if k:
                            origin = p.idx(zz, p.y, p.core)
                            on = 1 if sign == 1 else 0
                            when(p.guards[on], lambda: self.copy(on, origin, i).wait_send())
                            when(self.crosses(zz, i), lambda: self.copy(2, origin, i).wait_send())
                            self.copy(3, origin, i).wait_send()
                        self.both_chains(zz, sign, i, lambda way, o, i: self.copy(way, o, i).wait_send())
                        self.copy(3, p.idx(zz, 1 - p.y, p.core), i).wait_send()
                    when(guard, body)


class Reduce:
    def __init__(self, place, mine, result, acc, xrecv, yrecv, zsend, zrecv, sems):
        self.p, self.mine, self.result, self.acc = place, mine, result, acc
        self.xrecv, self.yrecv, self.zsend, self.zrecv = xrecv, yrecv, zsend, zrecv
        (self.xs, self.xr, self.ys, self.yr, self.zs, self.zr) = sems
        self.height = acc.shape[0] // place.zlen
        self.width = D // 2
        zlen = place.zlen
        ends = []
        for k in range(zlen // 2):
            ends += [zlen - 1 - k, k]
        self.order = ends

    @staticmethod
    def scratch(nf, zlen, height):
        dma = pltpu.SemaphoreType.DMA
        peers = max(nf - 1, 1)
        piece = VMEM((zlen, height // zlen, D // 2), BF16)
        return [
            VMEM((height // zlen, D // 2), BF16), VMEM((height, D), BF16), VMEM((peers, height, D), BF16),
            piece, piece, piece,
            dma((peers, zlen, 2)), dma((peers, zlen, 2)), dma((zlen,)), dma((zlen,)),
            dma((zlen,)), dma((zlen,)),
        ]

    def at(self, piece, side):
        return (
            pl.ds(al(piece * self.height, 16), self.height),
            pl.ds(al(side * self.width, 128), self.width),
        )

    def remote(self, src, dst, send, recv, c, f):
        return pltpu.make_async_remote_copy(
            src_ref=src, dst_ref=dst, send_sem=send, recv_sem=recv,
            device_id=(c, f), device_id_type=MESH,
        )

    def x_copy(self, s, peer, piece, turn):
        side = (self.p.y + 1 + turn) % 2
        where = self.at(piece, side)
        return self.remote(
            self.mine.at[peer].at[where], self.xrecv.at[s].at[where],
            self.xs.at[s, piece, turn], self.xr.at[s, piece, turn], self.p.c, peer,
        )

    def start_x(self, t):
        for turn in range(2):
            for s, peer in enumerate(self.p.fpeers):
                self.x_copy(s, peer, self.order[t], turn).start()

    def add(self, dst, terms, count=None):
        count = count or self.height
        step = 48 if count % 48 == 0 else 16
        @pl.loop(0, count // step)
        def _(t):
            at = pl.ds(al(t * step, 16), step)
            total = terms[0][at, :].astype(F32)
            for term in terms[1:]:
                total = total + term[at, :].astype(F32)
            dst[at, :] = total.astype(BF16)

    def sum_x(self, piece, turn):
        side = (self.p.y + 1 + turn) % 2
        where = self.at(piece, side)
        terms = [self.mine.at[self.p.f].at[where]]
        for s, peer in enumerate(self.p.fpeers):
            self.x_copy(s, peer, piece, turn).wait_recv()
            terms.append(self.xrecv.at[s].at[where])
        self.add(self.acc.at[where], terms)

    def y_copy(self, piece):
        src = self.acc.at[self.at(piece, 1 - self.p.y)]
        return self.remote(
            src, self.yrecv.at[piece], self.ys.at[piece], self.yr.at[piece], self.p.ypeer, self.p.f)

    def z_copy(self, piece, slot):
        p = self.p
        return self.remote(
            self.zsend.at[piece], self.zrecv.at[slot], self.zs.at[piece], self.zr.at[slot],
            p.idx(piece, p.y, p.core), p.f)

    def xy(self, t):
        piece = self.order[t]
        self.sum_x(piece, 0)
        self.y_copy(piece).start()
        self.sum_x(piece, 1)

    def after_y(self, t):
        p, piece = self.p, self.order[t]
        self.y_copy(piece).wait_recv()
        self.add(self.zsend.at[piece], [self.acc.at[self.at(piece, p.y)], self.yrecv.at[piece]])
        pl.when(p.z != piece)(lambda: self.z_copy(piece, p.z).start())

    def last(self):
        p = self.p
        terms = [self.zsend.at[p.z]]
        for k in range(1, p.zlen):
            other = lax.rem(p.z + k, p.zlen)
            self.z_copy(0, other).wait_recv()
            terms.append(self.zrecv.at[other])
        self.add(self.result, terms)

    def drain(self):
        p = self.p
        for piece in self.order:
            for turn in range(2):
                for s, peer in enumerate(p.fpeers):
                    self.x_copy(s, peer, piece, turn).wait_send()
            self.y_copy(piece).wait_send()
            pl.when(p.z != piece)(lambda piece=piece: self.z_copy(piece, p.z).wait_send())


class Loads:
    def __init__(self, sems):
        self.sems, self.copies = sems, []

    def start(self, src, dst):
        copy = pltpu.make_async_copy(src, dst, self.sems.at[len(self.copies)])
        self.copies.append(copy)
        copy.start()
        return copy

    def wait(self):
        for copy in self.copies:
            copy.wait()


class Swap:
    def __init__(self, place, src, dst, send_sem, recv_sem, own_sem):
        self.p, self.src, self.dst = place, src, dst
        self.send_sem, self.recv_sem, self.own_sem = send_sem, recv_sem, own_sem

    def copy(self, s, block):
        p = self.p
        return pltpu.make_async_remote_copy(
            src_ref=self.src(p.c ^ s), dst_ref=self.dst(block),
            send_sem=self.send_sem.at[s], recv_sem=self.recv_sem.at[s],
            device_id=(p.c ^ s, p.f), device_id_type=MESH,
        )

    def own(self):
        return pltpu.make_async_copy(self.src(self.p.c), self.dst(self.p.c), self.own_sem)

    def start(self):
        for s in range(1, self.p.n):
            self.copy(s, self.p.c).start()
        self.own().start()

    def wait(self):
        self.own().wait()
        for s in range(1, self.p.n):
            self.copy(s, self.p.c ^ s).wait_recv()

    def drain(self):
        for s in range(1, self.p.n):
            self.copy(s, self.p.c).wait_send()


def seq_start(ends, base, token):
    start = jnp.zeros_like(token)
    for e in ends:
        start = jnp.where(e - base <= token, jnp.maximum(start, e - base), start)
    return start


def read_ends(lengths_ref):
    ends, total = [], jnp.int32(0)
    for i in range(lengths_ref.shape[1]):
        total = total + lengths_ref[0, i]
        ends.append(total)
    return ends


def pad_rows(block):
    return jnp.concatenate([block, jnp.zeros((BLK - HD, block.shape[1]), block.dtype)], axis=0)


class Layout:
    def __init__(self, n, total_blocks):
        self.n = n
        self.hpd = 2 * H // n
        self.half_blocks = total_blocks // 2
        self.size = self.half_blocks * BLK
        self.rows = self.hpd * self.size
        self.tile = 512

    def half(self, i):
        return i if self.hpd == 2 else lax.axis_index("ctx") % 2

    def within(self, deal_ref, d, u):
        return deal_ref[2 * d + self.half(u)] & (self.half_blocks - 1)

    def base(self, unit):
        return self.half(unit) * self.size if self.hpd == 1 else unit * self.size


WIDE = 256


def over_columns(body):
    @pl.loop(0, D // WIDE)
    def _(j):
        body(pl.ds(al(j * WIDE, WIDE), WIDE))


def token_rows(
    x_ref, cot_ref, oswap, rows_ref, weights, w_loads,
    out_ref, dh_ref, gt_ref, ot, bt, zt, gb, du, dg2_ref,
    o_rows, hidden, nh, b, up, z, db, wide, stage,
):
    wo, w1, w2 = weights
    hpd = oswap.shape[1]
    for i in range(2):
        for h in range(H):
            ot[pl.ds(h * HD, HD), pl.ds(i * BLK, BLK)] = oswap[h, i] if hpd == 2 else oswap[2 * h + i, 0]
    @pl.loop(0, D // WIDE)
    def _(j):
        sl = pl.ds(al(j * WIDE, WIDE), WIDE)
        o_rows[:, sl] = ot[sl, :].astype(F32).T.astype(BF16)
    stage("ot")

    def body(sl):
        hidden[:, sl] = x_ref[:, sl].astype(F32) + dot(o_rows[...], wo[:, sl])
    over_columns(body)
    hid = hidden[...]
    r2 = lax.rsqrt(jnp.mean(hid * hid, axis=-1, keepdims=True) + EPS)
    nh[...] = hid * r2
    b[...] = (nh[...] * rows_ref[3:4, :]).astype(BF16)
    w_loads[1].wait()

    def body(sl):
        u = dot(b[...], w1[:, sl])
        up[:, sl] = u
        act = u * jax.nn.sigmoid(u)
        z[:, sl] = act.astype(BF16)
        zt[sl, :] = act.T.astype(BF16)
        bt[sl, :] = b[:, sl].astype(F32).T.astype(BF16)
    over_columns(body)
    stage("z")
    stage("b")

    w_loads[2].wait()

    def body(sl):
        out_ref[:, sl] = (hidden[:, sl] + dot(z[...], w2[:, sl])).astype(BF16)
        dz = dot(cot_ref[...], w2[sl, :], NT)
        u = up[:, sl]
        sig = jax.nn.sigmoid(u)
        du[:, sl] = (dz * sig * (1.0 + u * (1.0 - sig))).astype(BF16)
    over_columns(body)
    stage("out")
    stage("du")

    def body(sl):
        g = dot(du[...], w1[sl, :], NT)
        db[:, sl] = g * rows_ref[3:4, sl]
        dg2_ref[:, sl] = jnp.sum(g * nh[:, sl], axis=0, keepdims=True)
    over_columns(body)
    scaled = db[...]
    mean = jnp.mean(scaled * nh[...], axis=-1, keepdims=True)
    dh = cot_ref[...].astype(F32) + r2 * (scaled - nh[...] * mean)
    dh_ref[...] = dh
    gb[...] = dh.astype(BF16)
    stage("gb")

    @pl.loop(0, D // WIDE)
    def _(j):
        sl = pl.ds(al(j * WIDE, WIDE), WIDE)
        wide[sl, :] = dot(wo[sl, :], gb[...], NT).astype(BF16)
    for i in range(2):
        for h in range(H):
            gt_ref[h, i] = wide[pl.ds(h * HD, HD), pl.ds(i * BLK, BLK)]
    stage("gt")


def forward_kernel(
    lay, n, nf,
    deal_ref, inv_ref, len_ref, x_ref, cot_ref, *rest,
):
    row_refs, mat_refs, rest = rest[:5], rest[5:11], rest[11:]
    (a_out, mats_out, mine_out, other_out, twin_t, twin_r, rows_out, factor_out, dg2_out, *stored) = rest[: 9 + 12]
    (abuf, norm, windows, wh_ref, whbuf, wht, vec_ref, vecbuf, vcol, stage, wcast, qkv, osend, onat, oswap,
     qraw, qst, kt, vt, kn, ot, lse, layer, dh, gt, ot_t, bt, zt, gb, du,
     o_rows, hidden, nh, b_rows, up, z, db, wide, m_ref, l_ref, acc_ref,
     ag_send, ag_recv, wh_send, wh_recv, vec_send, vec_recv,
     ld_sem, mx_send, mx_recv, ms_send, ms_recv, a_sem, keep_sem, o_send, o_recv, o_own,
     st_sem, w_sem, tt_send, tt_recv, tr_send, tr_recv, win_sem) = rest[9 + 12 :]
    kept = (qraw, qst, kt, vt, kn, ot, lse)
    stores = Loads(st_sem)
    p = Place(n, nf)
    c, f, core, zlen, hpd, tile = p.c, p.f, p.core, p.zlen, lay.hpd, lay.tile
    rows = wh_ref.shape[0]
    part = rows // 2

    head = c * hpd // 2
    first = jnp.minimum(head * HD // BLK * BLK, D - 2 * BLK)
    window_loads = [
        pltpu.make_async_copy(
            mat_refs[3 + m].at[:, pl.ds(al(first, BLK), 2 * BLK)], windows.at[m], win_sem.at[m])
        for m in range(3)
    ]
    for copy in window_loads:
        copy.start()
    vec_ref[...] = jnp.zeros_like(vec_ref)
    vec_ref[4:5, 0 : row_refs[4].shape[0]] = row_refs[4][...].reshape(1, -1)
    for r, ref in enumerate(row_refs[:4]):
        for k in range(ref.shape[0]):
            vec_ref[r : r + 1, k * BLK : (k + 1) * BLK] = ref[k : k + 1, :]
    p.greet_all(True)
    spread = Spread(p, abuf, ag_send, ag_recv, 2)

    for i in range(2):
        abuf[c, i] = x_ref[pl.ds(i * BLK, BLK), :]
    spread.start(0)

    def wh_copy(s, peer):
        return pltpu.make_async_remote_copy(
            src_ref=wh_ref, dst_ref=whbuf.at[pl.ds(al(f * rows, 16), rows)],
            send_sem=wh_send.at[s], recv_sem=wh_recv.at[s],
            device_id=(c, peer), device_id_type=MESH,
        )

    def vec_copy(s, peer):
        return pltpu.make_async_remote_copy(
            src_ref=vec_ref, dst_ref=vecbuf.at[f],
            send_sem=vec_send.at[s], recv_sem=vec_recv.at[s],
            device_id=(c, peer), device_id_type=MESH,
        )

    for s, peer in enumerate(p.fpeers):
        vec_copy(s, peer).start()
    for copy in window_loads:
        copy.wait()
    strip = 128 if rows % 128 == 0 else 32

    @pl.loop(0, rows // strip)
    def _(t):
        at = pl.ds(al(t * strip, 32), strip)
        lane = lax.broadcasted_iota(jnp.int32, (strip, 2 * BLK), 1)
        value = jnp.zeros((strip, 2 * BLK), F32)
        for m in range(3):
            turned = pltpu.roll(windows[m, at, :], lax.rem(m * HD + 2 * BLK - (head * HD - first), 2 * BLK), 1)
            value = jnp.where((lane >= m * HD) & (lane < (m + 1) * HD), turned, value)
        wh_ref[at, :] = value.astype(BF16)

    for s, peer in enumerate(p.fpeers):
        wh_copy(s, peer).start()
    whbuf[pl.ds(al(f * rows, 16), rows), :] = wh_ref[...]
    vecbuf[f] = vec_ref[...]

    shards = mat_refs
    moved = len(mat_refs) - 1
    steps = [(m, 0) for m in range(moved)] + [(m, 1) for m in range(moved)] + [(moved, 0), (moved, 1)]

    def half_of(h):
        return (core + h) % 2

    def load(step):
        m, h = steps[step]
        return pltpu.make_async_copy(
            shards[m].at[pl.ds(al(half_of(h) * part, 16), part)],
            stage.at[step % 2], ld_sem.at[step % 2],
        )

    def mx_copy(m, s, peer, source):
        return pltpu.make_async_remote_copy(
            src_ref=wcast.at[m, core],
            dst_ref=mats_out.at[m, pl.ds(al(source * rows + core * part, 16), part)],
            send_sem=mx_send.at[m, s], recv_sem=mx_recv.at[m, s],
            device_id=(c, peer), device_id_type=MESH,
        )

    def keep_copies(m):
        if m < moved:
            return [
                pltpu.make_async_copy(
                    wcast.at[m, h], mats_out.at[m, pl.ds(al(f * rows + h * part, 16), part)],
                    keep_sem.at[m, h],
                ) for h in range(2)
            ]
        return [
            pltpu.make_async_copy(wcast.at[m, half_of(h)], out, keep_sem.at[m, h])
            for h, out in enumerate((mine_out, other_out))
        ]

    def cast(step):
        m, h = steps[step]
        if step + 1 < len(steps):
            load(step + 1).start()
        load(step).wait()
        chunk = part // 4 if part % 64 == 0 else part
        @pl.loop(0, part // chunk)
        def _(t):
            wcast[m, half_of(h), pl.ds(al(t * chunk, 16), chunk), :] = stage[
                step % 2, pl.ds(al(t * chunk, 16), chunk), :
            ].astype(BF16)
        if h == 0 and m < moved:
            for s, peer in enumerate(p.fpeers):
                mx_copy(m, s, peer, f).start()
        if h == 1:
            for copy in keep_copies(m):
                copy.start()

    load(0).start()
    done = [0]

    def casts(count):
        for step in range(done[0], min(done[0] + count, len(steps))):
            cast(step)
        done[0] += count

    casts(2)

    def gather_events(i, first, last):
        for k in range(first, last):
            if k < zlen:
                spread.chain(k, i)
            spread.pair(k - 1, i)

    def ms_copy(m, s, source, half):
        where = mats_out.at[m, pl.ds(al(source * rows + half * part, 16), part)]
        return pltpu.make_async_remote_copy(
            src_ref=where, dst_ref=where,
            send_sem=ms_send.at[m, s], recv_sem=ms_recv.at[m, s],
            device_id=(p.twin, f), device_id_type=MESH,
        )

    def pass_matrix(m):
        for s, (peer, source) in enumerate(zip(p.fpeers, p.fsources)):
            mx_copy(m, s, peer, source).wait_recv()
            ms_copy(m, s, source, core).start()

    def t_copy(m, source):
        mat = (ot_t, bt, zt)[m]
        return pltpu.make_async_remote_copy(
            src_ref=mat.at[pl.ds(al(source * rows + (1 - core) * part, 16), part)],
            dst_ref=twin_t.at[m, pl.ds(source * part, part)],
            send_sem=tt_send.at[m, source], recv_sem=tt_recv.at[m, source],
            device_id=(p.twin, f), device_id_type=MESH,
        )

    def r_copy(m):
        return pltpu.make_async_remote_copy(
            src_ref=(gb, du, cot_ref)[m], dst_ref=twin_r.at[m], send_sem=tr_send.at[m], recv_sem=tr_recv.at[m],
            device_id=(p.twin, f), device_id_type=MESH,
        )

    own_t, own_r = stored[10], stored[11]

    def to_twin(m, src):
        for source in range(nf):
            t_copy(m, source).start()
            stores.start(
                src.at[pl.ds(al(source * rows + core * part, 16), part)], own_t.at[m, pl.ds(source * part, part)])

    r_copy(2).start()
    gather_events(0, 1, 2)
    casts(1)

    for s, peer in enumerate(p.fpeers):
        vec_copy(s, peer).wait_recv()
        wh_copy(s, peer).wait_recv()
    wht[...] = whbuf[...].astype(F32).T.astype(BF16)
    for source in range(nf):
        rows_out[:, pl.ds(source * rows, rows)] = vecbuf[source, :, 0:rows].astype(BF16).astype(F32)
    share = HD // nf
    shares = [vecbuf[source, 4:5, 0:share].astype(BF16).astype(F32) for source in range(nf)]
    for source in range(nf):
        rows_out[4:5, source * share : (source + 1) * share] = shares[source]
    vcol[...] = rows_out[...].T
    here = pl.ds(al(head * HD, 16), HD)
    bias_q, bias_v = vcol[here, 1:2], vcol[here, 2:3]
    factor = jnp.log(1.0 + jnp.exp(vcol[0:HD, 4:5])) * (LOG2E / math.sqrt(HD))
    factor_out[...] = jnp.broadcast_to(factor, (HD, BLK))

    def a_copy(slot, origin, half):
        return pltpu.make_async_copy(norm.at[slot], a_out.at[pl.ds(origin, 2), half], a_sem.at[slot])

    def project(u, k, first=False):
        half = lay.half(u)
        for zz, guard, _ in p.level(k):
            def body(zz=zz):
                spread.from_twin(zz, [u] if hpd == 2 else range(2))
                for t in range(2):
                    origin = zz * 4 + 2 * t
                    if not first:
                        a_copy(t, origin, half).wait()
                    for i in range(2):
                        x = abuf[origin + i, half].astype(F32)
                        scale = lax.rsqrt(jnp.mean(x * x, axis=-1, keepdims=True) + EPS)
                        norm[t, i] = (x * scale * rows_out[0:1, :]).astype(BF16)
                    a_copy(t, origin, half).start()
                    value = dot(wht[: 3 * HD, :], norm[t].reshape(2 * BLK, D), NT)
                    qkv[origin] = value[:, :BLK]
                    qkv[origin + 1] = value[:, BLK:]
            when(guard, body)

    ends = read_ends(len_ref)

    def attend(u, during):
        base, row0 = lay.base(u), u * lay.size

        @pl.loop(0, lay.half_blocks)
        def _(b):
            cols = pl.ds(al(row0 + b * BLK, BLK), BLK)
            block = qkv[inv_ref[b + lay.half(u) * lay.half_blocks]]
            qr, kr, vr = block[:HD] + bias_q, block[HD : 2 * HD], block[2 * HD :] + bias_v
            qraw[:, cols] = qr
            qst[:, cols] = pad_rows(qr * factor).astype(BF16)
            kt[:, cols] = kr.astype(BF16)
            vt[:, cols] = vr.astype(BF16)
            kn[cols, :] = pad_rows(kr.astype(BF16)).T

        @pl.loop(0, lay.size // tile)
        def _(qi):
            cols = pl.ds(al(row0 + qi * tile, tile), tile)
            t_row = qi * tile + lax.broadcasted_iota(jnp.int32, (1, tile), 1)
            start = seq_start(ends, base, t_row)
            m_ref[...] = jnp.full_like(m_ref, NEG)
            l_ref[...] = jnp.zeros_like(l_ref)
            acc_ref[...] = jnp.zeros_like(acc_ref)

            def visit(key0, count, ahead, causal):
                keys = pl.ds(al(row0 + key0, count), count)
                side = slice(ahead, tile)
                s = dot(kn[keys, :], qst[:, pl.ds(al(row0 + qi * tile + ahead, BLK), tile - ahead)])
                token = key0 + lax.broadcasted_iota(jnp.int32, (count, 1), 0)
                seen = token >= start[:, side]
                if causal:
                    seen = seen & (token <= t_row[:, side])
                s = jnp.where(seen, s, NEG)
                m_old = m_ref[:, side]
                m_new = jnp.maximum(m_old, jnp.max(s, axis=0, keepdims=True))
                prob = jnp.exp(s - m_new)
                shrink = jnp.exp(m_old - m_new)
                m_ref[:, side] = m_new
                l_ref[:, side] = l_ref[:, side] * shrink + jnp.sum(prob, axis=0, keepdims=True)
                acc_ref[:, side] = acc_ref[:, side] * shrink + dot(vt[:, keys], prob.astype(BF16))

            @pl.loop(0, qi)
            def _(j):
                visit(j * tile, tile, 0, False)

            visit(qi * tile, tile // 2, 0, True)
            visit(qi * tile + tile // 2, tile // 2, tile // 2, True)

            out = acc_ref[...] / l_ref[...]
            ot[:, cols] = out
            lse[:, cols] = m_ref[...] + jnp.log(l_ref[...])
            for b in range(tile // BLK):
                onat[qi * (tile // BLK) + b] = out[:, b * BLK : (b + 1) * BLK].astype(BF16)
            for at, event in during:
                pl.when(qi == at)(event)

        @pl.loop(0, n)
        def _(d):
            osend[u, d] = onat[lay.within(deal_ref, d, u)]

        o_swaps[u].start()

    o_swaps = [
        Swap(p, lambda d, u=u: osend.at[u, d], lambda d, u=u: oswap.at[d, u],
             o_send.at[u], o_recv.at[u], o_own.at[u])
        for u in range(hpd)
    ]

    def handed(m):
        for s, (peer, source) in enumerate(zip(p.fpeers, p.fsources)):
            ms_copy(m, s, source, 1 - core).wait_recv()
        for copy in keep_copies(m):
            copy.wait()

    weights = [abuf.at[pl.ds(5 * m, 5)].reshape(5 * 2 * BLK, D) for m in range(3)]
    w_loads = [
        pltpu.make_async_copy(mats_out.at[m], weights[m], w_sem.at[m]) for m in range(3)
    ]

    if hpd == 2:
        project(0, 0, first=True)
        for k in range(2, zlen + 1):
            gather_events(0, k, k + 1)
            if k == 2:
                spread.start(1)
            casts(2)
            project(0, k - 1)
        pass_matrix(0)
        gather_events(1, 1, 2)
        attend(0, [(lay.size // tile // 2, lambda: gather_events(1, 2, 3))])
        pass_matrix(1)
        casts(len(steps))
        project(1, 0)
        for k in range(3, zlen + 1):
            gather_events(1, k, k + 1)
            project(1, k - 2)
        project(1, zlen - 1)
    else:
        spread.start(1)
        casts(len(steps))
        for k in range(1, zlen + 1):
            if k > 1:
                gather_events(0, k, k + 1)
            gather_events(1, k, k + 1)
            project(0, k - 1, first=k == 1)
        pass_matrix(0)
        pass_matrix(1)
    spread.drain()
    for m in range(2):
        handed(m)
        w_loads[m].start()
    attend(hpd - 1, [])
    for src, dst in zip(kept, stored):
        stores.start(src, dst)
    pass_matrix(2)
    handed(2)
    w_loads[2].start()
    for u in range(hpd):
        o_swaps[u].wait()
    w_loads[0].wait()

    def stage(name):
        if name == "ot":
            to_twin(0, ot_t)
        elif name == "z":
            to_twin(2, zt)
        elif name == "b":
            to_twin(1, bt)
        elif name == "out":
            stores.start(layer, stored[7])
        elif name == "du":
            r_copy(1).start()
            stores.start(du, own_r.at[1])
        elif name == "gb":
            r_copy(0).start()
            stores.start(gb, own_r.at[0])
            stores.start(dh, stored[8])
        elif name == "gt":
            stores.start(gt, stored[9])

    token_rows(
        x_ref, cot_ref, oswap, rows_out, weights, w_loads,
        layer, dh, gt, ot_t, bt, zt, gb, du, dg2_out, o_rows, hidden, nh, b_rows, up, z, db, wide, stage)

    for m in range(3, moved):
        pass_matrix(m)
    for m in range(3, moved):
        handed(m)
    for copy in keep_copies(moved):
        copy.wait()
    for m in range(moved):
        for s, (peer, source) in enumerate(zip(p.fpeers, p.fsources)):
            mx_copy(m, s, peer, f).wait_send()
            ms_copy(m, s, source, core).wait_send()
    for m in range(3):
        r_copy(m).wait()
        for source in range(nf):
            t_copy(m, source).wait()
    for s, peer in enumerate(p.fpeers):
        wh_copy(s, peer).wait_send()
        vec_copy(s, peer).wait_send()
    for u in range(hpd):
        o_swaps[u].drain()
    for slot in range(2):
        a_copy(slot, 2 * slot, lay.half(0)).wait()
    stores.wait()


def forward(lay, nf, deal, inverse, lengths, x, cot, vectors, mats):
    n, hpd, total = lay.n, lay.hpd, lay.rows
    rows, tok, count = mats[0].shape[0], x.shape[0], len(mats)
    dma = pltpu.SemaphoreType.DMA
    peers = max(nf - 1, 1)
    half = ((rows // 2, D), BF16)
    kept = [
        ((HD, total), F32), ((BLK, total), BF16), ((HD, total), BF16), ((HD, total), BF16), ((total, BLK), BF16),
        ((HD, total), F32), ((1, total), F32),
    ]
    plain, turned, wide = ((tok, D), BF16), ((D, tok), BF16), ((tok, D), F32)
    made = [plain, wide, ((H, 2, HD, BLK), BF16), turned, turned, turned, plain, plain]
    shared = ((3, D // 2, tok), BF16)
    results = made[:3] + [shared, ((2, tok, D), BF16)]
    outs = [
        ((n, 2, BLK, D), BF16), ((count - 1, nf * rows, D), BF16), half, half, shared, ((3, tok, D), BF16),
        ((8, D), F32), ((HD, BLK), F32), ((1, D), F32),
    ] + kept + results
    places = [in_any()] * 6 + [in_vmem()] * 3 + [in_any()] * (len(kept) + len(results))
    moves = dma((count - 1, peers))
    return pl.pallas_call(
        functools.partial(forward_kernel, lay, n, nf),
        out_shape=tuple(jax.ShapeDtypeStruct(*out) for out in outs),
        in_specs=[in_smem()] * 3 + [in_vmem()] * (2 + len(vectors)) + [in_any()] * count,
        out_specs=tuple(places),
        scratch_shapes=[
            VMEM((n, 2, BLK, D), BF16),
            VMEM((2, 2, BLK, D), BF16),
            VMEM((3, rows, 2 * BLK), F32),
            VMEM((rows, 2 * BLK), BF16),
            VMEM((nf * rows, 2 * BLK), BF16),
            VMEM((2 * BLK, nf * rows), BF16),
            VMEM((8, -(-rows // BLK) * BLK), F32),
            VMEM((nf, 8, -(-rows // BLK) * BLK), F32),
            VMEM((D, 8), F32),
            VMEM((2, rows // 2, D), F32),
            VMEM((count, 2, rows // 2, D), BF16),
            VMEM((n, 3 * HD, BLK), F32),
            VMEM((hpd, n, HD, BLK), BF16),
            VMEM((lay.half_blocks, HD, BLK), BF16),
            VMEM((n, hpd, HD, BLK), BF16),
        ] + [VMEM(*item) for item in kept + made] + [
            VMEM(*plain), VMEM(*wide), VMEM(*wide), VMEM(*plain), VMEM(*wide), VMEM(*plain), VMEM(*wide),
            VMEM(*turned),
            VMEM((1, lay.tile), F32), VMEM((1, lay.tile), F32), VMEM((HD, lay.tile), F32),
            dma((4, n, 2)), dma((n, 2)), dma((peers,)), dma((peers,)), dma((peers,)), dma((peers,)),
            dma((2,)), moves, moves, moves, moves,
            dma((2,)), dma((count, 2)), dma((hpd, n)), dma((hpd, n)), dma((hpd,)),
            dma((len(kept) + 6 + 3 * nf,)), dma((3,)), dma((3, nf)), dma((3, nf)), dma((3,)), dma((3,)),
            dma((3,)),
        ],
        compiler_params=pltpu.CompilerParams(
            collective_id=0, has_side_effects=True, vmem_limit_bytes=61 * MIB
        ),
        cost_estimate=cost(100),
        name="forward",
    )(deal, inverse, lengths, x, cot, *vectors, *mats)


VEC_ROWS = 24


def backward_kernel(
    lay, n, nf,
    deal_ref, inv_ref, len_ref, gt, c_ref, g1_ref, dg2_ref,
    own_t, own_r, twin_t, twin_r, cot_in,
    qraw_in, qst_in, kt_in, vt_in, kn_in, ot_in, lse_in,
    a_ref, mats_ref, mine_ref, other_ref, x_in, dh_in,
    gx_out, dw_out, fw_out, vec_out, xw_out, tw_out,
    big, sums, wide, abuf, qraw, qst, kt, vt, kn, ot, lse, x_ref, dh_ref,
    qn, vn, don, dost, delta, dk, dv, dqt, natural, part_sums, left, back, dw, dwsend, dwrecv, dwown, vx, vsum, vall,
    ld_sem, do_send, do_recv, do_own, dq_send, dq_recv, dq_own, xw_send, xw_recv, tg_send, tg_recv, a_sem,
    x_send, x_recv, own_sem, ag_send, ag_recv, fg_send, fg_recv, v_send, v_recv, u_send, u_recv,
    *rest,
):
    p = Place(n, nf)
    c, f, zlen, hpd, tile = p.c, p.f, p.zlen, lay.hpd, lay.tile
    dob, reduce_scratch = rest[:hpd], rest[hpd:]
    rows = D // nf
    part = rows // 2
    loads = Loads(ld_sem)
    flat = 3 * part
    deep = 4 * BLK

    def left_rows(m, source):
        return pl.ds(al(3 * deep + m * nf * part + source * part, 16), part)

    def right_rows(m):
        return pl.ds(m * deep, deep)

    ffn_loads = []
    for m in range(3):
        at = pl.ds(3 * deep + m * nf * part, nf * part)
        ffn_loads += [
            loads.start(own_t.at[m], big.at[at, pl.ds(0, 2 * BLK)]),
            loads.start(twin_t.at[m], big.at[at, pl.ds(2 * BLK, 2 * BLK)]),
            loads.start(own_r.at[m] if m < 2 else cot_in, big.at[pl.ds(m * deep, 2 * BLK)]),
            loads.start(twin_r.at[m], big.at[pl.ds(m * deep + 2 * BLK, 2 * BLK)]),
        ]
    att_loads = [
        loads.start(src, dst) for src, dst in zip(
            (qraw_in, qst_in, kt_in, vt_in, kn_in, ot_in, lse_in), (qraw, qst, kt, vt, kn, ot, lse))
    ]
    row_loads = [loads.start(x_in, x_ref), loads.start(dh_in, dh_ref)]
    p.greet_all(True)

    do_swaps = [
        Swap(p, lambda d, u=u: gt.at[d, u], lambda d, u=u: dob[u].at[d],
             do_send.at[u], do_recv.at[u], do_own.at[u])
        for u in range(hpd)
    ]
    for swap in do_swaps:
        swap.start()

    def xw_copy(s, peer):
        return pltpu.make_async_remote_copy(
            src_ref=mine_ref, dst_ref=xw_out.at[s], send_sem=xw_send.at[s], recv_sem=xw_recv.at[s],
            device_id=(c, peer), device_id_type=MESH,
        )

    def tg_copy(s):
        return pltpu.make_async_remote_copy(
            src_ref=xw_out.at[s], dst_ref=tw_out.at[s], send_sem=tg_send.at[s], recv_sem=tg_recv.at[s],
            device_id=(p.twin, f), device_id_type=MESH,
        )

    height = sums.shape[1]
    if height > flat:
        for source in range(nf):
            sums[source, flat:, :] = jnp.zeros((height - flat, D), BF16)
    for copy in ffn_loads:
        copy.wait()
    reduce = Reduce(p, sums, *reduce_scratch[:6], reduce_scratch[6:])

    def weight_grads(source):
        for m in range(3):
            @pl.loop(0, D // WIDE)
            def _(j):
                sl = pl.ds(al(j * WIDE, WIDE), WIDE)
                sums[source, pl.ds(m * part, part), sl] = dot(
                    big[left_rows(m, source), 0:deep], big[right_rows(m), sl]).astype(BF16)

    for peer in p.fpeers:
        weight_grads(peer)
    reduce.start_x(0)
    reduce.start_x(1)

    w_loads = []


    def load_w(src, source, half):
        at = pl.ds(al(2 * D + source * rows + half * part, 16), part)
        w_loads.append(loads.start(src, big.at[at]))

    def own_weight_grads():
        weight_grads(f)
        for m in range(2):
            w_loads.append(loads.start(mats_ref.at[3 + m], big.at[pl.ds(m * D, D)]))
        load_w(mine_ref, f, p.core)
        load_w(other_ref, f, 1 - p.core)

    for copy in att_loads:
        copy.wait()
    ends = read_ends(len_ref)
    part_sums[...] = jnp.zeros_like(part_sums)
    step = 8
    steps = [(u, q) for u in range(hpd) for q in range(n // step)]

    def a_copy(k):
        u, q = steps[k]
        half = lay.half(u)
        return pltpu.make_async_copy(
            a_ref.at[pl.ds(q * step, step), half], abuf.at[k % 2].reshape(step, BLK, D), a_sem.at[k % 2])

    def weights_of_head(k):
        u, q = steps[k]
        a_copy(k).wait()
        if k + 1 < len(steps):
            a_copy(k + 1).start()
        @pl.loop(0, D // WIDE)
        def _(j):
            sl = pl.ds(al(j * WIDE, WIDE), WIDE)
            term = dot(left[u, :, q * step * BLK : (q + 1) * step * BLK], abuf[k % 2, :, sl])
            dw[:, sl] = term if k == 0 else dw[:, sl] + term

    def gradient_swap(u):
        return Swap(
            p, lambda d: left.at[u, :, pl.ds(al(d * BLK, BLK), BLK)], lambda d: back.at[u, d],
            dq_send.at[u], dq_recv.at[u], dq_own.at[u])

    a_copy(0).start()
    for u in range(hpd):
        base = lay.base(u)
        row0 = u * lay.size

        @pl.loop(0, lay.half_blocks)
        def _(b):
            cols = pl.ds(al(b * BLK, BLK), BLK)
            here = pl.ds(al(row0 + b * BLK, BLK), BLK)
            qn[cols, :] = qst[:, here].T
            vn[cols, :] = pad_rows(vt[:, here]).T
            dk[cols, :] = jnp.zeros((BLK, BLK), F32)
            dv[cols, :] = jnp.zeros((BLK, BLK), F32)

        do_swaps[u].wait()

        @pl.loop(0, lay.half_blocks)
        def _(b):
            cols = pl.ds(al(b * BLK, BLK), BLK)
            here = pl.ds(al(row0 + b * BLK, BLK), BLK)
            block = dob[u][inv_ref[b + lay.half(u) * lay.half_blocks]].astype(F32)
            delta[:, cols] = jnp.sum(block * ot[:, here], axis=0, keepdims=True)
            block = pad_rows(block.astype(BF16))
            dost[:, cols] = block
            don[cols, :] = block.T

        @pl.loop(0, lay.size // tile)
        def _(qi):
            t_row = qi * tile + lax.broadcasted_iota(jnp.int32, (1, tile), 1)
            start = seq_start(ends, base, t_row)
            dqt[:, pl.ds(al(qi * tile, tile), tile)] = jnp.zeros((HD, tile), F32)

            def visit(key0, count, ahead, causal):
                side = slice(ahead, tile)
                cols = pl.ds(al(qi * tile + ahead, BLK), tile - ahead)
                here = pl.ds(al(row0 + qi * tile + ahead, BLK), tile - ahead)
                keys = pl.ds(al(key0, count), count)
                keys_here = pl.ds(al(row0 + key0, count), count)
                s = dot(kn[keys_here, :], qst[:, here])
                token = key0 + lax.broadcasted_iota(jnp.int32, (count, 1), 0)
                seen = token >= start[:, side]
                if causal:
                    seen = seen & (token <= t_row[:, side])
                prob = jnp.exp(jnp.where(seen, s - lse[:, here], NEG))
                dp = dot(vn[keys, :], dost[:, cols])
                ds = (prob * (dp - delta[:, cols])).astype(BF16)
                dv[keys, :] += dot(prob.astype(BF16), don[cols, :])
                dk[keys, :] += dot(ds, qn[cols, :])
                dqt[:, cols] += dot(kt[:, keys_here], ds)

            @pl.loop(0, qi)
            def _(j):
                visit(j * tile, tile, 0, False)

            visit(qi * tile, tile // 2, 0, True)
            visit(qi * tile + tile // 2, tile // 2, tile // 2, True)

            if u == hpd - 1:
                @pl.when(qi == lay.size // tile // 2 - 1)
                def _():
                    if hpd == 2:
                        reduce.xy(1)
                        reduce.after_y(0)

        @pl.loop(0, lay.half_blocks)
        def _(b):
            cols = pl.ds(al(b * BLK, BLK), BLK)
            here = pl.ds(al(row0 + b * BLK, BLK), BLK)
            dqs = dqt[:, cols]
            dq = (dqs * c_ref[...]).astype(BF16)
            dkt = dk[cols, :].astype(BF16).T[:HD]
            dvt = dv[cols, :].astype(BF16).T[:HD]
            natural[b, 0:HD] = dq
            natural[b, HD : 2 * HD] = dkt
            natural[b, 2 * HD : 3 * HD] = dvt
            part_sums[0, :HD] += dqs * qraw[:, here]
            part_sums[1, :HD] += dq.astype(F32)
            part_sums[2, :HD] += dvt.astype(F32)

        @pl.loop(0, n)
        def _(d):
            left[u, :, pl.ds(al(d * BLK, BLK), BLK)] = natural[lay.within(deal_ref, d, u)]

        if u == 0:
            own_weight_grads()
        if u < hpd - 1:
            reduce.xy(0)
            reduce.start_x(2)
        gradient_swap(u).start()
    if hpd == 1:
        reduce.xy(0)
        reduce.xy(1)
        reduce.start_x(2)
        reduce.after_y(0)

    for k in range(len(steps)):
        weights_of_head(k)
    for source in range(nf):
        dwsend[source] = dw[:, source * rows : (source + 1) * rows].astype(BF16)

    def x_copy(s, peer):
        return pltpu.make_async_remote_copy(
            src_ref=dwsend.at[peer], dst_ref=dwrecv.at[s],
            send_sem=x_send.at[s], recv_sem=x_recv.at[s],
            device_id=(c, peer), device_id_type=MESH,
        )

    for s, peer in enumerate(p.fpeers):
        x_copy(s, peer).start()
    for t in range(3, zlen):
        reduce.start_x(t)
    for s, peer in enumerate(p.fpeers):
        xw_copy(s, peer).start()

    pieces = fw_out.shape[1]
    result = reduce_scratch[0]
    cut = height // zlen // pieces
    spread = Spread(p, dw_out, ag_send, ag_recv, 3, (), lambda i: dwown.at[i], own_sem.at[0])
    spread2 = Spread(
        p, fw_out, fg_send, fg_recv, pieces, (0, 2, 4), lambda i: result.at[pl.ds(i * cut, cut)], own_sem.at[1])

    def start_spread():
        total = dwsend[f].astype(F32)
        for s, peer in enumerate(p.fpeers):
            x_copy(s, peer).wait_recv()
            total = total + dwrecv[s].astype(F32)
        for i in range(3):
            dwown[i] = total[i * HD : (i + 1) * HD].astype(BF16)
            spread.start(i)

    def spread_events(k):
        if 1 <= k < zlen:
            for i in range(3):
                spread.chain(k, i)
                spread.pair(k - 1, i)

    def gather_rows():
        for u in range(hpd):
            gradient_swap(u).wait()
        for m in range(3):
            for i in range(2):
                for h in range(H):
                    block = back[i, h] if hpd == 2 else back[0, 2 * h + i]
                    wide[m, pl.ds(h * HD, HD), pl.ds(i * BLK, BLK)] = block[m * HD : (m + 1) * HD]
        for copy in w_loads[:2]:
            copy.wait()

    def row_grads(mats, more):
        @pl.loop(0, D // WIDE)
        def _(j):
            at = pl.ds(al(j * WIDE, WIDE), WIDE)
            total = None
            for m in mats:
                term = dot(big[pl.ds(al(m * D + j * WIDE, WIDE), WIDE), :], wide[m])
                total = term if total is None else total + term
            total = total.T
            gx_out[:, at] = gx_out[:, at] + total if more else total

    for t in range(2, zlen):
        reduce.after_y(t - 1)
        reduce.xy(t)
        if t == 2:
            start_spread()
        else:
            spread_events(t - 2)
    gather_rows()
    row_grads((0, 1), False)
    reduce.after_y(zlen - 1)
    for k in range(zlen - 2, zlen):
        spread_events(k)
    reduce.last()
    for i in range(pieces):
        spread2.start(i)
    for i in range(3):
        spread.pair(zlen - 1, i)

    for s, (peer, source) in enumerate(zip(p.fpeers, p.fsources)):
        xw_copy(s, peer).wait_recv()
        tg_copy(s).start()
        load_w(xw_out.at[s], source, p.core)
    for copy in row_loads:
        copy.wait()
    for s, source in enumerate(p.fsources):
        tg_copy(s).wait_recv()
        load_w(tw_out.at[s], source, 1 - p.core)
    for copy in w_loads[2:]:
        copy.wait()
    row_grads((2,), True)
    for i in range(pieces):
        spread2.chain(1, i)
        spread2.pair(0, i)
    x = x_ref[...].astype(F32)
    r1 = lax.rsqrt(jnp.mean(x * x, axis=-1, keepdims=True) + EPS)
    na = x * r1
    da = gx_out[...]
    dg1 = jnp.sum(da * na, axis=0, keepdims=True)
    for r in range(D // BLK):
        vx[f, r : r + 1, :] = dg1[:, r * BLK : (r + 1) * BLK]
        vx[f, D // BLK + r : D // BLK + r + 1, :] = dg2_ref[:, r * BLK : (r + 1) * BLK]
    for r in range(3):
        vx[f, 20 + r : 21 + r, :] = jnp.sum(part_sums[r].T, axis=0, keepdims=True)
    vx[f, 23:24, :] = jnp.zeros((1, BLK), F32)

    def v_copy(s, peer, source):
        return pltpu.make_async_remote_copy(
            src_ref=vx.at[f], dst_ref=vx.at[source],
            send_sem=v_send.at[s], recv_sem=v_recv.at[s],
            device_id=(c, peer), device_id_type=MESH,
        )

    for s, peer in enumerate(p.fpeers):
        v_copy(s, peer, f).start()
    scaled = da * g1_ref[0:1, :]
    mean = jnp.mean(scaled * na, axis=-1, keepdims=True)
    gx_out[...] = dh_ref[...] + r1 * (scaled - na * mean)
    for s, (peer, source) in enumerate(zip(p.fpeers, p.fsources)):
        v_copy(s, peer, source).wait_recv()
    vsum[...] = jnp.sum(vx[...], axis=0)
    vall[c] = vsum[...]

    def u_copy(s, block):
        return pltpu.make_async_remote_copy(
            src_ref=vsum, dst_ref=vall.at[block],
            send_sem=u_send.at[s], recv_sem=u_recv.at[s],
            device_id=(c ^ s, f), device_id_type=MESH,
        )

    for s in range(1, n):
        u_copy(s, c).start()
    for k in range(2, zlen):
        for i in range(pieces):
            spread2.chain(k, i)
            spread2.pair(k - 1, i)
    for i in range(pieces):
        spread2.pair(zlen - 1, i)
    for k in range(zlen):
        for zz, guard, _ in p.level(k):
            when(guard, lambda zz=zz: spread.from_twin(zz))
            when(guard, lambda zz=zz: spread2.from_twin(zz))
    for s in range(1, n):
        u_copy(s, c ^ s).wait_recv()
    vec_out[...] = vall[...]

    for u in range(hpd):
        do_swaps[u].drain()
        gradient_swap(u).drain()
    spread.drain()
    spread2.drain()
    reduce.drain()
    for s, peer in enumerate(p.fpeers):
        xw_copy(s, peer).wait_send()
        tg_copy(s).wait_send()
        x_copy(s, peer).wait_send()
        v_copy(s, peer, f).wait_send()
    for s in range(1, n):
        u_copy(s, c).wait_send()


def backward(lay, nf, deal, inverse, lengths, gt, factor, g1, dg2, ffn_parts, cot, kept, tokens, mats, mine, other, x, dh):
    n, hpd, rows, size = lay.n, lay.hpd, lay.rows, lay.size
    dma = pltpu.SemaphoreType.DMA
    shard = D // nf
    part = shard // 2
    zlen = n // 4
    height = -(-3 * part // (16 * zlen)) * 16 * zlen
    piece = height // zlen
    pieces = 5 if piece % 80 == 0 else 1
    peers = max(nf - 1, 1)
    tok = x.shape[0]
    return pl.pallas_call(
        functools.partial(backward_kernel, lay, n, nf),
        out_shape=(
            jax.ShapeDtypeStruct((tok, D), F32),
            jax.ShapeDtypeStruct((n, 3, HD, shard), BF16),
            jax.ShapeDtypeStruct((n, pieces, piece // pieces, D // 2), BF16),
            jax.ShapeDtypeStruct((n, VEC_ROWS, BLK), F32),
            jax.ShapeDtypeStruct((peers, part, D), BF16),
            jax.ShapeDtypeStruct((peers, part, D), BF16),
        ),
        in_specs=[in_smem()] * 3 + [in_vmem()] * 4 + [in_any()] * 18,
        out_specs=(in_vmem(), in_any(), in_any(), in_vmem(), in_any(), in_any()),
        scratch_shapes=[
            VMEM((3 * D, D), BF16), VMEM((nf, height, D), BF16), VMEM((3, D, tok), BF16),
            VMEM((2, 8 * BLK, D), BF16),
            VMEM((HD, rows), F32), VMEM((BLK, rows), BF16), VMEM((HD, rows), BF16), VMEM((HD, rows), BF16),
            VMEM((rows, BLK), BF16), VMEM((HD, rows), F32), VMEM((1, rows), F32),
            VMEM((tok, D), BF16), VMEM((tok, D), F32),
            VMEM((size, BLK), BF16), VMEM((size, BLK), BF16), VMEM((size, BLK), BF16), VMEM((BLK, size), BF16),
            VMEM((1, size), F32), VMEM((size, BLK), F32), VMEM((size, BLK), F32), VMEM((HD, size), F32),
            VMEM((size // BLK, 3 * HD, BLK), BF16), VMEM((3, BLK, BLK), F32), VMEM((hpd, 3 * HD, n * BLK), BF16),
            VMEM((hpd, n, 3 * HD, BLK), BF16), VMEM((3 * HD, D), F32), VMEM((nf, 3 * HD, shard), BF16),
            VMEM((peers, 3 * HD, shard), BF16), VMEM((3, HD, shard), BF16),
            VMEM((nf, VEC_ROWS, BLK), F32), VMEM((VEC_ROWS, BLK), F32), VMEM((n, VEC_ROWS, BLK), F32),
            dma((25 + 2 * nf,)), dma((hpd, n)), dma((hpd, n)), dma((hpd,)), dma((hpd, n)), dma((hpd, n)), dma((hpd,)),
            dma((peers,)), dma((peers,)), dma((peers,)), dma((peers,)), dma((2,)),
            dma((peers,)), dma((peers,)), dma((2, 5)), dma((4, n, 3)), dma((n, 3)), dma((4, n, pieces)), dma((n, pieces)),
            dma((peers,)), dma((peers,)), dma((n,)), dma((n,)),
        ] + [VMEM((n, HD, BLK), BF16)] * hpd + Reduce.scratch(nf, zlen, height),
        compiler_params=pltpu.CompilerParams(
            collective_id=2, has_side_effects=True, vmem_limit_bytes=62 * MIB
        ),
        cost_estimate=cost(130),
        name="backward",
    )(deal, inverse, lengths, gt, factor, g1, dg2, *ffn_parts, cot, *kept, tokens, mats, mine, other, x, dh)


def results_kernel(
    n, nf, hpd,
    dw_in, pieces_in, vec_ref, scale_ref,
    q_out, k_out, v_out, o_out, u_out, d_out, ga_out, bq_out, bv_out, gf_out, sc_out,
    dw, pieces, wide, full, tail, ld_sem, st_sem,
):
    f = lax.axis_index("fsdp")
    rows = dw.shape[3]
    part = rows // 2
    zlen, height = pieces.shape[0], pieces.shape[3]
    loads = Loads(ld_sem)
    piece_load = loads.start(pieces_in, pieces)
    dw_load = loads.start(dw_in, dw)
    stores = Loads(st_sem)

    piece_load.wait()
    for m, out in enumerate((o_out, u_out, d_out)):
        for core in range(2):
            for y in range(2):
                for z in range(zlen):
                    first, last = max(m * part, z * height), min((m + 1) * part, (z + 1) * height)
                    if first < last:
                        at = core * part + first - m * part
                        full[m, at : at + last - first, y * (D // 2) : (y + 1) * (D // 2)] = pieces[
                            z, y, core, first - z * height : last - z * height, :
                        ].astype(F32)
        stores.start(full.at[m], out)

    dw_load.wait()
    for m, out in enumerate((q_out, k_out, v_out)):
        for h in range(H):
            if hpd == 2:
                block = dw[h, m].astype(F32)
            else:
                block = dw[2 * h, m].astype(F32) + dw[2 * h + 1, m].astype(F32)
            wide[pl.ds(h * HD, HD), :] = block
        for j in range(D // WIDE):
            full[3 + m, :, j * WIDE : (j + 1) * WIDE] = wide[j * WIDE : (j + 1) * WIDE, :].T
        stores.start(full.at[3 + m], out)

    tail[...] = jnp.zeros_like(tail)
    total = jnp.sum(vec_ref[...], axis=0)
    for r in range(D // BLK):
        tail[0:1, r * BLK : (r + 1) * BLK] = total[r : r + 1]
        tail[1:2, r * BLK : (r + 1) * BLK] = total[D // BLK + r : D // BLK + r + 1]
    for r in (21, 22):
        for h in range(H):
            if hpd == 2:
                row = vec_ref[h, r : r + 1, 0:HD]
            else:
                row = vec_ref[2 * h, r : r + 1, 0:HD] + vec_ref[2 * h + 1, r : r + 1, 0:HD]
            tail[r - 19 : r - 18, h * HD : (h + 1) * HD] = row
    scale = scale_ref[4:5, 0:BLK]
    tail[4:5, 0:BLK] = total[20:21] * (1.0 / (1.0 + jnp.exp(-scale))) * (LOG2E / math.sqrt(HD))
    share = HD // nf
    for source in range(nf):
        @pl.when(f == source)
        def _():
            for r, out in enumerate((ga_out, gf_out, bq_out, bv_out)):
                for k in range(out.shape[0]):
                    at = source * rows + k * BLK
                    out[k : k + 1, :] = tail[r : r + 1, at : at + BLK]
            sc_out[...] = tail[4:5, source * share : (source + 1) * share].reshape(share)
    stores.wait()


def results(n, nf, hpd, dw, pieces, vectors, scale):
    rows = dw.shape[3]
    zlen = n // 4
    height = pieces.shape[1] * pieces.shape[2]
    pieces = pieces.reshape(zlen, 2, 2, height, D // 2)
    dma = pltpu.SemaphoreType.DMA
    mat, row = jax.ShapeDtypeStruct((rows, D), F32), jax.ShapeDtypeStruct((-(-rows // BLK), BLK), F32)
    return pl.pallas_call(
        functools.partial(results_kernel, n, nf, hpd),
        out_shape=(mat,) * 6 + (row,) * 4 + (jax.ShapeDtypeStruct((HD // nf,), F32),),
        in_specs=[in_any(), in_any(), in_vmem(), in_vmem()],
        out_specs=(in_any(),) * 6 + (in_vmem(),) * 5,
        scratch_shapes=[
            VMEM(dw.shape, BF16), VMEM(pieces.shape, BF16), VMEM((D, rows), F32), VMEM((6, rows, D), F32),
            VMEM((8, D + 2 * BLK), F32), dma((2,)), dma((6,)),
        ],
        compiler_params=pltpu.CompilerParams(vmem_limit_bytes=60 * MIB),
        cost_estimate=cost(11),
        name="results",
    )(dw, pieces, vectors, scale)


def local(
    n, nf, tokens, cotangent, lengths, deal, gain_attn, query_weight, query_bias, key_weight,
    value_weight, value_bias, query_scale, proj_weight, gain_ffn, up_weight, down_weight,
):
    lay = Layout(n, deal.shape[0])
    rows = query_weight.shape[0]
    x, cot = tokens[0], cotangent[0]

    def in_rows(v):
        return jnp.pad(v, (0, -v.shape[0] % BLK)).reshape(-1, BLK)

    vectors = tuple(in_rows(v) for v in (gain_attn, query_bias, value_bias, gain_ffn)) + (query_scale,)
    blocks = jnp.arange(deal.shape[0], dtype=jnp.int32)
    inverse = jnp.sum(jnp.where(deal[None, :] == blocks[:, None], blocks[None, :] // 2, 0), axis=1, dtype=jnp.int32)

    a_all, mats, mine, other, twin_t, twin_r, whole, factor_col, dg2, *stored = forward(
        lay, nf, deal, inverse, lengths, x, cot, vectors,
        (proj_weight, up_weight, down_weight, query_weight, key_weight, value_weight),
    )
    kept, (layer_out, dh, gt, own_t, own_r) = stored[:7], stored[7:]
    grad_x, dw, pieces, sums, *_ = backward(
        lay, nf, deal, inverse, lengths, gt.reshape(n, lay.hpd, HD, BLK), factor_col, whole, dg2,
        (own_t, own_r, twin_t, twin_r), cot, kept, a_all, mats, mine, other, x, dh,
    )
    dwq, dwk, dwv, dwo, dw1, dw2, ga, bq, bv, gf, scale = results(
        n, nf, lay.hpd, dw, pieces, sums, whole)
    ga, bq, bv, gf = (v.reshape(-1)[:rows] for v in (ga, bq, bv, gf))
    return layer_out[None], grad_x[None], ga, dwq, bq, dwk, dwv, bv, scale, dwo, gf, dw1, dw2


def solution(mesh):
    whole, vector, matrix = P("fsdp", "ctx", None), P("fsdp"), P("fsdp", None)
    return jax.shard_map(
        functools.partial(local, mesh.shape["ctx"], mesh.shape["fsdp"]),
        mesh=mesh,
        in_specs=(
            whole, whole, matrix, P(), vector, matrix, vector, matrix, matrix, vector, vector,
            matrix, vector, matrix, matrix,
        ),
        out_specs=(
            whole, whole, vector, matrix, vector, matrix, matrix, vector, vector, matrix, vector,
            matrix, matrix,
        ),
        check_vma=False,
    )
```
